32 devices in a mesh: row: 8 (over y, x, core), col: 4 (over z).
Axes of the slice: x: 2, y: 2, z: 4, core: 2. Of those that a mesh axis runs over, the one named last changes fastest.
Arguments:
- grad_out: bfloat16 [65536, 256], P(('row', 'col')), may hold values from -6 to 6
- preact: bfloat16 [65536, 256], P(('row', 'col')), may hold values from -6 to 6
- features: bfloat16 [65536, 256], P(('col', 'row')), may hold values from -6 to 6
- weight: bfloat16 [256, 256], replicated, may hold values from -0.375 to 0.375
- tiles: bfloat16 [8, 4, 320, 128, 128], P('row', 'col'), may hold values from -0.099609375 to 0.099609375
- tile_rows: int32 [8, 4, 320], P('row', 'col'), may hold values from 0 to 63
- tile_cols: int32 [8, 4, 320], P('row', 'col'), may hold values from 0 to 127
- live_counts: int32 [8, 4], P('row', 'col'), may hold values from 80 to 320, as said below
Outputs:
- grad_features: bfloat16 [65536, 256], P(('col', 'row'))
- grad_weight: float32 [256, 256], replicated
The draws below stay inside these ranges and needn't reach their ends.
Inputs may be any that keep to these rules, and one draw needn't show every extreme that they name: `live_counts`: some block holds exactly 320 live tiles in every draw.
All inputs are finite; a program needn't handle non-finite values.
Results may differ from the reference program's by a relative error of at most 0.02.
Values may be sent and summed in bfloat16 or wider, within the bound.
No kernel may reach another device: no remote copies, remote signals or barrier semaphores. Data moves between devices by JAX's collectives and lax.ppermute only.
A program may use at most 192 MiB of HBM per device.

```python
import jax
import jax.numpy as jnp
from jax import lax

F = 256
ND = 2048
KT = 320
TILE = 128
NODES = 65536
RT = 64
CT = 128
N_ROW = 8
N_COL = 4


def draw_live_counts(key, part):
    counts = jax.random.randint(key, (N_ROW * N_COL,), KT // 4, KT + 1)
    chosen = jax.random.randint(jax.random.fold_in(key, 7), (), 0, N_ROW * N_COL)
    counts = counts.at[chosen].set(KT)
    return counts.reshape(N_ROW, N_COL).astype(jnp.int32)


def with_ends(drawn, key, low, top_value):
    longest = drawn.shape.index(max(drawn.shape))
    spots = []
    for shift in (0, 1):
        where = [jax.random.randint(jax.random.fold_in(key, axis), (), 0, length) for axis, length in enumerate(drawn.shape)]
        where[longest] = (where[longest] + shift) % drawn.shape[longest]
        spots.append(tuple(where))
    return drawn.at[spots[0]].set(low).at[spots[1]].set(top_value)


def block_scale(key, dims, split, smallest, high):
    level, own = 1.0, jax.random.fold_in(key, 6)
    for dim, parts in split:
        draws = jnp.exp(jax.random.uniform(jax.random.fold_in(own, dim), (parts,), jnp.float32, smallest / len(split), high / len(split)))
        level = level * jnp.repeat(draws, dims[dim] // parts).reshape([-1 if axis == dim else 1 for axis in range(len(dims))])
    return level


def noise(key, shape, scale, bound, cuts=(), held_as=jnp.bfloat16):
    result = jax.random.normal(key, shape, jnp.float32) * scale
    if len(cuts) > 0:
        result = block_scale(key, shape, cuts, -0.22, 0.18) * result
    return jnp.clip(result, min=-bound, max=bound).astype(held_as)


def setup_inputs(seed: int = 0) -> dict:
    arg_keys = jax.random.split(jax.random.key(seed), 9)
    grad_out = noise(arg_keys[0], (NODES, F), 1.0, 6.0, ((0, 32),))
    preact = noise(arg_keys[1], (NODES, F), 1.0, 6.0, ((0, 32),))
    features = noise(arg_keys[2], (NODES, F), 1.0, 6.0, ((0, 32),))
    weight = noise(arg_keys[3], (F, F), F ** -0.5, 0.375)
    tiles = noise(arg_keys[4], (N_ROW, N_COL, KT, TILE, TILE), 0.018, 0.099609375, ((0, 8), (1, 4)))
    tile_rows = with_ends(jax.random.randint(arg_keys[5], (N_ROW, N_COL, KT), 0, RT), jax.random.fold_in(arg_keys[5], 1), 0, RT - 1).astype(jnp.int32)
    tile_cols = with_ends(jax.random.randint(arg_keys[6], (N_ROW, N_COL, KT), 0, CT), jax.random.fold_in(arg_keys[6], 1), 0, CT - 1).astype(jnp.int32)
    live_counts = draw_live_counts(jax.random.fold_in(arg_keys[8], 71), 0)
    return dict(grad_out=grad_out, preact=preact, features=features, weight=weight, tiles=tiles, tile_rows=tile_rows, tile_cols=tile_cols, live_counts=live_counts)


def reference(grad_out, preact, features, weight, tiles, tile_rows, tile_cols, live_counts):
    masked = jnp.where(preact > 0, grad_out, jnp.zeros_like(grad_out)).astype(jnp.bfloat16)
    row_len = ND * N_COL
    col_len = ND * N_ROW
    accum = jnp.zeros((NODES, F), jnp.float32)

    def one_block(index, accum):
        brow = index // N_COL
        bcol = index % N_COL
        rows_here = lax.dynamic_slice_in_dim(masked, (brow * row_len).astype(jnp.int32), row_len, 0)
        rows_tiled = rows_here.reshape(RT, 128, F)
        tile_blk = tiles[brow, bcol]
        gathered = rows_tiled[tile_rows[brow, bcol]]
        prod = jnp.einsum('kab,kaf->kbf', tile_blk.astype(jnp.float32), gathered.astype(jnp.float32))
        live = jnp.arange(KT, dtype=jnp.int32) < live_counts[brow, bcol]
        prod = jnp.where(live[:, None, None], prod, jnp.zeros_like(prod))
        partial_value = jnp.zeros((CT, 128, F), jnp.float32).at[tile_cols[brow, bcol]].add(prod)
        partial_value = partial_value.reshape(col_len, F).astype(jnp.bfloat16).astype(jnp.float32)
        start = (bcol * col_len).astype(jnp.int32)
        current = lax.dynamic_slice_in_dim(accum, start, col_len, 0)
        return lax.dynamic_update_slice_in_dim(accum, current + partial_value, start, 0)

    accum = lax.fori_loop(0, N_ROW * N_COL, one_block, accum)
    colgrad_b = accum.astype(jnp.bfloat16)
    grad_features = jnp.dot(colgrad_b, weight.T, preferred_element_type=jnp.float32).astype(jnp.bfloat16)
    grad_weight = jnp.dot(features.T, colgrad_b, preferred_element_type=jnp.float32)
    return grad_features, grad_weight
```

```python
import functools

import jax
import jax.numpy as jnp
from jax import lax
from jax.experimental import pallas as pl
from jax.experimental.pallas import tpu as pltpu
from jax.sharding import PartitionSpec as P

SIDE = 128
UNROLL = 8
PREP_GROUP = 32
VMEM_BYTES = 60 * 1024 * 1024


def prep_kernel(order_ref, tiles_ref, out_ref, t_in, t_out, in_sem, out_sem):
    groups = t_in.shape[0] // PREP_GROUP
    loads = [
        pltpu.make_async_copy(
            tiles_ref.at[pl.ds(g * PREP_GROUP, PREP_GROUP)], t_in.at[pl.ds(g * PREP_GROUP, PREP_GROUP)], in_sem.at[g]
        )
        for g in range(groups)
    ]
    for load in loads:
        load.start()
    for load in loads:
        load.wait()
    stores = []
    for g in range(groups):

        def one(step, carry, g=g):
            for u in range(4):
                k = g * PREP_GROUP + step * 4 + u
                t_out[k] = t_in[order_ref[k]].T
            return carry

        lax.fori_loop(0, PREP_GROUP // 4, one, 0)
        store = pltpu.make_async_copy(
            t_out.at[pl.ds(g * PREP_GROUP, PREP_GROUP)], out_ref.at[pl.ds(g * PREP_GROUP, PREP_GROUP)], out_sem.at[g]
        )
        store.start()
        stores.append(store)
    for store in stores:
        store.wait()


def prep(order, tile_stack):
    slots = tile_stack.shape[0]
    groups = slots // PREP_GROUP
    return pl.pallas_call(
        prep_kernel,
        out_shape=jax.ShapeDtypeStruct(tile_stack.shape, tile_stack.dtype),
        grid_spec=pltpu.PrefetchScalarGridSpec(
            num_scalar_prefetch=1,
            grid=(),
            in_specs=[pl.BlockSpec(memory_space=pl.ANY)],
            out_specs=pl.BlockSpec(memory_space=pl.ANY),
            scratch_shapes=[
                pltpu.VMEM(tile_stack.shape, tile_stack.dtype),
                pltpu.VMEM(tile_stack.shape, tile_stack.dtype),
                pltpu.SemaphoreType.DMA((groups,)),
                pltpu.SemaphoreType.DMA((groups,)),
            ],
        ),
        compiler_params=pltpu.CompilerParams(vmem_limit_bytes=VMEM_BYTES),
        cost_estimate=pl.CostEstimate(flops=0, bytes_accessed=2 * tile_stack.size * 2, transcendentals=0),
        name="sort_tiles",
    )(order, tile_stack)


def spmm_kernel(n_pieces, rows_ref, cols_ref, same_ref, count_ref, *refs):
    pieces = refs[:n_pieces]
    tiles_ref, send_ref, keep_ref, m_vmem, t_vmem, o_vmem, total_ref, piece_sem, tile_sem, out_sem = refs[n_pieces:]
    nodes = pieces[0].shape[0]
    slots = t_vmem.shape[0]
    groups = slots // PREP_GROUP
    half = send_ref.shape[0]
    width = o_vmem.shape[1]
    piece_copies = [
        pltpu.make_async_copy(piece, m_vmem.at[pl.ds(p * nodes, nodes)], piece_sem.at[p]) for p, piece in enumerate(pieces)
    ]
    tile_copies = [
        pltpu.make_async_copy(
            tiles_ref.at[pl.ds(g * PREP_GROUP, PREP_GROUP)], t_vmem.at[pl.ds(g * PREP_GROUP, PREP_GROUP)], tile_sem.at[g]
        )
        for g in range(groups)
    ]
    for copy in piece_copies:
        copy.start()
    for copy in tile_copies:
        copy.start()

    def zero(step, carry):
        o_vmem[pl.ds(pl.multiple_of(step * 1024, 1024), 1024), :] = jnp.zeros((1024, width), o_vmem.dtype)
        return carry

    lax.fori_loop(0, 2 * half // 1024, zero, 0)
    for copy in piece_copies:
        copy.wait()
    count = count_ref[0]

    def add_slots(step, carry):
        prods = []
        total = total_ref[...]
        for u in range(UNROLL):
            k = step * UNROLL + u
            block = m_vmem[pl.ds(pl.multiple_of(rows_ref[k] * SIDE, SIDE), SIDE), :]
            prods.append(jnp.dot(t_vmem[k], block, preferred_element_type=jnp.float32))
        for u in range(UNROLL):
            k = step * UNROLL + u
            total = prods[u] + jnp.where(same_ref[k] == 1, total, jnp.zeros_like(total))
            o_vmem[pl.ds(pl.multiple_of(cols_ref[k] * SIDE, SIDE), SIDE), :] = total.astype(o_vmem.dtype)
        total_ref[...] = total
        return carry

    steps = (count + UNROLL - 1) // UNROLL
    per_group = PREP_GROUP // UNROLL
    total_ref[...] = jnp.zeros_like(total_ref)
    for g in range(groups):
        tile_copies[g].wait()
        low = jnp.minimum(steps, g * per_group)
        high = jnp.minimum(steps, (g + 1) * per_group)
        lax.fori_loop(low, high, add_slots, 0)
    out_copies = [
        pltpu.make_async_copy(o_vmem.at[pl.ds(0, half)], send_ref, out_sem.at[0]),
        pltpu.make_async_copy(o_vmem.at[pl.ds(half, half)], keep_ref, out_sem.at[1]),
    ]
    for copy in out_copies:
        copy.start()
    for copy in out_copies:
        copy.wait()


def spmm(rows, cols, same, count, pieces, tiles, n_row):
    nodes, width = pieces[0].shape
    slots = tiles.shape[0]
    groups = slots // PREP_GROUP
    half = n_row // 2 * nodes
    out = jax.ShapeDtypeStruct((half, width), jnp.bfloat16)
    return pl.pallas_call(
        functools.partial(spmm_kernel, len(pieces)),
        out_shape=(out, out),
        grid_spec=pltpu.PrefetchScalarGridSpec(
            num_scalar_prefetch=4,
            grid=(),
            in_specs=[pl.BlockSpec(memory_space=pl.ANY)] * (len(pieces) + 1),
            out_specs=[pl.BlockSpec(memory_space=pl.ANY)] * 2,
            scratch_shapes=[
                pltpu.VMEM((len(pieces) * nodes, width), jnp.bfloat16),
                pltpu.VMEM((slots, SIDE, SIDE), jnp.bfloat16),
                pltpu.VMEM((2 * half + SIDE, width), jnp.bfloat16),
                pltpu.VMEM((SIDE, width), jnp.float32),
                pltpu.SemaphoreType.DMA((len(pieces),)),
                pltpu.SemaphoreType.DMA((groups,)),
                pltpu.SemaphoreType.DMA((2,)),
            ],
        ),
        compiler_params=pltpu.CompilerParams(vmem_limit_bytes=VMEM_BYTES),
        cost_estimate=pl.CostEstimate(
            flops=2 * slots * SIDE * SIDE * width,
            bytes_accessed=2 * (slots * SIDE * SIDE + len(pieces) * nodes * width + 2 * half * width),
            transcendentals=0,
        ),
        name="spmm",
    )(rows, cols, same, count, *pieces, tiles)


def xor_permute(value, axis, mask):
    size = lax.axis_size(axis)
    return lax.ppermute(value, axis, [(i, i ^ mask) for i in range(size)])


def tree_sum(values):
    while len(values) > 1:
        values = [a + b for a, b in zip(values[::2], values[1::2])]
    return values[0]


def add_bf16(a, b):
    return (a.astype(jnp.float32) + b.astype(jnp.float32)).astype(jnp.bfloat16)


def reduce_scatter(keep, recv, bits, row):
    for pos in bits:
        axis = [b for b in sorted(bits, reverse=True) if b in reduce_scatter_left(bits, pos)].index(pos)
        mine = (row >> pos) & 1

        def pick(which, axis=axis):
            return add_bf16(
                lax.dynamic_index_in_dim(keep, which, axis, keepdims=False),
                lax.dynamic_index_in_dim(recv, which, axis, keepdims=False),
            )

        sent = pick(1 - mine)
        keep = pick(mine)
        recv = xor_permute(sent, "row", 1 << pos)
    return keep.astype(jnp.float32) + recv.astype(jnp.float32)


def reduce_scatter_left(bits, pos):
    return bits[bits.index(pos):]


def body(grad_out, preact, features, weight, tiles, tile_rows, tile_cols, live_counts):
    nodes, width = grad_out.shape
    n_row, n_col = lax.axis_size("row"), lax.axis_size("col")
    row, col = lax.axis_index("row"), lax.axis_index("col")
    slots = tiles.shape[2]
    per_dev = nodes // SIDE
    n_chunks = 2
    cw = width // n_chunks

    pieces = []
    for h in range(n_chunks):
        cols_h = slice(h * cw, (h + 1) * cw)
        masked = jnp.where(preact[:, cols_h] > 0, grad_out[:, cols_h], jnp.zeros_like(grad_out[:, cols_h]))
        pieces.append([masked] + [xor_permute(masked, "col", k) for k in range(1, n_col)])

    count = live_counts.reshape(1)
    row_index = tile_rows.reshape(slots)
    col_index = tile_cols.reshape(slots)
    row_pos = ((row_index // per_dev) ^ col) * per_dev + row_index % per_dev
    target = col_index // per_dev
    own_core = 1 - ((target & 1) ^ (row & 1))
    col_pos = (own_core * (n_row // 2) + target // 2) * per_dev + col_index % per_dev
    ids = jnp.arange(slots, dtype=jnp.int32)
    col_pos = jnp.where(ids < count, col_pos, n_row * per_dev)
    before = (col_pos[None, :] < col_pos[:, None]) | ((col_pos[None, :] == col_pos[:, None]) & (ids[None, :] < ids[:, None]))
    rank = jnp.sum(before.astype(jnp.int32), axis=1)
    hit = rank[None, :] == ids[:, None]

    def permuted(values):
        return jnp.sum(jnp.where(hit, values[None, :], 0), axis=1)

    order = permuted(ids)
    rows_sorted = permuted(row_pos)
    cols_sorted = permuted(col_pos)
    same = jnp.concatenate([jnp.zeros((1,), jnp.int32), (cols_sorted[1:] == cols_sorted[:-1]).astype(jnp.int32)])
    tiles_sorted = prep(order, tiles.reshape(slots, SIDE, SIDE))

    bits = list(range(1, n_row.bit_length() - 1))
    summed, terms = [], []
    for h in range(n_chunks):
        send, keep = spmm(rows_sorted, cols_sorted, same, count, pieces[h], tiles_sorted, n_row)
        recv = xor_permute(send, "row", 1)
        lead = (2,) * len(bits)
        keep = keep.reshape(lead + (nodes, cw))
        recv = recv.reshape(lead + (nodes, cw))
        first = reduce_scatter(keep[..., : nodes // 2, :], recv[..., : nodes // 2, :], bits, row)
        second = reduce_scatter(keep[..., nodes // 2 :, :], recv[..., nodes // 2 :, :], bits[::-1], row)
        colgrad = jnp.concatenate([first, second], axis=0).astype(jnp.bfloat16)
        summed.append(colgrad)
        term = lax.dot_general(features, colgrad, (((0,), (0,)), ((), ())), preferred_element_type=jnp.float32)
        term = term.astype(jnp.bfloat16)
        term = term.astype(jnp.float32) + xor_permute(term, "row", 1).astype(jnp.float32)
        for axis, masks in (("row", range(2, n_row, 2)), ("col", range(1, n_col))):
            term = term.astype(jnp.bfloat16)
            parts = [term] + [xor_permute(term, axis, m) for m in masks]
            term = tree_sum([p.astype(jnp.float32) for p in parts])
        terms.append(term)
    colgrad = jnp.concatenate(summed, axis=1)
    grad_features = lax.dot_general(
        colgrad, weight, (((1,), (1,)), ((), ())), preferred_element_type=jnp.float32
    ).astype(jnp.bfloat16)
    grad_weight = jnp.concatenate(terms, axis=1)
    return (grad_features, grad_weight)


def solution(mesh):
    in_specs = (
        P(("row", "col"), None),
        P(("row", "col"), None),
        P(("col", "row"), None),
        P(),
        P("row", "col", None, None, None),
        P("row", "col", None),
        P("row", "col", None),
        P("row", "col"),
    )
    out_specs = (P(("col", "row"), None), P())
    return jax.shard_map(body, mesh=mesh, in_specs=in_specs, out_specs=out_specs, check_vma=False)
```

```python
import functools

import jax
import jax.numpy as jnp
from jax import lax
from jax.experimental import pallas as pl
from jax.experimental.pallas import tpu as pltpu
from jax.sharding import PartitionSpec as P

SIDE = 128
UNROLL = 8
PREP_GROUP = 32
VMEM_BYTES = 60 * 1024 * 1024


def prep_kernel(order_ref, tiles_ref, out_ref, t_in, t_out, in_sem, out_sem):
    groups = t_in.shape[0] // PREP_GROUP
    loads = [
        pltpu.make_async_copy(
            tiles_ref.at[pl.ds(g * PREP_GROUP, PREP_GROUP)], t_in.at[pl.ds(g * PREP_GROUP, PREP_GROUP)], in_sem.at[g]
        )
        for g in range(groups)
    ]
    for load in loads:
        load.start()
    for load in loads:
        load.wait()
    stores = []
    for g in range(groups):

        def one(step, carry, g=g):
            for u in range(4):
                k = g * PREP_GROUP + step * 4 + u
                t_out[k] = t_in[order_ref[k]].T
            return carry

        lax.fori_loop(0, PREP_GROUP // 4, one, 0)
        store = pltpu.make_async_copy(
            t_out.at[pl.ds(g * PREP_GROUP, PREP_GROUP)], out_ref.at[pl.ds(g * PREP_GROUP, PREP_GROUP)], out_sem.at[g]
        )
        store.start()
        stores.append(store)
    for store in stores:
        store.wait()


def prep(order, tile_stack):
    slots = tile_stack.shape[0]
    groups = slots // PREP_GROUP
    return pl.pallas_call(
        prep_kernel,
        out_shape=jax.ShapeDtypeStruct(tile_stack.shape, tile_stack.dtype),
        grid_spec=pltpu.PrefetchScalarGridSpec(
            num_scalar_prefetch=1,
            grid=(),
            in_specs=[pl.BlockSpec(memory_space=pl.ANY)],
            out_specs=pl.BlockSpec(memory_space=pl.ANY),
            scratch_shapes=[
                pltpu.VMEM(tile_stack.shape, tile_stack.dtype),
                pltpu.VMEM(tile_stack.shape, tile_stack.dtype),
                pltpu.SemaphoreType.DMA((groups,)),
                pltpu.SemaphoreType.DMA((groups,)),
            ],
        ),
        compiler_params=pltpu.CompilerParams(vmem_limit_bytes=VMEM_BYTES),
        cost_estimate=pl.CostEstimate(flops=0, bytes_accessed=2 * tile_stack.size * 2, transcendentals=0),
        name="sort_tiles",
    )(order, tile_stack)


def spmm_kernel(layout, rows_ref, cols_ref, same_ref, info_ref, *refs):
    n_refs = sum(layout)
    refs_left = list(refs[:n_refs])
    pieces = [[refs_left.pop(0) for _ in range(n)] for n in layout]
    tiles_ref, send_ref, keep_ref, m_vmem, t_vmem, o_vmem, total_ref, piece_sem, tile_sem, out_sem = refs[n_refs:]
    nodes = pieces[0][0].shape[0]
    slots = t_vmem.shape[0]
    groups = slots // PREP_GROUP
    half = send_ref.shape[0]
    width = o_vmem.shape[1]
    piece_copies = [
        [pltpu.make_async_copy(ref, m_vmem.at[pl.ds(p * nodes, nodes)], piece_sem.at[p]) for ref in refs_p]
        for p, refs_p in enumerate(pieces)
    ]
    tile_copies = [
        pltpu.make_async_copy(
            tiles_ref.at[pl.ds(g * PREP_GROUP, PREP_GROUP)], t_vmem.at[pl.ds(g * PREP_GROUP, PREP_GROUP)], tile_sem.at[g]
        )
        for g in range(groups)
    ]
    for copies in piece_copies:
        if len(copies) == 1:
            copies[0].start()
        else:
            pl.when(info_ref[1] == 1)(copies[0].start)
            pl.when(info_ref[1] != 1)(copies[1].start)
    for copy in tile_copies:
        copy.start()

    def zero(step, carry):
        o_vmem[pl.ds(pl.multiple_of(step * 1024, 1024), 1024), :] = jnp.zeros((1024, width), o_vmem.dtype)
        return carry

    lax.fori_loop(0, 2 * half // 1024, zero, 0)
    for copies in piece_copies:
        copies[0].wait()
    count = info_ref[0]

    def add_slots(step, carry):
        prods = []
        total = total_ref[...]
        for u in range(UNROLL):
            k = step * UNROLL + u
            block = m_vmem[pl.ds(pl.multiple_of(rows_ref[k] * SIDE, SIDE), SIDE), :]
            prods.append(jnp.dot(t_vmem[k], block, preferred_element_type=jnp.float32))
        for u in range(UNROLL):
            k = step * UNROLL + u
            total = prods[u] + jnp.where(same_ref[k] == 1, total, jnp.zeros_like(total))
            o_vmem[pl.ds(pl.multiple_of(cols_ref[k] * SIDE, SIDE), SIDE), :] = total.astype(o_vmem.dtype)
        total_ref[...] = total
        return carry

    steps = (count + UNROLL - 1) // UNROLL
    per_group = PREP_GROUP // UNROLL
    total_ref[...] = jnp.zeros_like(total_ref)
    for g in range(groups):
        tile_copies[g].wait()
        low = jnp.minimum(steps, g * per_group)
        high = jnp.minimum(steps, (g + 1) * per_group)
        lax.fori_loop(low, high, add_slots, 0)
    out_copies = [
        pltpu.make_async_copy(o_vmem.at[pl.ds(0, half)], send_ref, out_sem.at[0]),
        pltpu.make_async_copy(o_vmem.at[pl.ds(half, half)], keep_ref, out_sem.at[1]),
    ]
    for copy in out_copies:
        copy.start()
    for copy in out_copies:
        copy.wait()


def spmm(rows, cols, same, info, pieces, tiles, n_row):
    nodes, width = pieces[0][0].shape
    slots = tiles.shape[0]
    groups = slots // PREP_GROUP
    half = n_row // 2 * nodes
    out = jax.ShapeDtypeStruct((half, width), jnp.bfloat16)
    return pl.pallas_call(
        functools.partial(spmm_kernel, [len(p) for p in pieces]),
        out_shape=(out, out),
        grid_spec=pltpu.PrefetchScalarGridSpec(
            num_scalar_prefetch=4,
            grid=(),
            in_specs=[pl.BlockSpec(memory_space=pl.ANY)] * (sum(len(p) for p in pieces) + 1),
            out_specs=[pl.BlockSpec(memory_space=pl.ANY)] * 2,
            scratch_shapes=[
                pltpu.VMEM((len(pieces) * nodes, width), jnp.bfloat16),
                pltpu.VMEM((slots, SIDE, SIDE), jnp.bfloat16),
                pltpu.VMEM((2 * half + SIDE, width), jnp.bfloat16),
                pltpu.VMEM((SIDE, width), jnp.float32),
                pltpu.SemaphoreType.DMA((len(pieces),)),
                pltpu.SemaphoreType.DMA((groups,)),
                pltpu.SemaphoreType.DMA((2,)),
            ],
        ),
        compiler_params=pltpu.CompilerParams(vmem_limit_bytes=VMEM_BYTES),
        cost_estimate=pl.CostEstimate(
            flops=2 * slots * SIDE * SIDE * width,
            bytes_accessed=2 * (slots * SIDE * SIDE + len(pieces) * nodes * width + 2 * half * width),
            transcendentals=0,
        ),
        name="spmm",
    )(rows, cols, same, info, *[ref for p in pieces for ref in p], tiles)


def xor_permute(value, axis, mask):
    size = lax.axis_size(axis)
    return lax.ppermute(value, axis, [(i, i ^ mask) for i in range(size)])


def tree_sum(values):
    while len(values) > 1:
        values = [a + b for a, b in zip(values[::2], values[1::2])]
    return values[0]


def gather_first(own):
    return xor_permute(own, "col", 1), xor_permute(own, "col", 2)


def gather_second(own, by_two, n_col):
    ends, middles = [], []
    for low in range(0, n_col, 4):
        ends += [(low + 1, low), (low + 2, low + 3)]
        middles += [(low + 1, low + 2), (low + 2, low + 1)]
    return lax.ppermute(own, "col", middles), lax.ppermute(by_two, "col", ends)


def as_pieces(own, first, second, mid, n_col):
    if n_col == 4:
        return [[own], [first[0]], [first[1]], list(second)]
    pieces = [own, first[0], first[1], jnp.where(mid, second[0], second[1])]
    for high in range(4, n_col, 4):
        pieces += [xor_permute(piece, "col", high) for piece in pieces[:4]]
    return [[piece] for piece in pieces]


def fence(*values):
    return lax.optimization_barrier(values)


def add_f32(a, b):
    return a.astype(jnp.float32) + b.astype(jnp.float32)


def plan_slots(tile_rows, tile_cols, count, row, col, n_row, per_dev):
    slots = tile_rows.shape[0]
    half, quarter = n_row // 2, n_row // 4
    row_pos = ((tile_rows // per_dev) ^ col) * per_dev + tile_rows % per_dev
    away = (tile_cols // per_dev) ^ row
    near, local = away >> 1, tile_cols % per_dev
    upper = local // (per_dev // 2)
    spot = local % (per_dev // 2)
    first_bit = jnp.where(upper == 0, near & 1, near // quarter)
    rest = jnp.where(upper == 0, near >> 1, near % quarter)
    group = (1 - (away & 1)) * 4 + upper * 2 + (1 - first_bit)
    col_pos = (group * quarter + rest) * (per_dev // 2) + spot
    ids = jnp.arange(slots, dtype=jnp.int32)
    col_pos = jnp.where(ids < count, col_pos, n_row * per_dev)
    before = (col_pos[None, :] < col_pos[:, None]) | ((col_pos[None, :] == col_pos[:, None]) & (ids[None, :] < ids[:, None]))
    rank = jnp.sum(before.astype(jnp.int32), axis=1)
    hit = rank[None, :] == ids[:, None]

    def permuted(values):
        return jnp.sum(jnp.where(hit, values[None, :], 0), axis=1)

    order = permuted(ids)
    rows_sorted = permuted(row_pos)
    cols_sorted = permuted(col_pos)
    same = jnp.concatenate([jnp.zeros((1,), jnp.int32), (cols_sorted[1:] == cols_sorted[:-1]).astype(jnp.int32)])
    return order, rows_sorted, cols_sorted, same


def core_sums(keep, recv):
    size = keep.shape[0] // 4
    return [add_f32(keep[g * size : (g + 1) * size], recv[g * size : (g + 1) * size]).astype(jnp.bfloat16) for g in range(4)]


def halve(value, upper, rows):
    blocks = value.shape[0] // rows
    shape = (2, blocks // 2) if upper else (blocks // 2, 2)
    cut = value.reshape(shape + (rows, value.shape[1]))
    if upper:
        sent, kept = cut[1], cut[0]
    else:
        sent, kept = cut[:, 1], cut[:, 0]
    return sent.reshape(-1, value.shape[1]), kept.reshape(-1, value.shape[1])


def exchange_first(sums, bits):
    return xor_permute(sums[0], "row", bits[0]), xor_permute(sums[2], "row", bits[-1])


def exchange_rest(sums, recv, bits, rows):
    done = []
    for upper in (0, 1):
        value = add_f32(sums[2 * upper + 1], recv[upper])
        for bit in (bits[::-1] if upper else bits)[1:]:
            sent, kept = halve(value.astype(jnp.bfloat16), upper, rows)
            value = add_f32(kept, xor_permute(sent, "row", bit))
        done.append(value.astype(jnp.bfloat16))
    return jnp.concatenate(done, axis=0)


def weight_term(features_groups, sums):
    terms = [
        lax.dot_general(f, s, (((0,), (0,)), ((), ())), preferred_element_type=jnp.float32)
        for f, s in zip(features_groups, sums)
    ]
    return tree_sum(terms)


def body(grad_out, preact, features, weight, tiles, tile_rows, tile_cols, live_counts):
    nodes, width = grad_out.shape
    n_row, n_col = lax.axis_size("row"), lax.axis_size("col")
    row, col = lax.axis_index("row"), lax.axis_index("col")
    slots = tiles.shape[2]
    cw = width // 2
    rows = nodes // 2
    bits = [1 << b for b in range(1, n_row.bit_length() - 1)]
    mid = ((col & 3) == 1) | ((col & 3) == 2)
    count = live_counts.reshape(())
    info = jnp.stack([count, mid.astype(jnp.int32)])

    own0, own1 = [
        jnp.where(preact[:, cut] > 0, grad_out[:, cut], jnp.zeros_like(grad_out[:, cut]))
        for cut in (slice(0, cw), slice(cw, width))
    ]
    first0 = gather_first(own0)
    near = [features]
    for bit in bits[:2]:
        near.append(xor_permute(features, "row", bit))
    order, rows_sorted, cols_sorted, same = plan_slots(
        tile_rows.reshape(slots), tile_cols.reshape(slots), count, row, col, n_row, nodes // SIDE
    )
    tiles_sorted = prep(order, tiles.reshape(slots, SIDE, SIDE))
    own0, own1, first0, near, tiles_sorted = fence(own0, own1, first0, near, tiles_sorted)

    second0 = gather_second(own0, first0[1], n_col)
    pieces0 = as_pieces(own0, first0, second0, mid, n_col)
    pieces0, own1, near = fence(pieces0, own1, near)

    first1 = gather_first(own1)
    near.append(xor_permute(near[1], "row", bits[1]))
    for bit in bits[2:]:
        near += [xor_permute(f, "row", bit) for f in near]
    send0, keep0 = spmm(rows_sorted, cols_sorted, same, info, pieces0, tiles_sorted, n_row)
    own1, first1, near, send0, keep0 = fence(own1, first1, near, send0, keep0)

    second1 = gather_second(own1, first1[1], n_col)
    pieces1 = as_pieces(own1, first1, second1, mid, n_col)
    sums0 = core_sums(keep0, xor_permute(send0, "row", 1))
    features_groups = []
    for upper in (0, 1):
        own_bit = (n_row // 4) if upper else 1
        for want in (1, 0):
            parts = [f[upper * rows : (upper + 1) * rows] for q, f in enumerate(near) if (q & own_bit != 0) == want]
            features_groups.append(jnp.concatenate(parts, axis=0))
    pieces1, sums0, features_groups = fence(pieces1, sums0, features_groups)

    recv0 = exchange_first(sums0, bits)
    send1, keep1 = spmm(rows_sorted, cols_sorted, same, info, pieces1, tiles_sorted, n_row)
    sums0, recv0, send1, keep1 = fence(sums0, recv0, send1, keep1)

    colgrad0 = exchange_rest(sums0, recv0, bits, rows)
    term0 = weight_term(features_groups, sums0)
    sums1 = core_sums(keep1, xor_permute(send1, "row", 1))
    colgrad0, term0, sums1 = fence(colgrad0, term0, sums1)

    recv1 = exchange_first(sums1, bits)
    term1 = weight_term(features_groups, sums1)
    term = jnp.concatenate([term0, term1], axis=1).astype(jnp.bfloat16)
    for axis, masks in (("row", [1]), ("col", range(1, n_col)), ("row", range(2, n_row, 2))):
        parts = [term] + [xor_permute(term, axis, m) for m in masks]
        grad_weight = tree_sum([p.astype(jnp.float32) for p in parts])
        term = grad_weight.astype(jnp.bfloat16)
    colgrad1 = exchange_rest(sums1, recv1, bits, rows)
    colgrad = jnp.concatenate([colgrad0, colgrad1], axis=1)
    grad_features = lax.dot_general(
        colgrad, weight, (((1,), (1,)), ((), ())), preferred_element_type=jnp.float32
    ).astype(jnp.bfloat16)
    return (grad_features, grad_weight)


def solution(mesh):
    in_specs = (
        P(("row", "col"), None),
        P(("row", "col"), None),
        P(("col", "row"), None),
        P(),
        P("row", "col", None, None, None),
        P("row", "col", None),
        P("row", "col", None),
        P("row", "col"),
    )
    out_specs = (P(("col", "row"), None), P())
    return jax.shard_map(body, mesh=mesh, in_specs=in_specs, out_specs=out_specs, check_vma=False)
```

```python
import functools

import jax
import jax.numpy as jnp
from jax import lax
from jax.experimental import pallas as pl
from jax.experimental.pallas import tpu as pltpu
from jax.sharding import PartitionSpec as P

SIDE = 128
UNROLL = 4
FLIP_GROUP = 32
FLIP_BYTES = 24 * 1024 * 1024
SPMM_BYTES = 8 * 1024 * 1024


def flip_kernel(tiles_ref, out_ref, t_in, sems):
    slots = t_in.shape[0]
    groups = slots // FLIP_GROUP
    loads = [
        pltpu.make_async_copy(
            tiles_ref.at[pl.ds(g * FLIP_GROUP, FLIP_GROUP)], t_in.at[pl.ds(g * FLIP_GROUP, FLIP_GROUP)], sems.at[g]
        )
        for g in range(groups)
    ]
    for load in loads:
        load.start()
    out_ref[slots] = jnp.zeros((SIDE, SIDE), out_ref.dtype)
    for g in range(groups):
        loads[g].wait()

        def some(step, carry, g=g):
            for u in range(4):
                k = g * FLIP_GROUP + step * 4 + u
                out_ref[k] = t_in[k].T
            return carry

        lax.fori_loop(0, FLIP_GROUP // 4, some, 0)


def flip_tiles(tile_stack):
    slots = tile_stack.shape[0]
    return pl.pallas_call(
        flip_kernel,
        out_shape=jax.ShapeDtypeStruct((slots + 1, SIDE, SIDE), tile_stack.dtype),
        in_specs=[pl.BlockSpec(memory_space=pl.ANY)],
        out_specs=pl.BlockSpec(memory_space=pltpu.VMEM),
        scratch_shapes=[pltpu.VMEM(tile_stack.shape, tile_stack.dtype), pltpu.SemaphoreType.DMA((slots // FLIP_GROUP,))],
        compiler_params=pltpu.CompilerParams(vmem_limit_bytes=FLIP_BYTES),
        cost_estimate=pl.CostEstimate(flops=0, bytes_accessed=4096, transcendentals=0),
        name="flip_tiles",
    )(tile_stack)


def spmm_kernel(layout, tile_at_ref, block_at_ref, out_at_ref, same_ref, info_ref, *refs):
    n_refs = sum(layout)
    refs_left = list(refs[:n_refs])
    pieces = [[refs_left.pop(0) for _ in range(n)] for n in layout]
    tiles_ref, send_ref, keep_ref, m_vmem, total_ref = refs[n_refs:]
    nodes, width = pieces[0][0].shape

    for out_ref in (send_ref, keep_ref):

        def clear(step, carry, out_ref=out_ref):
            out_ref[pl.ds(pl.multiple_of(step * 1024, 1024), 1024), :] = jnp.zeros((1024, width), out_ref.dtype)
            return carry

        lax.fori_loop(0, out_ref.shape[0] // 1024, clear, 0)
    for p, options in enumerate(pieces):

        def take(ref, p=p):
            def some(step, carry):
                at = pl.multiple_of(step * 512, 512)
                m_vmem[pl.ds(pl.multiple_of(p * nodes + at, 512), 512), :] = ref[pl.ds(at, 512), :]
                return carry

            lax.fori_loop(0, nodes // 512, some, 0)

        if len(options) == 1:
            take(options[0])
        else:
            pl.when(info_ref[0] == 1)(functools.partial(take, options[0]))
            pl.when(info_ref[0] != 1)(functools.partial(take, options[1]))

    def block(index):
        return m_vmem[pl.ds(pl.multiple_of(index * SIDE, SIDE), SIDE), :]

    def add_pairs(out_ref, step, carry):
        total = total_ref[...]
        prods = []
        for u in range(UNROLL):
            k = 2 * (step * UNROLL + u)
            left = jnp.concatenate([tiles_ref[tile_at_ref[k]], tiles_ref[tile_at_ref[k + 1]]], axis=1)
            right = jnp.concatenate([block(block_at_ref[k]), block(block_at_ref[k + 1])], axis=0)
            prods.append(jnp.dot(left, right, preferred_element_type=jnp.float32))
        for u in range(UNROLL):
            k = step * UNROLL + u
            total = prods[u] + jnp.where(same_ref[k] == 1, total, jnp.zeros_like(total))
            out_ref[pl.ds(pl.multiple_of(out_at_ref[k] * SIDE, SIDE), SIDE), :] = total.astype(out_ref.dtype)
        total_ref[...] = total
        return carry

    total_ref[...] = jnp.zeros_like(total_ref)
    lax.fori_loop(0, info_ref[1], functools.partial(add_pairs, send_ref), 0)
    lax.fori_loop(info_ref[1], info_ref[2], functools.partial(add_pairs, keep_ref), 0)


def spmm(plan, pieces, tiles, n_row):
    nodes, width = pieces[0][0].shape
    half = n_row // 2 * nodes
    out = jax.ShapeDtypeStruct((half + SIDE, width), jnp.bfloat16)
    n_refs = sum(len(p) for p in pieces)
    return pl.pallas_call(
        functools.partial(spmm_kernel, [len(p) for p in pieces]),
        out_shape=(out, out),
        grid_spec=pltpu.PrefetchScalarGridSpec(
            num_scalar_prefetch=5,
            grid=(),
            in_specs=[pl.BlockSpec(memory_space=pltpu.VMEM)] * (n_refs + 1),
            out_specs=[pl.BlockSpec(memory_space=pltpu.VMEM)] * 2,
            scratch_shapes=[
                pltpu.VMEM((len(pieces) * nodes, width), jnp.bfloat16),
                pltpu.VMEM((SIDE, width), jnp.float32),
            ],
        ),
        compiler_params=pltpu.CompilerParams(vmem_limit_bytes=SPMM_BYTES),
        cost_estimate=pl.CostEstimate(flops=0, bytes_accessed=4096, transcendentals=0),
        name="spmm",
    )(*plan, *[ref for p in pieces for ref in p], tiles)


def xor_permute(value, axis, mask):
    size = lax.axis_size(axis)
    return lax.ppermute(value, axis, [(i, i ^ mask) for i in range(size)])


def tree_sum(values):
    while len(values) > 1:
        values = [a + b for a, b in zip(values[::2], values[1::2])]
    return values[0]


def gather_first(own):
    return xor_permute(own, "col", 1), xor_permute(own, "col", 2)


def gather_second(own, by_two, n_col):
    ends, middles = [], []
    for low in range(0, n_col, 4):
        ends += [(low + 1, low), (low + 2, low + 3)]
        middles += [(low + 1, low + 2), (low + 2, low + 1)]
    return lax.ppermute(own, "col", middles), lax.ppermute(by_two, "col", ends)


def as_pieces(own, first, second, mid, n_col):
    if n_col == 4:
        return [[own], [first[0]], [first[1]], list(second)]
    pieces = [own, first[0], first[1], jnp.where(mid, second[0], second[1])]
    for high in range(4, n_col, 4):
        pieces += [xor_permute(piece, "col", high) for piece in pieces[:4]]
    return [[piece] for piece in pieces]


def fence(*values):
    return lax.optimization_barrier(values)


def add_f32(a, b):
    return a.astype(jnp.float32) + b.astype(jnp.float32)


def plan_slots(tile_rows, tile_cols, count, row, col, mid, n_row, per_dev):
    slots = tile_rows.shape[0]
    half, quarter = n_row // 2, n_row // 4
    row_pos = ((tile_rows // per_dev) ^ col) * per_dev + tile_rows % per_dev
    away = (tile_cols // per_dev) ^ row
    near, local = away >> 1, tile_cols % per_dev
    upper = local // (per_dev // 2)
    spot = local % (per_dev // 2)
    first_bit = jnp.where(upper == 0, near & 1, near // quarter)
    rest = jnp.where(upper == 0, near >> 1, near % quarter)
    group = upper * 2 + (1 - first_bit)
    out_pos = (group * quarter + rest) * (per_dev // 2) + spot
    kept = 1 - (away & 1)
    n_out = half * per_dev
    ids = jnp.arange(slots, dtype=jnp.int32)
    live = ids < count
    key = jnp.where(live, kept * n_out + out_pos, 2 * n_out)
    equal = key[None, :] == key[:, None]
    below = key[None, :] < key[:, None]
    earlier = jnp.sum((equal & (ids[None, :] < ids[:, None])).astype(jnp.int32), axis=1)
    later = jnp.sum((equal & (ids[None, :] > ids[:, None])).astype(jnp.int32), axis=1)
    weight = jnp.where(live, 1 + ((later == 0) & (earlier % 2 == 0)).astype(jnp.int32), 0)
    spot_at = jnp.sum(jnp.where(below, weight[None, :], 0), axis=1) + earlier
    send_len = jnp.sum(jnp.where(kept == 0, weight, 0))
    all_len = jnp.sum(weight)
    step = 2 * UNROLL
    send_steps = (send_len + step - 1) // step
    keep_steps = (all_len - send_len + step - 1) // step
    spot_at = spot_at + kept * (send_steps * step - send_len)
    spot_at = jnp.where(live, spot_at, -1)
    size = -(-(slots + 2 * n_out + 2 * step) // (2 * step)) * 2 * step
    hit = spot_at[None, :] == jnp.arange(size, dtype=jnp.int32)[:, None]

    def placed(values, empty):
        return jnp.sum(jnp.where(hit, values[None, :] - empty, 0), axis=1) + empty

    tile_at = placed(ids, slots)
    block_at = placed(row_pos, 0)
    out_at = placed(out_pos, n_out)[::2]
    same = jnp.concatenate([jnp.zeros((1,), jnp.int32), (out_at[1:] == out_at[:-1]).astype(jnp.int32)])
    info = jnp.stack([mid.astype(jnp.int32), send_steps, send_steps + keep_steps])
    return tile_at, block_at, out_at, same, info


def core_sums(keep, recv):
    size = (keep.shape[0] - SIDE) // 4
    return [add_f32(keep[g * size : (g + 1) * size], recv[g * size : (g + 1) * size]).astype(jnp.bfloat16) for g in range(4)]


def halve(value, upper, rows):
    blocks = value.shape[0] // rows
    shape = (2, blocks // 2) if upper else (blocks // 2, 2)
    cut = value.reshape(shape + (rows, value.shape[1]))
    if upper:
        sent, kept = cut[1], cut[0]
    else:
        sent, kept = cut[:, 1], cut[:, 0]
    return sent.reshape(-1, value.shape[1]), kept.reshape(-1, value.shape[1])


def exchange_first(sums, bits):
    return xor_permute(sums[0], "row", bits[0]), xor_permute(sums[2], "row", bits[-1])


def exchange_rest(sums, recv, bits, rows):
    done = []
    for upper in (0, 1):
        value = add_f32(sums[2 * upper + 1], recv[upper])
        for bit in (bits[::-1] if upper else bits)[1:]:
            sent, kept = halve(value.astype(jnp.bfloat16), upper, rows)
            value = add_f32(kept, xor_permute(sent, "row", bit))
        done.append(value.astype(jnp.bfloat16))
    return jnp.concatenate(done, axis=0)


def weight_term(features_groups, sums):
    terms = [
        lax.dot_general(f, s, (((0,), (0,)), ((), ())), preferred_element_type=jnp.float32)
        for f, s in zip(features_groups, sums)
    ]
    return tree_sum(terms)


def sum_over(term, axis, masks):
    parts = [term] + [xor_permute(term, axis, m) for m in masks]
    return tree_sum([p.astype(jnp.float32) for p in parts])


def body(grad_out, preact, features, weight, tiles, tile_rows, tile_cols, live_counts):
    nodes, width = grad_out.shape
    n_row, n_col = lax.axis_size("row"), lax.axis_size("col")
    row, col = lax.axis_index("row"), lax.axis_index("col")
    slots = tiles.shape[2]
    cw = width // 2
    rows = nodes // 2
    bits = [1 << b for b in range(1, n_row.bit_length() - 1)]
    mid = ((col & 3) == 1) | ((col & 3) == 2)
    count = live_counts.reshape(())

    own0, own1 = [
        jnp.where(preact[:, cut] > 0, grad_out[:, cut], jnp.zeros_like(grad_out[:, cut]))
        for cut in (slice(0, cw), slice(cw, width))
    ]
    first0 = gather_first(own0)
    plan = plan_slots(tile_rows.reshape(slots), tile_cols.reshape(slots), count, row, col, mid, n_row, nodes // SIDE)
    flipped = flip_tiles(tiles.reshape(slots, SIDE, SIDE))
    features, flipped = fence(features, flipped)
    near = [features]
    for bit in bits[:2]:
        near.append(xor_permute(features, "row", bit))
    own0, own1, first0, flipped, plan = fence(own0, own1, first0, flipped, plan)

    second0 = gather_second(own0, first0[1], n_col)
    pieces0 = as_pieces(own0, first0, second0, mid, n_col)
    pieces0, own1, near = fence(pieces0, own1, near)

    first1 = gather_first(own1)
    near.append(xor_permute(near[1], "row", bits[1]))
    for bit in bits[2:]:
        near += [xor_permute(f, "row", bit) for f in near]
    send0, keep0 = spmm(plan, pieces0, flipped, n_row)
    own1, first1, near, send0, keep0 = fence(own1, first1, near, send0, keep0)

    second1 = gather_second(own1, first1[1], n_col)
    pieces1 = as_pieces(own1, first1, second1, mid, n_col)
    sums0 = core_sums(keep0, xor_permute(send0, "row", 1))
    features_groups = []
    for upper in (0, 1):
        own_bit = (n_row // 4) if upper else 1
        for want in (1, 0):
            parts = [f[upper * rows : (upper + 1) * rows] for q, f in enumerate(near) if (q & own_bit != 0) == want]
            features_groups.append(jnp.concatenate(parts, axis=0))
    pieces1, sums0, features_groups = fence(pieces1, sums0, features_groups)

    recv0 = exchange_first(sums0, bits)
    send1, keep1 = spmm(plan, pieces1, flipped, n_row)
    recv0, send1, keep1 = fence(recv0, send1, keep1)

    colgrad0 = exchange_rest(sums0, recv0, bits, rows)
    sums1 = core_sums(keep1, xor_permute(send1, "row", 1))
    colgrad0, sums1 = fence(colgrad0, sums1)
    term1 = weight_term(features_groups, sums1).astype(jnp.bfloat16)
    term0 = weight_term(features_groups, sums0).astype(jnp.bfloat16)
    term = jnp.concatenate([term0, term1], axis=1)
    sums1, term = fence(sums1, term)

    recv1 = exchange_first(sums1, bits)
    term = sum_over(term, "col", range(1, n_col)).astype(jnp.bfloat16)
    recv1, term = fence(recv1, term)

    colgrad1 = exchange_rest(sums1, recv1, bits, rows)
    term = sum_over(term, "row", range(2, n_row, 2)).astype(jnp.bfloat16)
    colgrad1, term = fence(colgrad1, term)

    grad_weight = sum_over(term, "row", [1])
    colgrad = jnp.concatenate([colgrad0, colgrad1], axis=1)
    grad_features = lax.dot_general(
        colgrad, weight, (((1,), (1,)), ((), ())), preferred_element_type=jnp.float32
    ).astype(jnp.bfloat16)
    return (grad_features, grad_weight)


def solution(mesh):
    in_specs = (
        P(("row", "col"), None),
        P(("row", "col"), None),
        P(("col", "row"), None),
        P(),
        P("row", "col", None, None, None),
        P("row", "col", None),
        P("row", "col", None),
        P("row", "col"),
    )
    out_specs = (P(("col", "row"), None), P())
    return jax.shard_map(body, mesh=mesh, in_specs=in_specs, out_specs=out_specs, check_vma=False)
```

```python
import functools

import jax
import jax.numpy as jnp
from jax import lax
from jax.experimental import pallas as pl
from jax.experimental.pallas import tpu as pltpu
from jax.sharding import PartitionSpec as P

SIDE = 128
UNROLL = 8
FIRST_PIECES = 3
FLIP_GROUP = 32
FLIP_BYTES = 24 * 1024 * 1024
SPMM_BYTES = 8 * 1024 * 1024


def flip_kernel(tiles_ref, out_ref, t_in, sems):
    slots = t_in.shape[0]
    groups = slots // FLIP_GROUP
    loads = [
        pltpu.make_async_copy(
            tiles_ref.at[pl.ds(g * FLIP_GROUP, FLIP_GROUP)], t_in.at[pl.ds(g * FLIP_GROUP, FLIP_GROUP)], sems.at[g]
        )
        for g in range(groups)
    ]
    for load in loads:
        load.start()
    out_ref[slots] = jnp.zeros((SIDE, SIDE), out_ref.dtype)
    for g in range(groups):
        loads[g].wait()

        def some(step, carry, g=g):
            for u in range(4):
                k = g * FLIP_GROUP + step * 4 + u
                out_ref[k] = t_in[k].T
            return carry

        lax.fori_loop(0, FLIP_GROUP // 4, some, 0)


def flip_tiles(tile_stack):
    slots = tile_stack.shape[0]
    return pl.pallas_call(
        flip_kernel,
        out_shape=jax.ShapeDtypeStruct((slots + 1, SIDE, SIDE), tile_stack.dtype),
        in_specs=[pl.BlockSpec(memory_space=pl.ANY)],
        out_specs=pl.BlockSpec(memory_space=pltpu.VMEM),
        scratch_shapes=[pltpu.VMEM(tile_stack.shape, tile_stack.dtype), pltpu.SemaphoreType.DMA((slots // FLIP_GROUP,))],
        compiler_params=pltpu.CompilerParams(vmem_limit_bytes=FLIP_BYTES),
        cost_estimate=pl.CostEstimate(flops=0, bytes_accessed=4096, transcendentals=0),
        name="flip_tiles",
    )(tile_stack)


def spmm_kernel(layout, last, tile_at_ref, block_at_ref, out_at_ref, same_ref, info_ref, *refs):
    n_refs = sum(layout)
    refs_left = list(refs[:n_refs])
    pieces = [[refs_left.pop(0) for _ in range(n)] for n in layout]
    rest = list(refs[n_refs:])
    tiles_ref = rest.pop(0)
    acc_refs = (rest.pop(0), rest.pop(0)) if last else (None, None)
    out_refs = (rest.pop(0), rest.pop(0))
    m_vmem, total_ref = rest
    nodes, width = pieces[0][0].shape

    for out_ref, acc_ref in zip(out_refs, acc_refs):

        def begin(step, carry, out_ref=out_ref, acc_ref=acc_ref):
            at = pl.ds(pl.multiple_of(step * 256, 256), 256)
            if last:
                out_ref[at, :] = acc_ref[at, :].astype(out_ref.dtype)
            else:
                out_ref[at, :] = jnp.zeros((256, width), out_ref.dtype)
            return carry

        lax.fori_loop(0, out_ref.shape[0] // 256, begin, 0)
    for p, options in enumerate(pieces):

        def take(ref, p=p):
            def some(step, carry):
                at = pl.multiple_of(step * 512, 512)
                m_vmem[pl.ds(pl.multiple_of(p * nodes + at, 512), 512), :] = ref[pl.ds(at, 512), :]
                return carry

            lax.fori_loop(0, nodes // 512, some, 0)

        if len(options) == 1:
            take(options[0])
        else:
            pl.when(info_ref[0] == 1)(functools.partial(take, options[0]))
            pl.when(info_ref[0] != 1)(functools.partial(take, options[1]))

    def block(index):
        return m_vmem[pl.ds(pl.multiple_of(index * SIDE, SIDE), SIDE), :]

    def add_pairs(out_ref, acc_ref, step, carry):
        total = total_ref[...]
        prods = []
        for u in range(UNROLL):
            k = 2 * (step * UNROLL + u)
            left = jnp.concatenate([tiles_ref[tile_at_ref[k]], tiles_ref[tile_at_ref[k + 1]]], axis=1)
            right = jnp.concatenate([block(block_at_ref[k]), block(block_at_ref[k + 1])], axis=0)
            prods.append(jnp.dot(left, right, preferred_element_type=jnp.float32))
        for u in range(UNROLL):
            k = step * UNROLL + u
            at = pl.ds(pl.multiple_of(out_at_ref[k] * SIDE, SIDE), SIDE)
            before = acc_ref[at, :] if last else jnp.zeros_like(total)
            total = prods[u] + jnp.where(same_ref[k] == 1, total, before)
            out_ref[at, :] = total.astype(out_ref.dtype)
        total_ref[...] = total
        return carry

    total_ref[...] = jnp.zeros_like(total_ref)
    lax.fori_loop(0, info_ref[1], functools.partial(add_pairs, out_refs[0], acc_refs[0]), 0)
    lax.fori_loop(info_ref[1], info_ref[2], functools.partial(add_pairs, out_refs[1], acc_refs[1]), 0)


def spmm(plan, pieces, tiles, acc, n_row):
    nodes, width = pieces[0][0].shape
    half = n_row // 2 * nodes
    last = acc is not None
    out = jax.ShapeDtypeStruct((half + 2 * SIDE, width), jnp.bfloat16 if last else jnp.float32)
    operands = [ref for p in pieces for ref in p] + [tiles] + list(acc or [])
    return pl.pallas_call(
        functools.partial(spmm_kernel, [len(p) for p in pieces], last),
        out_shape=(out, out),
        grid_spec=pltpu.PrefetchScalarGridSpec(
            num_scalar_prefetch=5,
            grid=(),
            in_specs=[pl.BlockSpec(memory_space=pltpu.VMEM)] * len(operands),
            out_specs=[pl.BlockSpec(memory_space=pltpu.VMEM)] * 2,
            scratch_shapes=[
                pltpu.VMEM((len(pieces) * nodes, width), jnp.bfloat16),
                pltpu.VMEM((SIDE, width), jnp.float32),
            ],
        ),
        compiler_params=pltpu.CompilerParams(vmem_limit_bytes=SPMM_BYTES),
        cost_estimate=pl.CostEstimate(flops=0, bytes_accessed=4096, transcendentals=0),
        name="spmm_last" if last else "spmm_first",
    )(*plan, *operands)


def xor_permute(value, axis, mask):
    size = lax.axis_size(axis)
    return lax.ppermute(value, axis, [(i, i ^ mask) for i in range(size)])


def tree_sum(values):
    while len(values) > 1:
        values = [a + b for a, b in zip(values[::2], values[1::2])]
    return values[0]


def gather_first(own):
    return xor_permute(own, "col", 1), xor_permute(own, "col", 2)


def gather_second(own, by_two, n_col):
    ends, middles = [], []
    for low in range(0, n_col, 4):
        ends += [(low + 1, low), (low + 2, low + 3)]
        middles += [(low + 1, low + 2), (low + 2, low + 1)]
    return lax.ppermute(own, "col", middles), lax.ppermute(by_two, "col", ends)


def as_pieces(own, first, second, mid, n_col):
    if n_col == 4:
        return [[own], [first[0]], [first[1]], list(second)]
    pieces = [own, first[0], first[1], jnp.where(mid, second[0], second[1])]
    for high in range(4, n_col, 4):
        pieces += [xor_permute(piece, "col", high) for piece in pieces[:4]]
    return [[piece] for piece in pieces]


def fence(*values):
    return lax.optimization_barrier(values)


def add_f32(a, b):
    return a.astype(jnp.float32) + b.astype(jnp.float32)


def plan_slots(tile_rows, tile_cols, count, row, col, mid, n_row, per_dev, last):
    slots = tile_rows.shape[0]
    half, quarter = n_row // 2, n_row // 4
    row_pos = ((tile_rows // per_dev) ^ col) * per_dev + tile_rows % per_dev
    away = (tile_cols // per_dev) ^ row
    near, local = away >> 1, tile_cols % per_dev
    upper = local // (per_dev // 2)
    spot = local % (per_dev // 2)
    first_bit = jnp.where(upper == 0, near & 1, near // quarter)
    rest = jnp.where(upper == 0, near >> 1, near % quarter)
    group = upper * 2 + (1 - first_bit)
    out_pos = (group * quarter + rest) * (per_dev // 2) + spot
    kept = 1 - (away & 1)
    n_out = half * per_dev
    ids = jnp.arange(slots, dtype=jnp.int32)
    start = FIRST_PIECES * per_dev
    live = (ids < count) & ((row_pos >= start) == last)
    if last:
        row_pos = row_pos - start
    key = jnp.where(live, kept * n_out + out_pos, 2 * n_out)
    equal = key[None, :] == key[:, None]
    below = key[None, :] < key[:, None]
    earlier = jnp.sum((equal & (ids[None, :] < ids[:, None])).astype(jnp.int32), axis=1)
    later = jnp.sum((equal & (ids[None, :] > ids[:, None])).astype(jnp.int32), axis=1)
    weight = jnp.where(live, 1 + ((later == 0) & (earlier % 2 == 0)).astype(jnp.int32), 0)
    spot_at = jnp.sum(jnp.where(below, weight[None, :], 0), axis=1) + earlier
    send_len = jnp.sum(jnp.where(kept == 0, weight, 0))
    all_len = jnp.sum(weight)
    step = 2 * UNROLL
    send_steps = (send_len + step - 1) // step
    keep_steps = (all_len - send_len + step - 1) // step
    spot_at = spot_at + kept * (send_steps * step - send_len)
    spot_at = jnp.where(live, spot_at, -1)
    size = -(-(slots + 2 * n_out + 2 * step) // (2 * step)) * 2 * step
    hit = spot_at[None, :] == jnp.arange(size, dtype=jnp.int32)[:, None]

    def placed(values, empty):
        return jnp.sum(jnp.where(hit, values[None, :] - empty, 0), axis=1) + empty

    tile_at = placed(ids, slots)
    block_at = placed(row_pos, 0)
    out_at = placed(out_pos, n_out)[::2]
    same = jnp.concatenate([jnp.zeros((1,), jnp.int32), (out_at[1:] == out_at[:-1]).astype(jnp.int32)])
    info = jnp.stack([mid.astype(jnp.int32), send_steps, send_steps + keep_steps])
    return tile_at, block_at, out_at, same, info


def core_sums(keep, recv):
    size = (keep.shape[0] - 2 * SIDE) // 4
    return [add_f32(keep[g * size : (g + 1) * size], recv[g * size : (g + 1) * size]).astype(jnp.bfloat16) for g in range(4)]


def halve(value, upper, rows):
    blocks = value.shape[0] // rows
    shape = (2, blocks // 2) if upper else (blocks // 2, 2)
    cut = value.reshape(shape + (rows, value.shape[1]))
    if upper:
        sent, kept = cut[1], cut[0]
    else:
        sent, kept = cut[:, 1], cut[:, 0]
    return sent.reshape(-1, value.shape[1]), kept.reshape(-1, value.shape[1])


def exchange_first(sums, bits):
    return xor_permute(sums[0], "row", bits[0]), xor_permute(sums[2], "row", bits[-1])


def exchange_second(sums, recv, bits, rows):
    sent, kept = [], []
    for upper in (0, 1):
        value = add_f32(sums[2 * upper + 1], recv[upper]).astype(jnp.bfloat16)
        sent_u, kept_u = halve(value, upper, rows)
        sent.append(sent_u)
        kept.append(kept_u)
    return kept, sent


def exchange_last(kept, recv, bits, rows):
    done = []
    for upper in (0, 1):
        value = add_f32(kept[upper], recv[upper])
        for bit in (bits[::-1] if upper else bits)[2:]:
            sent_u, kept_u = halve(value.astype(jnp.bfloat16), upper, rows)
            value = add_f32(kept_u, xor_permute(sent_u, "row", bit))
        done.append(value.astype(jnp.bfloat16))
    return jnp.concatenate(done, axis=0)


def exchange_rest(sums, recv, bits, rows):
    kept, sent = exchange_second(sums, recv, bits, rows)
    recv = [xor_permute(s, "row", bit) for s, bit in zip(sent, (bits[1], bits[-2]))]
    return exchange_last(kept, recv, bits, rows)


def weight_term(features_groups, sums0, sums1):
    halves = []
    for sums in (sums0, sums1):
        terms = [
            lax.dot_general(f, s, (((0,), (0,)), ((), ())), preferred_element_type=jnp.float32)
            for f, s in zip(features_groups, sums)
        ]
        halves.append(tree_sum(terms).astype(jnp.bfloat16))
    return jnp.concatenate(halves, axis=1)


def sum_over(term, axis, masks):
    parts = [term] + [xor_permute(term, axis, m) for m in masks]
    return tree_sum([p.astype(jnp.float32) for p in parts])


def grow(stack, bits):
    for bit in bits:
        stack = jnp.concatenate([stack, xor_permute(stack, "row", bit)], axis=0)
    return stack


def body(grad_out, preact, features, weight, tiles, tile_rows, tile_cols, live_counts):
    nodes, width = grad_out.shape
    n_row, n_col = lax.axis_size("row"), lax.axis_size("col")
    row, col = lax.axis_index("row"), lax.axis_index("col")
    slots = tiles.shape[2]
    cw = width // 2
    rows = nodes // 2
    bits = [1 << b for b in range(1, n_row.bit_length() - 1)]
    mid = ((col & 3) == 1) | ((col & 3) == 2)
    count = live_counts.reshape(())

    own0, own1 = [
        jnp.where(preact[:, cut] > 0, grad_out[:, cut], jnp.zeros_like(grad_out[:, cut]))
        for cut in (slice(0, cw), slice(cw, width))
    ]
    first0 = gather_first(own0)
    flipped = flip_tiles(tiles.reshape(slots, SIDE, SIDE))
    count = count + flipped[slots, 0, 0].astype(jnp.int32)
    kept_near = [grow(features[:rows], bits[1:]), grow(features[rows:], bits[:-1])]
    plans = [
        plan_slots(tile_rows.reshape(slots), tile_cols.reshape(slots), count, row, col, mid, n_row, nodes // SIDE, last)
        for last in (False, True)
    ]
    sent_near = [xor_permute(stack, "row", bit) for stack, bit in zip(kept_near, (bits[0], bits[-1]))]
    own0, own1, first0, plans, kept_near = fence(own0, own1, first0, plans, kept_near)

    second0 = gather_second(own0, first0[1], n_col)
    pieces0 = as_pieces(own0, first0, second0, mid, n_col)
    features_groups = [sent_near[0], kept_near[0], sent_near[1], kept_near[1]]
    pieces0, own1, features_groups = fence(pieces0, own1, features_groups)
    core, in_half = row & 1, features.shape[1] // 2
    features_theirs = [lax.dynamic_slice_in_dim(f, (1 - core) * in_half, in_half, 1) for f in features_groups]
    features_mine = [lax.dynamic_slice_in_dim(f, core * in_half, in_half, 1) for f in features_groups]

    first1 = gather_first(own1)
    acc0 = spmm(plans[0], pieces0[:FIRST_PIECES], flipped, None, n_row)
    send0, keep0 = spmm(plans[1], pieces0[FIRST_PIECES:], flipped, acc0, n_row)
    own1, first1, send0, keep0, features_theirs, features_mine = fence(
        own1, first1, send0, keep0, features_theirs, features_mine
    )

    second1 = gather_second(own1, first1[1], n_col)
    pieces1 = as_pieces(own1, first1, second1, mid, n_col)
    sums0 = core_sums(keep0, xor_permute(send0, "row", 1))
    recv0 = exchange_first(sums0, bits)
    acc1 = spmm(plans[0], pieces1[:FIRST_PIECES], flipped, None, n_row)
    pieces1, sums0, acc1 = fence(pieces1, sums0, acc1)

    send1, keep1 = spmm(plans[1], pieces1[FIRST_PIECES:], flipped, acc1, n_row)
    send1, keep1, recv0, sums0 = fence(send1, keep1, recv0, sums0)

    sums1 = core_sums(keep1, xor_permute(send1, "row", 1))
    theirs = weight_term(features_theirs, sums0, sums1)
    rest0, sent0 = exchange_second(sums0, recv0, bits, rows)
    recv0 = [xor_permute(sent, "row", bit) for sent, bit in zip(sent0, (bits[1], bits[-2]))]
    sums1, theirs = fence(sums1, theirs)
    sums1, theirs, rest0, recv0 = fence(sums1, theirs, rest0, recv0)

    recv1 = exchange_first(sums1, bits)
    mine = weight_term(features_mine, sums0, sums1)
    mine = add_f32(mine, xor_permute(theirs, "row", 1)).astype(jnp.bfloat16)
    mine = sum_over(mine, "col", range(1, n_col)).astype(jnp.bfloat16)
    recv1, mine = fence(recv1, mine)

    rest1, sent1 = exchange_second(sums1, recv1, bits, rows)
    rest1, sent1, mine = fence(rest1, sent1, mine)
    recv1 = [xor_permute(sent, "row", bit) for sent, bit in zip(sent1, (bits[1], bits[-2]))]
    mine = sum_over(mine, "row", range(2, n_row, 2)).astype(jnp.bfloat16)
    colgrad0 = exchange_last(rest0, recv0, bits, rows)
    colgrad1 = exchange_last(rest1, recv1, bits, rows)
    colgrad1, mine = fence(colgrad1, mine)

    theirs = xor_permute(mine, "row", 1)
    low, high = jnp.where(core == 0, mine, theirs), jnp.where(core == 0, theirs, mine)
    grad_weight = jnp.concatenate([low, high], axis=0).astype(jnp.float32)
    colgrad = jnp.concatenate([colgrad0, colgrad1], axis=1)
    grad_features = lax.dot_general(
        colgrad, weight, (((1,), (1,)), ((), ())), preferred_element_type=jnp.float32
    ).astype(jnp.bfloat16)
    return (grad_features, grad_weight)


def solution(mesh):
    in_specs = (
        P(("row", "col"), None),
        P(("row", "col"), None),
        P(("col", "row"), None),
        P(),
        P("row", "col", None, None, None),
        P("row", "col", None),
        P("row", "col", None),
        P("row", "col"),
    )
    out_specs = (P(("col", "row"), None), P())
    return jax.shard_map(body, mesh=mesh, in_specs=in_specs, out_specs=out_specs, check_vma=False)
```

```python
import functools

import jax
import jax.numpy as jnp
from jax import lax
from jax.experimental import pallas as pl
from jax.experimental.pallas import tpu as pltpu
from jax.sharding import PartitionSpec as P

SIDE = 128
UNROLL = 8
GROUP = 32
FIRST_PIECES = 3
PLAN_ROWS = 8
FLIP_BYTES = 26 * 1024 * 1024
SPMM_BYTES = 24 * 1024 * 1024


def round_up(value, unit):
    return -(-value // unit) * unit


def total(mask, axis):
    return jnp.sum(jnp.where(mask, 1.0, 0.0), axis=axis, keepdims=True).astype(jnp.int32)


def total_of(values, axis):
    return jnp.sum(values.astype(jnp.float32), axis=axis, keepdims=True).astype(jnp.int32)


def plan_kernel(per_dev, n_out, place_ref, rows_r, cols_r, rows_c, cols_c, plan0_ref, plan1_ref, slot_ref):
    slots = rows_r.shape[1]
    size = plan0_ref.shape[1]
    count, row, col, mid = place_ref[0], place_ref[1], place_ref[2], place_ref[3]
    shift = per_dev.bit_length() - 1
    start = FIRST_PIECES * per_dev
    step = 2 * UNROLL

    def attributes(rows, cols, axis):
        ids = lax.broadcasted_iota(jnp.int32, rows.shape, axis)
        row_pos = (((rows >> shift) ^ col) << shift) + (rows & (per_dev - 1))
        away = (cols >> shift) ^ row
        out_pos = ((away >> 1) << shift) + (cols & (per_dev - 1))
        kept = 1 - (away & 1)
        last = (row_pos >= start).astype(jnp.int32)
        live = ids < count
        key = jnp.where(live, (2 * last + kept) * n_out + out_pos, 4 * n_out)
        return ids, row_pos, out_pos, 2 * last + kept, live, key

    ids_r, _, _, part_r, live_r, key_r = attributes(rows_r[...], cols_r[...], 1)
    ids_c, row_pos_c, out_pos_c, part_c, live_c, key_c = attributes(rows_c[...], cols_c[...], 0)
    equal = key_c == key_r
    below = key_r < key_c
    earlier_c = total(equal & (ids_r < ids_c), 1)
    earlier_r = total(equal & (ids_c < ids_r), 0)
    later_r = total(equal & (ids_c > ids_r), 0)
    odd_end = (later_r == 0) & ((earlier_r & 1) == 0)
    weight_r = jnp.where(live_r, jnp.where(odd_end, 2, 1), 0)
    rank_c = total(below, 1) + earlier_c
    rank_r = total(key_c < key_r, 0) + earlier_r
    padded_c = total_of(jnp.where(below, weight_r, 0), 1) + earlier_c
    length = [total_of(jnp.where(part_r == p, weight_r, 0), 1) for p in range(4)]
    n_first = total(live_r & (part_r < 2), 1)
    n_last = count - n_first
    last_base = ((n_first + GROUP - 1) >> 5) << 5
    slot_r = jnp.where(part_r >= 2, last_base + rank_r - n_first, rank_r)
    slot_ref[...] = jnp.where(live_r, slot_r, slots + GROUP)

    lane = lax.broadcasted_iota(jnp.int32, (1, size), 1)
    for p, plan_ref in enumerate((plan0_ref, plan1_ref)):
        sent, held = length[2 * p], length[2 * p + 1]
        sent_steps = (sent + step - 1) >> (step.bit_length() - 1)
        all_steps = sent_steps + ((held + step - 1) >> (step.bit_length() - 1))
        base = length[0] + length[1] if p else jnp.zeros_like(sent)
        in_plan = live_c & ((part_c >> 1) == p)
        pos = padded_c - base + jnp.where((part_c & 1) == 1, sent_steps * step - sent, 0)
        pos = jnp.where(in_plan, pos, -1)
        rank = rank_c - (n_first if p else 0)
        hit = pos == lane

        def placed(values, empty, hit=hit):
            return total_of(jnp.where(hit, values - empty, 0), 0) + empty

        plan_ref[0:1, :] = placed(rank, slots)
        plan_ref[1:2, :] = placed(row_pos_c - p * start, 0)
        taken = total(hit, 0) > 0
        ends = [
            jnp.max(jnp.where(in_plan & ((part_c & 1) == h), out_pos_c, 0).astype(jnp.float32), axis=0, keepdims=True)
            for h in range(2)
        ]
        end = jnp.where(lane < sent_steps * step, ends[0], ends[1]).astype(jnp.int32)
        plan_ref[2:3, :] = jnp.where(taken, placed(out_pos_c, 0), end)
        plan_ref[3:4, :] = jnp.where(taken, placed((earlier_c > 0).astype(jnp.int32), 0), 1)
        done = total(in_plan & (pos < (lane + 1) * step), 0)
        tiles = n_last if p else n_first
        info = [
            jnp.full((1, 1), mid, jnp.int32),
            sent_steps,
            (tiles + GROUP - 1) >> 5,
            last_base if p else jnp.zeros_like(last_base),
            jnp.zeros_like(last_base),
        ]
        for g in range(slots // GROUP):
            info.append(total((done <= (g + 1) * GROUP) & (lane < all_steps), 1))
        row_values = jnp.zeros((1, size), jnp.int32)
        for n, value in enumerate(info):
            row_values = jnp.where(lane == n, value, row_values)
        plan_ref[4:5, :] = row_values
        plan_ref[5:8, :] = jnp.zeros((3, size), jnp.int32)


def make_plans(tile_rows, tile_cols, place, n_row, per_dev):
    slots = tile_rows.size
    n_out = n_row // 2 * per_dev
    size = round_up(slots + 2 * n_out + 4 * UNROLL, SIDE)
    plan = jax.ShapeDtypeStruct((PLAN_ROWS, size), jnp.int32)
    return pl.pallas_call(
        functools.partial(plan_kernel, per_dev, n_out),
        out_shape=(plan, plan, jax.ShapeDtypeStruct((1, slots), jnp.int32)),
        in_specs=[pl.BlockSpec(memory_space=pltpu.SMEM)] + [pl.BlockSpec(memory_space=pltpu.VMEM)] * 4,
        out_specs=[pl.BlockSpec(memory_space=pltpu.VMEM)] * 3,
        compiler_params=pltpu.CompilerParams(vmem_limit_bytes=SPMM_BYTES),
        cost_estimate=pl.CostEstimate(flops=0, bytes_accessed=4096, transcendentals=0),
        name="plan_slots",
    )(place, tile_rows.reshape(1, slots), tile_cols.reshape(1, slots), tile_rows.reshape(slots, 1), tile_cols.reshape(slots, 1))


def flip_kernel(slot_ref, tiles_ref, out_ref, t_in, t_out, in_sem, out_sem):
    slots = t_in.shape[0]
    groups = slots // GROUP
    loads = [
        pltpu.make_async_copy(tiles_ref.at[pl.ds(g * GROUP, GROUP)], t_in.at[pl.ds(g * GROUP, GROUP)], in_sem.at[g])
        for g in range(groups)
    ]
    for load in loads:
        load.start()
    for g in range(groups):
        loads[g].wait()

        def some(step, carry, g=g):
            for u in range(4):
                k = g * GROUP + step * 4 + u
                t_out[slot_ref[0, k]] = t_in[k].T
            return carry

        lax.fori_loop(0, GROUP // 4, some, 0)
    stores = [
        pltpu.make_async_copy(t_out.at[pl.ds(g * GROUP, GROUP)], out_ref.at[pl.ds(g * GROUP, GROUP)], out_sem.at[g])
        for g in range(groups + 1)
    ]
    for store in stores:
        store.start()
    for store in stores:
        store.wait()


def flip_tiles(slot, tile_stack):
    slots = tile_stack.shape[0]
    groups = slots // GROUP
    return pl.pallas_call(
        flip_kernel,
        out_shape=jax.ShapeDtypeStruct((slots + GROUP, SIDE, SIDE), tile_stack.dtype),
        grid_spec=pltpu.PrefetchScalarGridSpec(
            num_scalar_prefetch=1,
            grid=(),
            in_specs=[pl.BlockSpec(memory_space=pl.ANY)],
            out_specs=pl.BlockSpec(memory_space=pl.ANY),
            scratch_shapes=[
                pltpu.VMEM(tile_stack.shape, tile_stack.dtype),
                pltpu.VMEM((slots + GROUP + 1, SIDE, SIDE), tile_stack.dtype),
                pltpu.SemaphoreType.DMA((groups,)),
                pltpu.SemaphoreType.DMA((groups + 1,)),
            ],
        ),
        compiler_params=pltpu.CompilerParams(vmem_limit_bytes=FLIP_BYTES),
        cost_estimate=pl.CostEstimate(flops=0, bytes_accessed=4096, transcendentals=0),
        name="flip_tiles",
    )(slot, tile_stack)


def spmm_kernel(layout, last, plan_ref, *refs):
    n_refs = sum(layout)
    refs_left = list(refs[:n_refs])
    pieces = [[refs_left.pop(0) for _ in range(n)] for n in layout]
    rest = list(refs[n_refs:])
    tiles_ref = rest.pop(0)
    acc_refs = (rest.pop(0), rest.pop(0)) if last else (None, None)
    out_refs = (rest.pop(0), rest.pop(0))
    m_vmem, t_vmem, total_ref, sems = rest
    nodes, width = pieces[0][0].shape
    slots = t_vmem.shape[0] - 1
    mid, sent_steps, n_groups, tile_base = [plan_ref[4, n] for n in range(4)]

    def group_copy(g):
        at = pl.multiple_of(g * GROUP, GROUP)
        return pltpu.make_async_copy(
            tiles_ref.at[pl.ds(tile_base + at, GROUP)], t_vmem.at[pl.ds(at, GROUP)], sems.at[g]
        )

    def begin_copy(g, carry):
        group_copy(g).start()
        return carry

    lax.fori_loop(0, n_groups, begin_copy, 0)
    t_vmem[slots] = jnp.zeros((SIDE, SIDE), t_vmem.dtype)
    for out_ref, acc_ref in zip(out_refs, acc_refs):

        def begin(step, carry, out_ref=out_ref, acc_ref=acc_ref):
            at = pl.ds(pl.multiple_of(step * 256, 256), 256)
            if last:
                out_ref[at, :] = acc_ref[at, :].astype(out_ref.dtype)
            else:
                out_ref[at, :] = jnp.zeros((256, width), out_ref.dtype)
            return carry

        lax.fori_loop(0, out_ref.shape[0] // 256, begin, 0)
    for p, options in enumerate(pieces):

        def take(ref, p=p):
            def some(step, carry):
                at = pl.multiple_of(step * 512, 512)
                m_vmem[pl.ds(pl.multiple_of(p * nodes + at, 512), 512), :] = ref[pl.ds(at, 512), :]
                return carry

            lax.fori_loop(0, nodes // 512, some, 0)

        if len(options) == 1:
            take(options[0])
        else:
            pl.when(mid == 1)(functools.partial(take, options[0]))
            pl.when(mid != 1)(functools.partial(take, options[1]))

    def block(index):
        return m_vmem[pl.ds(pl.multiple_of(index * SIDE, SIDE), SIDE), :]

    def add_pairs(out_ref, acc_ref, step, carry):
        running = total_ref[...]
        prods = []
        for u in range(UNROLL):
            k = 2 * (step * UNROLL + u)
            left = jnp.concatenate([t_vmem[plan_ref[0, k]], t_vmem[plan_ref[0, k + 1]]], axis=1)
            right = jnp.concatenate([block(plan_ref[1, k]), block(plan_ref[1, k + 1])], axis=0)
            prods.append(jnp.dot(left, right, preferred_element_type=jnp.float32))
        for u in range(UNROLL):
            k = 2 * (step * UNROLL + u)
            at = pl.ds(pl.multiple_of(plan_ref[2, k] * SIDE, SIDE), SIDE)
            before = acc_ref[at, :] if last else jnp.zeros_like(running)
            running = prods[u] + jnp.where(plan_ref[3, k] == 1, running, before)
            out_ref[at, :] = running.astype(out_ref.dtype)
        total_ref[...] = running
        return carry

    total_ref[...] = jnp.zeros_like(total_ref)

    def add_group(g, carry):
        group_copy(g).wait()
        low, high = plan_ref[4, 4 + g], plan_ref[4, 5 + g]
        lax.fori_loop(
            jnp.minimum(low, sent_steps), jnp.minimum(high, sent_steps),
            functools.partial(add_pairs, out_refs[0], acc_refs[0]), 0,
        )
        lax.fori_loop(
            jnp.maximum(low, sent_steps), jnp.maximum(high, sent_steps),
            functools.partial(add_pairs, out_refs[1], acc_refs[1]), 0,
        )
        return carry

    lax.fori_loop(0, n_groups, add_group, 0)


def spmm(plan, pieces, tiles, acc, n_row):
    nodes, width = pieces[0][0].shape
    half = n_row // 2 * nodes
    last = acc is not None
    slots = tiles.shape[0] - GROUP
    out = jax.ShapeDtypeStruct((half, width), jnp.bfloat16 if last else jnp.float32)
    blocks = [ref for p in pieces for ref in p]
    in_vmem, in_any = pl.BlockSpec(memory_space=pltpu.VMEM), pl.BlockSpec(memory_space=pl.ANY)
    return pl.pallas_call(
        functools.partial(spmm_kernel, [len(p) for p in pieces], last),
        out_shape=(out, out),
        grid_spec=pltpu.PrefetchScalarGridSpec(
            num_scalar_prefetch=1,
            grid=(),
            in_specs=[in_vmem] * len(blocks) + [in_any] + [in_vmem] * len(acc or []),
            out_specs=[in_vmem] * 2,
            scratch_shapes=[
                pltpu.VMEM((len(pieces) * nodes, width), jnp.bfloat16),
                pltpu.VMEM((slots + 1, SIDE, SIDE), jnp.bfloat16),
                pltpu.VMEM((SIDE, width), jnp.float32),
                pltpu.SemaphoreType.DMA((slots // GROUP,)),
            ],
        ),
        compiler_params=pltpu.CompilerParams(vmem_limit_bytes=SPMM_BYTES),
        cost_estimate=pl.CostEstimate(flops=0, bytes_accessed=4096, transcendentals=0),
        name="spmm_last" if last else "spmm_first",
    )(plan, *blocks, tiles, *(acc or []))


def xor_permute(value, axis, mask):
    size = lax.axis_size(axis)
    return lax.ppermute(value, axis, [(i, i ^ mask) for i in range(size)])


def tree_sum(values):
    while len(values) > 1:
        values = [a + b for a, b in zip(values[::2], values[1::2])]
    return values[0]


def gather_first(own):
    return xor_permute(own, "col", 1), xor_permute(own, "col", 2)


def gather_second(own, by_two, n_col):
    ends, middles = [], []
    for low in range(0, n_col, 4):
        ends += [(low + 1, low), (low + 2, low + 3)]
        middles += [(low + 1, low + 2), (low + 2, low + 1)]
    return lax.ppermute(own, "col", middles), lax.ppermute(by_two, "col", ends)


def as_pieces(own, first, second, mid, n_col):
    if n_col == 4:
        return [[own], [first[0]], [first[1]], list(second)]
    pieces = [own, first[0], first[1], jnp.where(mid, second[0], second[1])]
    for high in range(4, n_col, 4):
        pieces += [xor_permute(piece, "col", high) for piece in pieces[:4]]
    return [[piece] for piece in pieces]


def fence(*values):
    return lax.optimization_barrier(values)


def add_f32(a, b):
    return a.astype(jnp.float32) + b.astype(jnp.float32)


def stage_sums(keep, recv, n_blocks, rows):
    width = keep.shape[1]
    cut = (n_blocks // 2, 2, 2, rows, width)
    flat = (2, n_blocks // 2, 2, rows, width)

    def summed(shape, pick):
        both = add_f32(pick(keep.reshape(shape)), pick(recv.reshape(shape)))
        return both.astype(jnp.bfloat16).reshape(-1, width)

    stage = [
        summed(cut, lambda v: v[:, 1, 0]),
        summed(cut, lambda v: v[:, 0, 0]),
        summed(flat, lambda v: v[1, :, 1]),
        summed(flat, lambda v: v[0, :, 1]),
    ]
    return stage, add_f32(keep, recv).astype(jnp.bfloat16)


def halve(value, upper, rows):
    blocks = value.shape[0] // rows
    shape = (2, blocks // 2) if upper else (blocks // 2, 2)
    cut = value.reshape(shape + (rows, value.shape[1]))
    if upper:
        sent, kept = cut[1], cut[0]
    else:
        sent, kept = cut[:, 1], cut[:, 0]
    return sent.reshape(-1, value.shape[1]), kept.reshape(-1, value.shape[1])


def exchange_first(stage, bits):
    return xor_permute(stage[0], "row", bits[0]), xor_permute(stage[2], "row", bits[-1])


def exchange_second(stage, recv, bits, rows):
    sent, kept = [], []
    for upper in (0, 1):
        value = add_f32(stage[2 * upper + 1], recv[upper]).astype(jnp.bfloat16)
        sent_u, kept_u = halve(value, upper, rows)
        sent.append(sent_u)
        kept.append(kept_u)
    return kept, sent


def send_second(sent, bits):
    return [xor_permute(s, "row", bit) for s, bit in zip(sent, (bits[1], bits[-2]))]


def exchange_last(kept, recv, bits, rows):
    done = []
    for upper in (0, 1):
        value = add_f32(kept[upper], recv[upper])
        for bit in (bits[::-1] if upper else bits)[2:]:
            sent_u, kept_u = halve(value.astype(jnp.bfloat16), upper, rows)
            value = add_f32(kept_u, xor_permute(sent_u, "row", bit))
        done.append(value.astype(jnp.bfloat16))
    return jnp.concatenate(done, axis=0)


def weight_term(near, sums):
    nodes = near[0].shape[0]
    terms = [
        lax.dot_general(f, sums[q * nodes : (q + 1) * nodes], (((0,), (0,)), ((), ())), preferred_element_type=jnp.float32)
        for q, f in enumerate(near)
    ]
    return tree_sum(terms).astype(jnp.bfloat16)


def sum_over(term, axis, masks):
    parts = [term] + [xor_permute(term, axis, m) for m in masks]
    return tree_sum([p.astype(jnp.float32) for p in parts])


def body(grad_out, preact, features, weight, tiles, tile_rows, tile_cols, live_counts):
    nodes, width = grad_out.shape
    n_row, n_col = lax.axis_size("row"), lax.axis_size("col")
    row, col = lax.axis_index("row"), lax.axis_index("col")
    slots = tiles.shape[2]
    cw = width // 2
    rows = nodes // 2
    bits = [1 << b for b in range(1, n_row.bit_length() - 1)]
    mid = ((col & 3) == 1) | ((col & 3) == 2)

    own0, own1 = [
        jnp.where(preact[:, cut] > 0, grad_out[:, cut], jnp.zeros_like(grad_out[:, cut]))
        for cut in (slice(0, cw), slice(cw, width))
    ]
    first0 = gather_first(own0)
    place = jnp.stack([live_counts.reshape(()), row, col, mid.astype(jnp.int32)])
    plan0, plan1, slot = make_plans(tile_rows, tile_cols, place, n_row, nodes // SIDE)
    flipped = flip_tiles(slot, tiles.reshape(slots, SIDE, SIDE))
    features, flipped = fence(features, flipped)
    near = [features]
    for bit in bits[:2]:
        near.append(xor_permute(features, "row", bit))
    own0, own1, first0, plan0, plan1, flipped = fence(own0, own1, first0, plan0, plan1, flipped)

    second0 = gather_second(own0, first0[1], n_col)
    pieces0 = as_pieces(own0, first0, second0, mid, n_col)
    pieces0, own1, near = fence(pieces0, own1, near)

    first1 = gather_first(own1)
    near.append(xor_permute(near[1], "row", bits[1]))
    for bit in bits[2:]:
        near += [xor_permute(f, "row", bit) for f in near]
    acc0 = spmm(plan0, pieces0[:FIRST_PIECES], flipped, None, n_row)
    send0, keep0 = spmm(plan1, pieces0[FIRST_PIECES:], flipped, acc0, n_row)
    own1, first1, near, send0, keep0 = fence(own1, first1, near, send0, keep0)

    second1 = gather_second(own1, first1[1], n_col)
    pieces1 = as_pieces(own1, first1, second1, mid, n_col)
    stage0, sums0 = stage_sums(keep0, xor_permute(send0, "row", 1), n_row // 2, rows)
    recv0 = exchange_first(stage0, bits)
    acc1 = spmm(plan0, pieces1[:FIRST_PIECES], flipped, None, n_row)
    pieces1, stage0, acc1 = fence(pieces1, stage0, acc1)

    send1, keep1 = spmm(plan1, pieces1[FIRST_PIECES:], flipped, acc1, n_row)
    send1, keep1, recv0, stage0, sums0 = fence(send1, keep1, recv0, stage0, sums0)

    stage1, sums1 = stage_sums(keep1, xor_permute(send1, "row", 1), n_row // 2, rows)
    rest0, sent0 = exchange_second(stage0, recv0, bits, rows)
    recv0 = send_second(sent0, bits)
    term0 = weight_term(near, sums0)
    stage1, sums1, term0 = fence(stage1, sums1, term0)
    stage1, sums1, term0, rest0, recv0 = fence(stage1, sums1, term0, rest0, recv0)

    recv1 = exchange_first(stage1, bits)
    term1 = weight_term(near, sums1)
    even = (row & 1) == 0
    theirs, mine = jnp.where(even, term1, term0), jnp.where(even, term0, term1)
    mine = add_f32(mine, xor_permute(theirs, "row", 1)).astype(jnp.bfloat16)
    mine = sum_over(mine, "col", range(1, n_col)).astype(jnp.bfloat16)
    recv1, mine = fence(recv1, mine)

    rest1, sent1 = exchange_second(stage1, recv1, bits, rows)
    rest1, sent1, mine = fence(rest1, sent1, mine)
    recv1 = send_second(sent1, bits)
    mine = sum_over(mine, "row", range(2, n_row, 2)).astype(jnp.bfloat16)
    colgrad0 = exchange_last(rest0, recv0, bits, rows)
    colgrad1 = exchange_last(rest1, recv1, bits, rows)
    colgrad1, mine = fence(colgrad1, mine)

    theirs = xor_permute(mine, "row", 1)
    low, high = jnp.where(even, mine, theirs), jnp.where(even, theirs, mine)
    grad_weight = jnp.concatenate([low, high], axis=1).astype(jnp.float32)
    colgrad = jnp.concatenate([colgrad0, colgrad1], axis=1)
    grad_features = lax.dot_general(
        colgrad, weight, (((1,), (1,)), ((), ())), preferred_element_type=jnp.float32
    ).astype(jnp.bfloat16)
    return (grad_features, grad_weight)


def solution(mesh):
    in_specs = (
        P(("row", "col"), None),
        P(("row", "col"), None),
        P(("col", "row"), None),
        P(),
        P("row", "col", None, None, None),
        P("row", "col", None),
        P("row", "col", None),
        P("row", "col"),
    )
    out_specs = (P(("col", "row"), None), P())
    return jax.shard_map(body, mesh=mesh, in_specs=in_specs, out_specs=out_specs, check_vma=False)
```

```python
import functools

import jax
import jax.numpy as jnp
from jax import lax
from jax.experimental import pallas as pl
from jax.experimental.pallas import tpu as pltpu
from jax.sharding import PartitionSpec as P

SIDE = 128
UNROLL = 8
GROUP = 32
RING = 4
FIRST_PIECES = 3
PLAN_ROWS = 8
FLIP_BYTES = 26 * 1024 * 1024
PLAN_BYTES = 12 * 1024 * 1024
SPMM_BYTES = 16 * 1024 * 1024


def round_up(value, unit):
    return -(-value // unit) * unit


def total(mask, axis):
    return jnp.sum(jnp.where(mask, 1.0, 0.0), axis=axis, keepdims=True).astype(jnp.int32)


def total_of(values, axis):
    return jnp.sum(values.astype(jnp.float32), axis=axis, keepdims=True).astype(jnp.int32)


def plan_kernel(per_dev, n_out, place_ref, rows_r, cols_r, rows_c, cols_c, plan0_ref, plan1_ref, slot_ref):
    slots = rows_r.shape[1]
    size = plan0_ref.shape[1]
    count, row, col, mid = place_ref[0], place_ref[1], place_ref[2], place_ref[3]
    shift = per_dev.bit_length() - 1
    start = FIRST_PIECES * per_dev
    step = 2 * UNROLL

    def attributes(rows, cols, axis):
        ids = lax.broadcasted_iota(jnp.int32, rows.shape, axis)
        row_pos = (((rows >> shift) ^ col) << shift) + (rows & (per_dev - 1))
        away = (cols >> shift) ^ row
        out_pos = ((away >> 1) << shift) + (cols & (per_dev - 1))
        kept = 1 - (away & 1)
        last = (row_pos >= start).astype(jnp.int32)
        live = ids < count
        key = jnp.where(live, (2 * last + kept) * n_out + out_pos, 4 * n_out)
        return ids, row_pos, out_pos, 2 * last + kept, live, key

    ids_r, _, _, part_r, live_r, key_r = attributes(rows_r[...], cols_r[...], 1)
    ids_c, row_pos_c, out_pos_c, part_c, live_c, key_c = attributes(rows_c[...], cols_c[...], 0)
    equal = key_c == key_r
    below = key_r < key_c
    earlier_c = total(equal & (ids_r < ids_c), 1)
    earlier_r = total(equal & (ids_c < ids_r), 0)
    later_r = total(equal & (ids_c > ids_r), 0)
    odd_end = (later_r == 0) & ((earlier_r & 1) == 0)
    weight_r = jnp.where(live_r, jnp.where(odd_end, 2, 1), 0)
    rank_c = total(below, 1) + earlier_c
    rank_r = total(key_c < key_r, 0) + earlier_r
    padded_c = total_of(jnp.where(below, weight_r, 0), 1) + earlier_c
    length = [total_of(jnp.where(part_r == p, weight_r, 0), 1) for p in range(4)]
    n_first = total(live_r & (part_r < 2), 1)
    n_last = count - n_first
    last_base = ((n_first + GROUP - 1) >> 5) << 5
    slot_r = jnp.where(part_r >= 2, last_base + rank_r - n_first, rank_r)
    slot_ref[...] = jnp.where(live_r, slot_r, slots + GROUP)

    lane = lax.broadcasted_iota(jnp.int32, (1, size), 1)
    for p, plan_ref in enumerate((plan0_ref, plan1_ref)):
        sent, held = length[2 * p], length[2 * p + 1]
        sent_steps = (sent + step - 1) >> (step.bit_length() - 1)
        all_steps = sent_steps + ((held + step - 1) >> (step.bit_length() - 1))
        base = length[0] + length[1] if p else jnp.zeros_like(sent)
        in_plan = live_c & ((part_c >> 1) == p)
        pos = padded_c - base + jnp.where((part_c & 1) == 1, sent_steps * step - sent, 0)
        pos = jnp.where(in_plan, pos, -1)
        rank = rank_c - (n_first if p else 0)
        hit = pos == lane

        def placed(values, empty, hit=hit):
            return total_of(jnp.where(hit, values - empty, 0), 0) + empty

        plan_ref[0:1, :] = placed(rank & (RING * GROUP - 1), RING * GROUP)
        plan_ref[1:2, :] = placed(row_pos_c - p * start, 0)
        taken = total(hit, 0) > 0
        ends = [
            jnp.max(jnp.where(in_plan & ((part_c & 1) == h), out_pos_c, 0).astype(jnp.float32), axis=0, keepdims=True)
            for h in range(2)
        ]
        end = jnp.where(lane < sent_steps * step, ends[0], ends[1]).astype(jnp.int32)
        plan_ref[2:3, :] = jnp.where(taken, placed(out_pos_c, 0), end)
        plan_ref[3:4, :] = jnp.where(taken, placed((earlier_c > 0).astype(jnp.int32), 0), 1)
        done = total(in_plan & (pos < (lane + 1) * step), 0)
        tiles = n_last if p else n_first
        info = [
            jnp.full((1, 1), mid, jnp.int32),
            sent_steps,
            (tiles + GROUP - 1) >> 5,
            last_base if p else jnp.zeros_like(last_base),
            jnp.zeros_like(last_base),
        ]
        for g in range(slots // GROUP):
            info.append(total((done <= (g + 1) * GROUP) & (lane < all_steps), 1))
        row_values = jnp.zeros((1, size), jnp.int32)
        for n, value in enumerate(info):
            row_values = jnp.where(lane == n, value, row_values)
        plan_ref[4:5, :] = row_values
        plan_ref[5:8, :] = jnp.zeros((3, size), jnp.int32)


def make_plans(tile_rows, tile_cols, place, n_row, per_dev):
    slots = tile_rows.size
    n_out = n_row // 2 * per_dev
    size = round_up(slots + 2 * n_out + 4 * UNROLL, SIDE)
    plan = jax.ShapeDtypeStruct((PLAN_ROWS, size), jnp.int32)
    return pl.pallas_call(
        functools.partial(plan_kernel, per_dev, n_out),
        out_shape=(plan, plan, jax.ShapeDtypeStruct((1, slots), jnp.int32)),
        in_specs=[pl.BlockSpec(memory_space=pltpu.SMEM)] + [pl.BlockSpec(memory_space=pltpu.VMEM)] * 4,
        out_specs=[pl.BlockSpec(memory_space=pltpu.VMEM)] * 3,
        compiler_params=pltpu.CompilerParams(vmem_limit_bytes=PLAN_BYTES),
        cost_estimate=pl.CostEstimate(flops=0, bytes_accessed=4096, transcendentals=0),
        name="plan_slots",
    )(place, tile_rows.reshape(1, slots), tile_cols.reshape(1, slots), tile_rows.reshape(slots, 1), tile_cols.reshape(slots, 1))


def flip_kernel(slot_ref, tiles_ref, out_ref, t_in, t_out, in_sem, out_sem):
    slots = t_in.shape[0]
    groups = slots // GROUP
    loads = [
        pltpu.make_async_copy(tiles_ref.at[pl.ds(g * GROUP, GROUP)], t_in.at[pl.ds(g * GROUP, GROUP)], in_sem.at[g])
        for g in range(groups)
    ]
    for load in loads:
        load.start()
    for g in range(groups):
        loads[g].wait()

        def some(step, carry, g=g):
            for u in range(4):
                k = g * GROUP + step * 4 + u
                t_out[slot_ref[0, k]] = t_in[k].T
            return carry

        lax.fori_loop(0, GROUP // 4, some, 0)
    stores = [
        pltpu.make_async_copy(t_out.at[pl.ds(g * GROUP, GROUP)], out_ref.at[pl.ds(g * GROUP, GROUP)], out_sem.at[g])
        for g in range(groups + 1)
    ]
    for store in stores:
        store.start()
    for store in stores:
        store.wait()


def flip_tiles(slot, tile_stack):
    slots = tile_stack.shape[0]
    groups = slots // GROUP
    return pl.pallas_call(
        flip_kernel,
        out_shape=jax.ShapeDtypeStruct((slots + GROUP, SIDE, SIDE), tile_stack.dtype),
        grid_spec=pltpu.PrefetchScalarGridSpec(
            num_scalar_prefetch=1,
            grid=(),
            in_specs=[pl.BlockSpec(memory_space=pl.ANY)],
            out_specs=pl.BlockSpec(memory_space=pl.ANY),
            scratch_shapes=[
                pltpu.VMEM(tile_stack.shape, tile_stack.dtype),
                pltpu.VMEM((slots + GROUP + 1, SIDE, SIDE), tile_stack.dtype),
                pltpu.SemaphoreType.DMA((groups,)),
                pltpu.SemaphoreType.DMA((groups + 1,)),
            ],
        ),
        compiler_params=pltpu.CompilerParams(vmem_limit_bytes=FLIP_BYTES),
        cost_estimate=pl.CostEstimate(flops=0, bytes_accessed=4096, transcendentals=0),
        name="flip_tiles",
    )(slot, tile_stack)


def spmm_kernel(layout, last, plan_ref, *refs):
    n_refs = sum(layout)
    refs_left = list(refs[:n_refs])
    pieces = [[refs_left.pop(0) for _ in range(n)] for n in layout]
    rest = list(refs[n_refs:])
    tiles_ref = rest.pop(0)
    acc_refs = (rest.pop(0), rest.pop(0)) if last else (None, None)
    out_refs = (rest.pop(0), rest.pop(0))
    m_vmem, t_vmem, total_ref, sems = rest
    nodes, width = pieces[0][0].shape
    mid, sent_steps, n_groups, tile_base = [plan_ref[4, n] for n in range(4)]

    def group_copy(g):
        place = g & (RING - 1)
        return pltpu.make_async_copy(
            tiles_ref.at[pl.ds(tile_base + pl.multiple_of(g * GROUP, GROUP), GROUP)],
            t_vmem.at[pl.ds(pl.multiple_of(place * GROUP, GROUP), GROUP)],
            sems.at[place],
        )

    for g in range(2):
        pl.when(g < n_groups)(group_copy(g).start)
    t_vmem[RING * GROUP] = jnp.zeros((SIDE, SIDE), t_vmem.dtype)
    for out_ref, acc_ref in zip(out_refs, acc_refs):

        def begin(step, carry, out_ref=out_ref, acc_ref=acc_ref):
            at = pl.ds(pl.multiple_of(step * 256, 256), 256)
            out_ref[at, :] = acc_ref[at, :] if last else jnp.zeros((256, width), out_ref.dtype)
            return carry

        lax.fori_loop(0, out_ref.shape[0] // 256, begin, 0)
    for p, options in enumerate(pieces):

        def take(ref, p=p):
            def some(step, carry):
                at = pl.multiple_of(step * 512, 512)
                m_vmem[pl.ds(pl.multiple_of(p * nodes + at, 512), 512), :] = ref[pl.ds(at, 512), :]
                return carry

            lax.fori_loop(0, nodes // 512, some, 0)

        if len(options) == 1:
            take(options[0])
        else:
            pl.when(mid == 1)(functools.partial(take, options[0]))
            pl.when(mid != 1)(functools.partial(take, options[1]))

    def block(index):
        return m_vmem[pl.ds(pl.multiple_of(index * SIDE, SIDE), SIDE), :]

    def add_pairs(out_ref, acc_ref, step, carry):
        running = total_ref[...]
        prods = []
        for u in range(UNROLL):
            k = 2 * (step * UNROLL + u)
            left = jnp.concatenate([t_vmem[plan_ref[0, k]], t_vmem[plan_ref[0, k + 1]]], axis=1)
            right = jnp.concatenate([block(plan_ref[1, k]), block(plan_ref[1, k + 1])], axis=0)
            prods.append(jnp.dot(left, right, preferred_element_type=jnp.float32))
        for u in range(UNROLL):
            k = 2 * (step * UNROLL + u)
            at = pl.ds(pl.multiple_of(plan_ref[2, k] * SIDE, SIDE), SIDE)
            before = acc_ref[at, :].astype(jnp.float32) if last else jnp.zeros_like(running)
            running = prods[u] + jnp.where(plan_ref[3, k] == 1, running, before)
            out_ref[at, :] = running.astype(out_ref.dtype)
        total_ref[...] = running
        return carry

    total_ref[...] = jnp.zeros_like(total_ref)

    def add_group(g, carry):
        group_copy(g).wait()

        @pl.when(g + 2 < n_groups)
        def _():
            group_copy(g + 2).start()

        low, high = plan_ref[4, 4 + g], plan_ref[4, 5 + g]
        lax.fori_loop(
            jnp.minimum(low, sent_steps), jnp.minimum(high, sent_steps),
            functools.partial(add_pairs, out_refs[0], acc_refs[0]), 0,
        )
        lax.fori_loop(
            jnp.maximum(low, sent_steps), jnp.maximum(high, sent_steps),
            functools.partial(add_pairs, out_refs[1], acc_refs[1]), 0,
        )
        return carry

    lax.fori_loop(0, n_groups, add_group, 0)


def spmm(plan, pieces, tiles, acc, n_row):
    nodes, width = pieces[0][0].shape
    half = n_row // 2 * nodes
    last = acc is not None
    out = jax.ShapeDtypeStruct((half, width), jnp.bfloat16)
    blocks = [ref for p in pieces for ref in p]
    in_vmem, in_any = pl.BlockSpec(memory_space=pltpu.VMEM), pl.BlockSpec(memory_space=pl.ANY)
    return pl.pallas_call(
        functools.partial(spmm_kernel, [len(p) for p in pieces], last),
        out_shape=(out, out),
        grid_spec=pltpu.PrefetchScalarGridSpec(
            num_scalar_prefetch=1,
            grid=(),
            in_specs=[in_vmem] * len(blocks) + [in_any] + [in_vmem] * len(acc or []),
            out_specs=[in_vmem] * 2,
            scratch_shapes=[
                pltpu.VMEM((len(pieces) * nodes, width), jnp.bfloat16),
                pltpu.VMEM((RING * GROUP + 1, SIDE, SIDE), jnp.bfloat16),
                pltpu.VMEM((SIDE, width), jnp.float32),
                pltpu.SemaphoreType.DMA((RING,)),
            ],
        ),
        compiler_params=pltpu.CompilerParams(vmem_limit_bytes=SPMM_BYTES),
        cost_estimate=pl.CostEstimate(flops=0, bytes_accessed=4096, transcendentals=0),
        name="spmm_last" if last else "spmm_first",
    )(plan, *blocks, tiles, *(acc or []))


def xor_permute(value, axis, mask):
    size = lax.axis_size(axis)
    return lax.ppermute(value, axis, [(i, i ^ mask) for i in range(size)])


def tree_sum(values):
    while len(values) > 1:
        values = [a + b for a, b in zip(values[::2], values[1::2])]
    return values[0]


def gather_first(own):
    return xor_permute(own, "col", 1), xor_permute(own, "col", 2)


def gather_second(own, by_two, n_col):
    ends, middles = [], []
    for low in range(0, n_col, 4):
        ends += [(low + 1, low), (low + 2, low + 3)]
        middles += [(low + 1, low + 2), (low + 2, low + 1)]
    return lax.ppermute(own, "col", middles), lax.ppermute(by_two, "col", ends)


def as_pieces(own, first, second, mid, n_col):
    if n_col == 4:
        return [[own], [first[0]], [first[1]], list(second)]
    pieces = [own, first[0], first[1], jnp.where(mid, second[0], second[1])]
    for high in range(4, n_col, 4):
        pieces += [xor_permute(piece, "col", high) for piece in pieces[:4]]
    return [[piece] for piece in pieces]


def fence(*values):
    return lax.optimization_barrier(values)


def add_f32(a, b):
    return a.astype(jnp.float32) + b.astype(jnp.float32)


def stage_sums(keep, recv, n_blocks, rows):
    width = keep.shape[1]
    cut = (n_blocks // 2, 2, 2, rows, width)
    flat = (2, n_blocks // 2, 2, rows, width)

    def summed(shape, pick):
        both = add_f32(pick(keep.reshape(shape)), pick(recv.reshape(shape)))
        return both.astype(jnp.bfloat16).reshape(-1, width)

    stage = [
        summed(cut, lambda v: v[:, 1, 0]),
        summed(cut, lambda v: v[:, 0, 0]),
        summed(flat, lambda v: v[1, :, 1]),
        summed(flat, lambda v: v[0, :, 1]),
    ]
    return stage, add_f32(keep, recv).astype(jnp.bfloat16)


def halve(value, upper, rows):
    blocks = value.shape[0] // rows
    shape = (2, blocks // 2) if upper else (blocks // 2, 2)
    cut = value.reshape(shape + (rows, value.shape[1]))
    if upper:
        sent, kept = cut[1], cut[0]
    else:
        sent, kept = cut[:, 1], cut[:, 0]
    return sent.reshape(-1, value.shape[1]), kept.reshape(-1, value.shape[1])


def exchange_first(stage, bits):
    return xor_permute(stage[0], "row", bits[0]), xor_permute(stage[2], "row", bits[-1])


def exchange_second(stage, recv, bits, rows):
    sent, kept = [], []
    for upper in (0, 1):
        value = add_f32(stage[2 * upper + 1], recv[upper]).astype(jnp.bfloat16)
        sent_u, kept_u = halve(value, upper, rows)
        sent.append(sent_u)
        kept.append(kept_u)
    return kept, sent


def send_second(sent, bits):
    return [xor_permute(s, "row", bit) for s, bit in zip(sent, (bits[1], bits[-2]))]


def exchange_last(kept, recv, bits, rows):
    done = []
    for upper in (0, 1):
        value = add_f32(kept[upper], recv[upper])
        for bit in (bits[::-1] if upper else bits)[2:]:
            sent_u, kept_u = halve(value.astype(jnp.bfloat16), upper, rows)
            value = add_f32(kept_u, xor_permute(sent_u, "row", bit))
        done.append(value.astype(jnp.bfloat16))
    return jnp.concatenate(done, axis=0)


def weight_term(near, sums):
    nodes = near[0].shape[0]
    terms = [
        lax.dot_general(f, sums[q * nodes : (q + 1) * nodes], (((0,), (0,)), ((), ())), preferred_element_type=jnp.float32)
        for q, f in enumerate(near)
    ]
    return tree_sum(terms).astype(jnp.bfloat16)


def sum_over(term, axis, masks):
    parts = [term] + [xor_permute(term, axis, m) for m in masks]
    return tree_sum([p.astype(jnp.float32) for p in parts])


def body(grad_out, preact, features, weight, tiles, tile_rows, tile_cols, live_counts):
    nodes, width = grad_out.shape
    n_row, n_col = lax.axis_size("row"), lax.axis_size("col")
    row, col = lax.axis_index("row"), lax.axis_index("col")
    slots = tiles.shape[2]
    cw = width // 2
    rows = nodes // 2
    bits = [1 << b for b in range(1, n_row.bit_length() - 1)]
    mid = ((col & 3) == 1) | ((col & 3) == 2)

    own0, own1 = [
        jnp.where(preact[:, cut] > 0, grad_out[:, cut], jnp.zeros_like(grad_out[:, cut]))
        for cut in (slice(0, cw), slice(cw, width))
    ]
    first0 = gather_first(own0)
    place = jnp.stack([live_counts.reshape(()), row, col, mid.astype(jnp.int32)])
    plan0, plan1, slot = make_plans(tile_rows, tile_cols, place, n_row, nodes // SIDE)
    flipped = flip_tiles(slot, tiles.reshape(slots, SIDE, SIDE))
    features, plan0 = fence(features, plan0)
    near = [features]
    for bit in bits[:2]:
        near.append(xor_permute(features, "row", bit))
    own0, own1, first0, plan0, plan1, flipped = fence(own0, own1, first0, plan0, plan1, flipped)

    second0 = gather_second(own0, first0[1], n_col)
    pieces0 = as_pieces(own0, first0, second0, mid, n_col)
    pieces0, own1, near = fence(pieces0, own1, near)

    first1 = gather_first(own1)
    near.append(xor_permute(near[1], "row", bits[1]))
    for bit in bits[2:]:
        near += [xor_permute(f, "row", bit) for f in near]
    acc0 = spmm(plan0, pieces0[:FIRST_PIECES], flipped, None, n_row)
    send0, keep0 = spmm(plan1, pieces0[FIRST_PIECES:], flipped, acc0, n_row)
    own1, first1, near, send0, keep0 = fence(own1, first1, near, send0, keep0)

    second1 = gather_second(own1, first1[1], n_col)
    pieces1 = as_pieces(own1, first1, second1, mid, n_col)
    stage0, sums0 = stage_sums(keep0, xor_permute(send0, "row", 1), n_row // 2, rows)
    recv0 = exchange_first(stage0, bits)
    acc1 = spmm(plan0, pieces1[:FIRST_PIECES], flipped, None, n_row)
    pieces1, stage0, acc1 = fence(pieces1, stage0, acc1)

    send1, keep1 = spmm(plan1, pieces1[FIRST_PIECES:], flipped, acc1, n_row)
    send1, keep1, recv0, stage0, sums0 = fence(send1, keep1, recv0, stage0, sums0)

    stage1, sums1 = stage_sums(keep1, xor_permute(send1, "row", 1), n_row // 2, rows)
    rest0, sent0 = exchange_second(stage0, recv0, bits, rows)
    recv0 = send_second(sent0, bits)
    term0 = weight_term(near, sums0)
    stage1, sums1, term0 = fence(stage1, sums1, term0)
    stage1, sums1, term0, rest0, recv0 = fence(stage1, sums1, term0, rest0, recv0)

    recv1 = exchange_first(stage1, bits)
    term1 = weight_term(near, sums1)
    even = (row & 1) == 0
    theirs, mine = jnp.where(even, term1, term0), jnp.where(even, term0, term1)
    mine = add_f32(mine, xor_permute(theirs, "row", 1)).astype(jnp.bfloat16)
    mine = sum_over(mine, "col", range(1, n_col)).astype(jnp.bfloat16)
    colgrad0 = exchange_last(rest0, recv0, bits, rows)
    recv1, mine, colgrad0 = fence(recv1, mine, colgrad0)

    rest1, sent1 = exchange_second(stage1, recv1, bits, rows)
    rest1, sent1, mine = fence(rest1, sent1, mine)
    recv1 = send_second(sent1, bits)
    mine = sum_over(mine, "row", range(2, n_row, 2)).astype(jnp.bfloat16)
    colgrad1 = exchange_last(rest1, recv1, bits, rows)
    colgrad1, mine = fence(colgrad1, mine)

    theirs = xor_permute(mine, "row", 1)
    low, high = jnp.where(even, mine, theirs), jnp.where(even, theirs, mine)
    grad_weight = jnp.concatenate([low, high], axis=1).astype(jnp.float32)
    colgrad = jnp.concatenate([colgrad0, colgrad1], axis=1)
    grad_features = lax.dot_general(
        colgrad, weight, (((1,), (1,)), ((), ())), preferred_element_type=jnp.float32
    ).astype(jnp.bfloat16)
    return (grad_features, grad_weight)


def solution(mesh):
    in_specs = (
        P(("row", "col"), None),
        P(("row", "col"), None),
        P(("col", "row"), None),
        P(),
        P("row", "col", None, None, None),
        P("row", "col", None),
        P("row", "col", None),
        P("row", "col"),
    )
    out_specs = (P(("col", "row"), None), P())
    return jax.shard_map(body, mesh=mesh, in_specs=in_specs, out_specs=out_specs, check_vma=False)
```

```python
import functools

import jax
import jax.numpy as jnp
from jax import lax
from jax.experimental import pallas as pl
from jax.experimental.pallas import tpu as pltpu
from jax.sharding import PartitionSpec as P

SIDE = 128
UNROLL = 8
GROUP = 32
RING = 4
FIRST_PIECES = 3
PLAN_ROWS = 8
FLIP_BYTES = 26 * 1024 * 1024
PLAN_BYTES = 12 * 1024 * 1024
SPMM_BYTES = 16 * 1024 * 1024


def round_up(value, unit):
    return -(-value // unit) * unit


def total(mask, axis):
    return jnp.sum(jnp.where(mask, 1.0, 0.0), axis=axis, keepdims=True).astype(jnp.int32)


def total_of(values, axis):
    return jnp.sum(values.astype(jnp.float32), axis=axis, keepdims=True).astype(jnp.int32)


def plan_kernel(per_dev, n_out, place_ref, rows_r, cols_r, rows_c, cols_c, plan0_ref, plan1_ref, slot_ref):
    slots = rows_r.shape[1]
    size = plan0_ref.shape[1]
    count, row, col, mid = place_ref[0], place_ref[1], place_ref[2], place_ref[3]
    shift = per_dev.bit_length() - 1
    start = FIRST_PIECES * per_dev
    step = 2 * UNROLL

    def attributes(rows, cols, axis):
        ids = lax.broadcasted_iota(jnp.int32, rows.shape, axis)
        row_pos = (((rows >> shift) ^ col) << shift) + (rows & (per_dev - 1))
        away = (cols >> shift) ^ row
        out_pos = ((away >> 1) << shift) + (cols & (per_dev - 1))
        kept = 1 - (away & 1)
        last = (row_pos >= start).astype(jnp.int32)
        live = ids < count
        key = jnp.where(live, (2 * last + kept) * n_out + out_pos, 4 * n_out)
        return ids, row_pos, out_pos, 2 * last + kept, live, key

    ids_r, _, _, part_r, live_r, key_r = attributes(rows_r[...], cols_r[...], 1)
    ids_c, row_pos_c, out_pos_c, part_c, live_c, key_c = attributes(rows_c[...], cols_c[...], 0)
    equal = key_c == key_r
    below = key_r < key_c
    earlier_c = total(equal & (ids_r < ids_c), 1)
    earlier_r = total(equal & (ids_c < ids_r), 0)
    later_r = total(equal & (ids_c > ids_r), 0)
    odd_end = (later_r == 0) & ((earlier_r & 1) == 0)
    weight_r = jnp.where(live_r, jnp.where(odd_end, 2, 1), 0)
    rank_c = total(below, 1) + earlier_c
    rank_r = total(key_c < key_r, 0) + earlier_r
    padded_c = total_of(jnp.where(below, weight_r, 0), 1) + earlier_c
    length = [total_of(jnp.where(part_r == p, weight_r, 0), 1) for p in range(4)]
    n_first = total(live_r & (part_r < 2), 1)
    n_last = count - n_first
    last_base = ((n_first + GROUP - 1) >> 5) << 5
    slot_r = jnp.where(part_r >= 2, last_base + rank_r - n_first, rank_r)
    slot_ref[...] = jnp.where(live_r, slot_r, slots + GROUP)

    lane = lax.broadcasted_iota(jnp.int32, (1, size), 1)
    for p, plan_ref in enumerate((plan0_ref, plan1_ref)):
        sent, held = length[2 * p], length[2 * p + 1]
        sent_steps = (sent + step - 1) >> (step.bit_length() - 1)
        all_steps = sent_steps + ((held + step - 1) >> (step.bit_length() - 1))
        base = length[0] + length[1] if p else jnp.zeros_like(sent)
        in_plan = live_c & ((part_c >> 1) == p)
        pos = padded_c - base + jnp.where((part_c & 1) == 1, sent_steps * step - sent, 0)
        pos = jnp.where(in_plan, pos, -1)
        rank = rank_c - (n_first if p else 0)
        hit = pos == lane

        def placed(values, empty, hit=hit):
            return total_of(jnp.where(hit, values - empty, 0), 0) + empty

        plan_ref[0:1, :] = placed(rank & (RING * GROUP - 1), RING * GROUP)
        plan_ref[1:2, :] = placed(row_pos_c - p * start, 0)
        taken = total(hit, 0) > 0
        ends = [
            jnp.max(jnp.where(in_plan & ((part_c & 1) == h), out_pos_c, 0).astype(jnp.float32), axis=0, keepdims=True)
            for h in range(2)
        ]
        end = jnp.where(lane < sent_steps * step, ends[0], ends[1]).astype(jnp.int32)
        plan_ref[2:3, :] = jnp.where(taken, placed(out_pos_c, 0), end)
        plan_ref[3:4, :] = jnp.where(taken, placed((earlier_c > 0).astype(jnp.int32), 0), 1)
        done = total(in_plan & (pos < (lane + 1) * step), 0)
        tiles = n_last if p else n_first
        info = [
            jnp.full((1, 1), mid, jnp.int32),
            sent_steps,
            (tiles + GROUP - 1) >> 5,
            last_base if p else jnp.zeros_like(last_base),
            jnp.zeros_like(last_base),
        ]
        for g in range(slots // GROUP):
            info.append(total((done <= (g + 1) * GROUP) & (lane < all_steps), 1))
        row_values = jnp.zeros((1, size), jnp.int32)
        for n, value in enumerate(info):
            row_values = jnp.where(lane == n, value, row_values)
        plan_ref[4:5, :] = row_values
        plan_ref[5:6, :] = jnp.full((1, size), row & 1, jnp.int32)
        plan_ref[6:8, :] = jnp.zeros((2, size), jnp.int32)


def make_plans(tile_rows, tile_cols, place, n_row, per_dev):
    slots = tile_rows.size
    n_out = n_row // 2 * per_dev
    size = round_up(slots + 2 * n_out + 4 * UNROLL, SIDE)
    plan = jax.ShapeDtypeStruct((PLAN_ROWS, size), jnp.int32)
    return pl.pallas_call(
        functools.partial(plan_kernel, per_dev, n_out),
        out_shape=(plan, plan, jax.ShapeDtypeStruct((1, slots), jnp.int32)),
        in_specs=[pl.BlockSpec(memory_space=pltpu.SMEM)] + [pl.BlockSpec(memory_space=pltpu.VMEM)] * 4,
        out_specs=[pl.BlockSpec(memory_space=pltpu.VMEM)] * 3,
        compiler_params=pltpu.CompilerParams(vmem_limit_bytes=PLAN_BYTES),
        cost_estimate=pl.CostEstimate(flops=0, bytes_accessed=4096, transcendentals=0),
        name="plan_slots",
    )(place, tile_rows.reshape(1, slots), tile_cols.reshape(1, slots), tile_rows.reshape(slots, 1), tile_cols.reshape(slots, 1))


def flip_kernel(slot_ref, tiles_ref, out_ref, t_in, t_out, in_sem, out_sem):
    slots = t_in.shape[0]
    groups = slots // GROUP
    loads = [
        pltpu.make_async_copy(tiles_ref.at[pl.ds(g * GROUP, GROUP)], t_in.at[pl.ds(g * GROUP, GROUP)], in_sem.at[g])
        for g in range(groups)
    ]
    for load in loads:
        load.start()
    for g in range(groups):
        loads[g].wait()

        def some(step, carry, g=g):
            for u in range(4):
                k = g * GROUP + step * 4 + u
                t_out[slot_ref[0, k]] = t_in[k].T
            return carry

        lax.fori_loop(0, GROUP // 4, some, 0)
    stores = [
        pltpu.make_async_copy(t_out.at[pl.ds(g * GROUP, GROUP)], out_ref.at[pl.ds(g * GROUP, GROUP)], out_sem.at[g])
        for g in range(groups + 1)
    ]
    for store in stores:
        store.start()
    for store in stores:
        store.wait()


def flip_tiles(slot, tile_stack):
    slots = tile_stack.shape[0]
    groups = slots // GROUP
    return pl.pallas_call(
        flip_kernel,
        out_shape=jax.ShapeDtypeStruct((slots + GROUP, SIDE, SIDE), tile_stack.dtype),
        grid_spec=pltpu.PrefetchScalarGridSpec(
            num_scalar_prefetch=1,
            grid=(),
            in_specs=[pl.BlockSpec(memory_space=pl.ANY)],
            out_specs=pl.BlockSpec(memory_space=pl.ANY),
            scratch_shapes=[
                pltpu.VMEM(tile_stack.shape, tile_stack.dtype),
                pltpu.VMEM((slots + GROUP + 1, SIDE, SIDE), tile_stack.dtype),
                pltpu.SemaphoreType.DMA((groups,)),
                pltpu.SemaphoreType.DMA((groups + 1,)),
            ],
        ),
        compiler_params=pltpu.CompilerParams(vmem_limit_bytes=FLIP_BYTES),
        cost_estimate=pl.CostEstimate(flops=0, bytes_accessed=4096, transcendentals=0),
        name="flip_tiles",
    )(slot, tile_stack)


def spmm_kernel(layout, last, by_core, plan_ref, *refs):
    n_refs = sum(layout)
    refs_left = list(refs[:n_refs])
    pieces = [[refs_left.pop(0) for _ in range(n)] for n in layout]
    rest = list(refs[n_refs:])
    tiles_ref = rest.pop(0)
    acc_refs = (rest.pop(0), rest.pop(0)) if last else (None, None)
    if by_core:
        core = plan_ref[5, 0]
        out_ref = rest.pop(0)
        out_refs = (out_ref.at[1 - core], out_ref.at[core])
    else:
        out_refs = (rest.pop(0), rest.pop(0))
    m_vmem, t_vmem, total_ref, sems = rest
    nodes, width = pieces[0][0].shape
    mid, sent_steps, n_groups, tile_base = [plan_ref[4, n] for n in range(4)]

    def group_copy(g):
        place = g & (RING - 1)
        return pltpu.make_async_copy(
            tiles_ref.at[pl.ds(tile_base + pl.multiple_of(g * GROUP, GROUP), GROUP)],
            t_vmem.at[pl.ds(pl.multiple_of(place * GROUP, GROUP), GROUP)],
            sems.at[place],
        )

    for g in range(2):
        pl.when(g < n_groups)(group_copy(g).start)
    t_vmem[RING * GROUP] = jnp.zeros((SIDE, SIDE), t_vmem.dtype)
    for out_ref, acc_ref in zip(out_refs, acc_refs):

        def begin(step, carry, out_ref=out_ref, acc_ref=acc_ref):
            at = pl.ds(pl.multiple_of(step * 256, 256), 256)
            out_ref[at, :] = acc_ref[at, :] if last else jnp.zeros((256, width), out_ref.dtype)
            return carry

        lax.fori_loop(0, out_ref.shape[0] // 256, begin, 0)
    for p, options in enumerate(pieces):

        def take(ref, p=p):
            def some(step, carry):
                at = pl.multiple_of(step * 512, 512)
                m_vmem[pl.ds(pl.multiple_of(p * nodes + at, 512), 512), :] = ref[pl.ds(at, 512), :]
                return carry

            lax.fori_loop(0, nodes // 512, some, 0)

        if len(options) == 1:
            take(options[0])
        else:
            pl.when(mid == 1)(functools.partial(take, options[0]))
            pl.when(mid != 1)(functools.partial(take, options[1]))

    def block(index):
        return m_vmem[pl.ds(pl.multiple_of(index * SIDE, SIDE), SIDE), :]

    def add_pairs(out_ref, acc_ref, step, carry):
        running = total_ref[...]
        prods = []
        for u in range(UNROLL):
            k = 2 * (step * UNROLL + u)
            left = jnp.concatenate([t_vmem[plan_ref[0, k]], t_vmem[plan_ref[0, k + 1]]], axis=1)
            right = jnp.concatenate([block(plan_ref[1, k]), block(plan_ref[1, k + 1])], axis=0)
            prods.append(jnp.dot(left, right, preferred_element_type=jnp.float32))
        for u in range(UNROLL):
            k = 2 * (step * UNROLL + u)
            at = pl.ds(pl.multiple_of(plan_ref[2, k] * SIDE, SIDE), SIDE)
            before = acc_ref[at, :].astype(jnp.float32) if last else jnp.zeros_like(running)
            running = prods[u] + jnp.where(plan_ref[3, k] == 1, running, before)
            out_ref[at, :] = running.astype(out_ref.dtype)
        total_ref[...] = running
        return carry

    total_ref[...] = jnp.zeros_like(total_ref)

    def add_group(g, carry):
        group_copy(g).wait()

        @pl.when(g + 2 < n_groups)
        def _():
            group_copy(g + 2).start()

        low, high = plan_ref[4, 4 + g], plan_ref[4, 5 + g]
        lax.fori_loop(
            jnp.minimum(low, sent_steps), jnp.minimum(high, sent_steps),
            functools.partial(add_pairs, out_refs[0], acc_refs[0]), 0,
        )
        lax.fori_loop(
            jnp.maximum(low, sent_steps), jnp.maximum(high, sent_steps),
            functools.partial(add_pairs, out_refs[1], acc_refs[1]), 0,
        )
        return carry

    lax.fori_loop(0, n_groups, add_group, 0)


def spmm(plan, pieces, tiles, acc, n_row, by_core=False):
    nodes, width = pieces[0][0].shape
    half = n_row // 2 * nodes
    last = acc is not None
    out = jax.ShapeDtypeStruct((2, half, width) if by_core else (half, width), jnp.bfloat16)
    blocks = [ref for p in pieces for ref in p]
    in_vmem, in_any = pl.BlockSpec(memory_space=pltpu.VMEM), pl.BlockSpec(memory_space=pl.ANY)
    return pl.pallas_call(
        functools.partial(spmm_kernel, [len(p) for p in pieces], last, by_core),
        out_shape=(out,) if by_core else (out, out),
        grid_spec=pltpu.PrefetchScalarGridSpec(
            num_scalar_prefetch=1,
            grid=(),
            in_specs=[in_vmem] * len(blocks) + [in_any] + [in_vmem] * len(acc or []),
            out_specs=[in_vmem] * (1 if by_core else 2),
            scratch_shapes=[
                pltpu.VMEM((len(pieces) * nodes, width), jnp.bfloat16),
                pltpu.VMEM((RING * GROUP + 1, SIDE, SIDE), jnp.bfloat16),
                pltpu.VMEM((SIDE, width), jnp.float32),
                pltpu.SemaphoreType.DMA((RING,)),
            ],
        ),
        compiler_params=pltpu.CompilerParams(vmem_limit_bytes=SPMM_BYTES),
        cost_estimate=pl.CostEstimate(flops=0, bytes_accessed=4096, transcendentals=0),
        name="spmm_last" if last else "spmm_first",
    )(plan, *blocks, tiles, *(acc or []))


def xor_permute(value, axis, mask):
    size = lax.axis_size(axis)
    return lax.ppermute(value, axis, [(i, i ^ mask) for i in range(size)])


def tree_sum(values):
    while len(values) > 1:
        values = [a + b for a, b in zip(values[::2], values[1::2])]
    return values[0]


def gather_first(own):
    return xor_permute(own, "col", 1), xor_permute(own, "col", 2)


def gather_second(own, by_two, n_col):
    ends, middles = [], []
    for low in range(0, n_col, 4):
        ends += [(low + 1, low), (low + 2, low + 3)]
        middles += [(low + 1, low + 2), (low + 2, low + 1)]
    return lax.ppermute(own, "col", middles), lax.ppermute(by_two, "col", ends)


def as_pieces(own, first, second, mid, n_col):
    if n_col == 4:
        return [[own], [first[0]], [first[1]], list(second)]
    pieces = [own, first[0], first[1], jnp.where(mid, second[0], second[1])]
    for high in range(4, n_col, 4):
        pieces += [xor_permute(piece, "col", high) for piece in pieces[:4]]
    return [[piece] for piece in pieces]


def swap_cores(both):
    pairs = [[i, i + 1] for i in range(0, lax.axis_size("row"), 2)]
    return lax.all_to_all(both, "row", 0, 0, axis_index_groups=pairs)


def fence(*values):
    return lax.optimization_barrier(values)


def add_f32(a, b):
    return a.astype(jnp.float32) + b.astype(jnp.float32)


def stage_sums(keep, recv, n_blocks, rows, at_once=False):
    width = keep.shape[1]
    cut = (n_blocks // 2, 2, 2, rows, width)
    flat = (2, n_blocks // 2, 2, rows, width)
    sums = add_f32(keep, recv).astype(jnp.bfloat16)
    if at_once:
        (sums,) = fence(sums)

    def summed(shape, pick):
        if at_once:
            return pick(sums.reshape(shape)).reshape(-1, width)
        both = add_f32(pick(keep.reshape(shape)), pick(recv.reshape(shape)))
        return both.astype(jnp.bfloat16).reshape(-1, width)

    stage = [
        summed(cut, lambda v: v[:, 1, 0]),
        summed(cut, lambda v: v[:, 0, 0]),
        summed(flat, lambda v: v[1, :, 1]),
        summed(flat, lambda v: v[0, :, 1]),
    ]
    return stage, sums


def halve(value, upper, rows):
    blocks = value.shape[0] // rows
    shape = (2, blocks // 2) if upper else (blocks // 2, 2)
    cut = value.reshape(shape + (rows, value.shape[1]))
    if upper:
        sent, kept = cut[1], cut[0]
    else:
        sent, kept = cut[:, 1], cut[:, 0]
    return sent.reshape(-1, value.shape[1]), kept.reshape(-1, value.shape[1])


def exchange_first(stage, bits):
    return xor_permute(stage[0], "row", bits[0]), xor_permute(stage[2], "row", bits[-1])


def exchange_second(stage, recv, bits, rows):
    sent, kept = [], []
    for upper in (0, 1):
        value = add_f32(stage[2 * upper + 1], recv[upper]).astype(jnp.bfloat16)
        sent_u, kept_u = halve(value, upper, rows)
        sent.append(sent_u)
        kept.append(kept_u)
    return kept, sent


def send_second(sent, bits):
    return [xor_permute(s, "row", bit) for s, bit in zip(sent, (bits[1], bits[-2]))]


def exchange_last(kept, recv, bits, rows):
    done = []
    for upper in (0, 1):
        value = add_f32(kept[upper], recv[upper])
        for bit in (bits[::-1] if upper else bits)[2:]:
            sent_u, kept_u = halve(value.astype(jnp.bfloat16), upper, rows)
            value = add_f32(kept_u, xor_permute(sent_u, "row", bit))
        done.append(value.astype(jnp.bfloat16))
    return jnp.concatenate(done, axis=0)


def weight_term(near, sums):
    nodes = near[0].shape[0]
    terms = [
        lax.dot_general(f, sums[q * nodes : (q + 1) * nodes], (((0,), (0,)), ((), ())), preferred_element_type=jnp.float32)
        for q, f in enumerate(near)
    ]
    return tree_sum(terms).astype(jnp.bfloat16)


def sum_over(term, axis, masks):
    parts = [term] + [xor_permute(term, axis, m) for m in masks]
    return tree_sum([p.astype(jnp.float32) for p in parts])


def body(grad_out, preact, features, weight, tiles, tile_rows, tile_cols, live_counts):
    nodes, width = grad_out.shape
    n_row, n_col = lax.axis_size("row"), lax.axis_size("col")
    row, col = lax.axis_index("row"), lax.axis_index("col")
    slots = tiles.shape[2]
    cw = width // 2
    rows = nodes // 2
    bits = [1 << b for b in range(1, n_row.bit_length() - 1)]
    mid = ((col & 3) == 1) | ((col & 3) == 2)

    own0, own1 = [
        jnp.where(preact[:, cut] > 0, grad_out[:, cut], jnp.zeros_like(grad_out[:, cut]))
        for cut in (slice(0, cw), slice(cw, width))
    ]
    first0 = gather_first(own0)
    place = jnp.stack([live_counts.reshape(()), row, col, mid.astype(jnp.int32)])
    plan0, plan1, slot = make_plans(tile_rows, tile_cols, place, n_row, nodes // SIDE)
    flipped = flip_tiles(slot, tiles.reshape(slots, SIDE, SIDE))
    features, plan0 = fence(features, plan0)
    near = [features]
    for bit in bits[:2]:
        near.append(xor_permute(features, "row", bit))
    own0, own1, first0, plan0, plan1, flipped = fence(own0, own1, first0, plan0, plan1, flipped)

    second0 = gather_second(own0, first0[1], n_col)
    acc0 = spmm(plan0, [[own0], [first0[0]], [first0[1]]], flipped, None, n_row)
    own1, acc0 = fence(own1, acc0)
    first1 = gather_first(own1)
    pieces0 = as_pieces(own0, first0, second0, mid, n_col)
    pieces0, near, acc0 = fence(pieces0, near, acc0)

    near.append(xor_permute(near[1], "row", bits[1]))
    for bit in bits[2:]:
        near += [xor_permute(f, "row", bit) for f in near]
    (both0,) = spmm(plan1, pieces0[FIRST_PIECES:], flipped, acc0, n_row, by_core=True)
    got0 = swap_cores(both0)
    stage0, sums0 = stage_sums(got0[0], got0[1], n_row // 2, rows, at_once=True)
    own1, first1, near, stage0, sums0 = fence(own1, first1, near, stage0, sums0)

    second1 = gather_second(own1, first1[1], n_col)
    pieces1 = as_pieces(own1, first1, second1, mid, n_col)
    recv0 = exchange_first(stage0, bits)
    acc1 = spmm(plan0, pieces1[:FIRST_PIECES], flipped, None, n_row)
    pieces1, stage0, acc1 = fence(pieces1, stage0, acc1)

    send1, keep1 = spmm(plan1, pieces1[FIRST_PIECES:], flipped, acc1, n_row)
    send1, keep1, recv0, stage0, sums0 = fence(send1, keep1, recv0, stage0, sums0)

    stage1, sums1 = stage_sums(keep1, xor_permute(send1, "row", 1), n_row // 2, rows, at_once=True)
    rest0, sent0 = exchange_second(stage0, recv0, bits, rows)
    recv0 = send_second(sent0, bits)
    term0 = weight_term(near, sums0)
    stage1, sums1, term0 = fence(stage1, sums1, term0)
    stage1, sums1, term0, rest0, recv0 = fence(stage1, sums1, term0, rest0, recv0)

    recv1 = exchange_first(stage1, bits)
    term1 = weight_term(near, sums1)
    even = (row & 1) == 0
    theirs, mine = jnp.where(even, term1, term0), jnp.where(even, term0, term1)
    mine = add_f32(mine, xor_permute(theirs, "row", 1)).astype(jnp.bfloat16)
    mine = sum_over(mine, "col", range(1, n_col)).astype(jnp.bfloat16)
    colgrad0 = exchange_last(rest0, recv0, bits, rows)
    recv1, mine, colgrad0 = fence(recv1, mine, colgrad0)

    rest1, sent1 = exchange_second(stage1, recv1, bits, rows)
    rest1, sent1, mine = fence(rest1, sent1, mine)
    recv1 = send_second(sent1, bits)
    mine = sum_over(mine, "row", range(2, n_row, 2)).astype(jnp.bfloat16)
    colgrad1 = exchange_last(rest1, recv1, bits, rows)
    colgrad1, mine = fence(colgrad1, mine)

    theirs = xor_permute(mine, "row", 1)
    low, high = jnp.where(even, mine, theirs), jnp.where(even, theirs, mine)
    grad_weight = jnp.concatenate([low, high], axis=1).astype(jnp.float32)
    colgrad = jnp.concatenate([colgrad0, colgrad1], axis=1)
    grad_features = lax.dot_general(
        colgrad, weight, (((1,), (1,)), ((), ())), preferred_element_type=jnp.float32
    ).astype(jnp.bfloat16)
    return (grad_features, grad_weight)


def solution(mesh):
    in_specs = (
        P(("row", "col"), None),
        P(("row", "col"), None),
        P(("col", "row"), None),
        P(),
        P("row", "col", None, None, None),
        P("row", "col", None),
        P("row", "col", None),
        P("row", "col"),
    )
    out_specs = (P(("col", "row"), None), P())
    return jax.shard_map(body, mesh=mesh, in_specs=in_specs, out_specs=out_specs, check_vma=False)
```

```python
import functools

import jax
import jax.numpy as jnp
from jax import lax
from jax.experimental import pallas as pl
from jax.experimental.pallas import tpu as pltpu
from jax.sharding import PartitionSpec as P

SIDE = 128
UNROLL = 8
GROUP = 32
RING = 4
FIRST_PIECES = 3
PLAN_ROWS = 8
FLIP_BYTES = 26 * 1024 * 1024
PLAN_BYTES = 12 * 1024 * 1024
SPMM_BYTES = 16 * 1024 * 1024


def round_up(value, unit):
    return -(-value // unit) * unit


def total(mask, axis):
    return jnp.sum(jnp.where(mask, 1.0, 0.0), axis=axis, keepdims=True).astype(jnp.int32)


def total_of(values, axis):
    return jnp.sum(values.astype(jnp.float32), axis=axis, keepdims=True).astype(jnp.int32)


def plan_kernel(per_dev, n_out, place_ref, rows_r, cols_r, rows_c, cols_c, plan0_ref, plan1_ref, slot_ref):
    slots = rows_r.shape[1]
    size = plan0_ref.shape[1]
    count, row, col, mid = place_ref[0], place_ref[1], place_ref[2], place_ref[3]
    shift = per_dev.bit_length() - 1
    start = FIRST_PIECES * per_dev
    step = 2 * UNROLL

    def attributes(rows, cols, axis):
        ids = lax.broadcasted_iota(jnp.int32, rows.shape, axis)
        row_pos = (((rows >> shift) ^ col) << shift) + (rows & (per_dev - 1))
        away = (cols >> shift) ^ row
        out_pos = ((away >> 1) << shift) + (cols & (per_dev - 1))
        kept = 1 - (away & 1)
        last = (row_pos >= start).astype(jnp.int32)
        live = ids < count
        key = jnp.where(live, (2 * last + kept) * n_out + out_pos, 4 * n_out)
        return ids, row_pos, out_pos, 2 * last + kept, live, key

    ids_r, _, _, part_r, live_r, key_r = attributes(rows_r[...], cols_r[...], 1)
    ids_c, row_pos_c, out_pos_c, part_c, live_c, key_c = attributes(rows_c[...], cols_c[...], 0)
    equal = key_c == key_r
    below = key_r < key_c
    earlier_c = total(equal & (ids_r < ids_c), 1)
    earlier_r = total(equal & (ids_c < ids_r), 0)
    later_r = total(equal & (ids_c > ids_r), 0)
    odd_end = (later_r == 0) & ((earlier_r & 1) == 0)
    weight_r = jnp.where(live_r, jnp.where(odd_end, 2, 1), 0)
    rank_c = total(below, 1) + earlier_c
    rank_r = total(key_c < key_r, 0) + earlier_r
    padded_c = total_of(jnp.where(below, weight_r, 0), 1) + earlier_c
    length = [total_of(jnp.where(part_r == p, weight_r, 0), 1) for p in range(4)]
    n_first = total(live_r & (part_r < 2), 1)
    n_last = count - n_first
    last_base = ((n_first + GROUP - 1) >> 5) << 5
    slot_r = jnp.where(part_r >= 2, last_base + rank_r - n_first, rank_r)
    slot_ref[...] = jnp.where(live_r, slot_r, slots + GROUP)

    lane = lax.broadcasted_iota(jnp.int32, (1, size), 1)
    for p, plan_ref in enumerate((plan0_ref, plan1_ref)):
        sent, held = length[2 * p], length[2 * p + 1]
        sent_steps = (sent + step - 1) >> (step.bit_length() - 1)
        all_steps = sent_steps + ((held + step - 1) >> (step.bit_length() - 1))
        base = length[0] + length[1] if p else jnp.zeros_like(sent)
        in_plan = live_c & ((part_c >> 1) == p)
        pos = padded_c - base + jnp.where((part_c & 1) == 1, sent_steps * step - sent, 0)
        pos = jnp.where(in_plan, pos, -1)
        rank = rank_c - (n_first if p else 0)
        hit = pos == lane

        def placed(values, empty, hit=hit):
            return total_of(jnp.where(hit, values - empty, 0), 0) + empty

        plan_ref[0:1, :] = placed(rank & (RING * GROUP - 1), RING * GROUP)
        plan_ref[1:2, :] = placed(row_pos_c - p * start, 0)
        taken = total(hit, 0) > 0
        ends = [
            jnp.max(jnp.where(in_plan & ((part_c & 1) == h), out_pos_c, 0).astype(jnp.float32), axis=0, keepdims=True)
            for h in range(2)
        ]
        end = jnp.where(lane < sent_steps * step, ends[0], ends[1]).astype(jnp.int32)
        plan_ref[2:3, :] = jnp.where(taken, placed(out_pos_c, 0), end)
        plan_ref[3:4, :] = jnp.where(taken, placed((earlier_c > 0).astype(jnp.int32), 0), 1)
        done = total(in_plan & (pos < (lane + 1) * step), 0)
        tiles = n_last if p else n_first
        info = [
            jnp.full((1, 1), mid, jnp.int32),
            sent_steps,
            (tiles + GROUP - 1) >> 5,
            last_base if p else jnp.zeros_like(last_base),
            jnp.zeros_like(last_base),
        ]
        for g in range(slots // GROUP):
            info.append(total((done <= (g + 1) * GROUP) & (lane < all_steps), 1))
        row_values = jnp.zeros((1, size), jnp.int32)
        for n, value in enumerate(info):
            row_values = jnp.where(lane == n, value, row_values)
        plan_ref[4:5, :] = row_values
        plan_ref[5:6, :] = jnp.full((1, size), row & 1, jnp.int32)
        plan_ref[6:8, :] = jnp.zeros((2, size), jnp.int32)


def make_plans(tile_rows, tile_cols, place, n_row, per_dev):
    slots = tile_rows.size
    n_out = n_row // 2 * per_dev
    size = round_up(slots + 2 * n_out + 4 * UNROLL, SIDE)
    plan = jax.ShapeDtypeStruct((PLAN_ROWS, size), jnp.int32)
    return pl.pallas_call(
        functools.partial(plan_kernel, per_dev, n_out),
        out_shape=(plan, plan, jax.ShapeDtypeStruct((1, slots), jnp.int32)),
        in_specs=[pl.BlockSpec(memory_space=pltpu.SMEM)] + [pl.BlockSpec(memory_space=pltpu.VMEM)] * 4,
        out_specs=[pl.BlockSpec(memory_space=pltpu.VMEM)] * 3,
        compiler_params=pltpu.CompilerParams(vmem_limit_bytes=PLAN_BYTES),
        cost_estimate=pl.CostEstimate(flops=0, bytes_accessed=4096, transcendentals=0),
        name="plan_slots",
    )(place, tile_rows.reshape(1, slots), tile_cols.reshape(1, slots), tile_rows.reshape(slots, 1), tile_cols.reshape(slots, 1))


def flip_kernel(slot_ref, tiles_ref, out_ref, t_in, t_out, in_sem, out_sem):
    slots = t_in.shape[0]
    groups = slots // GROUP
    loads = [
        pltpu.make_async_copy(tiles_ref.at[pl.ds(g * GROUP, GROUP)], t_in.at[pl.ds(g * GROUP, GROUP)], in_sem.at[g])
        for g in range(groups)
    ]
    for load in loads:
        load.start()
    for g in range(groups):
        loads[g].wait()

        def some(step, carry, g=g):
            for u in range(4):
                k = g * GROUP + step * 4 + u
                t_out[slot_ref[0, k]] = t_in[k].T
            return carry

        lax.fori_loop(0, GROUP // 4, some, 0)
    stores = [
        pltpu.make_async_copy(t_out.at[pl.ds(g * GROUP, GROUP)], out_ref.at[pl.ds(g * GROUP, GROUP)], out_sem.at[g])
        for g in range(groups + 1)
    ]
    for store in stores:
        store.start()
    for store in stores:
        store.wait()


def flip_tiles(slot, tile_stack):
    slots = tile_stack.shape[0]
    groups = slots // GROUP
    return pl.pallas_call(
        flip_kernel,
        out_shape=jax.ShapeDtypeStruct((slots + GROUP, SIDE, SIDE), tile_stack.dtype),
        grid_spec=pltpu.PrefetchScalarGridSpec(
            num_scalar_prefetch=1,
            grid=(),
            in_specs=[pl.BlockSpec(memory_space=pl.ANY)],
            out_specs=pl.BlockSpec(memory_space=pl.ANY),
            scratch_shapes=[
                pltpu.VMEM(tile_stack.shape, tile_stack.dtype),
                pltpu.VMEM((slots + GROUP + 1, SIDE, SIDE), tile_stack.dtype),
                pltpu.SemaphoreType.DMA((groups,)),
                pltpu.SemaphoreType.DMA((groups + 1,)),
            ],
        ),
        compiler_params=pltpu.CompilerParams(vmem_limit_bytes=FLIP_BYTES),
        cost_estimate=pl.CostEstimate(flops=0, bytes_accessed=4096, transcendentals=0),
        name="flip_tiles",
    )(slot, tile_stack)


def spmm_kernel(layout, last, by_core, plan_ref, *refs):
    n_refs = sum(layout)
    refs_left = list(refs[:n_refs])
    pieces = [[refs_left.pop(0) for _ in range(n)] for n in layout]
    rest = list(refs[n_refs:])
    tiles_ref = rest.pop(0)
    acc_refs = (rest.pop(0), rest.pop(0)) if last else (None, None)
    if by_core:
        core = plan_ref[5, 0]
        out_ref = rest.pop(0)
        out_refs = (out_ref.at[1 - core], out_ref.at[core])
    else:
        out_refs = (rest.pop(0), rest.pop(0))
    m_vmem, t_vmem, total_ref, sems = rest
    nodes, width = pieces[0][0].shape
    mid, sent_steps, n_groups, tile_base = [plan_ref[4, n] for n in range(4)]

    def group_copy(g):
        place = g & (RING - 1)
        return pltpu.make_async_copy(
            tiles_ref.at[pl.ds(tile_base + pl.multiple_of(g * GROUP, GROUP), GROUP)],
            t_vmem.at[pl.ds(pl.multiple_of(place * GROUP, GROUP), GROUP)],
            sems.at[place],
        )

    for g in range(2):
        pl.when(g < n_groups)(group_copy(g).start)
    t_vmem[RING * GROUP] = jnp.zeros((SIDE, SIDE), t_vmem.dtype)
    for out_ref, acc_ref in zip(out_refs, acc_refs):

        def begin(step, carry, out_ref=out_ref, acc_ref=acc_ref):
            at = pl.ds(pl.multiple_of(step * 256, 256), 256)
            out_ref[at, :] = acc_ref[at, :] if last else jnp.zeros((256, width), out_ref.dtype)
            return carry

        lax.fori_loop(0, out_ref.shape[0] // 256, begin, 0)
    for p, options in enumerate(pieces):

        def take(ref, p=p):
            def some(step, carry):
                at = pl.multiple_of(step * 512, 512)
                m_vmem[pl.ds(pl.multiple_of(p * nodes + at, 512), 512), :] = ref[pl.ds(at, 512), :]
                return carry

            lax.fori_loop(0, nodes // 512, some, 0)

        if len(options) == 1:
            take(options[0])
        else:
            pl.when(mid == 1)(functools.partial(take, options[0]))
            pl.when(mid != 1)(functools.partial(take, options[1]))

    def block(index):
        return m_vmem[pl.ds(pl.multiple_of(index * SIDE, SIDE), SIDE), :]

    def add_pairs(out_ref, acc_ref, step, carry):
        running = total_ref[...]
        prods = []
        for u in range(UNROLL):
            k = 2 * (step * UNROLL + u)
            left = jnp.concatenate([t_vmem[plan_ref[0, k]], t_vmem[plan_ref[0, k + 1]]], axis=1)
            right = jnp.concatenate([block(plan_ref[1, k]), block(plan_ref[1, k + 1])], axis=0)
            prods.append(jnp.dot(left, right, preferred_element_type=jnp.float32))
        for u in range(UNROLL):
            k = 2 * (step * UNROLL + u)
            at = pl.ds(pl.multiple_of(plan_ref[2, k] * SIDE, SIDE), SIDE)
            before = acc_ref[at, :].astype(jnp.float32) if last else jnp.zeros_like(running)
            running = prods[u] + jnp.where(plan_ref[3, k] == 1, running, before)
            out_ref[at, :] = running.astype(out_ref.dtype)
        total_ref[...] = running
        return carry

    total_ref[...] = jnp.zeros_like(total_ref)

    def add_group(g, carry):
        group_copy(g).wait()

        @pl.when(g + 2 < n_groups)
        def _():
            group_copy(g + 2).start()

        low, high = plan_ref[4, 4 + g], plan_ref[4, 5 + g]
        lax.fori_loop(
            jnp.minimum(low, sent_steps), jnp.minimum(high, sent_steps),
            functools.partial(add_pairs, out_refs[0], acc_refs[0]), 0,
        )
        lax.fori_loop(
            jnp.maximum(low, sent_steps), jnp.maximum(high, sent_steps),
            functools.partial(add_pairs, out_refs[1], acc_refs[1]), 0,
        )
        return carry

    lax.fori_loop(0, n_groups, add_group, 0)


def spmm(plan, pieces, tiles, acc, n_row, by_core=False):
    nodes, width = pieces[0][0].shape
    half = n_row // 2 * nodes
    last = acc is not None
    out = jax.ShapeDtypeStruct((2, half, width) if by_core else (half, width), jnp.bfloat16)
    blocks = [ref for p in pieces for ref in p]
    in_vmem, in_any = pl.BlockSpec(memory_space=pltpu.VMEM), pl.BlockSpec(memory_space=pl.ANY)
    return pl.pallas_call(
        functools.partial(spmm_kernel, [len(p) for p in pieces], last, by_core),
        out_shape=(out,) if by_core else (out, out),
        grid_spec=pltpu.PrefetchScalarGridSpec(
            num_scalar_prefetch=1,
            grid=(),
            in_specs=[in_vmem] * len(blocks) + [in_any] + [in_vmem] * len(acc or []),
            out_specs=[in_vmem] * (1 if by_core else 2),
            scratch_shapes=[
                pltpu.VMEM((len(pieces) * nodes, width), jnp.bfloat16),
                pltpu.VMEM((RING * GROUP + 1, SIDE, SIDE), jnp.bfloat16),
                pltpu.VMEM((SIDE, width), jnp.float32),
                pltpu.SemaphoreType.DMA((RING,)),
            ],
        ),
        compiler_params=pltpu.CompilerParams(vmem_limit_bytes=SPMM_BYTES),
        cost_estimate=pl.CostEstimate(flops=0, bytes_accessed=4096, transcendentals=0),
        name="spmm_last" if last else "spmm_first",
    )(plan, *blocks, tiles, *(acc or []))


def xor_permute(value, axis, mask):
    size = lax.axis_size(axis)
    return lax.ppermute(value, axis, [(i, i ^ mask) for i in range(size)])


def tree_sum(values):
    while len(values) > 1:
        values = [a + b for a, b in zip(values[::2], values[1::2])]
    return values[0]


def gather_first(own):
    return xor_permute(own, "col", 1), xor_permute(own, "col", 2)


def gather_second(own, by_two, n_col):
    ends, middles = [], []
    for low in range(0, n_col, 4):
        ends += [(low + 1, low), (low + 2, low + 3)]
        middles += [(low + 1, low + 2), (low + 2, low + 1)]
    return lax.ppermute(own, "col", middles), lax.ppermute(by_two, "col", ends)


def as_pieces(own, first, second, mid, n_col):
    if n_col == 4:
        return [[own], [first[0]], [first[1]], list(second)]
    pieces = [own, first[0], first[1], jnp.where(mid, second[0], second[1])]
    for high in range(4, n_col, 4):
        pieces += [xor_permute(piece, "col", high) for piece in pieces[:4]]
    return [[piece] for piece in pieces]


def swap_cores(both):
    pairs = [[i, i + 1] for i in range(0, lax.axis_size("row"), 2)]
    return lax.all_to_all(both, "row", 0, 0, axis_index_groups=pairs)


def fence(*values):
    return lax.optimization_barrier(values)


def add_f32(a, b):
    return a.astype(jnp.float32) + b.astype(jnp.float32)


def stage_sums(keep, recv, n_blocks, rows, at_once=False):
    width = keep.shape[1]
    cut = (n_blocks // 2, 2, 2, rows, width)
    flat = (2, n_blocks // 2, 2, rows, width)
    sums = add_f32(keep, recv).astype(jnp.bfloat16)
    if at_once:
        (sums,) = fence(sums)

    def summed(shape, pick):
        if at_once:
            return pick(sums.reshape(shape)).reshape(-1, width)
        both = add_f32(pick(keep.reshape(shape)), pick(recv.reshape(shape)))
        return both.astype(jnp.bfloat16).reshape(-1, width)

    stage = [
        summed(cut, lambda v: v[:, 1, 0]),
        summed(cut, lambda v: v[:, 0, 0]),
        summed(flat, lambda v: v[1, :, 1]),
        summed(flat, lambda v: v[0, :, 1]),
    ]
    return stage, sums


def halve(value, upper, rows):
    blocks = value.shape[0] // rows
    shape = (2, blocks // 2) if upper else (blocks // 2, 2)
    cut = value.reshape(shape + (rows, value.shape[1]))
    if upper:
        sent, kept = cut[1], cut[0]
    else:
        sent, kept = cut[:, 1], cut[:, 0]
    return sent.reshape(-1, value.shape[1]), kept.reshape(-1, value.shape[1])


def exchange_first(stage, bits):
    return xor_permute(stage[0], "row", bits[0]), xor_permute(stage[2], "row", bits[-1])


def exchange_second(stage, recv, bits, rows):
    sent, kept = [], []
    for upper in (0, 1):
        value = add_f32(stage[2 * upper + 1], recv[upper]).astype(jnp.bfloat16)
        sent_u, kept_u = halve(value, upper, rows)
        sent.append(sent_u)
        kept.append(kept_u)
    return kept, sent


def send_second(sent, bits):
    return [xor_permute(s, "row", bit) for s, bit in zip(sent, (bits[1], bits[-2]))]


def exchange_last(kept, recv, bits, rows):
    done = []
    for upper in (0, 1):
        value = add_f32(kept[upper], recv[upper])
        for bit in (bits[::-1] if upper else bits)[2:]:
            sent_u, kept_u = halve(value.astype(jnp.bfloat16), upper, rows)
            value = add_f32(kept_u, xor_permute(sent_u, "row", bit))
        done.append(value.astype(jnp.bfloat16))
    return jnp.concatenate(done, axis=0)


def weight_term(near, sums):
    terms, at = [], 0
    for f in [part for parts in near for part in parts]:
        own = sums[at : at + f.shape[0]]
        terms.append(lax.dot_general(f, own, (((0,), (0,)), ((), ())), preferred_element_type=jnp.float32))
        at += f.shape[0]
    return sum(terms[1:], terms[0]).astype(jnp.bfloat16)


def sum_over(term, axis, masks):
    parts = [term] + [xor_permute(term, axis, m) for m in masks]
    return tree_sum([p.astype(jnp.float32) for p in parts])


def body(grad_out, preact, features, weight, tiles, tile_rows, tile_cols, live_counts):
    nodes, width = grad_out.shape
    n_row, n_col = lax.axis_size("row"), lax.axis_size("col")
    row, col = lax.axis_index("row"), lax.axis_index("col")
    slots = tiles.shape[2]
    cw = width // 2
    rows = nodes // 2
    bits = [1 << b for b in range(1, n_row.bit_length() - 1)]
    mid = ((col & 3) == 1) | ((col & 3) == 2)

    own0, own1 = [
        jnp.where(preact[:, cut] > 0, grad_out[:, cut], jnp.zeros_like(grad_out[:, cut]))
        for cut in (slice(0, cw), slice(cw, width))
    ]
    first0 = gather_first(own0)
    place = jnp.stack([live_counts.reshape(()), row, col, mid.astype(jnp.int32)])
    plan0, plan1, slot = make_plans(tile_rows, tile_cols, place, n_row, nodes // SIDE)
    flipped = flip_tiles(slot, tiles.reshape(slots, SIDE, SIDE))
    features, plan0 = fence(features, plan0)
    near = [[features]]
    for bit in bits[:2]:
        near.append([xor_permute(features, "row", bit)])
    own0, own1, first0, plan0, plan1, flipped = fence(own0, own1, first0, plan0, plan1, flipped)

    second0 = gather_second(own0, first0[1], n_col)
    acc0 = spmm(plan0, [[own0], [first0[0]], [first0[1]]], flipped, None, n_row)
    own1, acc0 = fence(own1, acc0)
    first1 = gather_first(own1)
    pieces0 = as_pieces(own0, first0, second0, mid, n_col)
    pieces0, near, acc0 = fence(pieces0, near, acc0)

    near.append([xor_permute(near[1][0][:rows], "row", bits[1]), xor_permute(near[2][0][rows:], "row", bits[0])])
    for bit in bits[2:]:
        near += [[xor_permute(f, "row", bit) for f in parts] for parts in near]
    (both0,) = spmm(plan1, pieces0[FIRST_PIECES:], flipped, acc0, n_row, by_core=True)
    got0 = swap_cores(both0)
    got0, near = fence(got0, near)
    stage0, sums0 = stage_sums(got0[0], got0[1], n_row // 2, rows, at_once=True)
    own1, first1, stage0, sums0 = fence(own1, first1, stage0, sums0)

    second1 = gather_second(own1, first1[1], n_col)
    pieces1 = as_pieces(own1, first1, second1, mid, n_col)
    recv0 = exchange_first(stage0, bits)
    acc1 = spmm(plan0, pieces1[:FIRST_PIECES], flipped, None, n_row)
    rest0, sent0 = exchange_second(stage0, recv0, bits, rows)
    pieces1, rest0, sent0, acc1 = fence(pieces1, rest0, sent0, acc1)

    send1, keep1 = spmm(plan1, pieces1[FIRST_PIECES:], flipped, acc1, n_row)
    send1, keep1, sent0, sums0 = fence(send1, keep1, sent0, sums0)

    stage1, sums1 = stage_sums(keep1, xor_permute(send1, "row", 1), n_row // 2, rows, at_once=True)
    recv0 = send_second(sent0, bits)
    term0 = weight_term(near, sums0)
    stage1, sums1, term0 = fence(stage1, sums1, term0)
    stage1, sums1, term0, rest0, recv0 = fence(stage1, sums1, term0, rest0, recv0)

    recv1 = exchange_first(stage1, bits)
    term1 = weight_term(near, sums1)
    even = (row & 1) == 0
    theirs, mine = jnp.where(even, term1, term0), jnp.where(even, term0, term1)
    mine = add_f32(mine, xor_permute(theirs, "row", 1)).astype(jnp.bfloat16)
    mine = sum_over(mine, "col", range(1, n_col)).astype(jnp.bfloat16)
    colgrad0 = exchange_last(rest0, recv0, bits, rows)
    recv1, mine, colgrad0 = fence(recv1, mine, colgrad0)

    rest1, sent1 = exchange_second(stage1, recv1, bits, rows)
    rest1, sent1, mine = fence(rest1, sent1, mine)
    recv1 = send_second(sent1, bits)
    mine = sum_over(mine, "row", range(2, n_row, 2)).astype(jnp.bfloat16)
    colgrad1 = exchange_last(rest1, recv1, bits, rows)
    colgrad1, mine = fence(colgrad1, mine)

    theirs = xor_permute(mine, "row", 1)
    low, high = jnp.where(even, mine, theirs), jnp.where(even, theirs, mine)
    grad_weight = jnp.concatenate([low, high], axis=1).astype(jnp.float32)
    colgrad = jnp.concatenate([colgrad0, colgrad1], axis=1)
    grad_features = lax.dot_general(
        colgrad, weight, (((1,), (1,)), ((), ())), preferred_element_type=jnp.float32
    ).astype(jnp.bfloat16)
    return (grad_features, grad_weight)


def solution(mesh):
    in_specs = (
        P(("row", "col"), None),
        P(("row", "col"), None),
        P(("col", "row"), None),
        P(),
        P("row", "col", None, None, None),
        P("row", "col", None),
        P("row", "col", None),
        P("row", "col"),
    )
    out_specs = (P(("col", "row"), None), P())
    return jax.shard_map(body, mesh=mesh, in_specs=in_specs, out_specs=out_specs, check_vma=False)
```

```python
import functools

import jax
import jax.numpy as jnp
from jax import lax
from jax.experimental import pallas as pl
from jax.experimental.pallas import tpu as pltpu
from jax.sharding import PartitionSpec as P

SIDE = 128
UNROLL = 8
GROUP = 32
RING = 4
FIRST_PIECES = 3
PLAN_ROWS = 8
FLIP_BYTES = 26 * 1024 * 1024
PLAN_BYTES = 12 * 1024 * 1024
SPMM_BYTES = 16 * 1024 * 1024


def round_up(value, unit):
    return -(-value // unit) * unit


def total(mask, axis):
    return jnp.sum(jnp.where(mask, 1.0, 0.0), axis=axis, keepdims=True).astype(jnp.int32)


def total_of(values, axis):
    return jnp.sum(values.astype(jnp.float32), axis=axis, keepdims=True).astype(jnp.int32)


def plan_kernel(per_dev, n_out, place_ref, rows_r, cols_r, rows_c, cols_c, plan0_ref, plan1_ref, slot_ref):
    slots = rows_r.shape[1]
    size = plan0_ref.shape[1]
    count, row, col, mid = place_ref[0], place_ref[1], place_ref[2], place_ref[3]
    shift = per_dev.bit_length() - 1
    start = FIRST_PIECES * per_dev
    step = 2 * UNROLL

    def attributes(rows, cols, axis):
        ids = lax.broadcasted_iota(jnp.int32, rows.shape, axis)
        row_pos = (((rows >> shift) ^ col) << shift) + (rows & (per_dev - 1))
        away = (cols >> shift) ^ row
        out_pos = ((away >> 1) << shift) + (cols & (per_dev - 1))
        kept = 1 - (away & 1)
        last = (row_pos >= start).astype(jnp.int32)
        live = ids < count
        key = jnp.where(live, (2 * last + kept) * n_out + out_pos, 4 * n_out)
        return ids, row_pos, out_pos, 2 * last + kept, live, key

    ids_r, _, _, part_r, live_r, key_r = attributes(rows_r[...], cols_r[...], 1)
    ids_c, row_pos_c, out_pos_c, part_c, live_c, key_c = attributes(rows_c[...], cols_c[...], 0)
    equal = key_c == key_r
    below = key_r < key_c
    earlier_c = total(equal & (ids_r < ids_c), 1)
    earlier_r = total(equal & (ids_c < ids_r), 0)
    later_r = total(equal & (ids_c > ids_r), 0)
    odd_end = (later_r == 0) & ((earlier_r & 1) == 0)
    weight_r = jnp.where(live_r, jnp.where(odd_end, 2, 1), 0)
    rank_c = total(below, 1) + earlier_c
    rank_r = total(key_c < key_r, 0) + earlier_r
    padded_c = total_of(jnp.where(below, weight_r, 0), 1) + earlier_c
    length = [total_of(jnp.where(part_r == p, weight_r, 0), 1) for p in range(4)]
    n_first = total(live_r & (part_r < 2), 1)
    n_last = count - n_first
    last_base = ((n_first + GROUP - 1) >> 5) << 5
    slot_r = jnp.where(part_r >= 2, last_base + rank_r - n_first, rank_r)
    slot_ref[...] = jnp.where(live_r, slot_r, slots + GROUP)

    lane = lax.broadcasted_iota(jnp.int32, (1, size), 1)
    for p, plan_ref in enumerate((plan0_ref, plan1_ref)):
        sent, held = length[2 * p], length[2 * p + 1]
        sent_steps = (sent + step - 1) >> (step.bit_length() - 1)
        all_steps = sent_steps + ((held + step - 1) >> (step.bit_length() - 1))
        base = length[0] + length[1] if p else jnp.zeros_like(sent)
        in_plan = live_c & ((part_c >> 1) == p)
        pos = padded_c - base + jnp.where((part_c & 1) == 1, sent_steps * step - sent, 0)
        pos = jnp.where(in_plan, pos, -1)
        rank = rank_c - (n_first if p else 0)
        hit = pos == lane

        def placed(values, empty, hit=hit):
            return total_of(jnp.where(hit, values - empty, 0), 0) + empty

        plan_ref[0:1, :] = placed(rank & (RING * GROUP - 1), RING * GROUP)
        plan_ref[1:2, :] = placed(row_pos_c - p * start, 0)
        taken = total(hit, 0) > 0
        ends = [
            jnp.max(jnp.where(in_plan & ((part_c & 1) == h), out_pos_c, 0).astype(jnp.float32), axis=0, keepdims=True)
            for h in range(2)
        ]
        end = jnp.where(lane < sent_steps * step, ends[0], ends[1]).astype(jnp.int32)
        plan_ref[2:3, :] = jnp.where(taken, placed(out_pos_c, 0), end)
        plan_ref[3:4, :] = jnp.where(taken, placed((earlier_c > 0).astype(jnp.int32), 0), 1)
        done = total(in_plan & (pos < (lane + 1) * step), 0)
        tiles = n_last if p else n_first
        info = [
            jnp.full((1, 1), mid, jnp.int32),
            sent_steps,
            (tiles + GROUP - 1) >> 5,
            last_base if p else jnp.zeros_like(last_base),
            jnp.zeros_like(last_base),
        ]
        for g in range(slots // GROUP):
            info.append(total((done <= (g + 1) * GROUP) & (lane < all_steps), 1))
        row_values = jnp.zeros((1, size), jnp.int32)
        for n, value in enumerate(info):
            row_values = jnp.where(lane == n, value, row_values)
        plan_ref[4:5, :] = row_values
        plan_ref[5:6, :] = jnp.full((1, size), row & 1, jnp.int32)
        plan_ref[6:8, :] = jnp.zeros((2, size), jnp.int32)


def make_plans(tile_rows, tile_cols, place, n_row, per_dev):
    slots = tile_rows.size
    n_out = n_row // 2 * per_dev
    size = round_up(slots + 2 * n_out + 4 * UNROLL, SIDE)
    plan = jax.ShapeDtypeStruct((PLAN_ROWS, size), jnp.int32)
    return pl.pallas_call(
        functools.partial(plan_kernel, per_dev, n_out),
        out_shape=(plan, plan, jax.ShapeDtypeStruct((1, slots), jnp.int32)),
        in_specs=[pl.BlockSpec(memory_space=pltpu.SMEM)] + [pl.BlockSpec(memory_space=pltpu.VMEM)] * 4,
        out_specs=[pl.BlockSpec(memory_space=pltpu.VMEM)] * 3,
        compiler_params=pltpu.CompilerParams(vmem_limit_bytes=PLAN_BYTES),
        cost_estimate=pl.CostEstimate(flops=0, bytes_accessed=4096, transcendentals=0),
        name="plan_slots",
    )(place, tile_rows.reshape(1, slots), tile_cols.reshape(1, slots), tile_rows.reshape(slots, 1), tile_cols.reshape(slots, 1))


def flip_kernel(slot_ref, tiles_ref, out_ref, t_in, t_out, in_sem, out_sem):
    slots = t_in.shape[0]
    groups = slots // GROUP
    loads = [
        pltpu.make_async_copy(tiles_ref.at[pl.ds(g * GROUP, GROUP)], t_in.at[pl.ds(g * GROUP, GROUP)], in_sem.at[g])
        for g in range(groups)
    ]
    for load in loads:
        load.start()
    for g in range(groups):
        loads[g].wait()

        def some(step, carry, g=g):
            for u in range(4):
                k = g * GROUP + step * 4 + u
                t_out[slot_ref[0, k]] = t_in[k].T
            return carry

        lax.fori_loop(0, GROUP // 4, some, 0)
    stores = [
        pltpu.make_async_copy(t_out.at[pl.ds(g * GROUP, GROUP)], out_ref.at[pl.ds(g * GROUP, GROUP)], out_sem.at[g])
        for g in range(groups + 1)
    ]
    for store in stores:
        store.start()
    for store in stores:
        store.wait()


def flip_tiles(slot, tile_stack):
    slots = tile_stack.shape[0]
    groups = slots // GROUP
    return pl.pallas_call(
        flip_kernel,
        out_shape=jax.ShapeDtypeStruct((slots + GROUP, SIDE, SIDE), tile_stack.dtype),
        grid_spec=pltpu.PrefetchScalarGridSpec(
            num_scalar_prefetch=1,
            grid=(),
            in_specs=[pl.BlockSpec(memory_space=pl.ANY)],
            out_specs=pl.BlockSpec(memory_space=pl.ANY),
            scratch_shapes=[
                pltpu.VMEM(tile_stack.shape, tile_stack.dtype),
                pltpu.VMEM((slots + GROUP + 1, SIDE, SIDE), tile_stack.dtype),
                pltpu.SemaphoreType.DMA((groups,)),
                pltpu.SemaphoreType.DMA((groups + 1,)),
            ],
        ),
        compiler_params=pltpu.CompilerParams(vmem_limit_bytes=FLIP_BYTES),
        cost_estimate=pl.CostEstimate(flops=0, bytes_accessed=4096, transcendentals=0),
        name="flip_tiles",
    )(slot, tile_stack)


def spmm_kernel(layout, last, by_core, plan_ref, *refs):
    n_refs = sum(layout)
    refs_left = list(refs[:n_refs])
    pieces = [[refs_left.pop(0) for _ in range(n)] for n in layout]
    rest = list(refs[n_refs:])
    tiles_ref = rest.pop(0)
    acc_refs = (rest.pop(0), rest.pop(0)) if last else (None, None)
    if by_core:
        core = plan_ref[5, 0]
        out_ref = rest.pop(0)
        out_refs = (out_ref.at[1 - core], out_ref.at[core])
    else:
        out_refs = (rest.pop(0), rest.pop(0))
    m_vmem, t_vmem, total_ref, sems = rest
    nodes, width = pieces[0][0].shape
    mid, sent_steps, n_groups, tile_base = [plan_ref[4, n] for n in range(4)]

    def group_copy(g):
        place = g & (RING - 1)
        return pltpu.make_async_copy(
            tiles_ref.at[pl.ds(tile_base + pl.multiple_of(g * GROUP, GROUP), GROUP)],
            t_vmem.at[pl.ds(pl.multiple_of(place * GROUP, GROUP), GROUP)],
            sems.at[place],
        )

    for g in range(2):
        pl.when(g < n_groups)(group_copy(g).start)
    t_vmem[RING * GROUP] = jnp.zeros((SIDE, SIDE), t_vmem.dtype)
    for out_ref, acc_ref in zip(out_refs, acc_refs):

        def begin(step, carry, out_ref=out_ref, acc_ref=acc_ref):
            at = pl.ds(pl.multiple_of(step * 256, 256), 256)
            out_ref[at, :] = acc_ref[at, :] if last else jnp.zeros((256, width), out_ref.dtype)
            return carry

        lax.fori_loop(0, out_ref.shape[0] // 256, begin, 0)
    for p, options in enumerate(pieces):

        def take(ref, p=p):
            def some(step, carry):
                at = pl.multiple_of(step * 512, 512)
                m_vmem[pl.ds(pl.multiple_of(p * nodes + at, 512), 512), :] = ref[pl.ds(at, 512), :]
                return carry

            lax.fori_loop(0, nodes // 512, some, 0)

        if len(options) == 1:
            take(options[0])
        else:
            pl.when(mid == 1)(functools.partial(take, options[0]))
            pl.when(mid != 1)(functools.partial(take, options[1]))

    def block(index):
        return m_vmem[pl.ds(pl.multiple_of(index * SIDE, SIDE), SIDE), :]

    def add_pairs(out_ref, acc_ref, step, carry):
        running = total_ref[...]
        prods = []
        for u in range(UNROLL):
            k = 2 * (step * UNROLL + u)
            left = jnp.concatenate([t_vmem[plan_ref[0, k]], t_vmem[plan_ref[0, k + 1]]], axis=1)
            right = jnp.concatenate([block(plan_ref[1, k]), block(plan_ref[1, k + 1])], axis=0)
            prods.append(jnp.dot(left, right, preferred_element_type=jnp.float32))
        for u in range(UNROLL):
            k = 2 * (step * UNROLL + u)
            at = pl.ds(pl.multiple_of(plan_ref[2, k] * SIDE, SIDE), SIDE)
            before = acc_ref[at, :].astype(jnp.float32) if last else jnp.zeros_like(running)
            running = prods[u] + jnp.where(plan_ref[3, k] == 1, running, before)
            out_ref[at, :] = running.astype(out_ref.dtype)
        total_ref[...] = running
        return carry

    total_ref[...] = jnp.zeros_like(total_ref)

    def add_group(g, carry):
        group_copy(g).wait()

        @pl.when(g + 2 < n_groups)
        def _():
            group_copy(g + 2).start()

        low, high = plan_ref[4, 4 + g], plan_ref[4, 5 + g]
        lax.fori_loop(
            jnp.minimum(low, sent_steps), jnp.minimum(high, sent_steps),
            functools.partial(add_pairs, out_refs[0], acc_refs[0]), 0,
        )
        lax.fori_loop(
            jnp.maximum(low, sent_steps), jnp.maximum(high, sent_steps),
            functools.partial(add_pairs, out_refs[1], acc_refs[1]), 0,
        )
        return carry

    lax.fori_loop(0, n_groups, add_group, 0)


def spmm(plan, pieces, tiles, acc, n_row, by_core=False):
    nodes, width = pieces[0][0].shape
    half = n_row // 2 * nodes
    last = acc is not None
    out = jax.ShapeDtypeStruct((2, half, width) if by_core else (half, width), jnp.bfloat16)
    blocks = [ref for p in pieces for ref in p]
    in_vmem, in_any = pl.BlockSpec(memory_space=pltpu.VMEM), pl.BlockSpec(memory_space=pl.ANY)
    return pl.pallas_call(
        functools.partial(spmm_kernel, [len(p) for p in pieces], last, by_core),
        out_shape=(out,) if by_core else (out, out),
        grid_spec=pltpu.PrefetchScalarGridSpec(
            num_scalar_prefetch=1,
            grid=(),
            in_specs=[in_vmem] * len(blocks) + [in_any] + [in_vmem] * len(acc or []),
            out_specs=[in_vmem] * (1 if by_core else 2),
            scratch_shapes=[
                pltpu.VMEM((len(pieces) * nodes, width), jnp.bfloat16),
                pltpu.VMEM((RING * GROUP + 1, SIDE, SIDE), jnp.bfloat16),
                pltpu.VMEM((SIDE, width), jnp.float32),
                pltpu.SemaphoreType.DMA((RING,)),
            ],
        ),
        compiler_params=pltpu.CompilerParams(vmem_limit_bytes=SPMM_BYTES),
        cost_estimate=pl.CostEstimate(flops=0, bytes_accessed=4096, transcendentals=0),
        name="spmm_last" if last else "spmm_first",
    )(plan, *blocks, tiles, *(acc or []))


def xor_permute(value, axis, mask):
    size = lax.axis_size(axis)
    return lax.ppermute(value, axis, [(i, i ^ mask) for i in range(size)])


def tree_sum(values):
    while len(values) > 1:
        values = [a + b for a, b in zip(values[::2], values[1::2])]
    return values[0]


def gather_first(own):
    return xor_permute(own, "col", 1), xor_permute(own, "col", 2)


def gather_second(own, by_two, n_col):
    ends, middles = [], []
    for low in range(0, n_col, 4):
        ends += [(low + 1, low), (low + 2, low + 3)]
        middles += [(low + 1, low + 2), (low + 2, low + 1)]
    return lax.ppermute(own, "col", middles), lax.ppermute(by_two, "col", ends)


def as_pieces(own, first, second, mid, n_col):
    if n_col == 4:
        return [[own], [first[0]], [first[1]], list(second)]
    pieces = [own, first[0], first[1], jnp.where(mid, second[0], second[1])]
    for high in range(4, n_col, 4):
        pieces += [xor_permute(piece, "col", high) for piece in pieces[:4]]
    return [[piece] for piece in pieces]


def swap_cores(both):
    pairs = [[i, i + 1] for i in range(0, lax.axis_size("row"), 2)]
    return lax.all_to_all(both, "row", 0, 0, axis_index_groups=pairs)


def fence(*values):
    return lax.optimization_barrier(values)


def add_f32(a, b):
    return a.astype(jnp.float32) + b.astype(jnp.float32)


def stage_sums(keep, recv, n_blocks, rows, at_once=False):
    width = keep.shape[1]
    cut = (n_blocks // 2, 2, 2, rows, width)
    flat = (2, n_blocks // 2, 2, rows, width)
    sums = add_f32(keep, recv).astype(jnp.bfloat16)
    if at_once:
        (sums,) = fence(sums)

    def summed(shape, pick):
        if at_once:
            return pick(sums.reshape(shape)).reshape(-1, width)
        both = add_f32(pick(keep.reshape(shape)), pick(recv.reshape(shape)))
        return both.astype(jnp.bfloat16).reshape(-1, width)

    stage = [
        summed(cut, lambda v: v[:, 1, 0]),
        summed(cut, lambda v: v[:, 0, 0]),
        summed(flat, lambda v: v[1, :, 1]),
        summed(flat, lambda v: v[0, :, 1]),
    ]
    return stage, sums


def halve(value, upper, rows):
    blocks = value.shape[0] // rows
    shape = (2, blocks // 2) if upper else (blocks // 2, 2)
    cut = value.reshape(shape + (rows, value.shape[1]))
    if upper:
        sent, kept = cut[1], cut[0]
    else:
        sent, kept = cut[:, 1], cut[:, 0]
    return sent.reshape(-1, value.shape[1]), kept.reshape(-1, value.shape[1])


def exchange_first(stage, bits):
    return xor_permute(stage[0], "row", bits[0]), xor_permute(stage[2], "row", bits[-1])


def exchange_second(stage, recv, bits, rows):
    sent, kept = [], []
    for upper in (0, 1):
        value = add_f32(stage[2 * upper + 1], recv[upper]).astype(jnp.bfloat16)
        sent_u, kept_u = halve(value, upper, rows)
        sent.append(sent_u)
        kept.append(kept_u)
    return kept, sent


def send_second(sent, bits):
    return [xor_permute(s, "row", bit) for s, bit in zip(sent, (bits[1], bits[-2]))]


def exchange_last(kept, recv, bits, rows):
    done = []
    for upper in (0, 1):
        value = add_f32(kept[upper], recv[upper])
        for bit in (bits[::-1] if upper else bits)[2:]:
            sent_u, kept_u = halve(value.astype(jnp.bfloat16), upper, rows)
            value = add_f32(kept_u, xor_permute(sent_u, "row", bit))
        done.append(value.astype(jnp.bfloat16))
    return jnp.concatenate(done, axis=0)


def weight_term(near, sums):
    terms, at = [], 0
    for f in [part for parts in near for part in parts]:
        own = sums[at : at + f.shape[0]]
        terms.append(lax.dot_general(f, own, (((0,), (0,)), ((), ())), preferred_element_type=jnp.float32))
        at += f.shape[0]
    return sum(terms[1:], terms[0]).astype(jnp.bfloat16)


def sum_over(term, axis, masks):
    parts = [term] + [xor_permute(term, axis, m) for m in masks]
    return tree_sum([p.astype(jnp.float32) for p in parts])


def body(grad_out, preact, features, weight, tiles, tile_rows, tile_cols, live_counts):
    nodes, width = grad_out.shape
    n_row, n_col = lax.axis_size("row"), lax.axis_size("col")
    row, col = lax.axis_index("row"), lax.axis_index("col")
    slots = tiles.shape[2]
    cw = width // 2
    rows = nodes // 2
    bits = [1 << b for b in range(1, n_row.bit_length() - 1)]
    mid = ((col & 3) == 1) | ((col & 3) == 2)

    own0, own1 = [
        jnp.where(preact[:, cut] > 0, grad_out[:, cut], jnp.zeros_like(grad_out[:, cut]))
        for cut in (slice(0, cw), slice(cw, width))
    ]
    first0 = gather_first(own0)
    place = jnp.stack([live_counts.reshape(()), row, col, mid.astype(jnp.int32)])
    plan0, plan1, slot = make_plans(tile_rows, tile_cols, place, n_row, nodes // SIDE)
    flipped = flip_tiles(slot, tiles.reshape(slots, SIDE, SIDE))
    features, plan0 = fence(features, plan0)
    near = [[features]]
    for bit in bits[:2]:
        near.append([xor_permute(features, "row", bit)])
    own0, own1, first0, plan0, plan1, flipped = fence(own0, own1, first0, plan0, plan1, flipped)

    second0 = gather_second(own0, first0[1], n_col)
    acc0 = spmm(plan0, [[own0], [first0[0]], [first0[1]]], flipped, None, n_row)
    own1, acc0 = fence(own1, acc0)
    first1 = gather_first(own1)
    pieces0 = as_pieces(own0, first0, second0, mid, n_col)
    pieces0, near, acc0 = fence(pieces0, near, acc0)

    near.append([xor_permute(near[1][0][:rows], "row", bits[1]), xor_permute(near[2][0][rows:], "row", bits[0])])
    for bit in bits[2:]:
        near += [[xor_permute(f, "row", bit) for f in parts] for parts in near]
    (both0,) = spmm(plan1, pieces0[FIRST_PIECES:], flipped, acc0, n_row, by_core=True)
    got0 = swap_cores(both0)
    got0, near = fence(got0, near)
    stage0, sums0 = stage_sums(got0[0], got0[1], n_row // 2, rows, at_once=True)
    own1, first1, stage0, sums0 = fence(own1, first1, stage0, sums0)

    second1 = gather_second(own1, first1[1], n_col)
    pieces1 = as_pieces(own1, first1, second1, mid, n_col)
    recv0 = exchange_first(stage0, bits)
    acc1 = spmm(plan0, pieces1[:FIRST_PIECES], flipped, None, n_row)
    pieces1, stage0, acc1 = fence(pieces1, stage0, acc1)

    send1, keep1 = spmm(plan1, pieces1[FIRST_PIECES:], flipped, acc1, n_row)
    send1, keep1, recv0, stage0, sums0 = fence(send1, keep1, recv0, stage0, sums0)

    stage1, sums1 = stage_sums(keep1, xor_permute(send1, "row", 1), n_row // 2, rows, at_once=True)
    rest0, sent0 = exchange_second(stage0, recv0, bits, rows)
    recv0 = send_second(sent0, bits)
    term0 = weight_term(near, sums0)
    stage1, sums1, term0 = fence(stage1, sums1, term0)
    stage1, sums1, term0, rest0, recv0 = fence(stage1, sums1, term0, rest0, recv0)

    recv1 = exchange_first(stage1, bits)
    term1 = weight_term(near, sums1)
    even = (row & 1) == 0
    theirs, mine = jnp.where(even, term1, term0), jnp.where(even, term0, term1)
    mine = add_f32(mine, xor_permute(theirs, "row", 1)).astype(jnp.bfloat16)
    mine = sum_over(mine, "col", range(1, n_col)).astype(jnp.bfloat16)
    colgrad0 = exchange_last(rest0, recv0, bits, rows)
    recv1, mine, colgrad0 = fence(recv1, mine, colgrad0)

    rest1, sent1 = exchange_second(stage1, recv1, bits, rows)
    rest1, sent1, mine = fence(rest1, sent1, mine)
    recv1 = send_second(sent1, bits)
    others = [xor_permute(mine, "row", m) for m in range(2, n_row, 2)]
    colgrad1 = exchange_last(rest1, recv1, bits, rows)
    colgrad1, mine = fence(colgrad1, mine)
    mine = tree_sum([p.astype(jnp.float32) for p in [mine] + others]).astype(jnp.bfloat16)

    theirs = xor_permute(mine, "row", 1)
    low, high = jnp.where(even, mine, theirs), jnp.where(even, theirs, mine)
    grad_weight = jnp.concatenate([low, high], axis=1).astype(jnp.float32)
    colgrad = jnp.concatenate([colgrad0, colgrad1], axis=1)
    grad_features = lax.dot_general(
        colgrad, weight, (((1,), (1,)), ((), ())), preferred_element_type=jnp.float32
    ).astype(jnp.bfloat16)
    return (grad_features, grad_weight)


def solution(mesh):
    in_specs = (
        P(("row", "col"), None),
        P(("row", "col"), None),
        P(("col", "row"), None),
        P(),
        P("row", "col", None, None, None),
        P("row", "col", None),
        P("row", "col", None),
        P("row", "col"),
    )
    out_specs = (P(("col", "row"), None), P())
    return jax.shard_map(body, mesh=mesh, in_specs=in_specs, out_specs=out_specs, check_vma=False)
```

```python
import functools

import jax
import jax.numpy as jnp
from jax import lax
from jax.experimental import pallas as pl
from jax.experimental.pallas import tpu as pltpu
from jax.sharding import PartitionSpec as P

SIDE = 128
UNROLL = 8
GROUP = 32
RING = 4
FIRST_PIECES = 3
PLAN_ROWS = 8
FLIP_BYTES = 26 * 1024 * 1024
PLAN_BYTES = 12 * 1024 * 1024
SPMM_BYTES = 16 * 1024 * 1024


def round_up(value, unit):
    return -(-value // unit) * unit


def total(mask, axis):
    return jnp.sum(jnp.where(mask, 1.0, 0.0), axis=axis, keepdims=True).astype(jnp.int32)


def total_of(values, axis):
    return jnp.sum(values.astype(jnp.float32), axis=axis, keepdims=True).astype(jnp.int32)


def plan_kernel(per_dev, n_out, place_ref, rows_r, cols_r, rows_c, cols_c, plan0_ref, plan1_ref, slot_ref):
    slots = rows_r.shape[1]
    size = plan0_ref.shape[1]
    count, row, col, mid = place_ref[0], place_ref[1], place_ref[2], place_ref[3]
    shift = per_dev.bit_length() - 1
    start = FIRST_PIECES * per_dev
    step = 2 * UNROLL

    def attributes(rows, cols, axis):
        ids = lax.broadcasted_iota(jnp.int32, rows.shape, axis)
        row_pos = (((rows >> shift) ^ col) << shift) + (rows & (per_dev - 1))
        away = (cols >> shift) ^ row
        out_pos = ((away >> 1) << shift) + (cols & (per_dev - 1))
        kept = 1 - (away & 1)
        last = (row_pos >= start).astype(jnp.int32)
        live = ids < count
        key = jnp.where(live, (2 * last + kept) * n_out + out_pos, 4 * n_out)
        return ids, row_pos, out_pos, 2 * last + kept, live, key

    ids_r, _, _, part_r, live_r, key_r = attributes(rows_r[...], cols_r[...], 1)
    ids_c, row_pos_c, out_pos_c, part_c, live_c, key_c = attributes(rows_c[...], cols_c[...], 0)
    equal = key_c == key_r
    below = key_r < key_c
    earlier_c = total(equal & (ids_r < ids_c), 1)
    earlier_r = total(equal & (ids_c < ids_r), 0)
    later_r = total(equal & (ids_c > ids_r), 0)
    odd_end = (later_r == 0) & ((earlier_r & 1) == 0)
    weight_r = jnp.where(live_r, jnp.where(odd_end, 2, 1), 0)
    rank_c = total(below, 1) + earlier_c
    rank_r = total(key_c < key_r, 0) + earlier_r
    padded_c = total_of(jnp.where(below, weight_r, 0), 1) + earlier_c
    length = [total_of(jnp.where(part_r == p, weight_r, 0), 1) for p in range(4)]
    n_first = total(live_r & (part_r < 2), 1)
    n_last = count - n_first
    last_base = ((n_first + GROUP - 1) >> 5) << 5
    slot_r = jnp.where(part_r >= 2, last_base + rank_r - n_first, rank_r)
    slot_ref[...] = jnp.where(live_r, slot_r, slots + GROUP)

    lane = lax.broadcasted_iota(jnp.int32, (1, size), 1)
    for p, plan_ref in enumerate((plan0_ref, plan1_ref)):
        sent, held = length[2 * p], length[2 * p + 1]
        sent_steps = (sent + step - 1) >> (step.bit_length() - 1)
        all_steps = sent_steps + ((held + step - 1) >> (step.bit_length() - 1))
        base = length[0] + length[1] if p else jnp.zeros_like(sent)
        in_plan = live_c & ((part_c >> 1) == p)
        pos = padded_c - base + jnp.where((part_c & 1) == 1, sent_steps * step - sent, 0)
        pos = jnp.where(in_plan, pos, -1)
        rank = rank_c - (n_first if p else 0)
        hit = pos == lane

        def placed(values, empty, hit=hit):
            return total_of(jnp.where(hit, values - empty, 0), 0) + empty

        plan_ref[0:1, :] = placed(rank & (RING * GROUP - 1), RING * GROUP)
        plan_ref[1:2, :] = placed(row_pos_c - p * start, 0)
        taken = total(hit, 0) > 0
        ends = [
            jnp.max(jnp.where(in_plan & ((part_c & 1) == h), out_pos_c, 0).astype(jnp.float32), axis=0, keepdims=True)
            for h in range(2)
        ]
        end = jnp.where(lane < sent_steps * step, ends[0], ends[1]).astype(jnp.int32)
        plan_ref[2:3, :] = jnp.where(taken, placed(out_pos_c, 0), end)
        plan_ref[3:4, :] = jnp.where(taken, placed((earlier_c > 0).astype(jnp.int32), 0), 1)
        done = total(in_plan & (pos < (lane + 1) * step), 0)
        tiles = n_last if p else n_first
        info = [
            jnp.full((1, 1), mid, jnp.int32),
            sent_steps,
            (tiles + GROUP - 1) >> 5,
            last_base if p else jnp.zeros_like(last_base),
            jnp.zeros_like(last_base),
        ]
        for g in range(slots // GROUP):
            info.append(total((done <= (g + 1) * GROUP) & (lane < all_steps), 1))
        row_values = jnp.zeros((1, size), jnp.int32)
        for n, value in enumerate(info):
            row_values = jnp.where(lane == n, value, row_values)
        plan_ref[4:5, :] = row_values
        plan_ref[5:6, :] = jnp.full((1, size), row & 1, jnp.int32)
        plan_ref[6:8, :] = jnp.zeros((2, size), jnp.int32)


def make_plans(tile_rows, tile_cols, place, n_row, per_dev):
    slots = tile_rows.size
    n_out = n_row // 2 * per_dev
    size = round_up(slots + 2 * n_out + 4 * UNROLL, SIDE)
    plan = jax.ShapeDtypeStruct((PLAN_ROWS, size), jnp.int32)
    return pl.pallas_call(
        functools.partial(plan_kernel, per_dev, n_out),
        out_shape=(plan, plan, jax.ShapeDtypeStruct((1, slots), jnp.int32)),
        in_specs=[pl.BlockSpec(memory_space=pltpu.SMEM)] + [pl.BlockSpec(memory_space=pltpu.VMEM)] * 4,
        out_specs=[pl.BlockSpec(memory_space=pltpu.VMEM)] * 3,
        compiler_params=pltpu.CompilerParams(vmem_limit_bytes=PLAN_BYTES),
        cost_estimate=pl.CostEstimate(flops=0, bytes_accessed=4096, transcendentals=0),
        name="plan_slots",
    )(place, tile_rows.reshape(1, slots), tile_cols.reshape(1, slots), tile_rows.reshape(slots, 1), tile_cols.reshape(slots, 1))


def flip_kernel(slot_ref, tiles_ref, out_ref, t_in, t_out, in_sem, out_sem):
    slots = t_in.shape[0]
    groups = slots // GROUP
    loads = [
        pltpu.make_async_copy(tiles_ref.at[pl.ds(g * GROUP, GROUP)], t_in.at[pl.ds(g * GROUP, GROUP)], in_sem.at[g])
        for g in range(groups)
    ]
    for load in loads:
        load.start()
    for g in range(groups):
        loads[g].wait()

        def some(step, carry, g=g):
            for u in range(4):
                k = g * GROUP + step * 4 + u
                t_out[slot_ref[0, k]] = t_in[k].T
            return carry

        lax.fori_loop(0, GROUP // 4, some, 0)
    stores = [
        pltpu.make_async_copy(t_out.at[pl.ds(g * GROUP, GROUP)], out_ref.at[pl.ds(g * GROUP, GROUP)], out_sem.at[g])
        for g in range(groups + 1)
    ]
    for store in stores:
        store.start()
    for store in stores:
        store.wait()


def flip_tiles(slot, tile_stack):
    slots = tile_stack.shape[0]
    groups = slots // GROUP
    return pl.pallas_call(
        flip_kernel,
        out_shape=jax.ShapeDtypeStruct((slots + GROUP, SIDE, SIDE), tile_stack.dtype),
        grid_spec=pltpu.PrefetchScalarGridSpec(
            num_scalar_prefetch=1,
            grid=(),
            in_specs=[pl.BlockSpec(memory_space=pl.ANY)],
            out_specs=pl.BlockSpec(memory_space=pl.ANY),
            scratch_shapes=[
                pltpu.VMEM(tile_stack.shape, tile_stack.dtype),
                pltpu.VMEM((slots + GROUP + 1, SIDE, SIDE), tile_stack.dtype),
                pltpu.SemaphoreType.DMA((groups,)),
                pltpu.SemaphoreType.DMA((groups + 1,)),
            ],
        ),
        compiler_params=pltpu.CompilerParams(vmem_limit_bytes=FLIP_BYTES),
        cost_estimate=pl.CostEstimate(flops=0, bytes_accessed=4096, transcendentals=0),
        name="flip_tiles",
    )(slot, tile_stack)


def spmm_kernel(layout, last, by_core, plan_ref, *refs):
    n_refs = sum(layout)
    refs_left = list(refs[:n_refs])
    pieces = [[refs_left.pop(0) for _ in range(n)] for n in layout]
    rest = list(refs[n_refs:])
    tiles_ref = rest.pop(0)
    acc_refs = (rest.pop(0), rest.pop(0)) if last else (None, None)
    if by_core:
        core = plan_ref[5, 0]
        out_ref = rest.pop(0)
        out_refs = (out_ref.at[1 - core], out_ref.at[core])
    else:
        out_refs = (rest.pop(0), rest.pop(0))
    m_vmem, t_vmem, total_ref, sems = rest
    nodes, width = pieces[0][0].shape
    mid, sent_steps, n_groups, tile_base = [plan_ref[4, n] for n in range(4)]

    def group_copy(g):
        place = g & (RING - 1)
        return pltpu.make_async_copy(
            tiles_ref.at[pl.ds(tile_base + pl.multiple_of(g * GROUP, GROUP), GROUP)],
            t_vmem.at[pl.ds(pl.multiple_of(place * GROUP, GROUP), GROUP)],
            sems.at[place],
        )

    for g in range(2):
        pl.when(g < n_groups)(group_copy(g).start)
    t_vmem[RING * GROUP] = jnp.zeros((SIDE, SIDE), t_vmem.dtype)
    for out_ref, acc_ref in zip(out_refs, acc_refs):

        def begin(step, carry, out_ref=out_ref, acc_ref=acc_ref):
            at = pl.ds(pl.multiple_of(step * 256, 256), 256)
            out_ref[at, :] = acc_ref[at, :] if last else jnp.zeros((256, width), out_ref.dtype)
            return carry

        lax.fori_loop(0, out_ref.shape[0] // 256, begin, 0)
    for p, options in enumerate(pieces):

        def take(ref, p=p):
            def some(step, carry):
                at = pl.multiple_of(step * 512, 512)
                m_vmem[pl.ds(pl.multiple_of(p * nodes + at, 512), 512), :] = ref[pl.ds(at, 512), :]
                return carry

            lax.fori_loop(0, nodes // 512, some, 0)

        if len(options) == 1:
            take(options[0])
        else:
            pl.when(mid == 1)(functools.partial(take, options[0]))
            pl.when(mid != 1)(functools.partial(take, options[1]))

    def block(index):
        return m_vmem[pl.ds(pl.multiple_of(index * SIDE, SIDE), SIDE), :]

    def add_pairs(out_ref, acc_ref, step, carry):
        running = total_ref[...]
        prods = []
        for u in range(UNROLL):
            k = 2 * (step * UNROLL + u)
            left = jnp.concatenate([t_vmem[plan_ref[0, k]], t_vmem[plan_ref[0, k + 1]]], axis=1)
            right = jnp.concatenate([block(plan_ref[1, k]), block(plan_ref[1, k + 1])], axis=0)
            prods.append(jnp.dot(left, right, preferred_element_type=jnp.float32))
        for u in range(UNROLL):
            k = 2 * (step * UNROLL + u)
            at = pl.ds(pl.multiple_of(plan_ref[2, k] * SIDE, SIDE), SIDE)
            before = acc_ref[at, :].astype(jnp.float32) if last else jnp.zeros_like(running)
            running = prods[u] + jnp.where(plan_ref[3, k] == 1, running, before)
            out_ref[at, :] = running.astype(out_ref.dtype)
        total_ref[...] = running
        return carry

    total_ref[...] = jnp.zeros_like(total_ref)

    def add_group(g, carry):
        group_copy(g).wait()

        @pl.when(g + 2 < n_groups)
        def _():
            group_copy(g + 2).start()

        low, high = plan_ref[4, 4 + g], plan_ref[4, 5 + g]
        lax.fori_loop(
            jnp.minimum(low, sent_steps), jnp.minimum(high, sent_steps),
            functools.partial(add_pairs, out_refs[0], acc_refs[0]), 0,
        )
        lax.fori_loop(
            jnp.maximum(low, sent_steps), jnp.maximum(high, sent_steps),
            functools.partial(add_pairs, out_refs[1], acc_refs[1]), 0,
        )
        return carry

    lax.fori_loop(0, n_groups, add_group, 0)


def spmm(plan, pieces, tiles, acc, n_row, by_core=False):
    nodes, width = pieces[0][0].shape
    half = n_row // 2 * nodes
    last = acc is not None
    out = jax.ShapeDtypeStruct((2, half, width) if by_core else (half, width), jnp.bfloat16)
    blocks = [ref for p in pieces for ref in p]
    in_vmem, in_any = pl.BlockSpec(memory_space=pltpu.VMEM), pl.BlockSpec(memory_space=pl.ANY)
    return pl.pallas_call(
        functools.partial(spmm_kernel, [len(p) for p in pieces], last, by_core),
        out_shape=(out,) if by_core else (out, out),
        grid_spec=pltpu.PrefetchScalarGridSpec(
            num_scalar_prefetch=1,
            grid=(),
            in_specs=[in_vmem] * len(blocks) + [in_any] + [in_vmem] * len(acc or []),
            out_specs=[in_vmem] * (1 if by_core else 2),
            scratch_shapes=[
                pltpu.VMEM((len(pieces) * nodes, width), jnp.bfloat16),
                pltpu.VMEM((RING * GROUP + 1, SIDE, SIDE), jnp.bfloat16),
                pltpu.VMEM((SIDE, width), jnp.float32),
                pltpu.SemaphoreType.DMA((RING,)),
            ],
        ),
        compiler_params=pltpu.CompilerParams(vmem_limit_bytes=SPMM_BYTES),
        cost_estimate=pl.CostEstimate(flops=0, bytes_accessed=4096, transcendentals=0),
        name="spmm_last" if last else "spmm_first",
    )(plan, *blocks, tiles, *(acc or []))


def xor_permute(value, axis, mask):
    size = lax.axis_size(axis)
    return lax.ppermute(value, axis, [(i, i ^ mask) for i in range(size)])


def tree_sum(values):
    while len(values) > 1:
        values = [a + b for a, b in zip(values[::2], values[1::2])]
    return values[0]


def gather_first(own):
    return xor_permute(own, "col", 1), xor_permute(own, "col", 2)


def gather_second(own, by_two, n_col):
    ends, middles = [], []
    for low in range(0, n_col, 4):
        ends += [(low + 1, low), (low + 2, low + 3)]
        middles += [(low + 1, low + 2), (low + 2, low + 1)]
    return lax.ppermute(own, "col", middles), lax.ppermute(by_two, "col", ends)


def as_pieces(own, first, second, mid, n_col):
    if n_col == 4:
        return [[own], [first[0]], [first[1]], list(second)]
    pieces = [own, first[0], first[1], jnp.where(mid, second[0], second[1])]
    for high in range(4, n_col, 4):
        pieces += [xor_permute(piece, "col", high) for piece in pieces[:4]]
    return [[piece] for piece in pieces]


def swap_cores(both):
    pairs = [[i, i + 1] for i in range(0, lax.axis_size("row"), 2)]
    return lax.all_to_all(both, "row", 0, 0, axis_index_groups=pairs)


def fence(*values):
    return lax.optimization_barrier(values)


def add_f32(a, b):
    return a.astype(jnp.float32) + b.astype(jnp.float32)


def stage_sums(keep, recv, n_blocks, rows, at_once=False):
    width = keep.shape[1]
    cut = (n_blocks // 2, 2, 2, rows, width)
    flat = (2, n_blocks // 2, 2, rows, width)
    sums = add_f32(keep, recv).astype(jnp.bfloat16)
    if at_once:
        (sums,) = fence(sums)

    def summed(shape, pick):
        if at_once:
            return pick(sums.reshape(shape)).reshape(-1, width)
        both = add_f32(pick(keep.reshape(shape)), pick(recv.reshape(shape)))
        return both.astype(jnp.bfloat16).reshape(-1, width)

    stage = [
        summed(cut, lambda v: v[:, 1, 0]),
        summed(cut, lambda v: v[:, 0, 0]),
        summed(flat, lambda v: v[1, :, 1]),
        summed(flat, lambda v: v[0, :, 1]),
    ]
    return stage, sums


def halve(value, upper, rows):
    blocks = value.shape[0] // rows
    shape = (2, blocks // 2) if upper else (blocks // 2, 2)
    cut = value.reshape(shape + (rows, value.shape[1]))
    if upper:
        sent, kept = cut[1], cut[0]
    else:
        sent, kept = cut[:, 1], cut[:, 0]
    return sent.reshape(-1, value.shape[1]), kept.reshape(-1, value.shape[1])


def exchange_first(stage, bits):
    return xor_permute(stage[0], "row", bits[0]), xor_permute(stage[2], "row", bits[-1])


def exchange_second(stage, recv, bits, rows):
    sent, kept = [], []
    for upper in (0, 1):
        value = add_f32(stage[2 * upper + 1], recv[upper]).astype(jnp.bfloat16)
        sent_u, kept_u = halve(value, upper, rows)
        sent.append(sent_u)
        kept.append(kept_u)
    return kept, sent


def send_second(sent, bits):
    return [xor_permute(s, "row", bit) for s, bit in zip(sent, (bits[1], bits[-2]))]


def exchange_last(kept, recv, bits, rows):
    done = []
    for upper in (0, 1):
        value = add_f32(kept[upper], recv[upper])
        for bit in (bits[::-1] if upper else bits)[2:]:
            sent_u, kept_u = halve(value.astype(jnp.bfloat16), upper, rows)
            value = add_f32(kept_u, xor_permute(sent_u, "row", bit))
        done.append(value.astype(jnp.bfloat16))
    return jnp.concatenate(done, axis=0)


def weight_term(near, sums):
    terms, at = [], 0
    for f in [part for parts in near for part in parts]:
        own = sums[at : at + f.shape[0]]
        terms.append(lax.dot_general(f, own, (((0,), (0,)), ((), ())), preferred_element_type=jnp.float32))
        at += f.shape[0]
    return sum(terms[1:], terms[0]).astype(jnp.bfloat16)


def sum_over(term, axis, masks):
    parts = [term] + [xor_permute(term, axis, m) for m in masks]
    return tree_sum([p.astype(jnp.float32) for p in parts])


def body(grad_out, preact, features, weight, tiles, tile_rows, tile_cols, live_counts):
    nodes, width = grad_out.shape
    n_row, n_col = lax.axis_size("row"), lax.axis_size("col")
    row, col = lax.axis_index("row"), lax.axis_index("col")
    slots = tiles.shape[2]
    cw = width // 2
    rows = nodes // 2
    bits = [1 << b for b in range(1, n_row.bit_length() - 1)]
    mid = ((col & 3) == 1) | ((col & 3) == 2)

    own0, own1 = [
        jnp.where(preact[:, cut] > 0, grad_out[:, cut], jnp.zeros_like(grad_out[:, cut]))
        for cut in (slice(0, cw), slice(cw, width))
    ]
    first0 = gather_first(own0)
    place = jnp.stack([live_counts.reshape(()), row, col, mid.astype(jnp.int32)])
    plan0, plan1, slot = make_plans(tile_rows, tile_cols, place, n_row, nodes // SIDE)
    flipped = flip_tiles(slot, tiles.reshape(slots, SIDE, SIDE))
    features, own1 = fence(features, own1)
    near = [[features]]
    for bit in bits[:2]:
        near.append([xor_permute(features, "row", bit)])
    own0, own1, first0, plan0, plan1, flipped = fence(own0, own1, first0, plan0, plan1, flipped)

    second0 = gather_second(own0, first0[1], n_col)
    acc0 = spmm(plan0, [[own0], [first0[0]], [first0[1]]], flipped, None, n_row)
    own1, acc0 = fence(own1, acc0)
    first1 = gather_first(own1)
    near.append([xor_permute(near[1][0][:rows], "row", bits[1]), xor_permute(near[2][0][rows:], "row", bits[0])])
    for bit in bits[2:]:
        near += [[xor_permute(f, "row", bit) for f in parts] for parts in near]
    pieces0 = as_pieces(own0, first0, second0, mid, n_col)
    pieces0, acc0 = fence(pieces0, acc0)

    (both0,) = spmm(plan1, pieces0[FIRST_PIECES:], flipped, acc0, n_row, by_core=True)
    both0, near = fence(both0, near)
    got0 = swap_cores(both0)
    stage0, sums0 = stage_sums(got0[0], got0[1], n_row // 2, rows, at_once=True)
    own1, first1, stage0, sums0 = fence(own1, first1, stage0, sums0)

    second1 = gather_second(own1, first1[1], n_col)
    pieces1 = as_pieces(own1, first1, second1, mid, n_col)
    recv0 = exchange_first(stage0, bits)
    acc1 = spmm(plan0, pieces1[:FIRST_PIECES], flipped, None, n_row)
    pieces1, stage0, acc1 = fence(pieces1, stage0, acc1)

    send1, keep1 = spmm(plan1, pieces1[FIRST_PIECES:], flipped, acc1, n_row)
    send1, keep1, recv0, stage0, sums0 = fence(send1, keep1, recv0, stage0, sums0)

    stage1, sums1 = stage_sums(keep1, xor_permute(send1, "row", 1), n_row // 2, rows, at_once=True)
    rest0, sent0 = exchange_second(stage0, recv0, bits, rows)
    recv0 = send_second(sent0, bits)
    term0, term1 = weight_term(near, sums0), weight_term(near, sums1)
    stage1, term0, term1 = fence(stage1, term0, term1)
    stage1, term0, term1, rest0, recv0 = fence(stage1, term0, term1, rest0, recv0)

    recv1 = exchange_first(stage1, bits)
    even = (row & 1) == 0
    theirs, mine = jnp.where(even, term1, term0), jnp.where(even, term0, term1)
    mine = add_f32(mine, xor_permute(theirs, "row", 1)).astype(jnp.bfloat16)
    mine = sum_over(mine, "col", range(1, n_col)).astype(jnp.bfloat16)
    colgrad0 = exchange_last(rest0, recv0, bits, rows)
    recv1, mine, colgrad0 = fence(recv1, mine, colgrad0)

    rest1, sent1 = exchange_second(stage1, recv1, bits, rows)
    rest1, sent1, mine = fence(rest1, sent1, mine)
    recv1 = send_second(sent1, bits)
    others = [xor_permute(mine, "row", m) for m in range(2, n_row, 2)]
    colgrad1 = exchange_last(rest1, recv1, bits, rows)
    colgrad1, mine = fence(colgrad1, mine)
    mine = tree_sum([p.astype(jnp.float32) for p in [mine] + others]).astype(jnp.bfloat16)

    theirs = xor_permute(mine, "row", 1)
    low, high = jnp.where(even, mine, theirs), jnp.where(even, theirs, mine)
    grad_weight = jnp.concatenate([low, high], axis=1).astype(jnp.float32)
    colgrad = jnp.concatenate([colgrad0, colgrad1], axis=1)
    grad_features = lax.dot_general(
        colgrad, weight, (((1,), (1,)), ((), ())), preferred_element_type=jnp.float32
    ).astype(jnp.bfloat16)
    return (grad_features, grad_weight)


def solution(mesh):
    in_specs = (
        P(("row", "col"), None),
        P(("row", "col"), None),
        P(("col", "row"), None),
        P(),
        P("row", "col", None, None, None),
        P("row", "col", None),
        P("row", "col", None),
        P("row", "col"),
    )
    out_specs = (P(("col", "row"), None), P())
    return jax.shard_map(body, mesh=mesh, in_specs=in_specs, out_specs=out_specs, check_vma=False)
```

```python
import functools

import jax
import jax.numpy as jnp
from jax import lax
from jax.experimental import pallas as pl
from jax.experimental.pallas import tpu as pltpu
from jax.sharding import PartitionSpec as P

SIDE = 128
UNROLL = 8
GROUP = 32
RING = 4
FIRST_PIECES = 3
PLAN_ROWS = 8
FLIP_BYTES = 26 * 1024 * 1024
PLAN_BYTES = 12 * 1024 * 1024
SPMM_BYTES = 16 * 1024 * 1024


def round_up(value, unit):
    return -(-value // unit) * unit


def total(mask, axis):
    return jnp.sum(jnp.where(mask, 1.0, 0.0), axis=axis, keepdims=True).astype(jnp.int32)


def total_of(values, axis):
    return jnp.sum(values.astype(jnp.float32), axis=axis, keepdims=True).astype(jnp.int32)


def plan_kernel(per_dev, n_out, place_ref, rows_r, cols_r, rows_c, cols_c, plan0_ref, plan1_ref, slot_ref):
    slots = rows_r.shape[1]
    size = plan0_ref.shape[1]
    count, row, col, mid = place_ref[0], place_ref[1], place_ref[2], place_ref[3]
    shift = per_dev.bit_length() - 1
    start = FIRST_PIECES * per_dev
    step = 2 * UNROLL

    def attributes(rows, cols, axis):
        ids = lax.broadcasted_iota(jnp.int32, rows.shape, axis)
        row_pos = (((rows >> shift) ^ col) << shift) + (rows & (per_dev - 1))
        away = (cols >> shift) ^ row
        out_pos = ((away >> 1) << shift) + (cols & (per_dev - 1))
        kept = 1 - (away & 1)
        last = (row_pos >= start).astype(jnp.int32)
        live = ids < count
        key = jnp.where(live, (2 * last + kept) * n_out + out_pos, 4 * n_out)
        return ids, row_pos, out_pos, 2 * last + kept, live, key

    ids_r, _, _, part_r, live_r, key_r = attributes(rows_r[...], cols_r[...], 1)
    ids_c, row_pos_c, out_pos_c, part_c, live_c, key_c = attributes(rows_c[...], cols_c[...], 0)
    equal = key_c == key_r
    below = key_r < key_c
    earlier_c = total(equal & (ids_r < ids_c), 1)
    earlier_r = total(equal & (ids_c < ids_r), 0)
    later_r = total(equal & (ids_c > ids_r), 0)
    odd_end = (later_r == 0) & ((earlier_r & 1) == 0)
    weight_r = jnp.where(live_r, jnp.where(odd_end, 2, 1), 0)
    rank_c = total(below, 1) + earlier_c
    rank_r = total(key_c < key_r, 0) + earlier_r
    padded_c = total_of(jnp.where(below, weight_r, 0), 1) + earlier_c
    length = [total_of(jnp.where(part_r == p, weight_r, 0), 1) for p in range(4)]
    n_first = total(live_r & (part_r < 2), 1)
    n_last = count - n_first
    last_base = ((n_first + GROUP - 1) >> 5) << 5
    slot_r = jnp.where(part_r >= 2, last_base + rank_r - n_first, rank_r)
    slot_ref[...] = jnp.where(live_r, slot_r, slots + GROUP)

    lane = lax.broadcasted_iota(jnp.int32, (1, size), 1)
    for p, plan_ref in enumerate((plan0_ref, plan1_ref)):
        sent, held = length[2 * p], length[2 * p + 1]
        sent_steps = (sent + step - 1) >> (step.bit_length() - 1)
        all_steps = sent_steps + ((held + step - 1) >> (step.bit_length() - 1))
        base = length[0] + length[1] if p else jnp.zeros_like(sent)
        in_plan = live_c & ((part_c >> 1) == p)
        pos = padded_c - base + jnp.where((part_c & 1) == 1, sent_steps * step - sent, 0)
        pos = jnp.where(in_plan, pos, -1)
        rank = rank_c - (n_first if p else 0)
        hit = pos == lane

        def placed(values, empty, hit=hit):
            return total_of(jnp.where(hit, values - empty, 0), 0) + empty

        plan_ref[0:1, :] = placed(rank & (RING * GROUP - 1), RING * GROUP)
        plan_ref[1:2, :] = placed(row_pos_c - p * start, 0)
        taken = total(hit, 0) > 0
        ends = [
            jnp.max(jnp.where(in_plan & ((part_c & 1) == h), out_pos_c, 0).astype(jnp.float32), axis=0, keepdims=True)
            for h in range(2)
        ]
        end = jnp.where(lane < sent_steps * step, ends[0], ends[1]).astype(jnp.int32)
        plan_ref[2:3, :] = jnp.where(taken, placed(out_pos_c, 0), end)
        plan_ref[3:4, :] = jnp.where(taken, placed((earlier_c > 0).astype(jnp.int32), 0), 1)
        done = total(in_plan & (pos < (lane + 1) * step), 0)
        tiles = n_last if p else n_first
        info = [
            jnp.full((1, 1), mid, jnp.int32),
            sent_steps,
            (tiles + GROUP - 1) >> 5,
            last_base if p else jnp.zeros_like(last_base),
            jnp.zeros_like(last_base),
        ]
        for g in range(slots // GROUP):
            info.append(total((done <= (g + 1) * GROUP) & (lane < all_steps), 1))
        row_values = jnp.zeros((1, size), jnp.int32)
        for n, value in enumerate(info):
            row_values = jnp.where(lane == n, value, row_values)
        plan_ref[4:5, :] = row_values
        plan_ref[5:6, :] = jnp.full((1, size), row & 1, jnp.int32)
        plan_ref[6:8, :] = jnp.zeros((2, size), jnp.int32)


def make_plans(tile_rows, tile_cols, place, n_row, per_dev):
    slots = tile_rows.size
    n_out = n_row // 2 * per_dev
    size = round_up(slots + 2 * n_out + 4 * UNROLL, SIDE)
    plan = jax.ShapeDtypeStruct((PLAN_ROWS, size), jnp.int32)
    return pl.pallas_call(
        functools.partial(plan_kernel, per_dev, n_out),
        out_shape=(plan, plan, jax.ShapeDtypeStruct((1, slots), jnp.int32)),
        in_specs=[pl.BlockSpec(memory_space=pltpu.SMEM)] + [pl.BlockSpec(memory_space=pltpu.VMEM)] * 4,
        out_specs=[pl.BlockSpec(memory_space=pltpu.VMEM)] * 3,
        compiler_params=pltpu.CompilerParams(vmem_limit_bytes=PLAN_BYTES),
        cost_estimate=pl.CostEstimate(flops=0, bytes_accessed=4096, transcendentals=0),
        name="plan_slots",
    )(place, tile_rows.reshape(1, slots), tile_cols.reshape(1, slots), tile_rows.reshape(slots, 1), tile_cols.reshape(slots, 1))


def flip_kernel(slot_ref, tiles_ref, out_ref, t_in, t_out, in_sem, out_sem):
    slots = t_in.shape[0]
    groups = slots // GROUP
    loads = [
        pltpu.make_async_copy(tiles_ref.at[pl.ds(g * GROUP, GROUP)], t_in.at[pl.ds(g * GROUP, GROUP)], in_sem.at[g])
        for g in range(groups)
    ]
    for load in loads:
        load.start()
    for g in range(groups):
        loads[g].wait()

        def some(step, carry, g=g):
            for u in range(4):
                k = g * GROUP + step * 4 + u
                t_out[slot_ref[0, k]] = t_in[k].T
            return carry

        lax.fori_loop(0, GROUP // 4, some, 0)
    stores = [
        pltpu.make_async_copy(t_out.at[pl.ds(g * GROUP, GROUP)], out_ref.at[pl.ds(g * GROUP, GROUP)], out_sem.at[g])
        for g in range(groups + 1)
    ]
    for store in stores:
        store.start()
    for store in stores:
        store.wait()


def flip_tiles(slot, tile_stack):
    slots = tile_stack.shape[0]
    groups = slots // GROUP
    return pl.pallas_call(
        flip_kernel,
        out_shape=jax.ShapeDtypeStruct((slots + GROUP, SIDE, SIDE), tile_stack.dtype),
        grid_spec=pltpu.PrefetchScalarGridSpec(
            num_scalar_prefetch=1,
            grid=(),
            in_specs=[pl.BlockSpec(memory_space=pl.ANY)],
            out_specs=pl.BlockSpec(memory_space=pl.ANY),
            scratch_shapes=[
                pltpu.VMEM(tile_stack.shape, tile_stack.dtype),
                pltpu.VMEM((slots + GROUP + 1, SIDE, SIDE), tile_stack.dtype),
                pltpu.SemaphoreType.DMA((groups,)),
                pltpu.SemaphoreType.DMA((groups + 1,)),
            ],
        ),
        compiler_params=pltpu.CompilerParams(vmem_limit_bytes=FLIP_BYTES),
        cost_estimate=pl.CostEstimate(flops=0, bytes_accessed=4096, transcendentals=0),
        name="flip_tiles",
    )(slot, tile_stack)


def spmm_kernel(layout, last, by_core, plan_ref, *refs):
    n_refs = sum(layout)
    refs_left = list(refs[:n_refs])
    pieces = [[refs_left.pop(0) for _ in range(n)] for n in layout]
    rest = list(refs[n_refs:])
    tiles_ref = rest.pop(0)
    acc_refs = (rest.pop(0), rest.pop(0)) if last else (None, None)
    if by_core:
        core = plan_ref[5, 0]
        out_ref = rest.pop(0)
        out_refs = (out_ref.at[1 - core], out_ref.at[core])
    else:
        out_refs = (rest.pop(0), rest.pop(0))
    m_vmem, t_vmem, total_ref, sems = rest
    nodes, width = pieces[0][0].shape
    mid, sent_steps, n_groups, tile_base = [plan_ref[4, n] for n in range(4)]

    def group_copy(g):
        place = g & (RING - 1)
        return pltpu.make_async_copy(
            tiles_ref.at[pl.ds(tile_base + pl.multiple_of(g * GROUP, GROUP), GROUP)],
            t_vmem.at[pl.ds(pl.multiple_of(place * GROUP, GROUP), GROUP)],
            sems.at[place],
        )

    for g in range(2):
        pl.when(g < n_groups)(group_copy(g).start)
    t_vmem[RING * GROUP] = jnp.zeros((SIDE, SIDE), t_vmem.dtype)
    for out_ref, acc_ref in zip(out_refs, acc_refs):

        def begin(step, carry, out_ref=out_ref, acc_ref=acc_ref):
            at = pl.ds(pl.multiple_of(step * 256, 256), 256)
            out_ref[at, :] = acc_ref[at, :] if last else jnp.zeros((256, width), out_ref.dtype)
            return carry

        lax.fori_loop(0, out_ref.shape[0] // 256, begin, 0)
    for p, options in enumerate(pieces):

        def take(ref, p=p):
            def some(step, carry):
                at = pl.multiple_of(step * 512, 512)
                m_vmem[pl.ds(pl.multiple_of(p * nodes + at, 512), 512), :] = ref[pl.ds(at, 512), :]
                return carry

            lax.fori_loop(0, nodes // 512, some, 0)

        if len(options) == 1:
            take(options[0])
        else:
            pl.when(mid == 1)(functools.partial(take, options[0]))
            pl.when(mid != 1)(functools.partial(take, options[1]))

    def block(index):
        return m_vmem[pl.ds(pl.multiple_of(index * SIDE, SIDE), SIDE), :]

    def add_pairs(out_ref, acc_ref, step, carry):
        running = total_ref[...]
        prods = []
        for u in range(UNROLL):
            k = 2 * (step * UNROLL + u)
            left = jnp.concatenate([t_vmem[plan_ref[0, k]], t_vmem[plan_ref[0, k + 1]]], axis=1)
            right = jnp.concatenate([block(plan_ref[1, k]), block(plan_ref[1, k + 1])], axis=0)
            prods.append(jnp.dot(left, right, preferred_element_type=jnp.float32))
        for u in range(UNROLL):
            k = 2 * (step * UNROLL + u)
            at = pl.ds(pl.multiple_of(plan_ref[2, k] * SIDE, SIDE), SIDE)
            before = acc_ref[at, :].astype(jnp.float32) if last else jnp.zeros_like(running)
            running = prods[u] + jnp.where(plan_ref[3, k] == 1, running, before)
            out_ref[at, :] = running.astype(out_ref.dtype)
        total_ref[...] = running
        return carry

    total_ref[...] = jnp.zeros_like(total_ref)

    def add_group(g, carry):
        group_copy(g).wait()

        @pl.when(g + 2 < n_groups)
        def _():
            group_copy(g + 2).start()

        low, high = plan_ref[4, 4 + g], plan_ref[4, 5 + g]
        lax.fori_loop(
            jnp.minimum(low, sent_steps), jnp.minimum(high, sent_steps),
            functools.partial(add_pairs, out_refs[0], acc_refs[0]), 0,
        )
        lax.fori_loop(
            jnp.maximum(low, sent_steps), jnp.maximum(high, sent_steps),
            functools.partial(add_pairs, out_refs[1], acc_refs[1]), 0,
        )
        return carry

    lax.fori_loop(0, n_groups, add_group, 0)


def spmm(plan, pieces, tiles, acc, n_row, by_core=False):
    nodes, width = pieces[0][0].shape
    half = n_row // 2 * nodes
    last = acc is not None
    out = jax.ShapeDtypeStruct((2, half, width) if by_core else (half, width), jnp.bfloat16)
    blocks = [ref for p in pieces for ref in p]
    in_vmem, in_any = pl.BlockSpec(memory_space=pltpu.VMEM), pl.BlockSpec(memory_space=pl.ANY)
    return pl.pallas_call(
        functools.partial(spmm_kernel, [len(p) for p in pieces], last, by_core),
        out_shape=(out,) if by_core else (out, out),
        grid_spec=pltpu.PrefetchScalarGridSpec(
            num_scalar_prefetch=1,
            grid=(),
            in_specs=[in_vmem] * len(blocks) + [in_any] + [in_vmem] * len(acc or []),
            out_specs=[in_vmem] * (1 if by_core else 2),
            scratch_shapes=[
                pltpu.VMEM((len(pieces) * nodes, width), jnp.bfloat16),
                pltpu.VMEM((RING * GROUP + 1, SIDE, SIDE), jnp.bfloat16),
                pltpu.VMEM((SIDE, width), jnp.float32),
                pltpu.SemaphoreType.DMA((RING,)),
            ],
        ),
        compiler_params=pltpu.CompilerParams(vmem_limit_bytes=SPMM_BYTES),
        cost_estimate=pl.CostEstimate(flops=0, bytes_accessed=4096, transcendentals=0),
        name="spmm_last" if last else "spmm_first",
    )(plan, *blocks, tiles, *(acc or []))


def xor_permute(value, axis, mask):
    size = lax.axis_size(axis)
    return lax.ppermute(value, axis, [(i, i ^ mask) for i in range(size)])


def tree_sum(values):
    while len(values) > 1:
        values = [a + b for a, b in zip(values[::2], values[1::2])]
    return values[0]


def gather_first(own):
    return xor_permute(own, "col", 1), xor_permute(own, "col", 2)


def gather_second(own, by_two, n_col):
    ends, middles = [], []
    for low in range(0, n_col, 4):
        ends += [(low + 1, low), (low + 2, low + 3)]
        middles += [(low + 1, low + 2), (low + 2, low + 1)]
    return lax.ppermute(own, "col", middles), lax.ppermute(by_two, "col", ends)


def as_pieces(own, first, second, mid, n_col):
    if n_col == 4:
        return [[own], [first[0]], [first[1]], list(second)]
    pieces = [own, first[0], first[1], jnp.where(mid, second[0], second[1])]
    for high in range(4, n_col, 4):
        pieces += [xor_permute(piece, "col", high) for piece in pieces[:4]]
    return [[piece] for piece in pieces]


def swap_cores(both):
    pairs = [[i, i + 1] for i in range(0, lax.axis_size("row"), 2)]
    return lax.all_to_all(both, "row", 0, 0, axis_index_groups=pairs)


def fence(*values):
    return lax.optimization_barrier(values)


def add_f32(a, b):
    return a.astype(jnp.float32) + b.astype(jnp.float32)


def stage_sums(keep, recv, n_blocks, rows, at_once=False):
    width = keep.shape[1]
    cut = (n_blocks // 2, 2, 2, rows, width)
    flat = (2, n_blocks // 2, 2, rows, width)
    sums = add_f32(keep, recv).astype(jnp.bfloat16)
    if at_once:
        (sums,) = fence(sums)

    def summed(shape, pick):
        if at_once:
            return pick(sums.reshape(shape)).reshape(-1, width)
        both = add_f32(pick(keep.reshape(shape)), pick(recv.reshape(shape)))
        return both.astype(jnp.bfloat16).reshape(-1, width)

    stage = [
        summed(cut, lambda v: v[:, 1, 0]),
        summed(cut, lambda v: v[:, 0, 0]),
        summed(flat, lambda v: v[1, :, 1]),
        summed(flat, lambda v: v[0, :, 1]),
    ]
    return stage, sums


def halve(value, upper, rows):
    blocks = value.shape[0] // rows
    shape = (2, blocks // 2) if upper else (blocks // 2, 2)
    cut = value.reshape(shape + (rows, value.shape[1]))
    if upper:
        sent, kept = cut[1], cut[0]
    else:
        sent, kept = cut[:, 1], cut[:, 0]
    return sent.reshape(-1, value.shape[1]), kept.reshape(-1, value.shape[1])


def exchange_first(stage, bits):
    return xor_permute(stage[0], "row", bits[0]), xor_permute(stage[2], "row", bits[-1])


def exchange_second(stage, recv, bits, rows):
    sent, kept = [], []
    for upper in (0, 1):
        value = add_f32(stage[2 * upper + 1], recv[upper]).astype(jnp.bfloat16)
        sent_u, kept_u = halve(value, upper, rows)
        sent.append(sent_u)
        kept.append(kept_u)
    return kept, sent


def send_second(sent, bits):
    return [xor_permute(s, "row", bit) for s, bit in zip(sent, (bits[1], bits[-2]))]


def exchange_last(kept, recv, bits, rows):
    done = []
    for upper in (0, 1):
        value = add_f32(kept[upper], recv[upper])
        for bit in (bits[::-1] if upper else bits)[2:]:
            sent_u, kept_u = halve(value.astype(jnp.bfloat16), upper, rows)
            value = add_f32(kept_u, xor_permute(sent_u, "row", bit))
        done.append(value.astype(jnp.bfloat16))
    return jnp.concatenate(done, axis=0)


def weight_term(near, sums):
    terms, at = [], 0
    for f in [part for parts in near for part in parts]:
        own = sums[at : at + f.shape[0]]
        terms.append(lax.dot_general(f, own, (((0,), (0,)), ((), ())), preferred_element_type=jnp.float32))
        at += f.shape[0]
    return sum(terms[1:], terms[0]).astype(jnp.bfloat16)


def sum_over(term, axis, masks):
    parts = [term] + [xor_permute(term, axis, m) for m in masks]
    return tree_sum([p.astype(jnp.float32) for p in parts])


def body(grad_out, preact, features, weight, tiles, tile_rows, tile_cols, live_counts):
    nodes, width = grad_out.shape
    n_row, n_col = lax.axis_size("row"), lax.axis_size("col")
    row, col = lax.axis_index("row"), lax.axis_index("col")
    slots = tiles.shape[2]
    cw = width // 2
    rows = nodes // 2
    bits = [1 << b for b in range(1, n_row.bit_length() - 1)]
    mid = ((col & 3) == 1) | ((col & 3) == 2)

    own0, own1 = [
        jnp.where(preact[:, cut] > 0, grad_out[:, cut], jnp.zeros_like(grad_out[:, cut]))
        for cut in (slice(0, cw), slice(cw, width))
    ]
    first0 = gather_first(own0)
    place = jnp.stack([live_counts.reshape(()), row, col, mid.astype(jnp.int32)])
    plan0, plan1, slot = make_plans(tile_rows, tile_cols, place, n_row, nodes // SIDE)
    flipped = flip_tiles(slot, tiles.reshape(slots, SIDE, SIDE))
    features, plan0 = fence(features, plan0)
    near = [[features]]
    for bit in bits[:2]:
        near.append([xor_permute(features, "row", bit)])
    own0, own1, first0, plan0, plan1, flipped = fence(own0, own1, first0, plan0, plan1, flipped)

    second0 = gather_second(own0, first0[1], n_col)
    acc0 = spmm(plan0, [[own0], [first0[0]], [first0[1]]], flipped, None, n_row)
    own1, acc0 = fence(own1, acc0)
    first1 = gather_first(own1)
    pieces0 = as_pieces(own0, first0, second0, mid, n_col)
    pieces0, near, acc0 = fence(pieces0, near, acc0)

    (both0,) = spmm(plan1, pieces0[FIRST_PIECES:], flipped, acc0, n_row, by_core=True)
    got0 = swap_cores(both0)
    for m in range(6, n_row, 2):
        near.append([xor_permute(features, "row", m)])
    got0, near = fence(got0, near)
    stage0, sums0 = stage_sums(got0[0], got0[1], n_row // 2, rows, at_once=True)
    own1, first1, stage0, sums0 = fence(own1, first1, stage0, sums0)

    second1 = gather_second(own1, first1[1], n_col)
    pieces1 = as_pieces(own1, first1, second1, mid, n_col)
    recv0 = exchange_first(stage0, bits)
    acc1 = spmm(plan0, pieces1[:FIRST_PIECES], flipped, None, n_row)
    pieces1, stage0, acc1 = fence(pieces1, stage0, acc1)

    send1, keep1 = spmm(plan1, pieces1[FIRST_PIECES:], flipped, acc1, n_row)
    send1, keep1, recv0, stage0, sums0 = fence(send1, keep1, recv0, stage0, sums0)

    stage1, sums1 = stage_sums(keep1, xor_permute(send1, "row", 1), n_row // 2, rows, at_once=True)
    rest0, sent0 = exchange_second(stage0, recv0, bits, rows)
    recv0 = send_second(sent0, bits)
    term0, term1 = weight_term(near, sums0), weight_term(near, sums1)
    stage1, term0, term1 = fence(stage1, term0, term1)
    stage1, term0, term1, rest0, recv0 = fence(stage1, term0, term1, rest0, recv0)

    recv1 = exchange_first(stage1, bits)
    even = (row & 1) == 0
    theirs, mine = jnp.where(even, term1, term0), jnp.where(even, term0, term1)
    mine = add_f32(mine, xor_permute(theirs, "row", 1)).astype(jnp.bfloat16)
    mine = sum_over(mine, "col", range(1, n_col)).astype(jnp.bfloat16)
    colgrad0 = exchange_last(rest0, recv0, bits, rows)
    recv1, mine, colgrad0 = fence(recv1, mine, colgrad0)

    rest1, sent1 = exchange_second(stage1, recv1, bits, rows)
    rest1, sent1, mine = fence(rest1, sent1, mine)
    recv1 = send_second(sent1, bits)
    others = [xor_permute(mine, "row", m) for m in range(2, n_row, 2)]
    colgrad1 = exchange_last(rest1, recv1, bits, rows)
    colgrad1, mine = fence(colgrad1, mine)
    mine = tree_sum([p.astype(jnp.float32) for p in [mine] + others]).astype(jnp.bfloat16)

    theirs = xor_permute(mine, "row", 1)
    low, high = jnp.where(even, mine, theirs), jnp.where(even, theirs, mine)
    grad_weight = jnp.concatenate([low, high], axis=1).astype(jnp.float32)
    colgrad = jnp.concatenate([colgrad0, colgrad1], axis=1)
    grad_features = lax.dot_general(
        colgrad, weight, (((1,), (1,)), ((), ())), preferred_element_type=jnp.float32
    ).astype(jnp.bfloat16)
    return (grad_features, grad_weight)


def solution(mesh):
    in_specs = (
        P(("row", "col"), None),
        P(("row", "col"), None),
        P(("col", "row"), None),
        P(),
        P("row", "col", None, None, None),
        P("row", "col", None),
        P("row", "col", None),
        P("row", "col"),
    )
    out_specs = (P(("col", "row"), None), P())
    return jax.shard_map(body, mesh=mesh, in_specs=in_specs, out_specs=out_specs, check_vma=False)
```

```python
import functools

import jax
import jax.numpy as jnp
from jax import lax
from jax.experimental import pallas as pl
from jax.experimental.pallas import tpu as pltpu
from jax.sharding import PartitionSpec as P

SIDE = 128
UNROLL = 8
GROUP = 32
RING = 4
FIRST_PIECES = 3
PLAN_ROWS = 8
FLIP_BYTES = 26 * 1024 * 1024
PLAN_BYTES = 12 * 1024 * 1024
SPMM_BYTES = 16 * 1024 * 1024


def round_up(value, unit):
    return -(-value // unit) * unit


def total(mask, axis):
    return jnp.sum(jnp.where(mask, 1.0, 0.0), axis=axis, keepdims=True).astype(jnp.int32)


def total_of(values, axis):
    return jnp.sum(values.astype(jnp.float32), axis=axis, keepdims=True).astype(jnp.int32)


def plan_kernel(per_dev, n_out, place_ref, rows_r, cols_r, rows_c, cols_c, plan0_ref, plan1_ref, slot_ref):
    slots = rows_r.shape[1]
    size = plan0_ref.shape[1]
    count, row, col, mid = place_ref[0], place_ref[1], place_ref[2], place_ref[3]
    shift = per_dev.bit_length() - 1
    start = FIRST_PIECES * per_dev
    step = 2 * UNROLL

    def attributes(rows, cols, axis):
        ids = lax.broadcasted_iota(jnp.int32, rows.shape, axis)
        row_pos = (((rows >> shift) ^ col) << shift) + (rows & (per_dev - 1))
        away = (cols >> shift) ^ row
        out_pos = ((away >> 1) << shift) + (cols & (per_dev - 1))
        kept = 1 - (away & 1)
        last = (row_pos >= start).astype(jnp.int32)
        live = ids < count
        key = jnp.where(live, (2 * last + kept) * n_out + out_pos, 4 * n_out)
        return ids, row_pos, out_pos, 2 * last + kept, live, key

    ids_r, _, _, part_r, live_r, key_r = attributes(rows_r[...], cols_r[...], 1)
    ids_c, row_pos_c, out_pos_c, part_c, live_c, key_c = attributes(rows_c[...], cols_c[...], 0)
    equal = key_c == key_r
    below = key_r < key_c
    earlier_c = total(equal & (ids_r < ids_c), 1)
    earlier_r = total(equal & (ids_c < ids_r), 0)
    later_r = total(equal & (ids_c > ids_r), 0)
    odd_end = (later_r == 0) & ((earlier_r & 1) == 0)
    weight_r = jnp.where(live_r, jnp.where(odd_end, 2, 1), 0)
    rank_c = total(below, 1) + earlier_c
    rank_r = total(key_c < key_r, 0) + earlier_r
    padded_c = total_of(jnp.where(below, weight_r, 0), 1) + earlier_c
    length = [total_of(jnp.where(part_r == p, weight_r, 0), 1) for p in range(4)]
    n_first = total(live_r & (part_r < 2), 1)
    n_last = count - n_first
    last_base = ((n_first + GROUP - 1) >> 5) << 5
    slot_r = jnp.where(part_r >= 2, last_base + rank_r - n_first, rank_r)
    slot_ref[...] = jnp.where(live_r, slot_r, slots + GROUP)

    lane = lax.broadcasted_iota(jnp.int32, (1, size), 1)
    for p, plan_ref in enumerate((plan0_ref, plan1_ref)):
        sent, held = length[2 * p], length[2 * p + 1]
        sent_steps = (sent + step - 1) >> (step.bit_length() - 1)
        all_steps = sent_steps + ((held + step - 1) >> (step.bit_length() - 1))
        base = length[0] + length[1] if p else jnp.zeros_like(sent)
        in_plan = live_c & ((part_c >> 1) == p)
        pos = padded_c - base + jnp.where((part_c & 1) == 1, sent_steps * step - sent, 0)
        pos = jnp.where(in_plan, pos, -1)
        rank = rank_c - (n_first if p else 0)
        hit = pos == lane

        def placed(values, empty, hit=hit):
            return total_of(jnp.where(hit, values - empty, 0), 0) + empty

        plan_ref[0:1, :] = placed(rank & (RING * GROUP - 1), RING * GROUP)
        plan_ref[1:2, :] = placed(row_pos_c - p * start, 0)
        taken = total(hit, 0) > 0
        ends = [
            jnp.max(jnp.where(in_plan & ((part_c & 1) == h), out_pos_c, 0).astype(jnp.float32), axis=0, keepdims=True)
            for h in range(2)
        ]
        end = jnp.where(lane < sent_steps * step, ends[0], ends[1]).astype(jnp.int32)
        plan_ref[2:3, :] = jnp.where(taken, placed(out_pos_c, 0), end)
        plan_ref[3:4, :] = jnp.where(taken, placed((earlier_c > 0).astype(jnp.int32), 0), 1)
        done = total(in_plan & (pos < (lane + 1) * step), 0)
        tiles = n_last if p else n_first
        info = [
            jnp.full((1, 1), mid, jnp.int32),
            sent_steps,
            (tiles + GROUP - 1) >> 5,
            last_base if p else jnp.zeros_like(last_base),
            jnp.zeros_like(last_base),
        ]
        for g in range(slots // GROUP):
            info.append(total((done <= (g + 1) * GROUP) & (lane < all_steps), 1))
        row_values = jnp.zeros((1, size), jnp.int32)
        for n, value in enumerate(info):
            row_values = jnp.where(lane == n, value, row_values)
        plan_ref[4:5, :] = row_values
        plan_ref[5:6, :] = jnp.full((1, size), row & 1, jnp.int32)
        plan_ref[6:8, :] = jnp.zeros((2, size), jnp.int32)


def make_plans(tile_rows, tile_cols, place, n_row, per_dev):
    slots = tile_rows.size
    n_out = n_row // 2 * per_dev
    size = round_up(slots + 2 * n_out + 4 * UNROLL, SIDE)
    plan = jax.ShapeDtypeStruct((PLAN_ROWS, size), jnp.int32)
    return pl.pallas_call(
        functools.partial(plan_kernel, per_dev, n_out),
        out_shape=(plan, plan, jax.ShapeDtypeStruct((1, slots), jnp.int32)),
        in_specs=[pl.BlockSpec(memory_space=pltpu.SMEM)] + [pl.BlockSpec(memory_space=pltpu.VMEM)] * 4,
        out_specs=[pl.BlockSpec(memory_space=pltpu.VMEM)] * 3,
        compiler_params=pltpu.CompilerParams(vmem_limit_bytes=PLAN_BYTES),
        cost_estimate=pl.CostEstimate(flops=0, bytes_accessed=4096, transcendentals=0),
        name="plan_slots",
    )(place, tile_rows.reshape(1, slots), tile_cols.reshape(1, slots), tile_rows.reshape(slots, 1), tile_cols.reshape(slots, 1))


def flip_kernel(slot_ref, tiles_ref, out_ref, t_in, t_out, in_sem, out_sem):
    slots = t_in.shape[0]
    groups = slots // GROUP
    loads = [
        pltpu.make_async_copy(tiles_ref.at[pl.ds(g * GROUP, GROUP)], t_in.at[pl.ds(g * GROUP, GROUP)], in_sem.at[g])
        for g in range(groups)
    ]
    for load in loads:
        load.start()
    for g in range(groups):
        loads[g].wait()

        def some(step, carry, g=g):
            for u in range(4):
                k = g * GROUP + step * 4 + u
                t_out[slot_ref[0, k]] = t_in[k].T
            return carry

        lax.fori_loop(0, GROUP // 4, some, 0)
    stores = [
        pltpu.make_async_copy(t_out.at[pl.ds(g * GROUP, GROUP)], out_ref.at[pl.ds(g * GROUP, GROUP)], out_sem.at[g])
        for g in range(groups + 1)
    ]
    for store in stores:
        store.start()
    for store in stores:
        store.wait()


def flip_tiles(slot, tile_stack):
    slots = tile_stack.shape[0]
    groups = slots // GROUP
    return pl.pallas_call(
        flip_kernel,
        out_shape=jax.ShapeDtypeStruct((slots + GROUP, SIDE, SIDE), tile_stack.dtype),
        grid_spec=pltpu.PrefetchScalarGridSpec(
            num_scalar_prefetch=1,
            grid=(),
            in_specs=[pl.BlockSpec(memory_space=pl.ANY)],
            out_specs=pl.BlockSpec(memory_space=pl.ANY),
            scratch_shapes=[
                pltpu.VMEM(tile_stack.shape, tile_stack.dtype),
                pltpu.VMEM((slots + GROUP + 1, SIDE, SIDE), tile_stack.dtype),
                pltpu.SemaphoreType.DMA((groups,)),
                pltpu.SemaphoreType.DMA((groups + 1,)),
            ],
        ),
        compiler_params=pltpu.CompilerParams(vmem_limit_bytes=FLIP_BYTES),
        cost_estimate=pl.CostEstimate(flops=0, bytes_accessed=4096, transcendentals=0),
        name="flip_tiles",
    )(slot, tile_stack)


def spmm_kernel(layout, last, by_core, plan_ref, *refs):
    n_refs = sum(layout)
    refs_left = list(refs[:n_refs])
    pieces = [[refs_left.pop(0) for _ in range(n)] for n in layout]
    rest = list(refs[n_refs:])
    tiles_ref = rest.pop(0)
    acc_refs = (rest.pop(0), rest.pop(0)) if last else (None, None)
    if by_core:
        core = plan_ref[5, 0]
        out_ref = rest.pop(0)
        out_refs = (out_ref.at[1 - core], out_ref.at[core])
    else:
        out_refs = (rest.pop(0), rest.pop(0))
    m_vmem, t_vmem, total_ref, sems = rest
    nodes, width = pieces[0][0].shape
    mid, sent_steps, n_groups, tile_base = [plan_ref[4, n] for n in range(4)]

    def group_copy(g):
        place = g & (RING - 1)
        return pltpu.make_async_copy(
            tiles_ref.at[pl.ds(tile_base + pl.multiple_of(g * GROUP, GROUP), GROUP)],
            t_vmem.at[pl.ds(pl.multiple_of(place * GROUP, GROUP), GROUP)],
            sems.at[place],
        )

    for g in range(2):
        pl.when(g < n_groups)(group_copy(g).start)
    t_vmem[RING * GROUP] = jnp.zeros((SIDE, SIDE), t_vmem.dtype)
    for out_ref, acc_ref in zip(out_refs, acc_refs):

        def begin(step, carry, out_ref=out_ref, acc_ref=acc_ref):
            at = pl.ds(pl.multiple_of(step * 256, 256), 256)
            out_ref[at, :] = acc_ref[at, :] if last else jnp.zeros((256, width), out_ref.dtype)
            return carry

        lax.fori_loop(0, out_ref.shape[0] // 256, begin, 0)
    for p, options in enumerate(pieces):

        def take(ref, p=p):
            def some(step, carry):
                at = pl.multiple_of(step * 512, 512)
                m_vmem[pl.ds(pl.multiple_of(p * nodes + at, 512), 512), :] = ref[pl.ds(at, 512), :]
                return carry

            lax.fori_loop(0, nodes // 512, some, 0)

        if len(options) == 1:
            take(options[0])
        else:
            pl.when(mid == 1)(functools.partial(take, options[0]))
            pl.when(mid != 1)(functools.partial(take, options[1]))

    def block(index):
        return m_vmem[pl.ds(pl.multiple_of(index * SIDE, SIDE), SIDE), :]

    def add_pairs(out_ref, acc_ref, step, carry):
        running = total_ref[...]
        prods = []
        for u in range(UNROLL):
            k = 2 * (step * UNROLL + u)
            left = jnp.concatenate([t_vmem[plan_ref[0, k]], t_vmem[plan_ref[0, k + 1]]], axis=1)
            right = jnp.concatenate([block(plan_ref[1, k]), block(plan_ref[1, k + 1])], axis=0)
            prods.append(jnp.dot(left, right, preferred_element_type=jnp.float32))
        for u in range(UNROLL):
            k = 2 * (step * UNROLL + u)
            at = pl.ds(pl.multiple_of(plan_ref[2, k] * SIDE, SIDE), SIDE)
            before = acc_ref[at, :].astype(jnp.float32) if last else jnp.zeros_like(running)
            running = prods[u] + jnp.where(plan_ref[3, k] == 1, running, before)
            out_ref[at, :] = running.astype(out_ref.dtype)
        total_ref[...] = running
        return carry

    total_ref[...] = jnp.zeros_like(total_ref)

    def add_group(g, carry):
        group_copy(g).wait()

        @pl.when(g + 2 < n_groups)
        def _():
            group_copy(g + 2).start()

        low, high = plan_ref[4, 4 + g], plan_ref[4, 5 + g]
        lax.fori_loop(
            jnp.minimum(low, sent_steps), jnp.minimum(high, sent_steps),
            functools.partial(add_pairs, out_refs[0], acc_refs[0]), 0,
        )
        lax.fori_loop(
            jnp.maximum(low, sent_steps), jnp.maximum(high, sent_steps),
            functools.partial(add_pairs, out_refs[1], acc_refs[1]), 0,
        )
        return carry

    lax.fori_loop(0, n_groups, add_group, 0)


def spmm(plan, pieces, tiles, acc, n_row, by_core=False):
    nodes, width = pieces[0][0].shape
    half = n_row // 2 * nodes
    last = acc is not None
    out = jax.ShapeDtypeStruct((2, half, width) if by_core else (half, width), jnp.bfloat16)
    blocks = [ref for p in pieces for ref in p]
    in_vmem, in_any = pl.BlockSpec(memory_space=pltpu.VMEM), pl.BlockSpec(memory_space=pl.ANY)
    return pl.pallas_call(
        functools.partial(spmm_kernel, [len(p) for p in pieces], last, by_core),
        out_shape=(out,) if by_core else (out, out),
        grid_spec=pltpu.PrefetchScalarGridSpec(
            num_scalar_prefetch=1,
            grid=(),
            in_specs=[in_vmem] * len(blocks) + [in_any] + [in_vmem] * len(acc or []),
            out_specs=[in_vmem] * (1 if by_core else 2),
            scratch_shapes=[
                pltpu.VMEM((len(pieces) * nodes, width), jnp.bfloat16),
                pltpu.VMEM((RING * GROUP + 1, SIDE, SIDE), jnp.bfloat16),
                pltpu.VMEM((SIDE, width), jnp.float32),
                pltpu.SemaphoreType.DMA((RING,)),
            ],
        ),
        compiler_params=pltpu.CompilerParams(vmem_limit_bytes=SPMM_BYTES),
        cost_estimate=pl.CostEstimate(flops=0, bytes_accessed=4096, transcendentals=0),
        name="spmm_last" if last else "spmm_first",
    )(plan, *blocks, tiles, *(acc or []))


def xor_permute(value, axis, mask):
    size = lax.axis_size(axis)
    return lax.ppermute(value, axis, [(i, i ^ mask) for i in range(size)])


def tree_sum(values):
    while len(values) > 1:
        values = [a + b for a, b in zip(values[::2], values[1::2])]
    return values[0]


def gather_first(own):
    return xor_permute(own, "col", 1), xor_permute(own, "col", 2)


def gather_second(own, by_two, n_col):
    ends, middles = [], []
    for low in range(0, n_col, 4):
        ends += [(low + 1, low), (low + 2, low + 3)]
        middles += [(low + 1, low + 2), (low + 2, low + 1)]
    return lax.ppermute(own, "col", middles), lax.ppermute(by_two, "col", ends)


def as_pieces(own, first, second, mid, n_col):
    if n_col == 4:
        return [[own], [first[0]], [first[1]], list(second)]
    pieces = [own, first[0], first[1], jnp.where(mid, second[0], second[1])]
    for high in range(4, n_col, 4):
        pieces += [xor_permute(piece, "col", high) for piece in pieces[:4]]
    return [[piece] for piece in pieces]


def swap_cores(both):
    pairs = [[i, i + 1] for i in range(0, lax.axis_size("row"), 2)]
    return lax.all_to_all(both, "row", 0, 0, axis_index_groups=pairs)


def fence(*values):
    return lax.optimization_barrier(values)


def add_f32(a, b):
    return a.astype(jnp.float32) + b.astype(jnp.float32)


def stage_sums(keep, recv, n_blocks, rows, at_once=False):
    width = keep.shape[1]
    cut = (n_blocks // 2, 2, 2, rows, width)
    flat = (2, n_blocks // 2, 2, rows, width)
    sums = add_f32(keep, recv).astype(jnp.bfloat16)
    if at_once:
        (sums,) = fence(sums)

    def summed(shape, pick):
        if at_once:
            return pick(sums.reshape(shape)).reshape(-1, width)
        both = add_f32(pick(keep.reshape(shape)), pick(recv.reshape(shape)))
        return both.astype(jnp.bfloat16).reshape(-1, width)

    stage = [
        summed(cut, lambda v: v[:, 1, 0]),
        summed(cut, lambda v: v[:, 0, 0]),
        summed(flat, lambda v: v[1, :, 1]),
        summed(flat, lambda v: v[0, :, 1]),
    ]
    return stage, sums


def halve(value, upper, rows):
    blocks = value.shape[0] // rows
    shape = (2, blocks // 2) if upper else (blocks // 2, 2)
    cut = value.reshape(shape + (rows, value.shape[1]))
    if upper:
        sent, kept = cut[1], cut[0]
    else:
        sent, kept = cut[:, 1], cut[:, 0]
    return sent.reshape(-1, value.shape[1]), kept.reshape(-1, value.shape[1])


def exchange_first(stage, bits):
    return xor_permute(stage[0], "row", bits[0]), xor_permute(stage[2], "row", bits[-1])


def exchange_second(stage, recv, bits, rows):
    sent, kept = [], []
    for upper in (0, 1):
        value = add_f32(stage[2 * upper + 1], recv[upper]).astype(jnp.bfloat16)
        sent_u, kept_u = halve(value, upper, rows)
        sent.append(sent_u)
        kept.append(kept_u)
    return kept, sent


def send_second(sent, bits):
    return [xor_permute(s, "row", bit) for s, bit in zip(sent, (bits[1], bits[-2]))]


def exchange_last(kept, recv, bits, rows):
    done = []
    for upper in (0, 1):
        value = add_f32(kept[upper], recv[upper])
        for bit in (bits[::-1] if upper else bits)[2:]:
            sent_u, kept_u = halve(value.astype(jnp.bfloat16), upper, rows)
            value = add_f32(kept_u, xor_permute(sent_u, "row", bit))
        done.append(value.astype(jnp.bfloat16))
    return jnp.concatenate(done, axis=0)


def weight_term(near, sums):
    terms, at = [], 0
    for f in [part for parts in near for part in parts]:
        own = sums[at : at + f.shape[0]]
        terms.append(lax.dot_general(f, own, (((0,), (0,)), ((), ())), preferred_element_type=jnp.float32))
        at += f.shape[0]
    return sum(terms[1:], terms[0]).astype(jnp.bfloat16)


def sum_over(term, axis, masks):
    parts = [term] + [xor_permute(term, axis, m) for m in masks]
    return tree_sum([p.astype(jnp.float32) for p in parts])


def body(grad_out, preact, features, weight, tiles, tile_rows, tile_cols, live_counts):
    nodes, width = grad_out.shape
    n_row, n_col = lax.axis_size("row"), lax.axis_size("col")
    row, col = lax.axis_index("row"), lax.axis_index("col")
    slots = tiles.shape[2]
    cw = width // 2
    rows = nodes // 2
    bits = [1 << b for b in range(1, n_row.bit_length() - 1)]
    mid = ((col & 3) == 1) | ((col & 3) == 2)

    own0, own1 = [
        jnp.where(preact[:, cut] > 0, grad_out[:, cut], jnp.zeros_like(grad_out[:, cut]))
        for cut in (slice(0, cw), slice(cw, width))
    ]
    first0 = gather_first(own0)
    place = jnp.stack([live_counts.reshape(()), row, col, mid.astype(jnp.int32)])
    plan0, plan1, slot = make_plans(tile_rows, tile_cols, place, n_row, nodes // SIDE)
    flipped = flip_tiles(slot, tiles.reshape(slots, SIDE, SIDE))
    features, plan0 = fence(features, plan0)
    near = [[features]]
    for bit in bits[:2]:
        near.append([xor_permute(features, "row", bit)])
    own0, own1, first0, plan0, plan1, flipped = fence(own0, own1, first0, plan0, plan1, flipped)

    second0 = gather_second(own0, first0[1], n_col)
    acc0 = spmm(plan0, [[own0], [first0[0]], [first0[1]]], flipped, None, n_row)
    own1, acc0 = fence(own1, acc0)
    first1 = gather_first(own1)
    pieces0 = as_pieces(own0, first0, second0, mid, n_col)
    pieces0, near, acc0 = fence(pieces0, near, acc0)

    near.append([xor_permute(near[1][0][:rows], "row", bits[1]), xor_permute(near[2][0][rows:], "row", bits[0])])
    for bit in bits[2:]:
        near += [[xor_permute(f, "row", bit) for f in parts] for parts in near]
    (both0,) = spmm(plan1, pieces0[FIRST_PIECES:], flipped, acc0, n_row, by_core=True)
    got0 = swap_cores(both0)
    got0, near = fence(got0, near)
    stage0, sums0 = stage_sums(got0[0], got0[1], n_row // 2, rows, at_once=True)
    recv0 = exchange_first(stage0, bits)
    own1, first1, stage0, sums0 = fence(own1, first1, stage0, sums0)

    second1 = gather_second(own1, first1[1], n_col)
    pieces1 = as_pieces(own1, first1, second1, mid, n_col)
    acc1 = spmm(plan0, pieces1[:FIRST_PIECES], flipped, None, n_row)
    acc1, recv0 = fence(acc1, recv0)
    rest0, sent0 = exchange_second(stage0, recv0, bits, rows)
    pieces1, acc1, rest0, sent0 = fence(pieces1, acc1, rest0, sent0)

    send1, keep1 = spmm(plan1, pieces1[FIRST_PIECES:], flipped, acc1, n_row)
    send1, keep1, rest0, sent0, sums0 = fence(send1, keep1, rest0, sent0, sums0)

    stage1, sums1 = stage_sums(keep1, xor_permute(send1, "row", 1), n_row // 2, rows, at_once=True)
    recv0 = send_second(sent0, bits)
    term0, term1 = weight_term(near, sums0), weight_term(near, sums1)
    stage1, term0, term1 = fence(stage1, term0, term1)
    stage1, term0, term1, rest0, recv0 = fence(stage1, term0, term1, rest0, recv0)

    recv1 = exchange_first(stage1, bits)
    even = (row & 1) == 0
    theirs, mine = jnp.where(even, term1, term0), jnp.where(even, term0, term1)
    mine = add_f32(mine, xor_permute(theirs, "row", 1)).astype(jnp.bfloat16)
    mine = sum_over(mine, "col", range(1, n_col)).astype(jnp.bfloat16)
    colgrad0 = exchange_last(rest0, recv0, bits, rows)
    recv1, mine, colgrad0 = fence(recv1, mine, colgrad0)

    rest1, sent1 = exchange_second(stage1, recv1, bits, rows)
    rest1, sent1, mine = fence(rest1, sent1, mine)
    recv1 = send_second(sent1, bits)
    others = [xor_permute(mine, "row", m) for m in range(2, n_row, 2)]
    colgrad1 = exchange_last(rest1, recv1, bits, rows)
    colgrad1, mine = fence(colgrad1, mine)
    mine = tree_sum([p.astype(jnp.float32) for p in [mine] + others]).astype(jnp.bfloat16)

    theirs = xor_permute(mine, "row", 1)
    low, high = jnp.where(even, mine, theirs), jnp.where(even, theirs, mine)
    grad_weight = jnp.concatenate([low, high], axis=1).astype(jnp.float32)
    colgrad = jnp.concatenate([colgrad0, colgrad1], axis=1)
    grad_features = lax.dot_general(
        colgrad, weight, (((1,), (1,)), ((), ())), preferred_element_type=jnp.float32
    ).astype(jnp.bfloat16)
    return (grad_features, grad_weight)


def solution(mesh):
    in_specs = (
        P(("row", "col"), None),
        P(("row", "col"), None),
        P(("col", "row"), None),
        P(),
        P("row", "col", None, None, None),
        P("row", "col", None),
        P("row", "col", None),
        P("row", "col"),
    )
    out_specs = (P(("col", "row"), None), P())
    return jax.shard_map(body, mesh=mesh, in_specs=in_specs, out_specs=out_specs, check_vma=False)
```

```python
import functools

import jax
import jax.numpy as jnp
from jax import lax
from jax.experimental import pallas as pl
from jax.experimental.pallas import tpu as pltpu
from jax.sharding import PartitionSpec as P

SIDE = 128
UNROLL = 8
GROUP = 32
RING = 4
FIRST_PIECES = 3
PLAN_ROWS = 8
FLIP_BYTES = 26 * 1024 * 1024
PLAN_BYTES = 12 * 1024 * 1024
TERM_BYTES = 14 * 1024 * 1024
TERM_ROWS = 512
SPMM_BYTES = 16 * 1024 * 1024


def round_up(value, unit):
    return -(-value // unit) * unit


def total(mask, axis):
    return jnp.sum(jnp.where(mask, 1.0, 0.0), axis=axis, keepdims=True).astype(jnp.int32)


def total_of(values, axis):
    return jnp.sum(values.astype(jnp.float32), axis=axis, keepdims=True).astype(jnp.int32)


def plan_kernel(per_dev, n_out, place_ref, rows_r, cols_r, rows_c, cols_c, plan0_ref, plan1_ref, slot_ref):
    slots = rows_r.shape[1]
    size = plan0_ref.shape[1]
    count, row, col, mid = place_ref[0], place_ref[1], place_ref[2], place_ref[3]
    shift = per_dev.bit_length() - 1
    start = FIRST_PIECES * per_dev
    step = 2 * UNROLL

    def attributes(rows, cols, axis):
        ids = lax.broadcasted_iota(jnp.int32, rows.shape, axis)
        row_pos = (((rows >> shift) ^ col) << shift) + (rows & (per_dev - 1))
        away = (cols >> shift) ^ row
        out_pos = ((away >> 1) << shift) + (cols & (per_dev - 1))
        kept = 1 - (away & 1)
        last = (row_pos >= start).astype(jnp.int32)
        live = ids < count
        key = jnp.where(live, (2 * last + kept) * n_out + out_pos, 4 * n_out)
        return ids, row_pos, out_pos, 2 * last + kept, live, key

    ids_r, _, _, part_r, live_r, key_r = attributes(rows_r[...], cols_r[...], 1)
    ids_c, row_pos_c, out_pos_c, part_c, live_c, key_c = attributes(rows_c[...], cols_c[...], 0)
    equal = key_c == key_r
    below = key_r < key_c
    earlier_c = total(equal & (ids_r < ids_c), 1)
    earlier_r = total(equal & (ids_c < ids_r), 0)
    later_r = total(equal & (ids_c > ids_r), 0)
    odd_end = (later_r == 0) & ((earlier_r & 1) == 0)
    weight_r = jnp.where(live_r, jnp.where(odd_end, 2, 1), 0)
    rank_c = total(below, 1) + earlier_c
    rank_r = total(key_c < key_r, 0) + earlier_r
    padded_c = total_of(jnp.where(below, weight_r, 0), 1) + earlier_c
    length = [total_of(jnp.where(part_r == p, weight_r, 0), 1) for p in range(4)]
    n_first = total(live_r & (part_r < 2), 1)
    n_last = count - n_first
    last_base = ((n_first + GROUP - 1) >> 5) << 5
    slot_r = jnp.where(part_r >= 2, last_base + rank_r - n_first, rank_r)
    slot_ref[...] = jnp.where(live_r, slot_r, slots + GROUP)

    lane = lax.broadcasted_iota(jnp.int32, (1, size), 1)
    for p, plan_ref in enumerate((plan0_ref, plan1_ref)):
        sent, held = length[2 * p], length[2 * p + 1]
        sent_steps = (sent + step - 1) >> (step.bit_length() - 1)
        all_steps = sent_steps + ((held + step - 1) >> (step.bit_length() - 1))
        base = length[0] + length[1] if p else jnp.zeros_like(sent)
        in_plan = live_c & ((part_c >> 1) == p)
        pos = padded_c - base + jnp.where((part_c & 1) == 1, sent_steps * step - sent, 0)
        pos = jnp.where(in_plan, pos, -1)
        rank = rank_c - (n_first if p else 0)
        hit = pos == lane

        def placed(values, empty, hit=hit):
            return total_of(jnp.where(hit, values - empty, 0), 0) + empty

        plan_ref[0:1, :] = placed(rank & (RING * GROUP - 1), RING * GROUP)
        plan_ref[1:2, :] = placed(row_pos_c - p * start, 0)
        taken = total(hit, 0) > 0
        ends = [
            jnp.max(jnp.where(in_plan & ((part_c & 1) == h), out_pos_c, 0).astype(jnp.float32), axis=0, keepdims=True)
            for h in range(2)
        ]
        end = jnp.where(lane < sent_steps * step, ends[0], ends[1]).astype(jnp.int32)
        plan_ref[2:3, :] = jnp.where(taken, placed(out_pos_c, 0), end)
        plan_ref[3:4, :] = jnp.where(taken, placed((earlier_c > 0).astype(jnp.int32), 0), 1)
        done = total(in_plan & (pos < (lane + 1) * step), 0)
        tiles = n_last if p else n_first
        info = [
            jnp.full((1, 1), mid, jnp.int32),
            sent_steps,
            (tiles + GROUP - 1) >> 5,
            last_base if p else jnp.zeros_like(last_base),
            jnp.zeros_like(last_base),
        ]
        for g in range(slots // GROUP):
            info.append(total((done <= (g + 1) * GROUP) & (lane < all_steps), 1))
        row_values = jnp.zeros((1, size), jnp.int32)
        for n, value in enumerate(info):
            row_values = jnp.where(lane == n, value, row_values)
        plan_ref[4:5, :] = row_values
        plan_ref[5:6, :] = jnp.full((1, size), row & 1, jnp.int32)
        plan_ref[6:8, :] = jnp.zeros((2, size), jnp.int32)


def make_plans(tile_rows, tile_cols, place, n_row, per_dev):
    slots = tile_rows.size
    n_out = n_row // 2 * per_dev
    size = round_up(slots + 2 * n_out + 4 * UNROLL, SIDE)
    plan = jax.ShapeDtypeStruct((PLAN_ROWS, size), jnp.int32)
    return pl.pallas_call(
        functools.partial(plan_kernel, per_dev, n_out),
        out_shape=(plan, plan, jax.ShapeDtypeStruct((1, slots), jnp.int32)),
        in_specs=[pl.BlockSpec(memory_space=pltpu.SMEM)] + [pl.BlockSpec(memory_space=pltpu.VMEM)] * 4,
        out_specs=[pl.BlockSpec(memory_space=pltpu.VMEM)] * 3,
        compiler_params=pltpu.CompilerParams(vmem_limit_bytes=PLAN_BYTES),
        cost_estimate=pl.CostEstimate(flops=0, bytes_accessed=4096, transcendentals=0),
        name="plan_slots",
    )(place, tile_rows.reshape(1, slots), tile_cols.reshape(1, slots), tile_rows.reshape(slots, 1), tile_cols.reshape(slots, 1))


def flip_kernel(slot_ref, tiles_ref, out_ref, t_in, t_out, in_sem, out_sem):
    slots = t_in.shape[0]
    groups = slots // GROUP
    loads = [
        pltpu.make_async_copy(tiles_ref.at[pl.ds(g * GROUP, GROUP)], t_in.at[pl.ds(g * GROUP, GROUP)], in_sem.at[g])
        for g in range(groups)
    ]
    for load in loads:
        load.start()
    for g in range(groups):
        loads[g].wait()

        def some(step, carry, g=g):
            for u in range(4):
                k = g * GROUP + step * 4 + u
                t_out[slot_ref[0, k]] = t_in[k].T
            return carry

        lax.fori_loop(0, GROUP // 4, some, 0)
    stores = [
        pltpu.make_async_copy(t_out.at[pl.ds(g * GROUP, GROUP)], out_ref.at[pl.ds(g * GROUP, GROUP)], out_sem.at[g])
        for g in range(groups + 1)
    ]
    for store in stores:
        store.start()
    for store in stores:
        store.wait()


def flip_tiles(slot, tile_stack):
    slots = tile_stack.shape[0]
    groups = slots // GROUP
    return pl.pallas_call(
        flip_kernel,
        out_shape=jax.ShapeDtypeStruct((slots + GROUP, SIDE, SIDE), tile_stack.dtype),
        grid_spec=pltpu.PrefetchScalarGridSpec(
            num_scalar_prefetch=1,
            grid=(),
            in_specs=[pl.BlockSpec(memory_space=pl.ANY)],
            out_specs=pl.BlockSpec(memory_space=pl.ANY),
            scratch_shapes=[
                pltpu.VMEM(tile_stack.shape, tile_stack.dtype),
                pltpu.VMEM((slots + GROUP + 1, SIDE, SIDE), tile_stack.dtype),
                pltpu.SemaphoreType.DMA((groups,)),
                pltpu.SemaphoreType.DMA((groups + 1,)),
            ],
        ),
        compiler_params=pltpu.CompilerParams(vmem_limit_bytes=FLIP_BYTES),
        cost_estimate=pl.CostEstimate(flops=0, bytes_accessed=4096, transcendentals=0),
        name="flip_tiles",
    )(slot, tile_stack)


def spmm_kernel(layout, last, by_core, plan_ref, *refs):
    n_refs = sum(layout)
    refs_left = list(refs[:n_refs])
    pieces = [[refs_left.pop(0) for _ in range(n)] for n in layout]
    rest = list(refs[n_refs:])
    tiles_ref = rest.pop(0)
    acc_refs = (rest.pop(0), rest.pop(0)) if last else (None, None)
    if by_core:
        core = plan_ref[5, 0]
        out_ref = rest.pop(0)
        out_refs = (out_ref.at[1 - core], out_ref.at[core])
    else:
        out_refs = (rest.pop(0), rest.pop(0))
    m_vmem, t_vmem, total_ref, sems = rest
    nodes, width = pieces[0][0].shape
    mid, sent_steps, n_groups, tile_base = [plan_ref[4, n] for n in range(4)]

    def group_copy(g):
        place = g & (RING - 1)
        return pltpu.make_async_copy(
            tiles_ref.at[pl.ds(tile_base + pl.multiple_of(g * GROUP, GROUP), GROUP)],
            t_vmem.at[pl.ds(pl.multiple_of(place * GROUP, GROUP), GROUP)],
            sems.at[place],
        )

    for g in range(2):
        pl.when(g < n_groups)(group_copy(g).start)
    t_vmem[RING * GROUP] = jnp.zeros((SIDE, SIDE), t_vmem.dtype)
    for out_ref, acc_ref in zip(out_refs, acc_refs):

        def begin(step, carry, out_ref=out_ref, acc_ref=acc_ref):
            at = pl.ds(pl.multiple_of(step * 256, 256), 256)
            out_ref[at, :] = acc_ref[at, :] if last else jnp.zeros((256, width), out_ref.dtype)
            return carry

        lax.fori_loop(0, out_ref.shape[0] // 256, begin, 0)
    for p, options in enumerate(pieces):

        def take(ref, p=p):
            def some(step, carry):
                at = pl.multiple_of(step * 512, 512)
                m_vmem[pl.ds(pl.multiple_of(p * nodes + at, 512), 512), :] = ref[pl.ds(at, 512), :]
                return carry

            lax.fori_loop(0, nodes // 512, some, 0)

        if len(options) == 1:
            take(options[0])
        else:
            pl.when(mid == 1)(functools.partial(take, options[0]))
            pl.when(mid != 1)(functools.partial(take, options[1]))

    def block(index):
        return m_vmem[pl.ds(pl.multiple_of(index * SIDE, SIDE), SIDE), :]

    def add_pairs(out_ref, acc_ref, step, carry):
        running = total_ref[...]
        prods = []
        for u in range(UNROLL):
            k = 2 * (step * UNROLL + u)
            left = jnp.concatenate([t_vmem[plan_ref[0, k]], t_vmem[plan_ref[0, k + 1]]], axis=1)
            right = jnp.concatenate([block(plan_ref[1, k]), block(plan_ref[1, k + 1])], axis=0)
            prods.append(jnp.dot(left, right, preferred_element_type=jnp.float32))
        for u in range(UNROLL):
            k = 2 * (step * UNROLL + u)
            at = pl.ds(pl.multiple_of(plan_ref[2, k] * SIDE, SIDE), SIDE)
            before = acc_ref[at, :].astype(jnp.float32) if last else jnp.zeros_like(running)
            running = prods[u] + jnp.where(plan_ref[3, k] == 1, running, before)
            out_ref[at, :] = running.astype(out_ref.dtype)
        total_ref[...] = running
        return carry

    total_ref[...] = jnp.zeros_like(total_ref)

    def add_group(g, carry):
        group_copy(g).wait()

        @pl.when(g + 2 < n_groups)
        def _():
            group_copy(g + 2).start()

        low, high = plan_ref[4, 4 + g], plan_ref[4, 5 + g]
        lax.fori_loop(
            jnp.minimum(low, sent_steps), jnp.minimum(high, sent_steps),
            functools.partial(add_pairs, out_refs[0], acc_refs[0]), 0,
        )
        lax.fori_loop(
            jnp.maximum(low, sent_steps), jnp.maximum(high, sent_steps),
            functools.partial(add_pairs, out_refs[1], acc_refs[1]), 0,
        )
        return carry

    lax.fori_loop(0, n_groups, add_group, 0)


def spmm(plan, pieces, tiles, acc, n_row, by_core=False):
    nodes, width = pieces[0][0].shape
    half = n_row // 2 * nodes
    last = acc is not None
    out = jax.ShapeDtypeStruct((2, half, width) if by_core else (half, width), jnp.bfloat16)
    blocks = [ref for p in pieces for ref in p]
    in_vmem, in_any = pl.BlockSpec(memory_space=pltpu.VMEM), pl.BlockSpec(memory_space=pl.ANY)
    return pl.pallas_call(
        functools.partial(spmm_kernel, [len(p) for p in pieces], last, by_core),
        out_shape=(out,) if by_core else (out, out),
        grid_spec=pltpu.PrefetchScalarGridSpec(
            num_scalar_prefetch=1,
            grid=(),
            in_specs=[in_vmem] * len(blocks) + [in_any] + [in_vmem] * len(acc or []),
            out_specs=[in_vmem] * (1 if by_core else 2),
            scratch_shapes=[
                pltpu.VMEM((len(pieces) * nodes, width), jnp.bfloat16),
                pltpu.VMEM((RING * GROUP + 1, SIDE, SIDE), jnp.bfloat16),
                pltpu.VMEM((SIDE, width), jnp.float32),
                pltpu.SemaphoreType.DMA((RING,)),
            ],
        ),
        compiler_params=pltpu.CompilerParams(vmem_limit_bytes=SPMM_BYTES),
        cost_estimate=pl.CostEstimate(flops=0, bytes_accessed=4096, transcendentals=0),
        name="spmm_last" if last else "spmm_first",
    )(plan, *blocks, tiles, *(acc or []))


def xor_permute(value, axis, mask):
    size = lax.axis_size(axis)
    return lax.ppermute(value, axis, [(i, i ^ mask) for i in range(size)])


def tree_sum(values):
    while len(values) > 1:
        values = [a + b for a, b in zip(values[::2], values[1::2])]
    return values[0]


def gather_first(own):
    return xor_permute(own, "col", 1), xor_permute(own, "col", 2)


def gather_second(own, by_two, n_col):
    ends, middles = [], []
    for low in range(0, n_col, 4):
        ends += [(low + 1, low), (low + 2, low + 3)]
        middles += [(low + 1, low + 2), (low + 2, low + 1)]
    return lax.ppermute(own, "col", middles), lax.ppermute(by_two, "col", ends)


def as_pieces(own, first, second, mid, n_col):
    if n_col == 4:
        return [[own], [first[0]], [first[1]], list(second)]
    pieces = [own, first[0], first[1], jnp.where(mid, second[0], second[1])]
    for high in range(4, n_col, 4):
        pieces += [xor_permute(piece, "col", high) for piece in pieces[:4]]
    return [[piece] for piece in pieces]


def swap_cores(both):
    pairs = [[i, i + 1] for i in range(0, lax.axis_size("row"), 2)]
    return lax.all_to_all(both, "row", 0, 0, axis_index_groups=pairs)


def fence(*values):
    return lax.optimization_barrier(values)


def add_f32(a, b):
    return a.astype(jnp.float32) + b.astype(jnp.float32)


def stage_sums(keep, recv, n_blocks, rows, at_once=False):
    width = keep.shape[1]
    cut = (n_blocks // 2, 2, 2, rows, width)
    flat = (2, n_blocks // 2, 2, rows, width)
    sums = add_f32(keep, recv).astype(jnp.bfloat16)
    if at_once:
        (sums,) = fence(sums)

    def summed(shape, pick):
        if at_once:
            return pick(sums.reshape(shape)).reshape(-1, width)
        both = add_f32(pick(keep.reshape(shape)), pick(recv.reshape(shape)))
        return both.astype(jnp.bfloat16).reshape(-1, width)

    stage = [
        summed(cut, lambda v: v[:, 1, 0]),
        summed(cut, lambda v: v[:, 0, 0]),
        summed(flat, lambda v: v[1, :, 1]),
        summed(flat, lambda v: v[0, :, 1]),
    ]
    return stage, sums


def halve(value, upper, rows):
    blocks = value.shape[0] // rows
    shape = (2, blocks // 2) if upper else (blocks // 2, 2)
    cut = value.reshape(shape + (rows, value.shape[1]))
    if upper:
        sent, kept = cut[1], cut[0]
    else:
        sent, kept = cut[:, 1], cut[:, 0]
    return sent.reshape(-1, value.shape[1]), kept.reshape(-1, value.shape[1])


def exchange_first(stage, bits):
    return xor_permute(stage[0], "row", bits[0]), xor_permute(stage[2], "row", bits[-1])


def exchange_second(stage, recv, bits, rows):
    sent, kept = [], []
    for upper in (0, 1):
        value = add_f32(stage[2 * upper + 1], recv[upper]).astype(jnp.bfloat16)
        sent_u, kept_u = halve(value, upper, rows)
        sent.append(sent_u)
        kept.append(kept_u)
    return kept, sent


def send_second(sent, bits):
    return [xor_permute(s, "row", bit) for s, bit in zip(sent, (bits[1], bits[-2]))]


def exchange_last(kept, recv, bits, rows):
    done = []
    for upper in (0, 1):
        value = add_f32(kept[upper], recv[upper])
        for bit in (bits[::-1] if upper else bits)[2:]:
            sent_u, kept_u = halve(value.astype(jnp.bfloat16), upper, rows)
            value = add_f32(kept_u, xor_permute(sent_u, "row", bit))
        done.append(value.astype(jnp.bfloat16))
    return jnp.concatenate(done, axis=0)


def weight_term(near, sums):
    terms, at = [], 0
    for f in [part for parts in near for part in parts]:
        own = sums[at : at + f.shape[0]]
        terms.append(lax.dot_general(f, own, (((0,), (0,)), ((), ())), preferred_element_type=jnp.float32))
        at += f.shape[0]
    return sum(terms[1:], terms[0]).astype(jnp.bfloat16)


def term_kernel(*refs):
    *parts, sums_ref, out_ref, acc_ref = refs
    acc_ref[...] = jnp.zeros_like(acc_ref)
    first = 0
    for part in parts:

        def add_rows(step, carry, part=part, first=first):
            at = pl.multiple_of(step * TERM_ROWS, TERM_ROWS)
            acc_ref[...] += lax.dot_general(
                sums_ref[pl.ds(first + at, TERM_ROWS), :], part[pl.ds(at, TERM_ROWS), :],
                (((0,), (0,)), ((), ())), preferred_element_type=jnp.float32,
            )
            return carry

        lax.fori_loop(0, part.shape[0] // TERM_ROWS, add_rows, 0)
        first += part.shape[0]
    out_ref[...] = acc_ref[...].T.astype(out_ref.dtype)


def weight_term_early(near, sums):
    parts = [part for group in near for part in group]
    shape = (parts[0].shape[1], sums.shape[1])
    return pl.pallas_call(
        term_kernel,
        out_shape=jax.ShapeDtypeStruct(shape, jnp.bfloat16),
        in_specs=[pl.BlockSpec(memory_space=pltpu.VMEM)] * (len(parts) + 1),
        out_specs=pl.BlockSpec(memory_space=pltpu.VMEM),
        scratch_shapes=[pltpu.VMEM(shape[::-1], jnp.float32)],
        compiler_params=pltpu.CompilerParams(vmem_limit_bytes=TERM_BYTES),
        cost_estimate=pl.CostEstimate(flops=0, bytes_accessed=4096, transcendentals=0),
        name="weight_term",
    )(*parts, sums)


def sum_over(term, axis, masks):
    parts = [term] + [xor_permute(term, axis, m) for m in masks]
    return tree_sum([p.astype(jnp.float32) for p in parts])


def body(grad_out, preact, features, weight, tiles, tile_rows, tile_cols, live_counts):
    nodes, width = grad_out.shape
    n_row, n_col = lax.axis_size("row"), lax.axis_size("col")
    row, col = lax.axis_index("row"), lax.axis_index("col")
    slots = tiles.shape[2]
    cw = width // 2
    rows = nodes // 2
    bits = [1 << b for b in range(1, n_row.bit_length() - 1)]
    mid = ((col & 3) == 1) | ((col & 3) == 2)

    own0, own1 = [
        jnp.where(preact[:, cut] > 0, grad_out[:, cut], jnp.zeros_like(grad_out[:, cut]))
        for cut in (slice(0, cw), slice(cw, width))
    ]
    first0 = gather_first(own0)
    place = jnp.stack([live_counts.reshape(()), row, col, mid.astype(jnp.int32)])
    plan0, plan1, slot = make_plans(tile_rows, tile_cols, place, n_row, nodes // SIDE)
    flipped = flip_tiles(slot, tiles.reshape(slots, SIDE, SIDE))
    features, plan0 = fence(features, plan0)
    near = [[features]]
    for bit in bits[:2]:
        near.append([xor_permute(features, "row", bit)])
    own0, own1, first0, plan0, plan1, flipped = fence(own0, own1, first0, plan0, plan1, flipped)

    second0 = gather_second(own0, first0[1], n_col)
    acc0 = spmm(plan0, [[own0], [first0[0]], [first0[1]]], flipped, None, n_row)
    own1, acc0 = fence(own1, acc0)
    first1 = gather_first(own1)
    pieces0 = as_pieces(own0, first0, second0, mid, n_col)
    pieces0, near, acc0 = fence(pieces0, near, acc0)

    near.append([xor_permute(near[1][0][:rows], "row", bits[1]), xor_permute(near[2][0][rows:], "row", bits[0])])
    for bit in bits[2:]:
        near += [[xor_permute(f, "row", bit) for f in parts] for parts in near]
    (both0,) = spmm(plan1, pieces0[FIRST_PIECES:], flipped, acc0, n_row, by_core=True)
    got0 = swap_cores(both0)
    got0, near = fence(got0, near)
    stage0, sums0 = stage_sums(got0[0], got0[1], n_row // 2, rows, at_once=True)
    recv0 = exchange_first(stage0, bits)
    term0 = weight_term_early(near, sums0)
    own1, first1, stage0, term0 = fence(own1, first1, stage0, term0)

    second1 = gather_second(own1, first1[1], n_col)
    pieces1 = as_pieces(own1, first1, second1, mid, n_col)
    acc1 = spmm(plan0, pieces1[:FIRST_PIECES], flipped, None, n_row)
    acc1, recv0 = fence(acc1, recv0)
    rest0, sent0 = exchange_second(stage0, recv0, bits, rows)
    pieces1, acc1, rest0, sent0 = fence(pieces1, acc1, rest0, sent0)

    send1, keep1 = spmm(plan1, pieces1[FIRST_PIECES:], flipped, acc1, n_row)
    send1, keep1, rest0, sent0 = fence(send1, keep1, rest0, sent0)

    stage1, sums1 = stage_sums(keep1, xor_permute(send1, "row", 1), n_row // 2, rows, at_once=True)
    recv0 = send_second(sent0, bits)
    term1 = weight_term(near, sums1)
    stage1, term0, term1 = fence(stage1, term0, term1)
    stage1, term0, term1, rest0, recv0 = fence(stage1, term0, term1, rest0, recv0)

    recv1 = exchange_first(stage1, bits)
    even = (row & 1) == 0
    theirs, mine = jnp.where(even, term1, term0), jnp.where(even, term0, term1)
    mine = add_f32(mine, xor_permute(theirs, "row", 1)).astype(jnp.bfloat16)
    mine = sum_over(mine, "col", range(1, n_col)).astype(jnp.bfloat16)
    colgrad0 = exchange_last(rest0, recv0, bits, rows)
    recv1, mine, colgrad0 = fence(recv1, mine, colgrad0)

    rest1, sent1 = exchange_second(stage1, recv1, bits, rows)
    rest1, sent1, mine = fence(rest1, sent1, mine)
    recv1 = send_second(sent1, bits)
    others = [xor_permute(mine, "row", m) for m in range(2, n_row, 2)]
    colgrad1 = exchange_last(rest1, recv1, bits, rows)
    colgrad1, mine = fence(colgrad1, mine)
    mine = tree_sum([p.astype(jnp.float32) for p in [mine] + others]).astype(jnp.bfloat16)

    theirs = xor_permute(mine, "row", 1)
    low, high = jnp.where(even, mine, theirs), jnp.where(even, theirs, mine)
    grad_weight = jnp.concatenate([low, high], axis=1).astype(jnp.float32)
    colgrad = jnp.concatenate([colgrad0, colgrad1], axis=1)
    grad_features = lax.dot_general(
        colgrad, weight, (((1,), (1,)), ((), ())), preferred_element_type=jnp.float32
    ).astype(jnp.bfloat16)
    return (grad_features, grad_weight)


def solution(mesh):
    in_specs = (
        P(("row", "col"), None),
        P(("row", "col"), None),
        P(("col", "row"), None),
        P(),
        P("row", "col", None, None, None),
        P("row", "col", None),
        P("row", "col", None),
        P("row", "col"),
    )
    out_specs = (P(("col", "row"), None), P())
    return jax.shard_map(body, mesh=mesh, in_specs=in_specs, out_specs=out_specs, check_vma=False)
```

```python
import functools

import jax
import jax.numpy as jnp
from jax import lax
from jax.experimental import pallas as pl
from jax.experimental.pallas import tpu as pltpu
from jax.sharding import PartitionSpec as P

SIDE = 128
UNROLL = 8
GROUP = 32
RING = 4
FIRST_PIECES = 3
PLAN_ROWS = 8
FLIP_BYTES = 50 * 1024 * 1024
PLAN_BYTES = 12 * 1024 * 1024
TERM_BYTES = 14 * 1024 * 1024
TERM_ROWS = 512
SPMM_BYTES = 40 * 1024 * 1024


def round_up(value, unit):
    return -(-value // unit) * unit


def total(mask, axis):
    return jnp.sum(jnp.where(mask, 1.0, 0.0), axis=axis, keepdims=True).astype(jnp.int32)


def total_of(values, axis):
    return jnp.sum(values.astype(jnp.float32), axis=axis, keepdims=True).astype(jnp.int32)


def plan_kernel(per_dev, n_out, place_ref, rows_r, cols_r, rows_c, cols_c, plan0_ref, plan1_ref, slot_ref):
    slots = rows_r.shape[1]
    size = plan0_ref.shape[1]
    count, row, col, mid = place_ref[0], place_ref[1], place_ref[2], place_ref[3]
    shift = per_dev.bit_length() - 1
    start = FIRST_PIECES * per_dev
    step = 2 * UNROLL

    def attributes(rows, cols, axis):
        ids = lax.broadcasted_iota(jnp.int32, rows.shape, axis)
        row_pos = (((rows >> shift) ^ col) << shift) + (rows & (per_dev - 1))
        away = (cols >> shift) ^ row
        out_pos = ((away >> 1) << shift) + (cols & (per_dev - 1))
        kept = 1 - (away & 1)
        last = (row_pos >= start).astype(jnp.int32)
        live = ids < count
        key = jnp.where(live, (2 * last + kept) * n_out + out_pos, 4 * n_out)
        return ids, row_pos, out_pos, 2 * last + kept, live, key

    ids_r, _, _, part_r, live_r, key_r = attributes(rows_r[...], cols_r[...], 1)
    ids_c, row_pos_c, out_pos_c, part_c, live_c, key_c = attributes(rows_c[...], cols_c[...], 0)
    equal = key_c == key_r
    below = key_r < key_c
    earlier_c = total(equal & (ids_r < ids_c), 1)
    earlier_r = total(equal & (ids_c < ids_r), 0)
    later_r = total(equal & (ids_c > ids_r), 0)
    odd_end = (later_r == 0) & ((earlier_r & 1) == 0)
    weight_r = jnp.where(live_r, jnp.where(odd_end, 2, 1), 0)
    rank_c = total(below, 1) + earlier_c
    rank_r = total(key_c < key_r, 0) + earlier_r
    padded_c = total_of(jnp.where(below, weight_r, 0), 1) + earlier_c
    length = [total_of(jnp.where(part_r == p, weight_r, 0), 1) for p in range(4)]
    n_first = total(live_r & (part_r < 2), 1)
    n_last = count - n_first
    last_base = ((n_first + GROUP - 1) >> 5) << 5
    slot_r = jnp.where(part_r >= 2, last_base + rank_r - n_first, rank_r)
    slot_ref[...] = jnp.where(live_r, slot_r, slots + GROUP)

    lane = lax.broadcasted_iota(jnp.int32, (1, size), 1)
    for p, plan_ref in enumerate((plan0_ref, plan1_ref)):
        sent, held = length[2 * p], length[2 * p + 1]
        sent_steps = (sent + step - 1) >> (step.bit_length() - 1)
        all_steps = sent_steps + ((held + step - 1) >> (step.bit_length() - 1))
        base = length[0] + length[1] if p else jnp.zeros_like(sent)
        in_plan = live_c & ((part_c >> 1) == p)
        pos = padded_c - base + jnp.where((part_c & 1) == 1, sent_steps * step - sent, 0)
        pos = jnp.where(in_plan, pos, -1)
        rank = rank_c - (n_first if p else 0)
        hit = pos == lane

        def placed(values, empty, hit=hit):
            return total_of(jnp.where(hit, values - empty, 0), 0) + empty

        plan_ref[0:1, :] = placed(rank & (RING * GROUP - 1), RING * GROUP)
        plan_ref[1:2, :] = placed(row_pos_c - p * start, 0)
        taken = total(hit, 0) > 0
        ends = [
            jnp.max(jnp.where(in_plan & ((part_c & 1) == h), out_pos_c, 0).astype(jnp.float32), axis=0, keepdims=True)
            for h in range(2)
        ]
        end = jnp.where(lane < sent_steps * step, ends[0], ends[1]).astype(jnp.int32)
        plan_ref[2:3, :] = jnp.where(taken, placed(out_pos_c, 0), end)
        plan_ref[3:4, :] = jnp.where(taken, placed((earlier_c > 0).astype(jnp.int32), 0), 1)
        done = total(in_plan & (pos < (lane + 1) * step), 0)
        tiles = n_last if p else n_first
        info = [
            jnp.full((1, 1), mid, jnp.int32),
            sent_steps,
            (tiles + GROUP - 1) >> 5,
            last_base if p else jnp.zeros_like(last_base),
            jnp.zeros_like(last_base),
        ]
        for g in range(slots // GROUP):
            info.append(total((done <= (g + 1) * GROUP) & (lane < all_steps), 1))
        row_values = jnp.zeros((1, size), jnp.int32)
        for n, value in enumerate(info):
            row_values = jnp.where(lane == n, value, row_values)
        plan_ref[4:5, :] = row_values
        plan_ref[5:6, :] = jnp.full((1, size), row & 1, jnp.int32)
        plan_ref[6:8, :] = jnp.zeros((2, size), jnp.int32)


def make_plans(tile_rows, tile_cols, place, n_row, per_dev):
    slots = tile_rows.size
    n_out = n_row // 2 * per_dev
    size = round_up(slots + 2 * n_out + 4 * UNROLL, SIDE)
    plan = jax.ShapeDtypeStruct((PLAN_ROWS, size), jnp.int32)
    return pl.pallas_call(
        functools.partial(plan_kernel, per_dev, n_out),
        out_shape=(plan, plan, jax.ShapeDtypeStruct((1, slots), jnp.int32)),
        in_specs=[pl.BlockSpec(memory_space=pltpu.SMEM)] + [pl.BlockSpec(memory_space=pltpu.VMEM)] * 4,
        out_specs=[pl.BlockSpec(memory_space=pltpu.VMEM)] * 3,
        compiler_params=pltpu.CompilerParams(vmem_limit_bytes=PLAN_BYTES),
        cost_estimate=pl.CostEstimate(flops=0, bytes_accessed=4096, transcendentals=0),
        name="plan_slots",
    )(place, tile_rows.reshape(1, slots), tile_cols.reshape(1, slots), tile_rows.reshape(slots, 1), tile_cols.reshape(slots, 1))


def flip_kernel(slot_ref, tiles_ref, out_ref, t_in, t_out, in_sem, out_sem):
    slots = t_in.shape[0]
    groups = slots // GROUP
    loads = [
        pltpu.make_async_copy(tiles_ref.at[pl.ds(g * GROUP, GROUP)], t_in.at[pl.ds(g * GROUP, GROUP)], in_sem.at[g])
        for g in range(groups)
    ]
    for load in loads:
        load.start()
    for g in range(groups):
        loads[g].wait()

        def some(step, carry, g=g):
            for u in range(4):
                k = g * GROUP + step * 4 + u
                t_out[slot_ref[0, k]] = t_in[k].T
            return carry

        lax.fori_loop(0, GROUP // 4, some, 0)
    stores = [
        pltpu.make_async_copy(t_out.at[pl.ds(g * GROUP, GROUP)], out_ref.at[pl.ds(g * GROUP, GROUP)], out_sem.at[g])
        for g in range(groups + 1)
    ]
    for store in stores:
        store.start()
    for store in stores:
        store.wait()


def flip_tiles(slot, tile_stack):
    slots = tile_stack.shape[0]
    groups = slots // GROUP
    return pl.pallas_call(
        flip_kernel,
        out_shape=jax.ShapeDtypeStruct((slots + GROUP, SIDE, SIDE), tile_stack.dtype),
        grid_spec=pltpu.PrefetchScalarGridSpec(
            num_scalar_prefetch=1,
            grid=(),
            in_specs=[pl.BlockSpec(memory_space=pl.ANY)],
            out_specs=pl.BlockSpec(memory_space=pl.ANY),
            scratch_shapes=[
                pltpu.VMEM(tile_stack.shape, tile_stack.dtype),
                pltpu.VMEM((slots + GROUP + 1, SIDE, SIDE), tile_stack.dtype),
                pltpu.SemaphoreType.DMA((groups,)),
                pltpu.SemaphoreType.DMA((groups + 1,)),
            ],
        ),
        compiler_params=pltpu.CompilerParams(vmem_limit_bytes=FLIP_BYTES),
        cost_estimate=pl.CostEstimate(flops=0, bytes_accessed=4096, transcendentals=0),
        name="flip_tiles",
    )(slot, tile_stack)


def spmm_kernel(layout, last, by_core, plan_ref, *refs):
    n_refs = sum(layout)
    refs_left = list(refs[:n_refs])
    pieces = [[refs_left.pop(0) for _ in range(n)] for n in layout]
    rest = list(refs[n_refs:])
    tiles_ref = rest.pop(0)
    acc_refs = (rest.pop(0), rest.pop(0)) if last else (None, None)
    if by_core:
        core = plan_ref[5, 0]
        out_ref = rest.pop(0)
        out_refs = (out_ref.at[1 - core], out_ref.at[core])
    else:
        out_refs = (rest.pop(0), rest.pop(0))
    m_vmem, t_vmem, total_ref, sems = rest
    nodes, width = pieces[0][0].shape
    mid, sent_steps, n_groups, tile_base = [plan_ref[4, n] for n in range(4)]

    def group_copy(g):
        place = g & (RING - 1)
        return pltpu.make_async_copy(
            tiles_ref.at[pl.ds(tile_base + pl.multiple_of(g * GROUP, GROUP), GROUP)],
            t_vmem.at[pl.ds(pl.multiple_of(place * GROUP, GROUP), GROUP)],
            sems.at[place],
        )

    for g in range(2):
        pl.when(g < n_groups)(group_copy(g).start)
    t_vmem[RING * GROUP] = jnp.zeros((SIDE, SIDE), t_vmem.dtype)
    for out_ref, acc_ref in zip(out_refs, acc_refs):

        def begin(step, carry, out_ref=out_ref, acc_ref=acc_ref):
            at = pl.ds(pl.multiple_of(step * 256, 256), 256)
            out_ref[at, :] = acc_ref[at, :] if last else jnp.zeros((256, width), out_ref.dtype)
            return carry

        lax.fori_loop(0, out_ref.shape[0] // 256, begin, 0)
    for p, options in enumerate(pieces):

        def take(ref, p=p):
            def some(step, carry):
                at = pl.multiple_of(step * 512, 512)
                m_vmem[pl.ds(pl.multiple_of(p * nodes + at, 512), 512), :] = ref[pl.ds(at, 512), :]
                return carry

            lax.fori_loop(0, nodes // 512, some, 0)

        if len(options) == 1:
            take(options[0])
        else:
            pl.when(mid == 1)(functools.partial(take, options[0]))
            pl.when(mid != 1)(functools.partial(take, options[1]))

    def block(index):
        return m_vmem[pl.ds(pl.multiple_of(index * SIDE, SIDE), SIDE), :]

    def add_pairs(out_ref, acc_ref, step, carry):
        running = total_ref[...]
        prods = []
        for u in range(UNROLL):
            k = 2 * (step * UNROLL + u)
            left = jnp.concatenate([t_vmem[plan_ref[0, k]], t_vmem[plan_ref[0, k + 1]]], axis=1)
            right = jnp.concatenate([block(plan_ref[1, k]), block(plan_ref[1, k + 1])], axis=0)
            prods.append(jnp.dot(left, right, preferred_element_type=jnp.float32))
        for u in range(UNROLL):
            k = 2 * (step * UNROLL + u)
            at = pl.ds(pl.multiple_of(plan_ref[2, k] * SIDE, SIDE), SIDE)
            before = acc_ref[at, :].astype(jnp.float32) if last else jnp.zeros_like(running)
            running = prods[u] + jnp.where(plan_ref[3, k] == 1, running, before)
            out_ref[at, :] = running.astype(out_ref.dtype)
        total_ref[...] = running
        return carry

    total_ref[...] = jnp.zeros_like(total_ref)

    def add_group(g, carry):
        group_copy(g).wait()

        @pl.when(g + 2 < n_groups)
        def _():
            group_copy(g + 2).start()

        low, high = plan_ref[4, 4 + g], plan_ref[4, 5 + g]
        lax.fori_loop(
            jnp.minimum(low, sent_steps), jnp.minimum(high, sent_steps),
            functools.partial(add_pairs, out_refs[0], acc_refs[0]), 0,
        )
        lax.fori_loop(
            jnp.maximum(low, sent_steps), jnp.maximum(high, sent_steps),
            functools.partial(add_pairs, out_refs[1], acc_refs[1]), 0,
        )
        return carry

    lax.fori_loop(0, n_groups, add_group, 0)


def spmm(plan, pieces, tiles, acc, n_row, by_core=False):
    nodes, width = pieces[0][0].shape
    half = n_row // 2 * nodes
    last = acc is not None
    out = jax.ShapeDtypeStruct((2, half, width) if by_core else (half, width), jnp.bfloat16)
    blocks = [ref for p in pieces for ref in p]
    in_vmem, in_any = pl.BlockSpec(memory_space=pltpu.VMEM), pl.BlockSpec(memory_space=pl.ANY)
    return pl.pallas_call(
        functools.partial(spmm_kernel, [len(p) for p in pieces], last, by_core),
        out_shape=(out,) if by_core else (out, out),
        grid_spec=pltpu.PrefetchScalarGridSpec(
            num_scalar_prefetch=1,
            grid=(),
            in_specs=[in_vmem] * len(blocks) + [in_any] + [in_vmem] * len(acc or []),
            out_specs=[in_vmem] * (1 if by_core else 2),
            scratch_shapes=[
                pltpu.VMEM((len(pieces) * nodes, width), jnp.bfloat16),
                pltpu.VMEM((RING * GROUP + 1, SIDE, SIDE), jnp.bfloat16),
                pltpu.VMEM((SIDE, width), jnp.float32),
                pltpu.SemaphoreType.DMA((RING,)),
            ],
        ),
        compiler_params=pltpu.CompilerParams(vmem_limit_bytes=SPMM_BYTES),
        cost_estimate=pl.CostEstimate(flops=0, bytes_accessed=4096, transcendentals=0),
        name="spmm_last" if last else "spmm_first",
    )(plan, *blocks, tiles, *(acc or []))


def xor_permute(value, axis, mask):
    size = lax.axis_size(axis)
    return lax.ppermute(value, axis, [(i, i ^ mask) for i in range(size)])


def tree_sum(values):
    while len(values) > 1:
        values = [a + b for a, b in zip(values[::2], values[1::2])]
    return values[0]


def gather_first(own):
    return xor_permute(own, "col", 1), xor_permute(own, "col", 2)


def gather_second(own, by_two, n_col):
    ends, middles = [], []
    for low in range(0, n_col, 4):
        ends += [(low + 1, low), (low + 2, low + 3)]
        middles += [(low + 1, low + 2), (low + 2, low + 1)]
    return lax.ppermute(own, "col", middles), lax.ppermute(by_two, "col", ends)


def as_pieces(own, first, second, mid, n_col):
    if n_col == 4:
        return [[own], [first[0]], [first[1]], list(second)]
    pieces = [own, first[0], first[1], jnp.where(mid, second[0], second[1])]
    for high in range(4, n_col, 4):
        pieces += [xor_permute(piece, "col", high) for piece in pieces[:4]]
    return [[piece] for piece in pieces]


def swap_cores(both):
    pairs = [[i, i + 1] for i in range(0, lax.axis_size("row"), 2)]
    return lax.all_to_all(both, "row", 0, 0, axis_index_groups=pairs)


def fence(*values):
    return lax.optimization_barrier(values)


def add_f32(a, b):
    return a.astype(jnp.float32) + b.astype(jnp.float32)


def stage_sums(keep, recv, n_blocks, rows, at_once=False):
    width = keep.shape[1]
    cut = (n_blocks // 2, 2, 2, rows, width)
    flat = (2, n_blocks // 2, 2, rows, width)
    sums = add_f32(keep, recv).astype(jnp.bfloat16)
    if at_once:
        (sums,) = fence(sums)

    def summed(shape, pick):
        if at_once:
            return pick(sums.reshape(shape)).reshape(-1, width)
        both = add_f32(pick(keep.reshape(shape)), pick(recv.reshape(shape)))
        return both.astype(jnp.bfloat16).reshape(-1, width)

    stage = [
        summed(cut, lambda v: v[:, 1, 0]),
        summed(cut, lambda v: v[:, 0, 0]),
        summed(flat, lambda v: v[1, :, 1]),
        summed(flat, lambda v: v[0, :, 1]),
    ]
    return stage, sums


def halve(value, upper, rows):
    blocks = value.shape[0] // rows
    shape = (2, blocks // 2) if upper else (blocks // 2, 2)
    cut = value.reshape(shape + (rows, value.shape[1]))
    if upper:
        sent, kept = cut[1], cut[0]
    else:
        sent, kept = cut[:, 1], cut[:, 0]
    return sent.reshape(-1, value.shape[1]), kept.reshape(-1, value.shape[1])


def exchange_first(stage, bits):
    return xor_permute(stage[0], "row", bits[0]), xor_permute(stage[2], "row", bits[-1])


def exchange_second(stage, recv, bits, rows):
    sent, kept = [], []
    for upper in (0, 1):
        value = add_f32(stage[2 * upper + 1], recv[upper]).astype(jnp.bfloat16)
        sent_u, kept_u = halve(value, upper, rows)
        sent.append(sent_u)
        kept.append(kept_u)
    return kept, sent


def send_second(sent, bits):
    return [xor_permute(s, "row", bit) for s, bit in zip(sent, (bits[1], bits[-2]))]


def exchange_last(kept, recv, bits, rows):
    done = []
    for upper in (0, 1):
        value = add_f32(kept[upper], recv[upper])
        for bit in (bits[::-1] if upper else bits)[2:]:
            sent_u, kept_u = halve(value.astype(jnp.bfloat16), upper, rows)
            value = add_f32(kept_u, xor_permute(sent_u, "row", bit))
        done.append(value.astype(jnp.bfloat16))
    return jnp.concatenate(done, axis=0)


def weight_term(near, sums):
    terms, at = [], 0
    for f in [part for parts in near for part in parts]:
        own = sums[at : at + f.shape[0]]
        terms.append(lax.dot_general(f, own, (((0,), (0,)), ((), ())), preferred_element_type=jnp.float32))
        at += f.shape[0]
    return sum(terms[1:], terms[0]).astype(jnp.bfloat16)


def term_kernel(*refs):
    *parts, sums_ref, out_ref, acc_ref = refs
    acc_ref[...] = jnp.zeros_like(acc_ref)
    first = 0
    for part in parts:

        def add_rows(step, carry, part=part, first=first):
            at = pl.multiple_of(step * TERM_ROWS, TERM_ROWS)
            acc_ref[...] += lax.dot_general(
                sums_ref[pl.ds(first + at, TERM_ROWS), :], part[pl.ds(at, TERM_ROWS), :],
                (((0,), (0,)), ((), ())), preferred_element_type=jnp.float32,
            )
            return carry

        lax.fori_loop(0, part.shape[0] // TERM_ROWS, add_rows, 0)
        first += part.shape[0]
    out_ref[...] = acc_ref[...].T.astype(out_ref.dtype)


def weight_term_early(near, sums):
    parts = [part for group in near for part in group]
    shape = (parts[0].shape[1], sums.shape[1])
    return pl.pallas_call(
        term_kernel,
        out_shape=jax.ShapeDtypeStruct(shape, jnp.bfloat16),
        in_specs=[pl.BlockSpec(memory_space=pltpu.VMEM)] * (len(parts) + 1),
        out_specs=pl.BlockSpec(memory_space=pltpu.VMEM),
        scratch_shapes=[pltpu.VMEM(shape[::-1], jnp.float32)],
        compiler_params=pltpu.CompilerParams(vmem_limit_bytes=TERM_BYTES),
        cost_estimate=pl.CostEstimate(flops=0, bytes_accessed=4096, transcendentals=0),
        name="weight_term",
    )(*parts, sums)


def sum_over(term, axis, masks):
    parts = [term] + [xor_permute(term, axis, m) for m in masks]
    return tree_sum([p.astype(jnp.float32) for p in parts])


def body(grad_out, preact, features, weight, tiles, tile_rows, tile_cols, live_counts):
    nodes, width = grad_out.shape
    n_row, n_col = lax.axis_size("row"), lax.axis_size("col")
    row, col = lax.axis_index("row"), lax.axis_index("col")
    slots = tiles.shape[2]
    cw = width // 2
    rows = nodes // 2
    bits = [1 << b for b in range(1, n_row.bit_length() - 1)]
    mid = ((col & 3) == 1) | ((col & 3) == 2)

    own0, own1 = [
        jnp.where(preact[:, cut] > 0, grad_out[:, cut], jnp.zeros_like(grad_out[:, cut]))
        for cut in (slice(0, cw), slice(cw, width))
    ]
    first0 = gather_first(own0)
    place = jnp.stack([live_counts.reshape(()), row, col, mid.astype(jnp.int32)])
    plan0, plan1, slot = make_plans(tile_rows, tile_cols, place, n_row, nodes // SIDE)
    flipped = flip_tiles(slot, tiles.reshape(slots, SIDE, SIDE))
    features, plan0 = fence(features, plan0)
    near = [[features]]
    for bit in bits[:2]:
        near.append([xor_permute(features, "row", bit)])
    own0, own1, first0, plan0, plan1, flipped = fence(own0, own1, first0, plan0, plan1, flipped)

    second0 = gather_second(own0, first0[1], n_col)
    acc0 = spmm(plan0, [[own0], [first0[0]], [first0[1]]], flipped, None, n_row)
    own1, acc0 = fence(own1, acc0)
    first1 = gather_first(own1)
    pieces0 = as_pieces(own0, first0, second0, mid, n_col)
    pieces0, near, acc0 = fence(pieces0, near, acc0)

    near.append([xor_permute(near[1][0][:rows], "row", bits[1]), xor_permute(near[2][0][rows:], "row", bits[0])])
    for bit in bits[2:]:
        near += [[xor_permute(f, "row", bit) for f in parts] for parts in near]
    (both0,) = spmm(plan1, pieces0[FIRST_PIECES:], flipped, acc0, n_row, by_core=True)
    got0 = swap_cores(both0)
    got0, near = fence(got0, near)
    stage0, sums0 = stage_sums(got0[0], got0[1], n_row // 2, rows, at_once=True)
    recv0 = exchange_first(stage0, bits)
    term0 = weight_term_early(near, sums0)
    own1, first1, stage0, term0 = fence(own1, first1, stage0, term0)

    second1 = gather_second(own1, first1[1], n_col)
    pieces1 = as_pieces(own1, first1, second1, mid, n_col)
    acc1 = spmm(plan0, pieces1[:FIRST_PIECES], flipped, None, n_row)
    acc1, recv0 = fence(acc1, recv0)
    rest0, sent0 = exchange_second(stage0, recv0, bits, rows)
    pieces1, acc1, rest0, sent0 = fence(pieces1, acc1, rest0, sent0)

    send1, keep1 = spmm(plan1, pieces1[FIRST_PIECES:], flipped, acc1, n_row)
    send1, keep1, rest0, sent0 = fence(send1, keep1, rest0, sent0)

    stage1, sums1 = stage_sums(keep1, xor_permute(send1, "row", 1), n_row // 2, rows, at_once=True)
    recv0 = send_second(sent0, bits)
    term1 = weight_term(near, sums1)
    stage1, term0, term1 = fence(stage1, term0, term1)
    stage1, term0, term1, rest0, recv0 = fence(stage1, term0, term1, rest0, recv0)

    recv1 = exchange_first(stage1, bits)
    even = (row & 1) == 0
    theirs, mine = jnp.where(even, term1, term0), jnp.where(even, term0, term1)
    mine = add_f32(mine, xor_permute(theirs, "row", 1)).astype(jnp.bfloat16)
    mine = sum_over(mine, "col", range(1, n_col)).astype(jnp.bfloat16)
    colgrad0 = exchange_last(rest0, recv0, bits, rows)
    recv1, mine, colgrad0 = fence(recv1, mine, colgrad0)

    rest1, sent1 = exchange_second(stage1, recv1, bits, rows)
    rest1, sent1, mine = fence(rest1, sent1, mine)
    recv1 = send_second(sent1, bits)
    others = [xor_permute(mine, "row", m) for m in range(2, n_row, 2)]
    colgrad1 = exchange_last(rest1, recv1, bits, rows)
    colgrad1, mine = fence(colgrad1, mine)
    mine = tree_sum([p.astype(jnp.float32) for p in [mine] + others]).astype(jnp.bfloat16)

    theirs = xor_permute(mine, "row", 1)
    low, high = jnp.where(even, mine, theirs), jnp.where(even, theirs, mine)
    grad_weight = jnp.concatenate([low, high], axis=1).astype(jnp.float32)
    colgrad = jnp.concatenate([colgrad0, colgrad1], axis=1)
    grad_features = lax.dot_general(
        colgrad, weight, (((1,), (1,)), ((), ())), preferred_element_type=jnp.float32
    ).astype(jnp.bfloat16)
    return (grad_features, grad_weight)


def solution(mesh):
    in_specs = (
        P(("row", "col"), None),
        P(("row", "col"), None),
        P(("col", "row"), None),
        P(),
        P("row", "col", None, None, None),
        P("row", "col", None),
        P("row", "col", None),
        P("row", "col"),
    )
    out_specs = (P(("col", "row"), None), P())
    return jax.shard_map(body, mesh=mesh, in_specs=in_specs, out_specs=out_specs, check_vma=False)
```

```python
import functools

import jax
import jax.numpy as jnp
from jax import lax
from jax.experimental import pallas as pl
from jax.experimental.pallas import tpu as pltpu
from jax.sharding import PartitionSpec as P

SIDE = 128
UNROLL = 8
GROUP = 32
RING = 4
FIRST_PIECES = 3
PLAN_ROWS = 8
FLIP_BYTES = 26 * 1024 * 1024
PLAN_BYTES = 12 * 1024 * 1024
TERM_BYTES = 14 * 1024 * 1024
TERM_ROWS = 512
SPMM_BYTES = 16 * 1024 * 1024


def round_up(value, unit):
    return -(-value // unit) * unit


def total(mask, axis):
    return jnp.sum(jnp.where(mask, 1.0, 0.0), axis=axis, keepdims=True).astype(jnp.int32)


def total_of(values, axis):
    return jnp.sum(values.astype(jnp.float32), axis=axis, keepdims=True).astype(jnp.int32)


def plan_kernel(per_dev, n_out, place_ref, rows_r, cols_r, rows_c, cols_c, plan0_ref, plan1_ref, slot_ref):
    slots = rows_r.shape[1]
    size = plan0_ref.shape[1]
    count, row, col, mid = place_ref[0], place_ref[1], place_ref[2], place_ref[3]
    shift = per_dev.bit_length() - 1
    start = FIRST_PIECES * per_dev
    step = 2 * UNROLL

    def attributes(rows, cols, axis):
        ids = lax.broadcasted_iota(jnp.int32, rows.shape, axis)
        row_pos = (((rows >> shift) ^ col) << shift) + (rows & (per_dev - 1))
        away = (cols >> shift) ^ row
        out_pos = ((away >> 1) << shift) + (cols & (per_dev - 1))
        kept = 1 - (away & 1)
        last = (row_pos >= start).astype(jnp.int32)
        live = ids < count
        key = jnp.where(live, (2 * last + kept) * n_out + out_pos, 4 * n_out)
        return ids, row_pos, out_pos, 2 * last + kept, live, key

    ids_r, _, _, part_r, live_r, key_r = attributes(rows_r[...], cols_r[...], 1)
    ids_c, row_pos_c, out_pos_c, part_c, live_c, key_c = attributes(rows_c[...], cols_c[...], 0)
    equal = key_c == key_r
    below = key_r < key_c
    earlier_c = total(equal & (ids_r < ids_c), 1)
    earlier_r = total(equal & (ids_c < ids_r), 0)
    later_r = total(equal & (ids_c > ids_r), 0)
    odd_end = (later_r == 0) & ((earlier_r & 1) == 0)
    weight_r = jnp.where(live_r, jnp.where(odd_end, 2, 1), 0)
    rank_c = total(below, 1) + earlier_c
    rank_r = total(key_c < key_r, 0) + earlier_r
    padded_c = total_of(jnp.where(below, weight_r, 0), 1) + earlier_c
    length = [total_of(jnp.where(part_r == p, weight_r, 0), 1) for p in range(4)]
    n_first = total(live_r & (part_r < 2), 1)
    n_last = count - n_first
    last_base = ((n_first + GROUP - 1) >> 5) << 5
    slot_r = jnp.where(part_r >= 2, last_base + rank_r - n_first, rank_r)
    slot_ref[...] = jnp.where(live_r, slot_r, slots + GROUP)

    lane = lax.broadcasted_iota(jnp.int32, (1, size), 1)
    for p, plan_ref in enumerate((plan0_ref, plan1_ref)):
        sent, held = length[2 * p], length[2 * p + 1]
        sent_steps = (sent + step - 1) >> (step.bit_length() - 1)
        all_steps = sent_steps + ((held + step - 1) >> (step.bit_length() - 1))
        base = length[0] + length[1] if p else jnp.zeros_like(sent)
        in_plan = live_c & ((part_c >> 1) == p)
        pos = padded_c - base + jnp.where((part_c & 1) == 1, sent_steps * step - sent, 0)
        pos = jnp.where(in_plan, pos, -1)
        rank = rank_c - (n_first if p else 0)
        hit = pos == lane

        def placed(values, empty, hit=hit):
            return total_of(jnp.where(hit, values - empty, 0), 0) + empty

        plan_ref[0:1, :] = placed(rank & (RING * GROUP - 1), RING * GROUP)
        plan_ref[1:2, :] = placed(row_pos_c - p * start, 0)
        taken = total(hit, 0) > 0
        ends = [
            jnp.max(jnp.where(in_plan & ((part_c & 1) == h), out_pos_c, 0).astype(jnp.float32), axis=0, keepdims=True)
            for h in range(2)
        ]
        end = jnp.where(lane < sent_steps * step, ends[0], ends[1]).astype(jnp.int32)
        plan_ref[2:3, :] = jnp.where(taken, placed(out_pos_c, 0), end)
        plan_ref[3:4, :] = jnp.where(taken, placed((earlier_c > 0).astype(jnp.int32), 0), 1)
        done = total(in_plan & (pos < (lane + 1) * step), 0)
        tiles = n_last if p else n_first
        info = [
            jnp.full((1, 1), mid, jnp.int32),
            sent_steps,
            (tiles + GROUP - 1) >> 5,
            last_base if p else jnp.zeros_like(last_base),
            jnp.zeros_like(last_base),
        ]
        for g in range(slots // GROUP):
            info.append(total((done <= (g + 1) * GROUP) & (lane < all_steps), 1))
        row_values = jnp.zeros((1, size), jnp.int32)
        for n, value in enumerate(info):
            row_values = jnp.where(lane == n, value, row_values)
        plan_ref[4:5, :] = row_values
        plan_ref[5:6, :] = jnp.full((1, size), row & 1, jnp.int32)
        plan_ref[6:8, :] = jnp.zeros((2, size), jnp.int32)


def make_plans(tile_rows, tile_cols, place, n_row, per_dev):
    slots = tile_rows.size
    n_out = n_row // 2 * per_dev
    size = round_up(slots + 2 * n_out + 4 * UNROLL, SIDE)
    plan = jax.ShapeDtypeStruct((PLAN_ROWS, size), jnp.int32)
    return pl.pallas_call(
        functools.partial(plan_kernel, per_dev, n_out),
        out_shape=(plan, plan, jax.ShapeDtypeStruct((1, slots), jnp.int32)),
        in_specs=[pl.BlockSpec(memory_space=pltpu.SMEM)] + [pl.BlockSpec(memory_space=pltpu.VMEM)] * 4,
        out_specs=[pl.BlockSpec(memory_space=pltpu.VMEM)] * 3,
        compiler_params=pltpu.CompilerParams(vmem_limit_bytes=PLAN_BYTES),
        cost_estimate=pl.CostEstimate(flops=0, bytes_accessed=4096, transcendentals=0),
        name="plan_slots",
    )(place, tile_rows.reshape(1, slots), tile_cols.reshape(1, slots), tile_rows.reshape(slots, 1), tile_cols.reshape(slots, 1))


def flip_kernel(slot_ref, tiles_ref, out_ref, t_in, t_out, in_sem, out_sem):
    slots = t_in.shape[0]
    groups = slots // GROUP
    loads = [
        pltpu.make_async_copy(tiles_ref.at[pl.ds(g * GROUP, GROUP)], t_in.at[pl.ds(g * GROUP, GROUP)], in_sem.at[g])
        for g in range(groups)
    ]
    for load in loads:
        load.start()
    for g in range(groups):
        loads[g].wait()

        def some(step, carry, g=g):
            for u in range(4):
                k = g * GROUP + step * 4 + u
                t_out[slot_ref[0, k]] = t_in[k].T
            return carry

        lax.fori_loop(0, GROUP // 4, some, 0)
    stores = [
        pltpu.make_async_copy(t_out.at[pl.ds(g * GROUP, GROUP)], out_ref.at[pl.ds(g * GROUP, GROUP)], out_sem.at[g])
        for g in range(groups + 1)
    ]
    for store in stores:
        store.start()
    for store in stores:
        store.wait()


def flip_tiles(slot, tile_stack):
    slots = tile_stack.shape[0]
    groups = slots // GROUP
    return pl.pallas_call(
        flip_kernel,
        out_shape=jax.ShapeDtypeStruct((slots + GROUP, SIDE, SIDE), tile_stack.dtype),
        grid_spec=pltpu.PrefetchScalarGridSpec(
            num_scalar_prefetch=1,
            grid=(),
            in_specs=[pl.BlockSpec(memory_space=pl.ANY)],
            out_specs=pl.BlockSpec(memory_space=pl.ANY),
            scratch_shapes=[
                pltpu.VMEM(tile_stack.shape, tile_stack.dtype),
                pltpu.VMEM((slots + GROUP + 1, SIDE, SIDE), tile_stack.dtype),
                pltpu.SemaphoreType.DMA((groups,)),
                pltpu.SemaphoreType.DMA((groups + 1,)),
            ],
        ),
        compiler_params=pltpu.CompilerParams(vmem_limit_bytes=FLIP_BYTES),
        cost_estimate=pl.CostEstimate(flops=0, bytes_accessed=4096, transcendentals=0),
        name="flip_tiles",
    )(slot, tile_stack)


def spmm_kernel(layout, last, by_core, plan_ref, *refs):
    n_refs = sum(layout)
    refs_left = list(refs[:n_refs])
    pieces = [[refs_left.pop(0) for _ in range(n)] for n in layout]
    rest = list(refs[n_refs:])
    tiles_ref = rest.pop(0)
    acc_refs = (rest.pop(0), rest.pop(0)) if last else (None, None)
    if by_core:
        core = plan_ref[5, 0]
        out_ref = rest.pop(0)
        out_refs = (out_ref.at[1 - core], out_ref.at[core])
    else:
        out_refs = (rest.pop(0), rest.pop(0))
    m_vmem, t_vmem, total_ref, sems = rest
    nodes, width = pieces[0][0].shape
    mid, sent_steps, n_groups, tile_base = [plan_ref[4, n] for n in range(4)]

    def group_copy(g):
        place = g & (RING - 1)
        return pltpu.make_async_copy(
            tiles_ref.at[pl.ds(tile_base + pl.multiple_of(g * GROUP, GROUP), GROUP)],
            t_vmem.at[pl.ds(pl.multiple_of(place * GROUP, GROUP), GROUP)],
            sems.at[place],
        )

    for g in range(2):
        pl.when(g < n_groups)(group_copy(g).start)
    t_vmem[RING * GROUP] = jnp.zeros((SIDE, SIDE), t_vmem.dtype)
    for out_ref, acc_ref in zip(out_refs, acc_refs):

        def begin(step, carry, out_ref=out_ref, acc_ref=acc_ref):
            at = pl.ds(pl.multiple_of(step * 256, 256), 256)
            out_ref[at, :] = acc_ref[at, :] if last else jnp.zeros((256, width), out_ref.dtype)
            return carry

        lax.fori_loop(0, out_ref.shape[0] // 256, begin, 0)
    for p, options in enumerate(pieces):

        def take(ref, p=p):
            def some(step, carry):
                at = pl.multiple_of(step * 512, 512)
                m_vmem[pl.ds(pl.multiple_of(p * nodes + at, 512), 512), :] = ref[pl.ds(at, 512), :]
                return carry

            lax.fori_loop(0, nodes // 512, some, 0)

        if len(options) == 1:
            take(options[0])
        else:
            pl.when(mid == 1)(functools.partial(take, options[0]))
            pl.when(mid != 1)(functools.partial(take, options[1]))

    def block(index):
        return m_vmem[pl.ds(pl.multiple_of(index * SIDE, SIDE), SIDE), :]

    def add_pairs(out_ref, acc_ref, step, carry):
        running = total_ref[...]
        prods = []
        for u in range(UNROLL):
            k = 2 * (step * UNROLL + u)
            left = jnp.concatenate([t_vmem[plan_ref[0, k]], t_vmem[plan_ref[0, k + 1]]], axis=1)
            right = jnp.concatenate([block(plan_ref[1, k]), block(plan_ref[1, k + 1])], axis=0)
            prods.append(jnp.dot(left, right, preferred_element_type=jnp.float32))
        for u in range(UNROLL):
            k = 2 * (step * UNROLL + u)
            at = pl.ds(pl.multiple_of(plan_ref[2, k] * SIDE, SIDE), SIDE)
            before = acc_ref[at, :].astype(jnp.float32) if last else jnp.zeros_like(running)
            running = prods[u] + jnp.where(plan_ref[3, k] == 1, running, before)
            out_ref[at, :] = running.astype(out_ref.dtype)
        total_ref[...] = running
        return carry

    total_ref[...] = jnp.zeros_like(total_ref)

    def add_group(g, carry):
        group_copy(g).wait()

        @pl.when(g + 2 < n_groups)
        def _():
            group_copy(g + 2).start()

        low, high = plan_ref[4, 4 + g], plan_ref[4, 5 + g]
        lax.fori_loop(
            jnp.minimum(low, sent_steps), jnp.minimum(high, sent_steps),
            functools.partial(add_pairs, out_refs[0], acc_refs[0]), 0,
        )
        lax.fori_loop(
            jnp.maximum(low, sent_steps), jnp.maximum(high, sent_steps),
            functools.partial(add_pairs, out_refs[1], acc_refs[1]), 0,
        )
        return carry

    lax.fori_loop(0, n_groups, add_group, 0)


def spmm(plan, pieces, tiles, acc, n_row, by_core=False):
    nodes, width = pieces[0][0].shape
    half = n_row // 2 * nodes
    last = acc is not None
    out = jax.ShapeDtypeStruct((2, half, width) if by_core else (half, width), jnp.bfloat16)
    blocks = [ref for p in pieces for ref in p]
    in_vmem, in_any = pl.BlockSpec(memory_space=pltpu.VMEM), pl.BlockSpec(memory_space=pl.ANY)
    return pl.pallas_call(
        functools.partial(spmm_kernel, [len(p) for p in pieces], last, by_core),
        out_shape=(out,) if by_core else (out, out),
        grid_spec=pltpu.PrefetchScalarGridSpec(
            num_scalar_prefetch=1,
            grid=(),
            in_specs=[in_vmem] * len(blocks) + [in_any] + [in_vmem] * len(acc or []),
            out_specs=[in_vmem] * (1 if by_core else 2),
            scratch_shapes=[
                pltpu.VMEM((len(pieces) * nodes, width), jnp.bfloat16),
                pltpu.VMEM((RING * GROUP + 1, SIDE, SIDE), jnp.bfloat16),
                pltpu.VMEM((SIDE, width), jnp.float32),
                pltpu.SemaphoreType.DMA((RING,)),
            ],
        ),
        compiler_params=pltpu.CompilerParams(vmem_limit_bytes=SPMM_BYTES),
        cost_estimate=pl.CostEstimate(flops=0, bytes_accessed=4096, transcendentals=0),
        name="spmm_last" if last else "spmm_first",
    )(plan, *blocks, tiles, *(acc or []))


def xor_permute(value, axis, mask):
    size = lax.axis_size(axis)
    return lax.ppermute(value, axis, [(i, i ^ mask) for i in range(size)])


def tree_sum(values):
    while len(values) > 1:
        values = [a + b for a, b in zip(values[::2], values[1::2])]
    return values[0]


def gather_first(own):
    return xor_permute(own, "col", 1), xor_permute(own, "col", 2)


def gather_second(own, by_two, n_col):
    ends, middles = [], []
    for low in range(0, n_col, 4):
        ends += [(low + 1, low), (low + 2, low + 3)]
        middles += [(low + 1, low + 2), (low + 2, low + 1)]
    return lax.ppermute(own, "col", middles), lax.ppermute(by_two, "col", ends)


def as_pieces(own, first, second, mid, n_col):
    if n_col == 4:
        return [[own], [first[0]], [first[1]], list(second)]
    pieces = [own, first[0], first[1], jnp.where(mid, second[0], second[1])]
    for high in range(4, n_col, 4):
        pieces += [xor_permute(piece, "col", high) for piece in pieces[:4]]
    return [[piece] for piece in pieces]


def swap_cores(both):
    pairs = [[i, i + 1] for i in range(0, lax.axis_size("row"), 2)]
    return lax.all_to_all(both, "row", 0, 0, axis_index_groups=pairs)


def fence(*values):
    return lax.optimization_barrier(values)


def add_f32(a, b):
    return a.astype(jnp.float32) + b.astype(jnp.float32)


def stage_sums(keep, recv, n_blocks, rows, at_once=False):
    width = keep.shape[1]
    cut = (n_blocks // 2, 2, 2, rows, width)
    flat = (2, n_blocks // 2, 2, rows, width)
    sums = add_f32(keep, recv).astype(jnp.bfloat16)
    if at_once:
        (sums,) = fence(sums)

    def summed(shape, pick):
        if at_once:
            return pick(sums.reshape(shape)).reshape(-1, width)
        both = add_f32(pick(keep.reshape(shape)), pick(recv.reshape(shape)))
        return both.astype(jnp.bfloat16).reshape(-1, width)

    stage = [
        summed(cut, lambda v: v[:, 1, 0]),
        summed(cut, lambda v: v[:, 0, 0]),
        summed(flat, lambda v: v[1, :, 1]),
        summed(flat, lambda v: v[0, :, 1]),
    ]
    return stage, sums


def halve(value, upper, rows):
    blocks = value.shape[0] // rows
    shape = (2, blocks // 2) if upper else (blocks // 2, 2)
    cut = value.reshape(shape + (rows, value.shape[1]))
    if upper:
        sent, kept = cut[1], cut[0]
    else:
        sent, kept = cut[:, 1], cut[:, 0]
    return sent.reshape(-1, value.shape[1]), kept.reshape(-1, value.shape[1])


def exchange_first(stage, bits):
    return xor_permute(stage[0], "row", bits[0]), xor_permute(stage[2], "row", bits[-1])


def exchange_second(stage, recv, bits, rows):
    sent, kept = [], []
    for upper in (0, 1):
        value = add_f32(stage[2 * upper + 1], recv[upper]).astype(jnp.bfloat16)
        sent_u, kept_u = halve(value, upper, rows)
        sent.append(sent_u)
        kept.append(kept_u)
    return kept, sent


def send_second(sent, bits):
    return [xor_permute(s, "row", bit) for s, bit in zip(sent, (bits[1], bits[-2]))]


def exchange_last(kept, recv, bits, rows):
    done = []
    for upper in (0, 1):
        value = add_f32(kept[upper], recv[upper])
        for bit in (bits[::-1] if upper else bits)[2:]:
            sent_u, kept_u = halve(value.astype(jnp.bfloat16), upper, rows)
            value = add_f32(kept_u, xor_permute(sent_u, "row", bit))
        done.append(value.astype(jnp.bfloat16))
    return jnp.concatenate(done, axis=0)


def term_kernel(*refs):
    *parts, sums_ref, out_ref, acc_ref = refs
    acc_ref[...] = jnp.zeros_like(acc_ref)
    first = 0
    for part in parts:

        def add_rows(step, carry, part=part, first=first):
            at = pl.multiple_of(step * TERM_ROWS, TERM_ROWS)
            acc_ref[...] += lax.dot_general(
                sums_ref[pl.ds(first + at, TERM_ROWS), :], part[pl.ds(at, TERM_ROWS), :],
                (((0,), (0,)), ((), ())), preferred_element_type=jnp.float32,
            )
            return carry

        lax.fori_loop(0, part.shape[0] // TERM_ROWS, add_rows, 0)
        first += part.shape[0]
    out_ref[...] = acc_ref[...].T.astype(out_ref.dtype)


def weight_term(near, sums):
    parts = [part for group in near for part in group]
    shape = (parts[0].shape[1], sums.shape[1])
    return pl.pallas_call(
        term_kernel,
        out_shape=jax.ShapeDtypeStruct(shape, jnp.bfloat16),
        in_specs=[pl.BlockSpec(memory_space=pltpu.VMEM)] * (len(parts) + 1),
        out_specs=pl.BlockSpec(memory_space=pltpu.VMEM),
        scratch_shapes=[pltpu.VMEM(shape[::-1], jnp.float32)],
        compiler_params=pltpu.CompilerParams(vmem_limit_bytes=TERM_BYTES),
        cost_estimate=pl.CostEstimate(flops=0, bytes_accessed=4096, transcendentals=0),
        name="weight_term",
    )(*parts, sums)


def sum_over(term, axis, masks):
    parts = [term] + [xor_permute(term, axis, m) for m in masks]
    return tree_sum([p.astype(jnp.float32) for p in parts])


def body(grad_out, preact, features, weight, tiles, tile_rows, tile_cols, live_counts):
    nodes, width = grad_out.shape
    n_row, n_col = lax.axis_size("row"), lax.axis_size("col")
    row, col = lax.axis_index("row"), lax.axis_index("col")
    slots = tiles.shape[2]
    cw = width // 2
    rows = nodes // 2
    bits = [1 << b for b in range(1, n_row.bit_length() - 1)]
    mid = ((col & 3) == 1) | ((col & 3) == 2)

    def masked(preact, grad_out, cut):
        return jnp.where(preact[:, cut] > 0, grad_out[:, cut], jnp.zeros_like(grad_out[:, cut]))

    own0 = masked(preact, grad_out, slice(0, cw))
    own0, preact, grad_out = fence(own0, preact, grad_out)
    own1 = masked(preact, grad_out, slice(cw, width))
    first0 = gather_first(own0)
    place = jnp.stack([live_counts.reshape(()), row, col, mid.astype(jnp.int32)])
    plan0, plan1, slot = make_plans(tile_rows, tile_cols, place, n_row, nodes // SIDE)
    flipped = flip_tiles(slot, tiles.reshape(slots, SIDE, SIDE))
    features, plan0 = fence(features, plan0)
    near = [[features]]
    for bit in bits[:2]:
        near.append([xor_permute(features, "row", bit)])
    own0, own1, first0, plan0, plan1, flipped = fence(own0, own1, first0, plan0, plan1, flipped)

    second0 = gather_second(own0, first0[1], n_col)
    acc0 = spmm(plan0, [[own0], [first0[0]], [first0[1]]], flipped, None, n_row)
    own1, acc0 = fence(own1, acc0)
    first1 = gather_first(own1)
    pieces0 = as_pieces(own0, first0, second0, mid, n_col)
    pieces0, near, acc0 = fence(pieces0, near, acc0)

    near.append([xor_permute(near[1][0][:rows], "row", bits[1]), xor_permute(near[2][0][rows:], "row", bits[0])])
    for bit in bits[2:]:
        near += [[xor_permute(f, "row", bit) for f in parts] for parts in near]
    (both0,) = spmm(plan1, pieces0[FIRST_PIECES:], flipped, acc0, n_row, by_core=True)
    got0 = swap_cores(both0)
    got0, near = fence(got0, near)
    stage0, sums0 = stage_sums(got0[0], got0[1], n_row // 2, rows, at_once=True)
    recv0 = exchange_first(stage0, bits)
    term0 = weight_term(near, sums0)
    own1, first1, stage0, term0 = fence(own1, first1, stage0, term0)

    second1 = gather_second(own1, first1[1], n_col)
    pieces1 = as_pieces(own1, first1, second1, mid, n_col)
    acc1 = spmm(plan0, pieces1[:FIRST_PIECES], flipped, None, n_row)
    acc1, recv0 = fence(acc1, recv0)
    rest0, sent0 = exchange_second(stage0, recv0, bits, rows)
    pieces1, acc1, rest0, sent0 = fence(pieces1, acc1, rest0, sent0)

    send1, keep1 = spmm(plan1, pieces1[FIRST_PIECES:], flipped, acc1, n_row)
    send1, keep1, rest0, sent0 = fence(send1, keep1, rest0, sent0)

    stage1, sums1 = stage_sums(keep1, xor_permute(send1, "row", 1), n_row // 2, rows, at_once=True)
    recv0 = send_second(sent0, bits)
    term1 = weight_term(near, sums1)
    stage1, term0, term1 = fence(stage1, term0, term1)
    stage1, term0, term1, rest0, recv0 = fence(stage1, term0, term1, rest0, recv0)

    recv1 = exchange_first(stage1, bits)
    even = (row & 1) == 0
    theirs, mine = jnp.where(even, term1, term0), jnp.where(even, term0, term1)
    mine = add_f32(mine, xor_permute(theirs, "row", 1)).astype(jnp.bfloat16)
    mine = sum_over(mine, "col", range(1, n_col)).astype(jnp.bfloat16)
    colgrad0 = exchange_last(rest0, recv0, bits, rows)
    recv1, mine, colgrad0 = fence(recv1, mine, colgrad0)

    rest1, sent1 = exchange_second(stage1, recv1, bits, rows)
    rest1, sent1, mine = fence(rest1, sent1, mine)
    recv1 = send_second(sent1, bits)
    others = [xor_permute(mine, "row", m) for m in range(2, n_row, 2)]
    colgrad1 = exchange_last(rest1, recv1, bits, rows)
    colgrad1, mine = fence(colgrad1, mine)
    mine = tree_sum([p.astype(jnp.float32) for p in [mine] + others]).astype(jnp.bfloat16)

    theirs = xor_permute(mine, "row", 1)
    low, high = jnp.where(even, mine, theirs), jnp.where(even, theirs, mine)
    grad_weight = jnp.concatenate([low, high], axis=1).astype(jnp.float32)
    colgrad = jnp.concatenate([colgrad0, colgrad1], axis=1)
    grad_features = lax.dot_general(
        colgrad, weight, (((1,), (1,)), ((), ())), preferred_element_type=jnp.float32
    ).astype(jnp.bfloat16)
    return (grad_features, grad_weight)


def solution(mesh):
    in_specs = (
        P(("row", "col"), None),
        P(("row", "col"), None),
        P(("col", "row"), None),
        P(),
        P("row", "col", None, None, None),
        P("row", "col", None),
        P("row", "col", None),
        P("row", "col"),
    )
    out_specs = (P(("col", "row"), None), P())
    return jax.shard_map(body, mesh=mesh, in_specs=in_specs, out_specs=out_specs, check_vma=False)
```

```python
import functools

import jax
import jax.numpy as jnp
from jax import lax
from jax.experimental import pallas as pl
from jax.experimental.pallas import tpu as pltpu
from jax.sharding import PartitionSpec as P

SIDE = 128
UNROLL = 8
GROUP = 32
RING = 4
FIRST_PIECES = 3
PLAN_ROWS = 8
FLIP_BYTES = 26 * 1024 * 1024
PLAN_BYTES = 12 * 1024 * 1024
TERM_BYTES = 14 * 1024 * 1024
TERM_ROWS = 512
SPMM_BYTES = 16 * 1024 * 1024


def round_up(value, unit):
    return -(-value // unit) * unit


def total(mask, axis):
    return jnp.sum(jnp.where(mask, 1.0, 0.0), axis=axis, keepdims=True).astype(jnp.int32)


def total_of(values, axis):
    return jnp.sum(values.astype(jnp.float32), axis=axis, keepdims=True).astype(jnp.int32)


def plan_kernel(per_dev, n_out, place_ref, rows_r, cols_r, rows_c, cols_c, plan0_ref, plan1_ref, slot_ref):
    slots = rows_r.shape[1]
    size = plan0_ref.shape[1]
    count, row, col, mid = place_ref[0], place_ref[1], place_ref[2], place_ref[3]
    shift = per_dev.bit_length() - 1
    start = FIRST_PIECES * per_dev
    step = 2 * UNROLL

    def attributes(rows, cols, axis):
        ids = lax.broadcasted_iota(jnp.int32, rows.shape, axis)
        row_pos = (((rows >> shift) ^ col) << shift) + (rows & (per_dev - 1))
        away = (cols >> shift) ^ row
        out_pos = ((away >> 1) << shift) + (cols & (per_dev - 1))
        kept = 1 - (away & 1)
        last = (row_pos >= start).astype(jnp.int32)
        live = ids < count
        key = jnp.where(live, (2 * last + kept) * n_out + out_pos, 4 * n_out)
        return ids, row_pos, out_pos, 2 * last + kept, live, key

    ids_r, _, _, part_r, live_r, key_r = attributes(rows_r[...], cols_r[...], 1)
    ids_c, row_pos_c, out_pos_c, part_c, live_c, key_c = attributes(rows_c[...], cols_c[...], 0)
    equal = key_c == key_r
    below = key_r < key_c
    earlier_c = total(equal & (ids_r < ids_c), 1)
    earlier_r = total(equal & (ids_c < ids_r), 0)
    later_r = total(equal & (ids_c > ids_r), 0)
    odd_end = (later_r == 0) & ((earlier_r & 1) == 0)
    weight_r = jnp.where(live_r, jnp.where(odd_end, 2, 1), 0)
    rank_c = total(below, 1) + earlier_c
    rank_r = total(key_c < key_r, 0) + earlier_r
    padded_c = total_of(jnp.where(below, weight_r, 0), 1) + earlier_c
    length = [total_of(jnp.where(part_r == p, weight_r, 0), 1) for p in range(4)]
    n_first = total(live_r & (part_r < 2), 1)
    n_last = count - n_first
    last_base = ((n_first + GROUP - 1) >> 5) << 5
    slot_r = jnp.where(part_r >= 2, last_base + rank_r - n_first, rank_r)
    slot_ref[...] = jnp.where(live_r, slot_r, slots + GROUP)

    lane = lax.broadcasted_iota(jnp.int32, (1, size), 1)
    for p, plan_ref in enumerate((plan0_ref, plan1_ref)):
        sent, held = length[2 * p], length[2 * p + 1]
        sent_steps = (sent + step - 1) >> (step.bit_length() - 1)
        all_steps = sent_steps + ((held + step - 1) >> (step.bit_length() - 1))
        base = length[0] + length[1] if p else jnp.zeros_like(sent)
        in_plan = live_c & ((part_c >> 1) == p)
        pos = padded_c - base + jnp.where((part_c & 1) == 1, sent_steps * step - sent, 0)
        pos = jnp.where(in_plan, pos, -1)
        rank = rank_c - (n_first if p else 0)
        hit = pos == lane

        def placed(values, empty, hit=hit):
            return total_of(jnp.where(hit, values - empty, 0), 0) + empty

        plan_ref[0:1, :] = placed(rank & (RING * GROUP - 1), RING * GROUP)
        plan_ref[1:2, :] = placed(row_pos_c - p * start, 0)
        taken = total(hit, 0) > 0
        ends = [
            jnp.max(jnp.where(in_plan & ((part_c & 1) == h), out_pos_c, 0).astype(jnp.float32), axis=0, keepdims=True)
            for h in range(2)
        ]
        end = jnp.where(lane < sent_steps * step, ends[0], ends[1]).astype(jnp.int32)
        plan_ref[2:3, :] = jnp.where(taken, placed(out_pos_c, 0), end)
        plan_ref[3:4, :] = jnp.where(taken, placed((earlier_c > 0).astype(jnp.int32), 0), 1)
        done = total(in_plan & (pos < (lane + 1) * step), 0)
        tiles = n_last if p else n_first
        info = [
            jnp.full((1, 1), mid, jnp.int32),
            sent_steps,
            (tiles + GROUP - 1) >> 5,
            last_base if p else jnp.zeros_like(last_base),
            jnp.zeros_like(last_base),
        ]
        for g in range(slots // GROUP):
            info.append(total((done <= (g + 1) * GROUP) & (lane < all_steps), 1))
        row_values = jnp.zeros((1, size), jnp.int32)
        for n, value in enumerate(info):
            row_values = jnp.where(lane == n, value, row_values)
        plan_ref[4:5, :] = row_values
        plan_ref[5:6, :] = jnp.full((1, size), row & 1, jnp.int32)
        plan_ref[6:8, :] = jnp.zeros((2, size), jnp.int32)


def make_plans(tile_rows, tile_cols, place, n_row, per_dev):
    slots = tile_rows.size
    n_out = n_row // 2 * per_dev
    size = round_up(slots + 2 * n_out + 4 * UNROLL, SIDE)
    plan = jax.ShapeDtypeStruct((PLAN_ROWS, size), jnp.int32)
    return pl.pallas_call(
        functools.partial(plan_kernel, per_dev, n_out),
        out_shape=(plan, plan, jax.ShapeDtypeStruct((1, slots), jnp.int32)),
        in_specs=[pl.BlockSpec(memory_space=pltpu.SMEM)] + [pl.BlockSpec(memory_space=pltpu.VMEM)] * 4,
        out_specs=[pl.BlockSpec(memory_space=pltpu.VMEM)] * 3,
        compiler_params=pltpu.CompilerParams(vmem_limit_bytes=PLAN_BYTES),
        cost_estimate=pl.CostEstimate(flops=0, bytes_accessed=4096, transcendentals=0),
        name="plan_slots",
    )(place, tile_rows.reshape(1, slots), tile_cols.reshape(1, slots), tile_rows.reshape(slots, 1), tile_cols.reshape(slots, 1))


def flip_kernel(slot_ref, tiles_ref, out_ref, t_in, t_out, in_sem, out_sem):
    slots = t_in.shape[0]
    groups = slots // GROUP
    loads = [
        pltpu.make_async_copy(tiles_ref.at[pl.ds(g * GROUP, GROUP)], t_in.at[pl.ds(g * GROUP, GROUP)], in_sem.at[g])
        for g in range(groups)
    ]
    for load in loads:
        load.start()
    for g in range(groups):
        loads[g].wait()

        def some(step, carry, g=g):
            for u in range(4):
                k = g * GROUP + step * 4 + u
                t_out[slot_ref[0, k]] = t_in[k].T
            return carry

        lax.fori_loop(0, GROUP // 4, some, 0)
    stores = [
        pltpu.make_async_copy(t_out.at[pl.ds(g * GROUP, GROUP)], out_ref.at[pl.ds(g * GROUP, GROUP)], out_sem.at[g])
        for g in range(groups + 1)
    ]
    for store in stores:
        store.start()
    for store in stores:
        store.wait()


def flip_tiles(slot, tile_stack):
    slots = tile_stack.shape[0]
    groups = slots // GROUP
    return pl.pallas_call(
        flip_kernel,
        out_shape=jax.ShapeDtypeStruct((slots + GROUP, SIDE, SIDE), tile_stack.dtype),
        grid_spec=pltpu.PrefetchScalarGridSpec(
            num_scalar_prefetch=1,
            grid=(),
            in_specs=[pl.BlockSpec(memory_space=pl.ANY)],
            out_specs=pl.BlockSpec(memory_space=pl.ANY),
            scratch_shapes=[
                pltpu.VMEM(tile_stack.shape, tile_stack.dtype),
                pltpu.VMEM((slots + GROUP + 1, SIDE, SIDE), tile_stack.dtype),
                pltpu.SemaphoreType.DMA((groups,)),
                pltpu.SemaphoreType.DMA((groups + 1,)),
            ],
        ),
        compiler_params=pltpu.CompilerParams(vmem_limit_bytes=FLIP_BYTES),
        cost_estimate=pl.CostEstimate(flops=0, bytes_accessed=4096, transcendentals=0),
        name="flip_tiles",
    )(slot, tile_stack)


def spmm_kernel(layout, last, by_core, plan_ref, *refs):
    n_refs = sum(layout)
    refs_left = list(refs[:n_refs])
    pieces = [[refs_left.pop(0) for _ in range(n)] for n in layout]
    rest = list(refs[n_refs:])
    tiles_ref = rest.pop(0)
    acc_refs = (rest.pop(0), rest.pop(0)) if last else (None, None)
    if by_core:
        core = plan_ref[5, 0]
        out_ref = rest.pop(0)
        out_refs = (out_ref.at[1 - core], out_ref.at[core])
    else:
        out_refs = (rest.pop(0), rest.pop(0))
    m_vmem, t_vmem, total_ref, sems = rest
    nodes, width = pieces[0][0].shape
    mid, sent_steps, n_groups, tile_base = [plan_ref[4, n] for n in range(4)]

    def group_copy(g):
        place = g & (RING - 1)
        return pltpu.make_async_copy(
            tiles_ref.at[pl.ds(tile_base + pl.multiple_of(g * GROUP, GROUP), GROUP)],
            t_vmem.at[pl.ds(pl.multiple_of(place * GROUP, GROUP), GROUP)],
            sems.at[place],
        )

    for g in range(2):
        pl.when(g < n_groups)(group_copy(g).start)
    t_vmem[RING * GROUP] = jnp.zeros((SIDE, SIDE), t_vmem.dtype)
    for out_ref, acc_ref in zip(out_refs, acc_refs):

        def begin(step, carry, out_ref=out_ref, acc_ref=acc_ref):
            at = pl.ds(pl.multiple_of(step * 256, 256), 256)
            out_ref[at, :] = acc_ref[at, :] if last else jnp.zeros((256, width), out_ref.dtype)
            return carry

        lax.fori_loop(0, out_ref.shape[0] // 256, begin, 0)
    for p, options in enumerate(pieces):

        def take(ref, p=p):
            def some(step, carry):
                at = pl.multiple_of(step * 512, 512)
                m_vmem[pl.ds(pl.multiple_of(p * nodes + at, 512), 512), :] = ref[pl.ds(at, 512), :]
                return carry

            lax.fori_loop(0, nodes // 512, some, 0)

        if len(options) == 1:
            take(options[0])
        else:
            pl.when(mid == 1)(functools.partial(take, options[0]))
            pl.when(mid != 1)(functools.partial(take, options[1]))

    def block(index):
        return m_vmem[pl.ds(pl.multiple_of(index * SIDE, SIDE), SIDE), :]

    def add_pairs(out_ref, acc_ref, step, carry):
        running = total_ref[...]
        prods = []
        for u in range(UNROLL):
            k = 2 * (step * UNROLL + u)
            left = jnp.concatenate([t_vmem[plan_ref[0, k]], t_vmem[plan_ref[0, k + 1]]], axis=1)
            right = jnp.concatenate([block(plan_ref[1, k]), block(plan_ref[1, k + 1])], axis=0)
            prods.append(jnp.dot(left, right, preferred_element_type=jnp.float32))
        for u in range(UNROLL):
            k = 2 * (step * UNROLL + u)
            at = pl.ds(pl.multiple_of(plan_ref[2, k] * SIDE, SIDE), SIDE)
            before = acc_ref[at, :].astype(jnp.float32) if last else jnp.zeros_like(running)
            running = prods[u] + jnp.where(plan_ref[3, k] == 1, running, before)
            out_ref[at, :] = running.astype(out_ref.dtype)
        total_ref[...] = running
        return carry

    total_ref[...] = jnp.zeros_like(total_ref)

    def add_group(g, carry):
        group_copy(g).wait()

        @pl.when(g + 2 < n_groups)
        def _():
            group_copy(g + 2).start()

        low, high = plan_ref[4, 4 + g], plan_ref[4, 5 + g]
        lax.fori_loop(
            jnp.minimum(low, sent_steps), jnp.minimum(high, sent_steps),
            functools.partial(add_pairs, out_refs[0], acc_refs[0]), 0,
        )
        lax.fori_loop(
            jnp.maximum(low, sent_steps), jnp.maximum(high, sent_steps),
            functools.partial(add_pairs, out_refs[1], acc_refs[1]), 0,
        )
        return carry

    lax.fori_loop(0, n_groups, add_group, 0)


def spmm(plan, pieces, tiles, acc, n_row, by_core=False):
    nodes, width = pieces[0][0].shape
    half = n_row // 2 * nodes
    last = acc is not None
    out = jax.ShapeDtypeStruct((2, half, width) if by_core else (half, width), jnp.bfloat16)
    blocks = [ref for p in pieces for ref in p]
    in_vmem, in_any = pl.BlockSpec(memory_space=pltpu.VMEM), pl.BlockSpec(memory_space=pl.ANY)
    return pl.pallas_call(
        functools.partial(spmm_kernel, [len(p) for p in pieces], last, by_core),
        out_shape=(out,) if by_core else (out, out),
        grid_spec=pltpu.PrefetchScalarGridSpec(
            num_scalar_prefetch=1,
            grid=(),
            in_specs=[in_vmem] * len(blocks) + [in_any] + [in_vmem] * len(acc or []),
            out_specs=[in_vmem] * (1 if by_core else 2),
            scratch_shapes=[
                pltpu.VMEM((len(pieces) * nodes, width), jnp.bfloat16),
                pltpu.VMEM((RING * GROUP + 1, SIDE, SIDE), jnp.bfloat16),
                pltpu.VMEM((SIDE, width), jnp.float32),
                pltpu.SemaphoreType.DMA((RING,)),
            ],
        ),
        compiler_params=pltpu.CompilerParams(vmem_limit_bytes=SPMM_BYTES),
        cost_estimate=pl.CostEstimate(flops=0, bytes_accessed=4096, transcendentals=0),
        name="spmm_last" if last else "spmm_first",
    )(plan, *blocks, tiles, *(acc or []))


def xor_permute(value, axis, mask):
    size = lax.axis_size(axis)
    return lax.ppermute(value, axis, [(i, i ^ mask) for i in range(size)])


def tree_sum(values):
    while len(values) > 1:
        values = [a + b for a, b in zip(values[::2], values[1::2])]
    return values[0]


def gather_first(own):
    return xor_permute(own, "col", 1), xor_permute(own, "col", 2)


def gather_second(own, by_two, n_col):
    ends, middles = [], []
    for low in range(0, n_col, 4):
        ends += [(low + 1, low), (low + 2, low + 3)]
        middles += [(low + 1, low + 2), (low + 2, low + 1)]
    return lax.ppermute(own, "col", middles), lax.ppermute(by_two, "col", ends)


def as_pieces(own, first, second, mid, n_col):
    if n_col == 4:
        return [[own], [first[0]], [first[1]], list(second)]
    pieces = [own, first[0], first[1], jnp.where(mid, second[0], second[1])]
    for high in range(4, n_col, 4):
        pieces += [xor_permute(piece, "col", high) for piece in pieces[:4]]
    return [[piece] for piece in pieces]


def swap_cores(both):
    pairs = [[i, i + 1] for i in range(0, lax.axis_size("row"), 2)]
    return lax.all_to_all(both, "row", 0, 0, axis_index_groups=pairs)


def fence(*values):
    return lax.optimization_barrier(values)


def add_f32(a, b):
    return a.astype(jnp.float32) + b.astype(jnp.float32)


def stage_sums(keep, recv, n_blocks, rows, at_once=False):
    width = keep.shape[1]
    cut = (n_blocks // 2, 2, 2, rows, width)
    flat = (2, n_blocks // 2, 2, rows, width)
    sums = add_f32(keep, recv).astype(jnp.bfloat16)
    if at_once:
        (sums,) = fence(sums)

    def summed(shape, pick):
        if at_once:
            return pick(sums.reshape(shape)).reshape(-1, width)
        both = add_f32(pick(keep.reshape(shape)), pick(recv.reshape(shape)))
        return both.astype(jnp.bfloat16).reshape(-1, width)

    stage = [
        summed(cut, lambda v: v[:, 1, 0]),
        summed(cut, lambda v: v[:, 0, 0]),
        summed(flat, lambda v: v[1, :, 1]),
        summed(flat, lambda v: v[0, :, 1]),
    ]
    return stage, sums


def halve(value, upper, rows):
    blocks = value.shape[0] // rows
    shape = (2, blocks // 2) if upper else (blocks // 2, 2)
    cut = value.reshape(shape + (rows, value.shape[1]))
    if upper:
        sent, kept = cut[1], cut[0]
    else:
        sent, kept = cut[:, 1], cut[:, 0]
    return sent.reshape(-1, value.shape[1]), kept.reshape(-1, value.shape[1])


def exchange_first(stage, bits):
    return xor_permute(stage[0], "row", bits[0]), xor_permute(stage[2], "row", bits[-1])


def exchange_second(stage, recv, bits, rows):
    sent, kept = [], []
    for upper in (0, 1):
        value = add_f32(stage[2 * upper + 1], recv[upper]).astype(jnp.bfloat16)
        sent_u, kept_u = halve(value, upper, rows)
        sent.append(sent_u)
        kept.append(kept_u)
    return kept, sent


def send_second(sent, bits):
    return [xor_permute(s, "row", bit) for s, bit in zip(sent, (bits[1], bits[-2]))]


def exchange_last(kept, recv, bits, rows):
    done = []
    for upper in (0, 1):
        value = add_f32(kept[upper], recv[upper])
        for bit in (bits[::-1] if upper else bits)[2:]:
            sent_u, kept_u = halve(value.astype(jnp.bfloat16), upper, rows)
            value = add_f32(kept_u, xor_permute(sent_u, "row", bit))
        done.append(value.astype(jnp.bfloat16))
    return jnp.concatenate(done, axis=0)


def weight_term(near, sums):
    terms, at = [], 0
    for f in [part for parts in near for part in parts]:
        own = sums[at : at + f.shape[0]]
        terms.append(lax.dot_general(f, own, (((0,), (0,)), ((), ())), preferred_element_type=jnp.float32))
        at += f.shape[0]
    return sum(terms[1:], terms[0]).astype(jnp.bfloat16)


def term_kernel(*refs):
    *parts, sums_ref, out_ref, acc_ref = refs
    acc_ref[...] = jnp.zeros_like(acc_ref)
    first = 0
    for part in parts:

        def add_rows(step, carry, part=part, first=first):
            at = pl.multiple_of(step * TERM_ROWS, TERM_ROWS)
            acc_ref[...] += lax.dot_general(
                sums_ref[pl.ds(first + at, TERM_ROWS), :], part[pl.ds(at, TERM_ROWS), :],
                (((0,), (0,)), ((), ())), preferred_element_type=jnp.float32,
            )
            return carry

        lax.fori_loop(0, part.shape[0] // TERM_ROWS, add_rows, 0)
        first += part.shape[0]
    out_ref[...] = acc_ref[...].T.astype(out_ref.dtype)


def weight_term_early(near, sums):
    parts = [part for group in near for part in group]
    shape = (parts[0].shape[1], sums.shape[1])
    return pl.pallas_call(
        term_kernel,
        out_shape=jax.ShapeDtypeStruct(shape, jnp.bfloat16),
        in_specs=[pl.BlockSpec(memory_space=pltpu.VMEM)] * (len(parts) + 1),
        out_specs=pl.BlockSpec(memory_space=pltpu.VMEM),
        scratch_shapes=[pltpu.VMEM(shape[::-1], jnp.float32)],
        compiler_params=pltpu.CompilerParams(vmem_limit_bytes=TERM_BYTES),
        cost_estimate=pl.CostEstimate(flops=0, bytes_accessed=4096, transcendentals=0),
        name="weight_term",
    )(*parts, sums)


def sum_over(term, axis, masks):
    parts = [term] + [xor_permute(term, axis, m) for m in masks]
    return tree_sum([p.astype(jnp.float32) for p in parts])


def body(grad_out, preact, features, weight, tiles, tile_rows, tile_cols, live_counts):
    nodes, width = grad_out.shape
    n_row, n_col = lax.axis_size("row"), lax.axis_size("col")
    row, col = lax.axis_index("row"), lax.axis_index("col")
    slots = tiles.shape[2]
    cw = width // 2
    rows = nodes // 2
    bits = [1 << b for b in range(1, n_row.bit_length() - 1)]
    mid = ((col & 3) == 1) | ((col & 3) == 2)
    even = (row & 1) == 0

    own0, own1 = [
        jnp.where(preact[:, cut] > 0, grad_out[:, cut], jnp.zeros_like(grad_out[:, cut]))
        for cut in (slice(0, cw), slice(cw, width))
    ]
    first0 = gather_first(own0)
    place = jnp.stack([live_counts.reshape(()), row, col, mid.astype(jnp.int32)])
    plan0, plan1, slot = make_plans(tile_rows, tile_cols, place, n_row, nodes // SIDE)
    flipped = flip_tiles(slot, tiles.reshape(slots, SIDE, SIDE))
    features, plan0 = fence(features, plan0)
    near = [[features]]
    for bit in bits[:2]:
        near.append([xor_permute(features, "row", bit)])
    own0, own1, first0, plan0, plan1, flipped, even = fence(own0, own1, first0, plan0, plan1, flipped, even)

    second0 = gather_second(own0, first0[1], n_col)
    acc0 = spmm(plan0, [[own0], [first0[0]], [first0[1]]], flipped, None, n_row)
    own1, acc0 = fence(own1, acc0)
    first1 = gather_first(own1)
    pieces0 = as_pieces(own0, first0, second0, mid, n_col)
    pieces0, near, acc0 = fence(pieces0, near, acc0)

    near.append([xor_permute(near[1][0][:rows], "row", bits[1]), xor_permute(near[2][0][rows:], "row", bits[0])])
    for bit in bits[2:]:
        near += [[xor_permute(f, "row", bit) for f in parts] for parts in near]
    (both0,) = spmm(plan1, pieces0[FIRST_PIECES:], flipped, acc0, n_row, by_core=True)
    got0 = swap_cores(both0)
    got0, near = fence(got0, near)
    stage0, sums0 = stage_sums(got0[0], got0[1], n_row // 2, rows, at_once=True)
    recv0 = exchange_first(stage0, bits)
    term0 = weight_term_early(near, sums0)
    own1, first1, stage0, term0 = fence(own1, first1, stage0, term0)

    second1 = gather_second(own1, first1[1], n_col)
    pieces1 = as_pieces(own1, first1, second1, mid, n_col)
    acc1 = spmm(plan0, pieces1[:FIRST_PIECES], flipped, None, n_row)
    acc1, recv0 = fence(acc1, recv0)
    rest0, sent0 = exchange_second(stage0, recv0, bits, rows)
    pieces1, acc1, rest0, sent0 = fence(pieces1, acc1, rest0, sent0)

    send1, keep1 = spmm(plan1, pieces1[FIRST_PIECES:], flipped, acc1, n_row)
    send1, keep1, rest0, sent0 = fence(send1, keep1, rest0, sent0)

    stage1, sums1 = stage_sums(keep1, xor_permute(send1, "row", 1), n_row // 2, rows, at_once=True)
    recv0 = send_second(sent0, bits)
    term1 = weight_term(near, sums1)
    stage1, term0, term1 = fence(stage1, term0, term1)
    stage1, term0, term1, rest0, recv0 = fence(stage1, term0, term1, rest0, recv0)

    recv1 = exchange_first(stage1, bits)
    theirs, mine = jnp.where(even, term1, term0), jnp.where(even, term0, term1)
    mine = add_f32(mine, xor_permute(theirs, "row", 1)).astype(jnp.bfloat16)
    mine = sum_over(mine, "col", range(1, n_col)).astype(jnp.bfloat16)
    colgrad0 = exchange_last(rest0, recv0, bits, rows)
    recv1, mine, colgrad0 = fence(recv1, mine, colgrad0)

    rest1, sent1 = exchange_second(stage1, recv1, bits, rows)
    rest1, sent1, mine = fence(rest1, sent1, mine)
    recv1 = send_second(sent1, bits)
    others = [xor_permute(mine, "row", m) for m in range(2, n_row, 2)]
    colgrad1 = exchange_last(rest1, recv1, bits, rows)
    colgrad1, mine = fence(colgrad1, mine)
    mine = tree_sum([p.astype(jnp.float32) for p in [mine] + others]).astype(jnp.bfloat16)

    theirs = xor_permute(mine, "row", 1)
    low, high = jnp.where(even, mine, theirs), jnp.where(even, theirs, mine)
    grad_weight = jnp.concatenate([low, high], axis=1).astype(jnp.float32)
    colgrad = jnp.concatenate([colgrad0, colgrad1], axis=1)
    grad_features = lax.dot_general(
        colgrad, weight, (((1,), (1,)), ((), ())), preferred_element_type=jnp.float32
    ).astype(jnp.bfloat16)
    return (grad_features, grad_weight)


def solution(mesh):
    in_specs = (
        P(("row", "col"), None),
        P(("row", "col"), None),
        P(("col", "row"), None),
        P(),
        P("row", "col", None, None, None),
        P("row", "col", None),
        P("row", "col", None),
        P("row", "col"),
    )
    out_specs = (P(("col", "row"), None), P())
    return jax.shard_map(body, mesh=mesh, in_specs=in_specs, out_specs=out_specs, check_vma=False)
```

```python
import functools

import jax
import jax.numpy as jnp
from jax import lax
from jax.experimental import pallas as pl
from jax.experimental.pallas import tpu as pltpu
from jax.sharding import PartitionSpec as P

SIDE = 128
UNROLL = 8
GROUP = 32
RING = 4
FIRST_PIECES = 3
PLAN_ROWS = 8
FLIP_BYTES = 26 * 1024 * 1024
PLAN_BYTES = 12 * 1024 * 1024
TERM_BYTES = 14 * 1024 * 1024
TERM_ROWS = 512
SPMM_BYTES = 16 * 1024 * 1024


def round_up(value, unit):
    return -(-value // unit) * unit


def total(mask, axis):
    return jnp.sum(jnp.where(mask, 1.0, 0.0), axis=axis, keepdims=True).astype(jnp.int32)


def total_of(values, axis):
    return jnp.sum(values.astype(jnp.float32), axis=axis, keepdims=True).astype(jnp.int32)


def plan_kernel(per_dev, n_out, place_ref, rows_r, cols_r, rows_c, cols_c, plan0_ref, plan1_ref, slot_ref):
    slots = rows_r.shape[1]
    size = plan0_ref.shape[1]
    count, row, col, mid = place_ref[0], place_ref[1], place_ref[2], place_ref[3]
    shift = per_dev.bit_length() - 1
    start = FIRST_PIECES * per_dev
    step = 2 * UNROLL

    def attributes(rows, cols, axis):
        ids = lax.broadcasted_iota(jnp.int32, rows.shape, axis)
        row_pos = (((rows >> shift) ^ col) << shift) + (rows & (per_dev - 1))
        away = (cols >> shift) ^ row
        out_pos = ((away >> 1) << shift) + (cols & (per_dev - 1))
        kept = 1 - (away & 1)
        last = (row_pos >= start).astype(jnp.int32)
        live = ids < count
        key = jnp.where(live, (2 * last + kept) * n_out + out_pos, 4 * n_out)
        return ids, row_pos, out_pos, 2 * last + kept, live, key

    ids_r, _, _, part_r, live_r, key_r = attributes(rows_r[...], cols_r[...], 1)
    ids_c, row_pos_c, out_pos_c, part_c, live_c, key_c = attributes(rows_c[...], cols_c[...], 0)
    equal = key_c == key_r
    below = key_r < key_c
    earlier_c = total(equal & (ids_r < ids_c), 1)
    earlier_r = total(equal & (ids_c < ids_r), 0)
    later_r = total(equal & (ids_c > ids_r), 0)
    odd_end = (later_r == 0) & ((earlier_r & 1) == 0)
    weight_r = jnp.where(live_r, jnp.where(odd_end, 2, 1), 0)
    rank_c = total(below, 1) + earlier_c
    rank_r = total(key_c < key_r, 0) + earlier_r
    padded_c = total_of(jnp.where(below, weight_r, 0), 1) + earlier_c
    length = [total_of(jnp.where(part_r == p, weight_r, 0), 1) for p in range(4)]
    n_first = total(live_r & (part_r < 2), 1)
    n_last = count - n_first
    last_base = ((n_first + GROUP - 1) >> 5) << 5
    slot_r = jnp.where(part_r >= 2, last_base + rank_r - n_first, rank_r)
    slot_ref[...] = jnp.where(live_r, slot_r, slots + GROUP)

    lane = lax.broadcasted_iota(jnp.int32, (1, size), 1)
    for p, plan_ref in enumerate((plan0_ref, plan1_ref)):
        sent, held = length[2 * p], length[2 * p + 1]
        sent_steps = (sent + step - 1) >> (step.bit_length() - 1)
        all_steps = sent_steps + ((held + step - 1) >> (step.bit_length() - 1))
        base = length[0] + length[1] if p else jnp.zeros_like(sent)
        in_plan = live_c & ((part_c >> 1) == p)
        pos = padded_c - base + jnp.where((part_c & 1) == 1, sent_steps * step - sent, 0)
        pos = jnp.where(in_plan, pos, -1)
        rank = rank_c - (n_first if p else 0)
        hit = pos == lane

        def placed(values, empty, hit=hit):
            return total_of(jnp.where(hit, values - empty, 0), 0) + empty

        plan_ref[0:1, :] = placed(rank & (RING * GROUP - 1), RING * GROUP)
        plan_ref[1:2, :] = placed(row_pos_c - p * start, 0)
        taken = total(hit, 0) > 0
        ends = [
            jnp.max(jnp.where(in_plan & ((part_c & 1) == h), out_pos_c, 0).astype(jnp.float32), axis=0, keepdims=True)
            for h in range(2)
        ]
        end = jnp.where(lane < sent_steps * step, ends[0], ends[1]).astype(jnp.int32)
        plan_ref[2:3, :] = jnp.where(taken, placed(out_pos_c, 0), end)
        plan_ref[3:4, :] = jnp.where(taken, placed((earlier_c > 0).astype(jnp.int32), 0), 1)
        done = total(in_plan & (pos < (lane + 1) * step), 0)
        tiles = n_last if p else n_first
        info = [
            jnp.full((1, 1), mid, jnp.int32),
            sent_steps,
            (tiles + GROUP - 1) >> 5,
            last_base if p else jnp.zeros_like(last_base),
            jnp.zeros_like(last_base),
        ]
        for g in range(slots // GROUP):
            info.append(total((done <= (g + 1) * GROUP) & (lane < all_steps), 1))
        row_values = jnp.zeros((1, size), jnp.int32)
        for n, value in enumerate(info):
            row_values = jnp.where(lane == n, value, row_values)
        plan_ref[4:5, :] = row_values
        plan_ref[5:6, :] = jnp.full((1, size), row & 1, jnp.int32)
        plan_ref[6:8, :] = jnp.zeros((2, size), jnp.int32)


def make_plans(tile_rows, tile_cols, place, n_row, per_dev):
    slots = tile_rows.size
    n_out = n_row // 2 * per_dev
    size = round_up(slots + 2 * n_out + 4 * UNROLL, SIDE)
    plan = jax.ShapeDtypeStruct((PLAN_ROWS, size), jnp.int32)
    return pl.pallas_call(
        functools.partial(plan_kernel, per_dev, n_out),
        out_shape=(plan, plan, jax.ShapeDtypeStruct((1, slots), jnp.int32)),
        in_specs=[pl.BlockSpec(memory_space=pltpu.SMEM)] + [pl.BlockSpec(memory_space=pltpu.VMEM)] * 4,
        out_specs=[pl.BlockSpec(memory_space=pltpu.VMEM)] * 3,
        compiler_params=pltpu.CompilerParams(vmem_limit_bytes=PLAN_BYTES),
        cost_estimate=pl.CostEstimate(flops=0, bytes_accessed=4096, transcendentals=0),
        name="plan_slots",
    )(place, tile_rows.reshape(1, slots), tile_cols.reshape(1, slots), tile_rows.reshape(slots, 1), tile_cols.reshape(slots, 1))


def flip_kernel(slot_ref, tiles_ref, out_ref, t_in, t_out, in_sem, out_sem):
    slots = t_in.shape[0]
    groups = slots // GROUP
    loads = [
        pltpu.make_async_copy(tiles_ref.at[pl.ds(g * GROUP, GROUP)], t_in.at[pl.ds(g * GROUP, GROUP)], in_sem.at[g])
        for g in range(groups)
    ]
    for load in loads:
        load.start()
    for g in range(groups):
        loads[g].wait()

        def some(step, carry, g=g):
            for u in range(4):
                k = g * GROUP + step * 4 + u
                t_out[slot_ref[0, k]] = t_in[k].T
            return carry

        lax.fori_loop(0, GROUP // 4, some, 0)
    stores = [
        pltpu.make_async_copy(t_out.at[pl.ds(g * GROUP, GROUP)], out_ref.at[pl.ds(g * GROUP, GROUP)], out_sem.at[g])
        for g in range(groups + 1)
    ]
    for store in stores:
        store.start()
    for store in stores:
        store.wait()


def flip_tiles(slot, tile_stack):
    slots = tile_stack.shape[0]
    groups = slots // GROUP
    return pl.pallas_call(
        flip_kernel,
        out_shape=jax.ShapeDtypeStruct((slots + GROUP, SIDE, SIDE), tile_stack.dtype),
        grid_spec=pltpu.PrefetchScalarGridSpec(
            num_scalar_prefetch=1,
            grid=(),
            in_specs=[pl.BlockSpec(memory_space=pl.ANY)],
            out_specs=pl.BlockSpec(memory_space=pl.ANY),
            scratch_shapes=[
                pltpu.VMEM(tile_stack.shape, tile_stack.dtype),
                pltpu.VMEM((slots + GROUP + 1, SIDE, SIDE), tile_stack.dtype),
                pltpu.SemaphoreType.DMA((groups,)),
                pltpu.SemaphoreType.DMA((groups + 1,)),
            ],
        ),
        compiler_params=pltpu.CompilerParams(vmem_limit_bytes=FLIP_BYTES),
        cost_estimate=pl.CostEstimate(flops=0, bytes_accessed=4096, transcendentals=0),
        name="flip_tiles",
    )(slot, tile_stack)


def spmm_kernel(layout, last, by_core, plan_ref, *refs):
    n_refs = sum(layout)
    refs_left = list(refs[:n_refs])
    pieces = [[refs_left.pop(0) for _ in range(n)] for n in layout]
    rest = list(refs[n_refs:])
    tiles_ref = rest.pop(0)
    acc_refs = (rest.pop(0), rest.pop(0)) if last else (None, None)
    if by_core:
        core = plan_ref[5, 0]
        out_ref = rest.pop(0)
        out_refs = (out_ref.at[1 - core], out_ref.at[core])
    else:
        out_refs = (rest.pop(0), rest.pop(0))
    m_vmem, t_vmem, total_ref, sems = rest
    nodes, width = pieces[0][0].shape
    mid, sent_steps, n_groups, tile_base = [plan_ref[4, n] for n in range(4)]

    def group_copy(g):
        place = g & (RING - 1)
        return pltpu.make_async_copy(
            tiles_ref.at[pl.ds(tile_base + pl.multiple_of(g * GROUP, GROUP), GROUP)],
            t_vmem.at[pl.ds(pl.multiple_of(place * GROUP, GROUP), GROUP)],
            sems.at[place],
        )

    for g in range(2):
        pl.when(g < n_groups)(group_copy(g).start)
    t_vmem[RING * GROUP] = jnp.zeros((SIDE, SIDE), t_vmem.dtype)
    for out_ref, acc_ref in zip(out_refs, acc_refs):

        def begin(step, carry, out_ref=out_ref, acc_ref=acc_ref):
            at = pl.ds(pl.multiple_of(step * 256, 256), 256)
            out_ref[at, :] = acc_ref[at, :] if last else jnp.zeros((256, width), out_ref.dtype)
            return carry

        lax.fori_loop(0, out_ref.shape[0] // 256, begin, 0)
    for p, options in enumerate(pieces):

        def take(ref, p=p):
            def some(step, carry):
                at = pl.multiple_of(step * 512, 512)
                m_vmem[pl.ds(pl.multiple_of(p * nodes + at, 512), 512), :] = ref[pl.ds(at, 512), :]
                return carry

            lax.fori_loop(0, nodes // 512, some, 0)

        if len(options) == 1:
            take(options[0])
        else:
            pl.when(mid == 1)(functools.partial(take, options[0]))
            pl.when(mid != 1)(functools.partial(take, options[1]))

    def block(index):
        return m_vmem[pl.ds(pl.multiple_of(index * SIDE, SIDE), SIDE), :]

    def add_pairs(out_ref, acc_ref, step, carry):
        running = total_ref[...]
        prods = []
        for u in range(UNROLL):
            k = 2 * (step * UNROLL + u)
            left = jnp.concatenate([t_vmem[plan_ref[0, k]], t_vmem[plan_ref[0, k + 1]]], axis=1)
            right = jnp.concatenate([block(plan_ref[1, k]), block(plan_ref[1, k + 1])], axis=0)
            prods.append(jnp.dot(left, right, preferred_element_type=jnp.float32))
        for u in range(UNROLL):
            k = 2 * (step * UNROLL + u)
            at = pl.ds(pl.multiple_of(plan_ref[2, k] * SIDE, SIDE), SIDE)
            before = acc_ref[at, :].astype(jnp.float32) if last else jnp.zeros_like(running)
            running = prods[u] + jnp.where(plan_ref[3, k] == 1, running, before)
            out_ref[at, :] = running.astype(out_ref.dtype)
        total_ref[...] = running
        return carry

    total_ref[...] = jnp.zeros_like(total_ref)

    def add_group(g, carry):
        group_copy(g).wait()

        @pl.when(g + 2 < n_groups)
        def _():
            group_copy(g + 2).start()

        low, high = plan_ref[4, 4 + g], plan_ref[4, 5 + g]
        lax.fori_loop(
            jnp.minimum(low, sent_steps), jnp.minimum(high, sent_steps),
            functools.partial(add_pairs, out_refs[0], acc_refs[0]), 0,
        )
        lax.fori_loop(
            jnp.maximum(low, sent_steps), jnp.maximum(high, sent_steps),
            functools.partial(add_pairs, out_refs[1], acc_refs[1]), 0,
        )
        return carry

    lax.fori_loop(0, n_groups, add_group, 0)


def spmm(plan, pieces, tiles, acc, n_row, by_core=False):
    nodes, width = pieces[0][0].shape
    half = n_row // 2 * nodes
    last = acc is not None
    out = jax.ShapeDtypeStruct((2, half, width) if by_core else (half, width), jnp.bfloat16)
    blocks = [ref for p in pieces for ref in p]
    in_vmem, in_any = pl.BlockSpec(memory_space=pltpu.VMEM), pl.BlockSpec(memory_space=pl.ANY)
    return pl.pallas_call(
        functools.partial(spmm_kernel, [len(p) for p in pieces], last, by_core),
        out_shape=(out,) if by_core else (out, out),
        grid_spec=pltpu.PrefetchScalarGridSpec(
            num_scalar_prefetch=1,
            grid=(),
            in_specs=[in_vmem] * len(blocks) + [in_any] + [in_vmem] * len(acc or []),
            out_specs=[in_vmem] * (1 if by_core else 2),
            scratch_shapes=[
                pltpu.VMEM((len(pieces) * nodes, width), jnp.bfloat16),
                pltpu.VMEM((RING * GROUP + 1, SIDE, SIDE), jnp.bfloat16),
                pltpu.VMEM((SIDE, width), jnp.float32),
                pltpu.SemaphoreType.DMA((RING,)),
            ],
        ),
        compiler_params=pltpu.CompilerParams(vmem_limit_bytes=SPMM_BYTES),
        cost_estimate=pl.CostEstimate(flops=0, bytes_accessed=4096, transcendentals=0),
        name="spmm_last" if last else "spmm_first",
    )(plan, *blocks, tiles, *(acc or []))


def xor_permute(value, axis, mask):
    size = lax.axis_size(axis)
    return lax.ppermute(value, axis, [(i, i ^ mask) for i in range(size)])


def tree_sum(values):
    while len(values) > 1:
        values = [a + b for a, b in zip(values[::2], values[1::2])]
    return values[0]


def gather_first(own):
    return xor_permute(own, "col", 1), xor_permute(own, "col", 2)


def gather_second(own, by_two, n_col):
    ends, middles = [], []
    for low in range(0, n_col, 4):
        ends += [(low + 1, low), (low + 2, low + 3)]
        middles += [(low + 1, low + 2), (low + 2, low + 1)]
    return lax.ppermute(own, "col", middles), lax.ppermute(by_two, "col", ends)


def as_pieces(own, first, second, mid, n_col):
    if n_col == 4:
        return [[own], [first[0]], [first[1]], list(second)]
    pieces = [own, first[0], first[1], jnp.where(mid, second[0], second[1])]
    for high in range(4, n_col, 4):
        pieces += [xor_permute(piece, "col", high) for piece in pieces[:4]]
    return [[piece] for piece in pieces]


def swap_cores(both):
    pairs = [[i, i + 1] for i in range(0, lax.axis_size("row"), 2)]
    return lax.all_to_all(both, "row", 0, 0, axis_index_groups=pairs)


def fence(*values):
    return lax.optimization_barrier(values)


def add_f32(a, b):
    return a.astype(jnp.float32) + b.astype(jnp.float32)


def stage_sums(keep, recv, n_blocks, rows, at_once=False):
    width = keep.shape[1]
    cut = (n_blocks // 2, 2, 2, rows, width)
    flat = (2, n_blocks // 2, 2, rows, width)
    sums = add_f32(keep, recv).astype(jnp.bfloat16)
    if at_once:
        (sums,) = fence(sums)

    def summed(shape, pick):
        if at_once:
            return pick(sums.reshape(shape)).reshape(-1, width)
        both = add_f32(pick(keep.reshape(shape)), pick(recv.reshape(shape)))
        return both.astype(jnp.bfloat16).reshape(-1, width)

    stage = [
        summed(cut, lambda v: v[:, 1, 0]),
        summed(cut, lambda v: v[:, 0, 0]),
        summed(flat, lambda v: v[1, :, 1]),
        summed(flat, lambda v: v[0, :, 1]),
    ]
    return stage, sums


def halve(value, upper, rows):
    blocks = value.shape[0] // rows
    shape = (2, blocks // 2) if upper else (blocks // 2, 2)
    cut = value.reshape(shape + (rows, value.shape[1]))
    if upper:
        sent, kept = cut[1], cut[0]
    else:
        sent, kept = cut[:, 1], cut[:, 0]
    return sent.reshape(-1, value.shape[1]), kept.reshape(-1, value.shape[1])


def exchange_first(stage, bits):
    return xor_permute(stage[0], "row", bits[0]), xor_permute(stage[2], "row", bits[-1])


def exchange_second(stage, recv, bits, rows):
    sent, kept = [], []
    for upper in (0, 1):
        value = add_f32(stage[2 * upper + 1], recv[upper]).astype(jnp.bfloat16)
        sent_u, kept_u = halve(value, upper, rows)
        sent.append(sent_u)
        kept.append(kept_u)
    return kept, sent


def send_second(sent, bits):
    return [xor_permute(s, "row", bit) for s, bit in zip(sent, (bits[1], bits[-2]))]


def exchange_last(kept, recv, bits, rows):
    done = []
    for upper in (0, 1):
        value = add_f32(kept[upper], recv[upper])
        for bit in (bits[::-1] if upper else bits)[2:]:
            sent_u, kept_u = halve(value.astype(jnp.bfloat16), upper, rows)
            value = add_f32(kept_u, xor_permute(sent_u, "row", bit))
        done.append(value.astype(jnp.bfloat16))
    return jnp.concatenate(done, axis=0)


def weight_term(near, sums):
    terms, at = [], 0
    for f in [part for parts in near for part in parts]:
        own = sums[at : at + f.shape[0]]
        terms.append(lax.dot_general(f, own, (((0,), (0,)), ((), ())), preferred_element_type=jnp.float32))
        at += f.shape[0]
    return sum(terms[1:], terms[0]).astype(jnp.bfloat16)


def term_kernel(*refs):
    *parts, sums_ref, out_ref, acc_ref = refs
    acc_ref[...] = jnp.zeros_like(acc_ref)
    first = 0
    for part in parts:

        def add_rows(step, carry, part=part, first=first):
            at = pl.multiple_of(step * TERM_ROWS, TERM_ROWS)
            acc_ref[...] += lax.dot_general(
                sums_ref[pl.ds(first + at, TERM_ROWS), :], part[pl.ds(at, TERM_ROWS), :],
                (((0,), (0,)), ((), ())), preferred_element_type=jnp.float32,
            )
            return carry

        lax.fori_loop(0, part.shape[0] // TERM_ROWS, add_rows, 0)
        first += part.shape[0]
    out_ref[...] = acc_ref[...].T.astype(out_ref.dtype)


def weight_term_early(near, sums):
    parts = [part for group in near for part in group]
    shape = (parts[0].shape[1], sums.shape[1])
    return pl.pallas_call(
        term_kernel,
        out_shape=jax.ShapeDtypeStruct(shape, jnp.bfloat16),
        in_specs=[pl.BlockSpec(memory_space=pltpu.VMEM)] * (len(parts) + 1),
        out_specs=pl.BlockSpec(memory_space=pltpu.VMEM),
        scratch_shapes=[pltpu.VMEM(shape[::-1], jnp.float32)],
        compiler_params=pltpu.CompilerParams(vmem_limit_bytes=TERM_BYTES),
        cost_estimate=pl.CostEstimate(flops=0, bytes_accessed=4096, transcendentals=0),
        name="weight_term",
    )(*parts, sums)


def sum_over(term, axis, masks):
    parts = [term] + [xor_permute(term, axis, m) for m in masks]
    return tree_sum([p.astype(jnp.float32) for p in parts])


def body(grad_out, preact, features, weight, tiles, tile_rows, tile_cols, live_counts):
    nodes, width = grad_out.shape
    n_row, n_col = lax.axis_size("row"), lax.axis_size("col")
    row, col = lax.axis_index("row"), lax.axis_index("col")
    slots = tiles.shape[2]
    cw = width // 2
    rows = nodes // 2
    bits = [1 << b for b in range(1, n_row.bit_length() - 1)]
    mid = ((col & 3) == 1) | ((col & 3) == 2)
    even = (row & 1) == 0

    own0, own1 = [
        jnp.where(preact[:, cut] > 0, grad_out[:, cut], jnp.zeros_like(grad_out[:, cut]))
        for cut in (slice(0, cw), slice(cw, width))
    ]
    first0 = gather_first(own0)
    place = jnp.stack([live_counts.reshape(()), row, col, mid.astype(jnp.int32)])
    plan0, plan1, slot = make_plans(tile_rows, tile_cols, place, n_row, nodes // SIDE)
    flipped = flip_tiles(slot, tiles.reshape(slots, SIDE, SIDE))
    features, plan0 = fence(features, plan0)
    near = [[features]]
    for bit in bits[:2]:
        near.append([xor_permute(features, "row", bit)])
    own0, own1, first0, plan0, plan1, flipped, even = fence(own0, own1, first0, plan0, plan1, flipped, even)

    second0 = gather_second(own0, first0[1], n_col)
    acc0 = spmm(plan0, [[own0], [first0[0]], [first0[1]]], flipped, None, n_row)
    own1, acc0 = fence(own1, acc0)
    first1 = gather_first(own1)
    pieces0 = as_pieces(own0, first0, second0, mid, n_col)
    pieces0, near, acc0 = fence(pieces0, near, acc0)

    near.append([xor_permute(near[1][0][:rows], "row", bits[1]), xor_permute(near[2][0][rows:], "row", bits[0])])
    for bit in bits[2:]:
        near += [[xor_permute(f, "row", bit) for f in parts] for parts in near]
    (both0,) = spmm(plan1, pieces0[FIRST_PIECES:], flipped, acc0, n_row, by_core=True)
    got0 = swap_cores(both0)
    got0, near = fence(got0, near)
    stage0, sums0 = stage_sums(got0[0], got0[1], n_row // 2, rows, at_once=True)
    recv0 = exchange_first(stage0, bits)
    term0 = weight_term_early(near, sums0)
    own1, first1, stage0, term0 = fence(own1, first1, stage0, term0)

    second1 = gather_second(own1, first1[1], n_col)
    pieces1 = as_pieces(own1, first1, second1, mid, n_col)
    acc1 = spmm(plan0, pieces1[:FIRST_PIECES], flipped, None, n_row)
    acc1, recv0 = fence(acc1, recv0)
    rest0, sent0 = exchange_second(stage0, recv0, bits, rows)
    recv0 = send_second(sent0, bits)
    pieces1, acc1 = fence(pieces1, acc1)

    send1, keep1 = spmm(plan1, pieces1[FIRST_PIECES:], flipped, acc1, n_row)
    send1, keep1, rest0, recv0 = fence(send1, keep1, rest0, recv0)

    stage1, sums1 = stage_sums(keep1, xor_permute(send1, "row", 1), n_row // 2, rows, at_once=True)
    term1 = weight_term(near, sums1)
    stage1, term0, term1 = fence(stage1, term0, term1)

    recv1 = exchange_first(stage1, bits)
    theirs, mine = jnp.where(even, term1, term0), jnp.where(even, term0, term1)
    mine = add_f32(mine, xor_permute(theirs, "row", 1)).astype(jnp.bfloat16)
    mine = sum_over(mine, "col", range(1, n_col)).astype(jnp.bfloat16)
    colgrad0 = exchange_last(rest0, recv0, bits, rows)
    recv1, mine, colgrad0 = fence(recv1, mine, colgrad0)

    rest1, sent1 = exchange_second(stage1, recv1, bits, rows)
    rest1, sent1, mine = fence(rest1, sent1, mine)
    recv1 = send_second(sent1, bits)
    others = [xor_permute(mine, "row", m) for m in range(2, n_row, 2)]
    colgrad1 = exchange_last(rest1, recv1, bits, rows)
    colgrad1, mine = fence(colgrad1, mine)
    mine = tree_sum([p.astype(jnp.float32) for p in [mine] + others]).astype(jnp.bfloat16)

    theirs = xor_permute(mine, "row", 1)
    low, high = jnp.where(even, mine, theirs), jnp.where(even, theirs, mine)
    grad_weight = jnp.concatenate([low, high], axis=1).astype(jnp.float32)
    colgrad = jnp.concatenate([colgrad0, colgrad1], axis=1)
    grad_features = lax.dot_general(
        colgrad, weight, (((1,), (1,)), ((), ())), preferred_element_type=jnp.float32
    ).astype(jnp.bfloat16)
    return (grad_features, grad_weight)


def solution(mesh):
    in_specs = (
        P(("row", "col"), None),
        P(("row", "col"), None),
        P(("col", "row"), None),
        P(),
        P("row", "col", None, None, None),
        P("row", "col", None),
        P("row", "col", None),
        P("row", "col"),
    )
    out_specs = (P(("col", "row"), None), P())
    return jax.shard_map(body, mesh=mesh, in_specs=in_specs, out_specs=out_specs, check_vma=False)
```

```python
import functools

import jax
import jax.numpy as jnp
from jax import lax
from jax.experimental import pallas as pl
from jax.experimental.pallas import tpu as pltpu
from jax.sharding import PartitionSpec as P

SIDE = 128
UNROLL = 8
GROUP = 32
RING = 4
FIRST_PIECES = 3
PLAN_ROWS = 8
FLIP_BYTES = 26 * 1024 * 1024
PLAN_BYTES = 12 * 1024 * 1024
TERM_BYTES = 14 * 1024 * 1024
TERM_ROWS = 512
SPMM_BYTES = 16 * 1024 * 1024


def round_up(value, unit):
    return -(-value // unit) * unit


def total(mask, axis):
    return jnp.sum(jnp.where(mask, 1.0, 0.0), axis=axis, keepdims=True).astype(jnp.int32)


def total_of(values, axis):
    return jnp.sum(values.astype(jnp.float32), axis=axis, keepdims=True).astype(jnp.int32)


def plan_kernel(per_dev, n_out, place_ref, rows_r, cols_r, rows_c, cols_c, plan0_ref, plan1_ref, slot_ref):
    slots = rows_r.shape[1]
    size = plan0_ref.shape[1]
    count, row, col, mid = place_ref[0], place_ref[1], place_ref[2], place_ref[3]
    shift = per_dev.bit_length() - 1
    start = FIRST_PIECES * per_dev
    step = 2 * UNROLL

    def attributes(rows, cols, axis):
        ids = lax.broadcasted_iota(jnp.int32, rows.shape, axis)
        row_pos = (((rows >> shift) ^ col) << shift) + (rows & (per_dev - 1))
        away = (cols >> shift) ^ row
        out_pos = ((away >> 1) << shift) + (cols & (per_dev - 1))
        kept = 1 - (away & 1)
        last = (row_pos >= start).astype(jnp.int32)
        live = ids < count
        key = jnp.where(live, (2 * last + kept) * n_out + out_pos, 4 * n_out)
        return ids, row_pos, out_pos, 2 * last + kept, live, key

    ids_r, _, _, part_r, live_r, key_r = attributes(rows_r[...], cols_r[...], 1)
    ids_c, row_pos_c, out_pos_c, part_c, live_c, key_c = attributes(rows_c[...], cols_c[...], 0)
    equal = key_c == key_r
    below = key_r < key_c
    earlier_c = total(equal & (ids_r < ids_c), 1)
    earlier_r = total(equal & (ids_c < ids_r), 0)
    later_r = total(equal & (ids_c > ids_r), 0)
    odd_end = (later_r == 0) & ((earlier_r & 1) == 0)
    weight_r = jnp.where(live_r, jnp.where(odd_end, 2, 1), 0)
    rank_c = total(below, 1) + earlier_c
    rank_r = total(key_c < key_r, 0) + earlier_r
    padded_c = total_of(jnp.where(below, weight_r, 0), 1) + earlier_c
    length = [total_of(jnp.where(part_r == p, weight_r, 0), 1) for p in range(4)]
    n_first = total(live_r & (part_r < 2), 1)
    n_last = count - n_first
    last_base = ((n_first + GROUP - 1) >> 5) << 5
    slot_r = jnp.where(part_r >= 2, last_base + rank_r - n_first, rank_r)
    slot_ref[...] = jnp.where(live_r, slot_r, slots + GROUP)

    lane = lax.broadcasted_iota(jnp.int32, (1, size), 1)
    for p, plan_ref in enumerate((plan0_ref, plan1_ref)):
        sent, held = length[2 * p], length[2 * p + 1]
        sent_steps = (sent + step - 1) >> (step.bit_length() - 1)
        all_steps = sent_steps + ((held + step - 1) >> (step.bit_length() - 1))
        base = length[0] + length[1] if p else jnp.zeros_like(sent)
        in_plan = live_c & ((part_c >> 1) == p)
        pos = padded_c - base + jnp.where((part_c & 1) == 1, sent_steps * step - sent, 0)
        pos = jnp.where(in_plan, pos, -1)
        rank = rank_c - (n_first if p else 0)
        hit = pos == lane

        def placed(values, empty, hit=hit):
            return total_of(jnp.where(hit, values - empty, 0), 0) + empty

        plan_ref[0:1, :] = placed(rank & (RING * GROUP - 1), RING * GROUP)
        plan_ref[1:2, :] = placed(row_pos_c - p * start, 0)
        taken = total(hit, 0) > 0
        ends = [
            jnp.max(jnp.where(in_plan & ((part_c & 1) == h), out_pos_c, 0).astype(jnp.float32), axis=0, keepdims=True)
            for h in range(2)
        ]
        end = jnp.where(lane < sent_steps * step, ends[0], ends[1]).astype(jnp.int32)
        plan_ref[2:3, :] = jnp.where(taken, placed(out_pos_c, 0), end)
        plan_ref[3:4, :] = jnp.where(taken, placed((earlier_c > 0).astype(jnp.int32), 0), 1)
        done = total(in_plan & (pos < (lane + 1) * step), 0)
        tiles = n_last if p else n_first
        info = [
            jnp.full((1, 1), mid, jnp.int32),
            sent_steps,
            (tiles + GROUP - 1) >> 5,
            last_base if p else jnp.zeros_like(last_base),
            jnp.zeros_like(last_base),
        ]
        for g in range(slots // GROUP):
            info.append(total((done <= (g + 1) * GROUP) & (lane < all_steps), 1))
        row_values = jnp.zeros((1, size), jnp.int32)
        for n, value in enumerate(info):
            row_values = jnp.where(lane == n, value, row_values)
        plan_ref[4:5, :] = row_values
        plan_ref[5:6, :] = jnp.full((1, size), row & 1, jnp.int32)
        plan_ref[6:8, :] = jnp.zeros((2, size), jnp.int32)


def make_plans(tile_rows, tile_cols, place, n_row, per_dev):
    slots = tile_rows.size
    n_out = n_row // 2 * per_dev
    size = round_up(slots + 2 * n_out + 4 * UNROLL, SIDE)
    plan = jax.ShapeDtypeStruct((PLAN_ROWS, size), jnp.int32)
    return pl.pallas_call(
        functools.partial(plan_kernel, per_dev, n_out),
        out_shape=(plan, plan, jax.ShapeDtypeStruct((1, slots), jnp.int32)),
        in_specs=[pl.BlockSpec(memory_space=pltpu.SMEM)] + [pl.BlockSpec(memory_space=pltpu.VMEM)] * 4,
        out_specs=[pl.BlockSpec(memory_space=pltpu.VMEM)] * 3,
        compiler_params=pltpu.CompilerParams(vmem_limit_bytes=PLAN_BYTES),
        cost_estimate=pl.CostEstimate(flops=0, bytes_accessed=4096, transcendentals=0),
        name="plan_slots",
    )(place, tile_rows.reshape(1, slots), tile_cols.reshape(1, slots), tile_rows.reshape(slots, 1), tile_cols.reshape(slots, 1))


def flip_kernel(slot_ref, tiles_ref, out_ref, t_in, t_out, in_sem, out_sem):
    slots = t_in.shape[0]
    groups = slots // GROUP
    loads = [
        pltpu.make_async_copy(tiles_ref.at[pl.ds(g * GROUP, GROUP)], t_in.at[pl.ds(g * GROUP, GROUP)], in_sem.at[g])
        for g in range(groups)
    ]
    for load in loads:
        load.start()
    for g in range(groups):
        loads[g].wait()

        def some(step, carry, g=g):
            for u in range(4):
                k = g * GROUP + step * 4 + u
                t_out[slot_ref[0, k]] = t_in[k].T
            return carry

        lax.fori_loop(0, GROUP // 4, some, 0)
    stores = [
        pltpu.make_async_copy(t_out.at[pl.ds(g * GROUP, GROUP)], out_ref.at[pl.ds(g * GROUP, GROUP)], out_sem.at[g])
        for g in range(groups + 1)
    ]
    for store in stores:
        store.start()
    for store in stores:
        store.wait()


def flip_tiles(slot, tile_stack):
    slots = tile_stack.shape[0]
    groups = slots // GROUP
    return pl.pallas_call(
        flip_kernel,
        out_shape=jax.ShapeDtypeStruct((slots + GROUP, SIDE, SIDE), tile_stack.dtype),
        grid_spec=pltpu.PrefetchScalarGridSpec(
            num_scalar_prefetch=1,
            grid=(),
            in_specs=[pl.BlockSpec(memory_space=pl.ANY)],
            out_specs=pl.BlockSpec(memory_space=pl.ANY),
            scratch_shapes=[
                pltpu.VMEM(tile_stack.shape, tile_stack.dtype),
                pltpu.VMEM((slots + GROUP + 1, SIDE, SIDE), tile_stack.dtype),
                pltpu.SemaphoreType.DMA((groups,)),
                pltpu.SemaphoreType.DMA((groups + 1,)),
            ],
        ),
        compiler_params=pltpu.CompilerParams(vmem_limit_bytes=FLIP_BYTES),
        cost_estimate=pl.CostEstimate(flops=0, bytes_accessed=4096, transcendentals=0),
        name="flip_tiles",
    )(slot, tile_stack)


def spmm_kernel(layout, last, by_core, plan_ref, *refs):
    n_refs = sum(layout)
    refs_left = list(refs[:n_refs])
    pieces = [[refs_left.pop(0) for _ in range(n)] for n in layout]
    rest = list(refs[n_refs:])
    tiles_ref = rest.pop(0)
    acc_refs = (rest.pop(0), rest.pop(0)) if last else (None, None)
    if by_core:
        core = plan_ref[5, 0]
        out_ref = rest.pop(0)
        out_refs = (out_ref.at[1 - core], out_ref.at[core])
    else:
        out_refs = (rest.pop(0), rest.pop(0))
    m_vmem, t_vmem, total_ref, sems = rest
    nodes, width = pieces[0][0].shape
    mid, sent_steps, n_groups, tile_base = [plan_ref[4, n] for n in range(4)]

    def group_copy(g):
        place = g & (RING - 1)
        return pltpu.make_async_copy(
            tiles_ref.at[pl.ds(tile_base + pl.multiple_of(g * GROUP, GROUP), GROUP)],
            t_vmem.at[pl.ds(pl.multiple_of(place * GROUP, GROUP), GROUP)],
            sems.at[place],
        )

    for g in range(2):
        pl.when(g < n_groups)(group_copy(g).start)
    t_vmem[RING * GROUP] = jnp.zeros((SIDE, SIDE), t_vmem.dtype)
    for out_ref, acc_ref in zip(out_refs, acc_refs):

        def begin(step, carry, out_ref=out_ref, acc_ref=acc_ref):
            at = pl.ds(pl.multiple_of(step * 256, 256), 256)
            out_ref[at, :] = acc_ref[at, :] if last else jnp.zeros((256, width), out_ref.dtype)
            return carry

        lax.fori_loop(0, out_ref.shape[0] // 256, begin, 0)
    for p, options in enumerate(pieces):

        def take(ref, p=p):
            def some(step, carry):
                at = pl.multiple_of(step * 512, 512)
                m_vmem[pl.ds(pl.multiple_of(p * nodes + at, 512), 512), :] = ref[pl.ds(at, 512), :]
                return carry

            lax.fori_loop(0, nodes // 512, some, 0)

        if len(options) == 1:
            take(options[0])
        else:
            pl.when(mid == 1)(functools.partial(take, options[0]))
            pl.when(mid != 1)(functools.partial(take, options[1]))

    def block(index):
        return m_vmem[pl.ds(pl.multiple_of(index * SIDE, SIDE), SIDE), :]

    def add_pairs(out_ref, acc_ref, step, carry):
        running = total_ref[...]
        prods = []
        for u in range(UNROLL):
            k = 2 * (step * UNROLL + u)
            left = jnp.concatenate([t_vmem[plan_ref[0, k]], t_vmem[plan_ref[0, k + 1]]], axis=1)
            right = jnp.concatenate([block(plan_ref[1, k]), block(plan_ref[1, k + 1])], axis=0)
            prods.append(jnp.dot(left, right, preferred_element_type=jnp.float32))
        for u in range(UNROLL):
            k = 2 * (step * UNROLL + u)
            at = pl.ds(pl.multiple_of(plan_ref[2, k] * SIDE, SIDE), SIDE)
            before = acc_ref[at, :].astype(jnp.float32) if last else jnp.zeros_like(running)
            running = prods[u] + jnp.where(plan_ref[3, k] == 1, running, before)
            out_ref[at, :] = running.astype(out_ref.dtype)
        total_ref[...] = running
        return carry

    total_ref[...] = jnp.zeros_like(total_ref)

    def add_group(g, carry):
        group_copy(g).wait()

        @pl.when(g + 2 < n_groups)
        def _():
            group_copy(g + 2).start()

        low, high = plan_ref[4, 4 + g], plan_ref[4, 5 + g]
        lax.fori_loop(
            jnp.minimum(low, sent_steps), jnp.minimum(high, sent_steps),
            functools.partial(add_pairs, out_refs[0], acc_refs[0]), 0,
        )
        lax.fori_loop(
            jnp.maximum(low, sent_steps), jnp.maximum(high, sent_steps),
            functools.partial(add_pairs, out_refs[1], acc_refs[1]), 0,
        )
        return carry

    lax.fori_loop(0, n_groups, add_group, 0)


def spmm(plan, pieces, tiles, acc, n_row, by_core=False):
    nodes, width = pieces[0][0].shape
    half = n_row // 2 * nodes
    last = acc is not None
    out = jax.ShapeDtypeStruct((2, half, width) if by_core else (half, width), jnp.bfloat16)
    blocks = [ref for p in pieces for ref in p]
    in_vmem, in_any = pl.BlockSpec(memory_space=pltpu.VMEM), pl.BlockSpec(memory_space=pl.ANY)
    return pl.pallas_call(
        functools.partial(spmm_kernel, [len(p) for p in pieces], last, by_core),
        out_shape=(out,) if by_core else (out, out),
        grid_spec=pltpu.PrefetchScalarGridSpec(
            num_scalar_prefetch=1,
            grid=(),
            in_specs=[in_vmem] * len(blocks) + [in_any] + [in_vmem] * len(acc or []),
            out_specs=[in_vmem] * (1 if by_core else 2),
            scratch_shapes=[
                pltpu.VMEM((len(pieces) * nodes, width), jnp.bfloat16),
                pltpu.VMEM((RING * GROUP + 1, SIDE, SIDE), jnp.bfloat16),
                pltpu.VMEM((SIDE, width), jnp.float32),
                pltpu.SemaphoreType.DMA((RING,)),
            ],
        ),
        compiler_params=pltpu.CompilerParams(vmem_limit_bytes=SPMM_BYTES),
        cost_estimate=pl.CostEstimate(flops=0, bytes_accessed=4096, transcendentals=0),
        name="spmm_last" if last else "spmm_first",
    )(plan, *blocks, tiles, *(acc or []))


def xor_permute(value, axis, mask):
    size = lax.axis_size(axis)
    return lax.ppermute(value, axis, [(i, i ^ mask) for i in range(size)])


def tree_sum(values):
    while len(values) > 1:
        values = [a + b for a, b in zip(values[::2], values[1::2])]
    return values[0]


def gather_first(own):
    return xor_permute(own, "col", 1), xor_permute(own, "col", 2)


def gather_second(own, by_two, n_col):
    ends, middles = [], []
    for low in range(0, n_col, 4):
        ends += [(low + 1, low), (low + 2, low + 3)]
        middles += [(low + 1, low + 2), (low + 2, low + 1)]
    return lax.ppermute(own, "col", middles), lax.ppermute(by_two, "col", ends)


def as_pieces(own, first, second, mid, n_col):
    if n_col == 4:
        return [[own], [first[0]], [first[1]], list(second)]
    pieces = [own, first[0], first[1], jnp.where(mid, second[0], second[1])]
    for high in range(4, n_col, 4):
        pieces += [xor_permute(piece, "col", high) for piece in pieces[:4]]
    return [[piece] for piece in pieces]


def swap_cores(both):
    pairs = [[i, i + 1] for i in range(0, lax.axis_size("row"), 2)]
    return lax.all_to_all(both, "row", 0, 0, axis_index_groups=pairs)


def fence(*values):
    return lax.optimization_barrier(values)


def add_f32(a, b):
    return a.astype(jnp.float32) + b.astype(jnp.float32)


def stage_sums(keep, recv, n_blocks, rows, at_once=False):
    width = keep.shape[1]
    cut = (n_blocks // 2, 2, 2, rows, width)
    flat = (2, n_blocks // 2, 2, rows, width)
    sums = add_f32(keep, recv).astype(jnp.bfloat16)
    if at_once:
        (sums,) = fence(sums)

    def summed(shape, pick):
        if at_once:
            return pick(sums.reshape(shape)).reshape(-1, width)
        both = add_f32(pick(keep.reshape(shape)), pick(recv.reshape(shape)))
        return both.astype(jnp.bfloat16).reshape(-1, width)

    stage = [
        summed(cut, lambda v: v[:, 1, 0]),
        summed(cut, lambda v: v[:, 0, 0]),
        summed(flat, lambda v: v[1, :, 1]),
        summed(flat, lambda v: v[0, :, 1]),
    ]
    return stage, sums


def halve(value, upper, rows):
    blocks = value.shape[0] // rows
    shape = (2, blocks // 2) if upper else (blocks // 2, 2)
    cut = value.reshape(shape + (rows, value.shape[1]))
    if upper:
        sent, kept = cut[1], cut[0]
    else:
        sent, kept = cut[:, 1], cut[:, 0]
    return sent.reshape(-1, value.shape[1]), kept.reshape(-1, value.shape[1])


def exchange_first(stage, bits):
    return xor_permute(stage[0], "row", bits[0]), xor_permute(stage[2], "row", bits[-1])


def exchange_second(stage, recv, bits, rows):
    sent, kept = [], []
    for upper in (0, 1):
        value = add_f32(stage[2 * upper + 1], recv[upper]).astype(jnp.bfloat16)
        sent_u, kept_u = halve(value, upper, rows)
        sent.append(sent_u)
        kept.append(kept_u)
    return kept, sent


def send_second(sent, bits):
    return [xor_permute(s, "row", bit) for s, bit in zip(sent, (bits[1], bits[-2]))]


def exchange_last(kept, recv, bits, rows):
    done = []
    for upper in (0, 1):
        value = add_f32(kept[upper], recv[upper])
        for bit in (bits[::-1] if upper else bits)[2:]:
            sent_u, kept_u = halve(value.astype(jnp.bfloat16), upper, rows)
            value = add_f32(kept_u, xor_permute(sent_u, "row", bit))
        done.append(value.astype(jnp.bfloat16))
    return jnp.concatenate(done, axis=0)


def weight_term(near, sums):
    terms, at = [], 0
    for f in [part for parts in near for part in parts]:
        own = sums[at : at + f.shape[0]]
        terms.append(lax.dot_general(f, own, (((0,), (0,)), ((), ())), preferred_element_type=jnp.float32))
        at += f.shape[0]
    return sum(terms[1:], terms[0]).astype(jnp.bfloat16)


def term_kernel(*refs):
    *parts, sums_ref, out_ref, acc_ref = refs
    acc_ref[...] = jnp.zeros_like(acc_ref)
    first = 0
    for part in parts:

        def add_rows(step, carry, part=part, first=first):
            at = pl.multiple_of(step * TERM_ROWS, TERM_ROWS)
            acc_ref[...] += lax.dot_general(
                sums_ref[pl.ds(first + at, TERM_ROWS), :], part[pl.ds(at, TERM_ROWS), :],
                (((0,), (0,)), ((), ())), preferred_element_type=jnp.float32,
            )
            return carry

        lax.fori_loop(0, part.shape[0] // TERM_ROWS, add_rows, 0)
        first += part.shape[0]
    out_ref[...] = acc_ref[...].T.astype(out_ref.dtype)


def weight_term_early(near, sums):
    parts = [part for group in near for part in group]
    shape = (parts[0].shape[1], sums.shape[1])
    return pl.pallas_call(
        term_kernel,
        out_shape=jax.ShapeDtypeStruct(shape, jnp.bfloat16),
        in_specs=[pl.BlockSpec(memory_space=pltpu.VMEM)] * (len(parts) + 1),
        out_specs=pl.BlockSpec(memory_space=pltpu.VMEM),
        scratch_shapes=[pltpu.VMEM(shape[::-1], jnp.float32)],
        compiler_params=pltpu.CompilerParams(vmem_limit_bytes=TERM_BYTES),
        cost_estimate=pl.CostEstimate(flops=0, bytes_accessed=4096, transcendentals=0),
        name="weight_term",
    )(*parts, sums)


def sum_over(term, axis, masks):
    parts = [term] + [xor_permute(term, axis, m) for m in masks]
    return tree_sum([p.astype(jnp.float32) for p in parts])


def body(grad_out, preact, features, weight, tiles, tile_rows, tile_cols, live_counts):
    nodes, width = grad_out.shape
    n_row, n_col = lax.axis_size("row"), lax.axis_size("col")
    row, col = lax.axis_index("row"), lax.axis_index("col")
    slots = tiles.shape[2]
    cw = width // 2
    rows = nodes // 2
    bits = [1 << b for b in range(1, n_row.bit_length() - 1)]
    mid = ((col & 3) == 1) | ((col & 3) == 2)
    even = (row & 1) == 0
    place = jnp.stack([live_counts.reshape(()), row, col, mid.astype(jnp.int32)])
    place, even, grad_out, preact = fence(place, even, grad_out, preact)

    own0, own1 = [
        jnp.where(preact[:, cut] > 0, grad_out[:, cut], jnp.zeros_like(grad_out[:, cut]))
        for cut in (slice(0, cw), slice(cw, width))
    ]
    first0 = gather_first(own0)
    plan0, plan1, slot = make_plans(tile_rows, tile_cols, place, n_row, nodes // SIDE)
    flipped = flip_tiles(slot, tiles.reshape(slots, SIDE, SIDE))
    features, plan0 = fence(features, plan0)
    near = [[features]]
    for bit in bits[:2]:
        near.append([xor_permute(features, "row", bit)])
    own0, own1, first0, plan0, plan1, flipped = fence(own0, own1, first0, plan0, plan1, flipped)

    second0 = gather_second(own0, first0[1], n_col)
    acc0 = spmm(plan0, [[own0], [first0[0]], [first0[1]]], flipped, None, n_row)
    own1, acc0 = fence(own1, acc0)
    first1 = gather_first(own1)
    pieces0 = as_pieces(own0, first0, second0, mid, n_col)
    pieces0, near, acc0 = fence(pieces0, near, acc0)

    near.append([xor_permute(near[1][0][:rows], "row", bits[1]), xor_permute(near[2][0][rows:], "row", bits[0])])
    for bit in bits[2:]:
        near += [[xor_permute(f, "row", bit) for f in parts] for parts in near]
    (both0,) = spmm(plan1, pieces0[FIRST_PIECES:], flipped, acc0, n_row, by_core=True)
    got0 = swap_cores(both0)
    got0, near = fence(got0, near)
    stage0, sums0 = stage_sums(got0[0], got0[1], n_row // 2, rows, at_once=True)
    recv0 = exchange_first(stage0, bits)
    term0 = weight_term_early(near, sums0)
    own1, first1, stage0, term0 = fence(own1, first1, stage0, term0)

    second1 = gather_second(own1, first1[1], n_col)
    pieces1 = as_pieces(own1, first1, second1, mid, n_col)
    acc1 = spmm(plan0, pieces1[:FIRST_PIECES], flipped, None, n_row)
    acc1, recv0 = fence(acc1, recv0)
    rest0, sent0 = exchange_second(stage0, recv0, bits, rows)
    recv0 = send_second(sent0, bits)
    pieces1, acc1 = fence(pieces1, acc1)

    send1, keep1 = spmm(plan1, pieces1[FIRST_PIECES:], flipped, acc1, n_row)
    send1, keep1, rest0, recv0 = fence(send1, keep1, rest0, recv0)

    stage1, sums1 = stage_sums(keep1, xor_permute(send1, "row", 1), n_row // 2, rows, at_once=True)
    term1 = weight_term(near, sums1)
    stage1, term0, term1 = fence(stage1, term0, term1)

    recv1 = exchange_first(stage1, bits)
    theirs, mine = jnp.where(even, term1, term0), jnp.where(even, term0, term1)
    mine = add_f32(mine, xor_permute(theirs, "row", 1)).astype(jnp.bfloat16)
    mine = sum_over(mine, "col", range(1, n_col)).astype(jnp.bfloat16)
    colgrad0 = exchange_last(rest0, recv0, bits, rows)
    recv1, mine, colgrad0 = fence(recv1, mine, colgrad0)

    rest1, sent1 = exchange_second(stage1, recv1, bits, rows)
    rest1, sent1, mine = fence(rest1, sent1, mine)
    recv1 = send_second(sent1, bits)
    others = [xor_permute(mine, "row", m) for m in range(2, n_row, 2)]
    colgrad1 = exchange_last(rest1, recv1, bits, rows)
    colgrad1, mine = fence(colgrad1, mine)
    mine = tree_sum([p.astype(jnp.float32) for p in [mine] + others]).astype(jnp.bfloat16)

    theirs = xor_permute(mine, "row", 1)
    low, high = jnp.where(even, mine, theirs), jnp.where(even, theirs, mine)
    grad_weight = jnp.concatenate([low, high], axis=1).astype(jnp.float32)
    colgrad = jnp.concatenate([colgrad0, colgrad1], axis=1)
    grad_features = lax.dot_general(
        colgrad, weight, (((1,), (1,)), ((), ())), preferred_element_type=jnp.float32
    ).astype(jnp.bfloat16)
    return (grad_features, grad_weight)


def solution(mesh):
    in_specs = (
        P(("row", "col"), None),
        P(("row", "col"), None),
        P(("col", "row"), None),
        P(),
        P("row", "col", None, None, None),
        P("row", "col", None),
        P("row", "col", None),
        P("row", "col"),
    )
    out_specs = (P(("col", "row"), None), P())
    return jax.shard_map(body, mesh=mesh, in_specs=in_specs, out_specs=out_specs, check_vma=False)
```

```python
import functools

import jax
import jax.numpy as jnp
from jax import lax
from jax.experimental import pallas as pl
from jax.experimental.pallas import tpu as pltpu
from jax.sharding import PartitionSpec as P

SIDE = 128
UNROLL = 16
GROUP = 32
RING = 4
FIRST_PIECES = 3
PLAN_ROWS = 8
FLIP_BYTES = 26 * 1024 * 1024
PLAN_BYTES = 12 * 1024 * 1024
TERM_BYTES = 14 * 1024 * 1024
TERM_ROWS = 512
SPMM_BYTES = 16 * 1024 * 1024


def round_up(value, unit):
    return -(-value // unit) * unit


def total(mask, axis):
    return jnp.sum(jnp.where(mask, 1.0, 0.0), axis=axis, keepdims=True).astype(jnp.int32)


def total_of(values, axis):
    return jnp.sum(values.astype(jnp.float32), axis=axis, keepdims=True).astype(jnp.int32)


def plan_kernel(per_dev, n_out, place_ref, rows_r, cols_r, rows_c, cols_c, plan0_ref, plan1_ref, slot_ref):
    slots = rows_r.shape[1]
    size = plan0_ref.shape[1]
    count, row, col, mid = place_ref[0], place_ref[1], place_ref[2], place_ref[3]
    shift = per_dev.bit_length() - 1
    start = FIRST_PIECES * per_dev
    step = 2 * UNROLL

    def attributes(rows, cols, axis):
        ids = lax.broadcasted_iota(jnp.int32, rows.shape, axis)
        row_pos = (((rows >> shift) ^ col) << shift) + (rows & (per_dev - 1))
        away = (cols >> shift) ^ row
        out_pos = ((away >> 1) << shift) + (cols & (per_dev - 1))
        kept = 1 - (away & 1)
        last = (row_pos >= start).astype(jnp.int32)
        live = ids < count
        key = jnp.where(live, (2 * last + kept) * n_out + out_pos, 4 * n_out)
        return ids, row_pos, out_pos, 2 * last + kept, live, key

    ids_r, _, _, part_r, live_r, key_r = attributes(rows_r[...], cols_r[...], 1)
    ids_c, row_pos_c, out_pos_c, part_c, live_c, key_c = attributes(rows_c[...], cols_c[...], 0)
    equal = key_c == key_r
    below = key_r < key_c
    earlier_c = total(equal & (ids_r < ids_c), 1)
    earlier_r = total(equal & (ids_c < ids_r), 0)
    later_r = total(equal & (ids_c > ids_r), 0)
    odd_end = (later_r == 0) & ((earlier_r & 1) == 0)
    weight_r = jnp.where(live_r, jnp.where(odd_end, 2, 1), 0)
    rank_c = total(below, 1) + earlier_c
    rank_r = total(key_c < key_r, 0) + earlier_r
    padded_c = total_of(jnp.where(below, weight_r, 0), 1) + earlier_c
    length = [total_of(jnp.where(part_r == p, weight_r, 0), 1) for p in range(4)]
    n_first = total(live_r & (part_r < 2), 1)
    n_last = count - n_first
    last_base = ((n_first + GROUP - 1) >> 5) << 5
    slot_r = jnp.where(part_r >= 2, last_base + rank_r - n_first, rank_r)
    slot_ref[...] = jnp.where(live_r, slot_r, slots + GROUP)

    lane = lax.broadcasted_iota(jnp.int32, (1, size), 1)
    for p, plan_ref in enumerate((plan0_ref, plan1_ref)):
        sent, held = length[2 * p], length[2 * p + 1]
        sent_steps = (sent + step - 1) >> (step.bit_length() - 1)
        all_steps = sent_steps + ((held + step - 1) >> (step.bit_length() - 1))
        base = length[0] + length[1] if p else jnp.zeros_like(sent)
        in_plan = live_c & ((part_c >> 1) == p)
        pos = padded_c - base + jnp.where((part_c & 1) == 1, sent_steps * step - sent, 0)
        pos = jnp.where(in_plan, pos, -1)
        rank = rank_c - (n_first if p else 0)
        hit = pos == lane

        def placed(values, empty, hit=hit):
            return total_of(jnp.where(hit, values - empty, 0), 0) + empty

        plan_ref[0:1, :] = placed(rank & (RING * GROUP - 1), RING * GROUP)
        plan_ref[1:2, :] = placed(row_pos_c - p * start, 0)
        taken = total(hit, 0) > 0
        ends = [
            jnp.max(jnp.where(in_plan & ((part_c & 1) == h), out_pos_c, 0).astype(jnp.float32), axis=0, keepdims=True)
            for h in range(2)
        ]
        end = jnp.where(lane < sent_steps * step, ends[0], ends[1]).astype(jnp.int32)
        plan_ref[2:3, :] = jnp.where(taken, placed(out_pos_c, 0), end)
        plan_ref[3:4, :] = jnp.where(taken, placed((earlier_c > 0).astype(jnp.int32), 0), 1)
        done = total(in_plan & (pos < (lane + 1) * step), 0)
        tiles = n_last if p else n_first
        info = [
            jnp.full((1, 1), mid, jnp.int32),
            sent_steps,
            (tiles + GROUP - 1) >> 5,
            last_base if p else jnp.zeros_like(last_base),
            jnp.zeros_like(last_base),
        ]
        for g in range(slots // GROUP):
            info.append(total((done <= (g + 1) * GROUP) & (lane < all_steps), 1))
        row_values = jnp.zeros((1, size), jnp.int32)
        for n, value in enumerate(info):
            row_values = jnp.where(lane == n, value, row_values)
        plan_ref[4:5, :] = row_values
        plan_ref[5:6, :] = jnp.full((1, size), row & 1, jnp.int32)
        plan_ref[6:8, :] = jnp.zeros((2, size), jnp.int32)


def make_plans(tile_rows, tile_cols, place, n_row, per_dev):
    slots = tile_rows.size
    n_out = n_row // 2 * per_dev
    size = round_up(slots + 2 * n_out + 4 * UNROLL, SIDE)
    plan = jax.ShapeDtypeStruct((PLAN_ROWS, size), jnp.int32)
    return pl.pallas_call(
        functools.partial(plan_kernel, per_dev, n_out),
        out_shape=(plan, plan, jax.ShapeDtypeStruct((1, slots), jnp.int32)),
        in_specs=[pl.BlockSpec(memory_space=pltpu.SMEM)] + [pl.BlockSpec(memory_space=pltpu.VMEM)] * 4,
        out_specs=[pl.BlockSpec(memory_space=pltpu.VMEM)] * 3,
        compiler_params=pltpu.CompilerParams(vmem_limit_bytes=PLAN_BYTES),
        cost_estimate=pl.CostEstimate(flops=0, bytes_accessed=4096, transcendentals=0),
        name="plan_slots",
    )(place, tile_rows.reshape(1, slots), tile_cols.reshape(1, slots), tile_rows.reshape(slots, 1), tile_cols.reshape(slots, 1))


def flip_kernel(slot_ref, tiles_ref, out_ref, t_in, t_out, in_sem, out_sem):
    slots = t_in.shape[0]
    groups = slots // GROUP
    loads = [
        pltpu.make_async_copy(tiles_ref.at[pl.ds(g * GROUP, GROUP)], t_in.at[pl.ds(g * GROUP, GROUP)], in_sem.at[g])
        for g in range(groups)
    ]
    for load in loads:
        load.start()
    for g in range(groups):
        loads[g].wait()

        def some(step, carry, g=g):
            for u in range(4):
                k = g * GROUP + step * 4 + u
                t_out[slot_ref[0, k]] = t_in[k].T
            return carry

        lax.fori_loop(0, GROUP // 4, some, 0)
    stores = [
        pltpu.make_async_copy(t_out.at[pl.ds(g * GROUP, GROUP)], out_ref.at[pl.ds(g * GROUP, GROUP)], out_sem.at[g])
        for g in range(groups + 1)
    ]
    for store in stores:
        store.start()
    for store in stores:
        store.wait()


def flip_tiles(slot, tile_stack):
    slots = tile_stack.shape[0]
    groups = slots // GROUP
    return pl.pallas_call(
        flip_kernel,
        out_shape=jax.ShapeDtypeStruct((slots + GROUP, SIDE, SIDE), tile_stack.dtype),
        grid_spec=pltpu.PrefetchScalarGridSpec(
            num_scalar_prefetch=1,
            grid=(),
            in_specs=[pl.BlockSpec(memory_space=pl.ANY)],
            out_specs=pl.BlockSpec(memory_space=pl.ANY),
            scratch_shapes=[
                pltpu.VMEM(tile_stack.shape, tile_stack.dtype),
                pltpu.VMEM((slots + GROUP + 1, SIDE, SIDE), tile_stack.dtype),
                pltpu.SemaphoreType.DMA((groups,)),
                pltpu.SemaphoreType.DMA((groups + 1,)),
            ],
        ),
        compiler_params=pltpu.CompilerParams(vmem_limit_bytes=FLIP_BYTES),
        cost_estimate=pl.CostEstimate(flops=0, bytes_accessed=4096, transcendentals=0),
        name="flip_tiles",
    )(slot, tile_stack)


def spmm_kernel(layout, last, by_core, plan_ref, *refs):
    n_refs = sum(layout)
    refs_left = list(refs[:n_refs])
    pieces = [[refs_left.pop(0) for _ in range(n)] for n in layout]
    rest = list(refs[n_refs:])
    tiles_ref = rest.pop(0)
    acc_refs = (rest.pop(0), rest.pop(0)) if last else (None, None)
    if by_core:
        core = plan_ref[5, 0]
        out_ref = rest.pop(0)
        out_refs = (out_ref.at[1 - core], out_ref.at[core])
    else:
        out_refs = (rest.pop(0), rest.pop(0))
    m_vmem, t_vmem, total_ref, sems = rest
    nodes, width = pieces[0][0].shape
    mid, sent_steps, n_groups, tile_base = [plan_ref[4, n] for n in range(4)]

    def group_copy(g):
        place = g & (RING - 1)
        return pltpu.make_async_copy(
            tiles_ref.at[pl.ds(tile_base + pl.multiple_of(g * GROUP, GROUP), GROUP)],
            t_vmem.at[pl.ds(pl.multiple_of(place * GROUP, GROUP), GROUP)],
            sems.at[place],
        )

    for g in range(2):
        pl.when(g < n_groups)(group_copy(g).start)
    t_vmem[RING * GROUP] = jnp.zeros((SIDE, SIDE), t_vmem.dtype)
    for out_ref, acc_ref in zip(out_refs, acc_refs):

        def begin(step, carry, out_ref=out_ref, acc_ref=acc_ref):
            at = pl.ds(pl.multiple_of(step * 256, 256), 256)
            out_ref[at, :] = acc_ref[at, :] if last else jnp.zeros((256, width), out_ref.dtype)
            return carry

        lax.fori_loop(0, out_ref.shape[0] // 256, begin, 0)
    for p, options in enumerate(pieces):

        def take(ref, p=p):
            def some(step, carry):
                at = pl.multiple_of(step * 512, 512)
                m_vmem[pl.ds(pl.multiple_of(p * nodes + at, 512), 512), :] = ref[pl.ds(at, 512), :]
                return carry

            lax.fori_loop(0, nodes // 512, some, 0)

        if len(options) == 1:
            take(options[0])
        else:
            pl.when(mid == 1)(functools.partial(take, options[0]))
            pl.when(mid != 1)(functools.partial(take, options[1]))

    def block(index):
        return m_vmem[pl.ds(pl.multiple_of(index * SIDE, SIDE), SIDE), :]

    def add_pairs(out_ref, acc_ref, step, carry):
        running = total_ref[...]
        prods = []
        for u in range(UNROLL):
            k = 2 * (step * UNROLL + u)
            left = jnp.concatenate([t_vmem[plan_ref[0, k]], t_vmem[plan_ref[0, k + 1]]], axis=1)
            right = jnp.concatenate([block(plan_ref[1, k]), block(plan_ref[1, k + 1])], axis=0)
            prods.append(jnp.dot(left, right, preferred_element_type=jnp.float32))
        for u in range(UNROLL):
            k = 2 * (step * UNROLL + u)
            at = pl.ds(pl.multiple_of(plan_ref[2, k] * SIDE, SIDE), SIDE)
            before = acc_ref[at, :].astype(jnp.float32) if last else jnp.zeros_like(running)
            running = prods[u] + jnp.where(plan_ref[3, k] == 1, running, before)
            out_ref[at, :] = running.astype(out_ref.dtype)
        total_ref[...] = running
        return carry

    total_ref[...] = jnp.zeros_like(total_ref)

    def add_group(g, carry):
        group_copy(g).wait()

        @pl.when(g + 2 < n_groups)
        def _():
            group_copy(g + 2).start()

        low, high = plan_ref[4, 4 + g], plan_ref[4, 5 + g]
        lax.fori_loop(
            jnp.minimum(low, sent_steps), jnp.minimum(high, sent_steps),
            functools.partial(add_pairs, out_refs[0], acc_refs[0]), 0,
        )
        lax.fori_loop(
            jnp.maximum(low, sent_steps), jnp.maximum(high, sent_steps),
            functools.partial(add_pairs, out_refs[1], acc_refs[1]), 0,
        )
        return carry

    lax.fori_loop(0, n_groups, add_group, 0)


def spmm(plan, pieces, tiles, acc, n_row, by_core=False):
    nodes, width = pieces[0][0].shape
    half = n_row // 2 * nodes
    last = acc is not None
    out = jax.ShapeDtypeStruct((2, half, width) if by_core else (half, width), jnp.bfloat16)
    blocks = [ref for p in pieces for ref in p]
    in_vmem, in_any = pl.BlockSpec(memory_space=pltpu.VMEM), pl.BlockSpec(memory_space=pl.ANY)
    return pl.pallas_call(
        functools.partial(spmm_kernel, [len(p) for p in pieces], last, by_core),
        out_shape=(out,) if by_core else (out, out),
        grid_spec=pltpu.PrefetchScalarGridSpec(
            num_scalar_prefetch=1,
            grid=(),
            in_specs=[in_vmem] * len(blocks) + [in_any] + [in_vmem] * len(acc or []),
            out_specs=[in_vmem] * (1 if by_core else 2),
            scratch_shapes=[
                pltpu.VMEM((len(pieces) * nodes, width), jnp.bfloat16),
                pltpu.VMEM((RING * GROUP + 1, SIDE, SIDE), jnp.bfloat16),
                pltpu.VMEM((SIDE, width), jnp.float32),
                pltpu.SemaphoreType.DMA((RING,)),
            ],
        ),
        compiler_params=pltpu.CompilerParams(vmem_limit_bytes=SPMM_BYTES),
        cost_estimate=pl.CostEstimate(flops=0, bytes_accessed=4096, transcendentals=0),
        name="spmm_last" if last else "spmm_first",
    )(plan, *blocks, tiles, *(acc or []))


def xor_permute(value, axis, mask):
    size = lax.axis_size(axis)
    return lax.ppermute(value, axis, [(i, i ^ mask) for i in range(size)])


def tree_sum(values):
    while len(values) > 1:
        values = [a + b for a, b in zip(values[::2], values[1::2])]
    return values[0]


def gather_first(own):
    return xor_permute(own, "col", 1), xor_permute(own, "col", 2)


def gather_second(own, by_two, n_col):
    ends, middles = [], []
    for low in range(0, n_col, 4):
        ends += [(low + 1, low), (low + 2, low + 3)]
        middles += [(low + 1, low + 2), (low + 2, low + 1)]
    return lax.ppermute(own, "col", middles), lax.ppermute(by_two, "col", ends)


def as_pieces(own, first, second, mid, n_col):
    if n_col == 4:
        return [[own], [first[0]], [first[1]], list(second)]
    pieces = [own, first[0], first[1], jnp.where(mid, second[0], second[1])]
    for high in range(4, n_col, 4):
        pieces += [xor_permute(piece, "col", high) for piece in pieces[:4]]
    return [[piece] for piece in pieces]


def swap_cores(both):
    pairs = [[i, i + 1] for i in range(0, lax.axis_size("row"), 2)]
    return lax.all_to_all(both, "row", 0, 0, axis_index_groups=pairs)


def fence(*values):
    return lax.optimization_barrier(values)


def add_f32(a, b):
    return a.astype(jnp.float32) + b.astype(jnp.float32)


def stage_sums(keep, recv, n_blocks, rows, at_once=False):
    width = keep.shape[1]
    cut = (n_blocks // 2, 2, 2, rows, width)
    flat = (2, n_blocks // 2, 2, rows, width)
    sums = add_f32(keep, recv).astype(jnp.bfloat16)
    if at_once:
        (sums,) = fence(sums)

    def summed(shape, pick):
        if at_once:
            return pick(sums.reshape(shape)).reshape(-1, width)
        both = add_f32(pick(keep.reshape(shape)), pick(recv.reshape(shape)))
        return both.astype(jnp.bfloat16).reshape(-1, width)

    stage = [
        summed(cut, lambda v: v[:, 1, 0]),
        summed(cut, lambda v: v[:, 0, 0]),
        summed(flat, lambda v: v[1, :, 1]),
        summed(flat, lambda v: v[0, :, 1]),
    ]
    return stage, sums


def halve(value, upper, rows):
    blocks = value.shape[0] // rows
    shape = (2, blocks // 2) if upper else (blocks // 2, 2)
    cut = value.reshape(shape + (rows, value.shape[1]))
    if upper:
        sent, kept = cut[1], cut[0]
    else:
        sent, kept = cut[:, 1], cut[:, 0]
    return sent.reshape(-1, value.shape[1]), kept.reshape(-1, value.shape[1])


def exchange_first(stage, bits):
    return xor_permute(stage[0], "row", bits[0]), xor_permute(stage[2], "row", bits[-1])


def exchange_second(stage, recv, bits, rows):
    sent, kept = [], []
    for upper in (0, 1):
        value = add_f32(stage[2 * upper + 1], recv[upper]).astype(jnp.bfloat16)
        sent_u, kept_u = halve(value, upper, rows)
        sent.append(sent_u)
        kept.append(kept_u)
    return kept, sent


def send_second(sent, bits):
    return [xor_permute(s, "row", bit) for s, bit in zip(sent, (bits[1], bits[-2]))]


def exchange_last(kept, recv, bits, rows):
    done = []
    for upper in (0, 1):
        value = add_f32(kept[upper], recv[upper])
        for bit in (bits[::-1] if upper else bits)[2:]:
            sent_u, kept_u = halve(value.astype(jnp.bfloat16), upper, rows)
            value = add_f32(kept_u, xor_permute(sent_u, "row", bit))
        done.append(value.astype(jnp.bfloat16))
    return jnp.concatenate(done, axis=0)


def weight_term(near, sums):
    terms, at = [], 0
    for f in [part for parts in near for part in parts]:
        own = sums[at : at + f.shape[0]]
        terms.append(lax.dot_general(f, own, (((0,), (0,)), ((), ())), preferred_element_type=jnp.float32))
        at += f.shape[0]
    return sum(terms[1:], terms[0]).astype(jnp.bfloat16)


def term_kernel(*refs):
    *parts, sums_ref, out_ref, acc_ref = refs
    acc_ref[...] = jnp.zeros_like(acc_ref)
    first = 0
    for part in parts:

        def add_rows(step, carry, part=part, first=first):
            at = pl.multiple_of(step * TERM_ROWS, TERM_ROWS)
            acc_ref[...] += lax.dot_general(
                sums_ref[pl.ds(first + at, TERM_ROWS), :], part[pl.ds(at, TERM_ROWS), :],
                (((0,), (0,)), ((), ())), preferred_element_type=jnp.float32,
            )
            return carry

        lax.fori_loop(0, part.shape[0] // TERM_ROWS, add_rows, 0)
        first += part.shape[0]
    out_ref[...] = acc_ref[...].T.astype(out_ref.dtype)


def weight_term_early(near, sums):
    parts = [part for group in near for part in group]
    shape = (parts[0].shape[1], sums.shape[1])
    return pl.pallas_call(
        term_kernel,
        out_shape=jax.ShapeDtypeStruct(shape, jnp.bfloat16),
        in_specs=[pl.BlockSpec(memory_space=pltpu.VMEM)] * (len(parts) + 1),
        out_specs=pl.BlockSpec(memory_space=pltpu.VMEM),
        scratch_shapes=[pltpu.VMEM(shape[::-1], jnp.float32)],
        compiler_params=pltpu.CompilerParams(vmem_limit_bytes=TERM_BYTES),
        cost_estimate=pl.CostEstimate(flops=0, bytes_accessed=4096, transcendentals=0),
        name="weight_term",
    )(*parts, sums)


def sum_over(term, axis, masks):
    parts = [term] + [xor_permute(term, axis, m) for m in masks]
    return tree_sum([p.astype(jnp.float32) for p in parts])


def body(grad_out, preact, features, weight, tiles, tile_rows, tile_cols, live_counts):
    nodes, width = grad_out.shape
    n_row, n_col = lax.axis_size("row"), lax.axis_size("col")
    row, col = lax.axis_index("row"), lax.axis_index("col")
    slots = tiles.shape[2]
    cw = width // 2
    rows = nodes // 2
    bits = [1 << b for b in range(1, n_row.bit_length() - 1)]
    mid = ((col & 3) == 1) | ((col & 3) == 2)
    even = (row & 1) == 0
    place = jnp.stack([live_counts.reshape(()), row, col, mid.astype(jnp.int32)])
    place, even, grad_out, preact = fence(place, even, grad_out, preact)

    own0, own1 = [
        jnp.where(preact[:, cut] > 0, grad_out[:, cut], jnp.zeros_like(grad_out[:, cut]))
        for cut in (slice(0, cw), slice(cw, width))
    ]
    first0 = gather_first(own0)
    plan0, plan1, slot = make_plans(tile_rows, tile_cols, place, n_row, nodes // SIDE)
    flipped = flip_tiles(slot, tiles.reshape(slots, SIDE, SIDE))
    features, plan0 = fence(features, plan0)
    near = [[features]]
    for bit in bits[:2]:
        near.append([xor_permute(features, "row", bit)])
    own0, own1, first0, plan0, plan1, flipped = fence(own0, own1, first0, plan0, plan1, flipped)

    second0 = gather_second(own0, first0[1], n_col)
    acc0 = spmm(plan0, [[own0], [first0[0]], [first0[1]]], flipped, None, n_row)
    own1, acc0 = fence(own1, acc0)
    first1 = gather_first(own1)
    pieces0 = as_pieces(own0, first0, second0, mid, n_col)
    pieces0, near, acc0 = fence(pieces0, near, acc0)

    near.append([xor_permute(near[1][0][:rows], "row", bits[1]), xor_permute(near[2][0][rows:], "row", bits[0])])
    for bit in bits[2:]:
        near += [[xor_permute(f, "row", bit) for f in parts] for parts in near]
    (both0,) = spmm(plan1, pieces0[FIRST_PIECES:], flipped, acc0, n_row, by_core=True)
    got0 = swap_cores(both0)
    got0, near = fence(got0, near)
    stage0, sums0 = stage_sums(got0[0], got0[1], n_row // 2, rows, at_once=True)
    recv0 = exchange_first(stage0, bits)
    term0 = weight_term_early(near, sums0)
    own1, first1, stage0, term0 = fence(own1, first1, stage0, term0)

    second1 = gather_second(own1, first1[1], n_col)
    pieces1 = as_pieces(own1, first1, second1, mid, n_col)
    acc1 = spmm(plan0, pieces1[:FIRST_PIECES], flipped, None, n_row)
    acc1, recv0 = fence(acc1, recv0)
    rest0, sent0 = exchange_second(stage0, recv0, bits, rows)
    recv0 = send_second(sent0, bits)
    pieces1, acc1 = fence(pieces1, acc1)

    send1, keep1 = spmm(plan1, pieces1[FIRST_PIECES:], flipped, acc1, n_row)
    send1, keep1, rest0, recv0 = fence(send1, keep1, rest0, recv0)

    stage1, sums1 = stage_sums(keep1, xor_permute(send1, "row", 1), n_row // 2, rows, at_once=True)
    term1 = weight_term(near, sums1)
    stage1, term0, term1 = fence(stage1, term0, term1)

    recv1 = exchange_first(stage1, bits)
    theirs, mine = jnp.where(even, term1, term0), jnp.where(even, term0, term1)
    mine = add_f32(mine, xor_permute(theirs, "row", 1)).astype(jnp.bfloat16)
    mine = sum_over(mine, "col", range(1, n_col)).astype(jnp.bfloat16)
    colgrad0 = exchange_last(rest0, recv0, bits, rows)
    recv1, mine, colgrad0 = fence(recv1, mine, colgrad0)

    rest1, sent1 = exchange_second(stage1, recv1, bits, rows)
    rest1, sent1, mine = fence(rest1, sent1, mine)
    recv1 = send_second(sent1, bits)
    others = [xor_permute(mine, "row", m) for m in range(2, n_row, 2)]
    colgrad1 = exchange_last(rest1, recv1, bits, rows)
    colgrad1, mine = fence(colgrad1, mine)
    mine = tree_sum([p.astype(jnp.float32) for p in [mine] + others]).astype(jnp.bfloat16)

    theirs = xor_permute(mine, "row", 1)
    low, high = jnp.where(even, mine, theirs), jnp.where(even, theirs, mine)
    grad_weight = jnp.concatenate([low, high], axis=1).astype(jnp.float32)
    colgrad = jnp.concatenate([colgrad0, colgrad1], axis=1)
    grad_features = lax.dot_general(
        colgrad, weight, (((1,), (1,)), ((), ())), preferred_element_type=jnp.float32
    ).astype(jnp.bfloat16)
    return (grad_features, grad_weight)


def solution(mesh):
    in_specs = (
        P(("row", "col"), None),
        P(("row", "col"), None),
        P(("col", "row"), None),
        P(),
        P("row", "col", None, None, None),
        P("row", "col", None),
        P("row", "col", None),
        P("row", "col"),
    )
    out_specs = (P(("col", "row"), None), P())
    return jax.shard_map(body, mesh=mesh, in_specs=in_specs, out_specs=out_specs, check_vma=False)
```
